512 devices in a mesh: depth: 8 (over z_lo), plan: 64 (over x, y, z_hi, core).
Axes of the slice: x: 4, y: 4, z: 16 (z_hi: 2, z_lo: 8; z = z_hi * 8 + z_lo), core: 2. Of those that a mesh axis runs over, the one named last changes fastest.
Arguments:
- level_set: float32 [16, 1024, 1024], P('depth', 'plan'), may hold values from -4.6 to 4.6
- contrast: float32 [16], P('depth'), may hold values from -2 to 2
Outputs:
- gravity: float32 [1024, 1024], P('plan', 'depth')
The draws below stay inside these ranges and needn't reach their ends.
All inputs are finite; a program needn't handle non-finite values.
Results may differ from the reference program's by a relative error of at most 0.00012.
Values sent between devices are 32-bit elements; how exact they have to be, the bound alone decides.
A program may use at most 64 MiB of HBM per device.

```python
import math
import jax
import jax.numpy as jnp
from jax import lax

NX = 1024
NY = 1024
LAYERS = 16


def body_field(key, bodies, smallest, largest):
    subkeys = jax.random.split(key, 5)
    extent = 0.5 * (NX + NY)
    centre_x = jax.random.uniform(subkeys[0], (bodies,), jnp.float32, 0.0, NX * 1.0)
    centre_y = jax.random.uniform(subkeys[1], (bodies,), jnp.float32, 0.0, NY * 1.0)
    centre_l = jax.random.uniform(subkeys[2], (bodies,), jnp.float32, -1.0, LAYERS + 1.0)
    radius = extent * jnp.exp(jax.random.uniform(subkeys[3], (bodies,), jnp.float32, math.log(smallest), math.log(largest)))
    half_depth = jax.random.uniform(subkeys[4], (bodies,), jnp.float32, 2.0, 2.0 + LAYERS)
    layer_pos = jnp.arange(LAYERS, dtype=jnp.float32)[:, None, None]
    row_pos = (jnp.arange(NX, dtype=jnp.float32) + 0.5)[:, None]
    col_pos = (jnp.arange(NY, dtype=jnp.float32) + 0.5)[None, :]

    def add_body(number, merged):
        plan_gap = jnp.sqrt((row_pos - centre_x[number]) ** 2 + (col_pos - centre_y[number]) ** 2)
        inside = jnp.minimum(radius[number] - plan_gap[None], half_depth[number] - jnp.abs(layer_pos - centre_l[number]))
        return jnp.maximum(merged, inside)
    merged = lax.fori_loop(0, bodies, add_body, jnp.full((LAYERS, NX, NY), -4.0, jnp.float32))
    return jnp.clip(merged, -4.0, 4.0)


def draw_level_set(key, part):
    key = jax.random.fold_in(key, 11)
    shape_key, noise_key = jax.random.split(key)
    smooth = body_field(shape_key, 40, 0.02, 0.12)
    roughness = jnp.clip(0.15 * jax.random.normal(noise_key, (LAYERS, NX, NY), jnp.float32), -0.6, 0.6)
    return smooth + roughness


def block_scale(own_key, dims, cuts, low, high):
    def one(position, shards_of):
        draws = jax.random.uniform(jax.random.fold_in(jax.random.fold_in(own_key, 6), position), (shards_of,), jnp.float32, low / len(cuts), high / len(cuts))
        return jnp.repeat(jnp.exp(draws), dims[position] // shards_of).reshape((-1,) + (1,) * (len(dims) - position - 1))

    factor_of = one(*cuts[0])
    for cut in cuts[1:]:
        factor_of = factor_of * one(*cut)
    return factor_of


def setup_inputs(seed: int = 0) -> dict:
    key_list = jax.random.split(jax.random.key(seed), 3)
    return {
        "level_set": draw_level_set(jax.random.fold_in(key_list[2], 71), 0),
        "contrast": jnp.clip(jax.random.uniform(key_list[1], (LAYERS,), jnp.float32, -2.0, 2.0) * block_scale(key_list[1], (LAYERS,), ((0, 8),), -0.4, 0.0), -2.0, 2.0),
    }


sharpness = 1.0
bend_weight = 0.5
grav_scale = 0.05
top_depth = 0.0
thickness = 1.0

def flux(step):
    return step / jnp.sqrt(1.0 + step * step)

def reference(level_set, contrast):
    padded = jnp.pad(level_set, 1)
    centre = level_set
    bend = flux(padded[2:, 1:-1, 1:-1] - centre) - flux(centre - padded[:-2, 1:-1, 1:-1])
    bend = bend + flux(padded[1:-1, 2:, 1:-1] - centre) - flux(centre - padded[1:-1, :-2, 1:-1])
    bend = bend + flux(padded[1:-1, 1:-1, 2:] - centre) - flux(centre - padded[1:-1, 1:-1, :-2])
    heavy = 0.5 * (1.0 + jnp.tanh(centre / sharpness))
    density = contrast[:, None, None] * heavy + bend_weight * bend
    freq_x = jnp.fft.fftfreq(2 * NX).astype(jnp.float32)
    freq_y = jnp.fft.fftfreq(2 * NY).astype(jnp.float32)
    kappa = 2.0 * math.pi * jnp.sqrt(freq_x[:, None] ** 2 + freq_y[None, :] ** 2)
    depths = top_depth + (jnp.arange(LAYERS, dtype=jnp.int32).astype(jnp.float32) + 0.5) * thickness

    def accumulate(total, pair):
        layer, depth_now = pair
        response = 2.0 * math.pi * grav_scale * thickness * jnp.exp(-depth_now * kappa)
        spectrum = jnp.fft.fft2(layer, s=(2 * NX, 2 * NY))
        field = jnp.real(jnp.fft.ifft2(spectrum * response))[:NX, :NY]
        return (total + field.astype(jnp.float32), None)
    total, _ = lax.scan(accumulate, jnp.zeros((NX, NY), jnp.float32), (density, depths))
    return total
```

```python
import functools
import math

import jax
import jax.numpy as jnp
import ml_dtypes
import numpy as np
from jax import lax
from jax.experimental import pallas as pl
from jax.experimental.pallas import tpu as pltpu
from jax.sharding import PartitionSpec as P

MESH = pl.DeviceIdType.MESH
F32 = jnp.float32
BF16 = jnp.bfloat16

NX = 1024
HALF = NX // 2
LAYERS = 16
DEPTH = 8
PLAN = 64
ROWS = NX // PLAN
GROUP = 32
RING = 16
COEF = 2 * NX // GROUP

bend_weight = 0.5
grav_scale = 0.05
top_depth = 0.0
thickness = 1.0


def basis():
    j = np.arange(HALF, dtype=np.float64)[:, None] + 0.5
    v = np.arange(NX, dtype=np.float64)[None, :]
    v_sin = np.where(v == 0, float(NX), v)
    both = np.stack([np.cos(np.pi * v * j / NX), np.sin(np.pi * v_sin * j / NX)])
    high = both.astype(ml_dtypes.bfloat16)
    low = (both - high.astype(np.float64)).astype(ml_dtypes.bfloat16)
    wide = np.stack([high, low], axis=1)
    return wide, np.ascontiguousarray(np.swapaxes(wide, 2, 3))


def flux(step):
    return step * lax.rsqrt(1.0 + step * step)


def flip(value, axis, size):
    index = lax.broadcasted_iota(jnp.int32, value.shape, axis)
    step = size // 2
    value = pltpu.roll(value, step, axis)
    while step > 1:
        step //= 2
        up = pltpu.roll(value, step, axis)
        down = pltpu.roll(value, size - step, axis)
        value = jnp.where((index & step) != 0, up, down)
    return value


def flip_lanes(value):
    blocks = value.shape[1] // 128
    parts = [flip(value[:, 128 * k : 128 * (k + 1)], 1, 128) for k in reversed(range(blocks))]
    return jnp.concatenate(parts, axis=1) if blocks > 1 else parts[0]


def split(value):
    high = value.astype(BF16)
    low = (value - high.astype(F32)).astype(BF16)
    return high, low


def matmul(a, b):
    return jnp.dot(a, b, preferred_element_type=F32)


def table_right(value, high_table, low_table):
    n = value.shape[0]
    high, low = split(value)
    both = matmul(jnp.concatenate([high, low], axis=0), high_table)
    return both[:n] + both[n:] + matmul(high, low_table)


def kernel(
    ls_hbm, con_hbm, wide_hbm, tall_hbm, out_ref,
    ls_ref, con_ref, wide, tall, zhalo, rsend, rhalo, csend, sbuf, sst, rsp, rsp_first, pst, phi, xsend, cbuf, gsend, gbuf,
    ls_sem, con_sem, wide_sem, tall_sem, hs, hr, cs, cr, xs, xr, gs, gr,
):
    d = lax.axis_index("depth")
    p = lax.axis_index("plan")
    core = p % 2
    zh = (p // 2) % 2
    q = (p // 4) * 2 + core
    z = zh * DEPTH + d
    lower = p < PLAN // 2

    def at_q(other):
        return (d, (other // 2) * 4 + zh * 2 + other % 2)

    def at_z(other):
        return (other % DEPTH, (q // 2) * 4 + (other // DEPTH) * 2 + core)

    ls_copy = pltpu.make_async_copy(ls_hbm, ls_ref, ls_sem)
    con_copy = pltpu.make_async_copy(con_hbm, con_ref, con_sem)
    ls_copy.start()
    con_copy.start()
    wide_copy = pltpu.make_async_copy(wide_hbm, wide, wide_sem)
    tall_copy = pltpu.make_async_copy(tall_hbm, tall, tall_sem)
    wide_copy.start()
    tall_copy.start()

    barrier = pltpu.get_barrier_semaphore()

    def greet(target):
        pl.semaphore_signal(barrier, inc=1, device_id=target, device_id_type=MESH)

    @pl.loop(1, GROUP)
    def _(k):
        greet(at_q((q + k) % GROUP))

    @pl.loop(1, RING)
    def _(k):
        greet(at_z((z + k) % RING))

    outer = jnp.where(core == 0, p - 1, p + 1)

    has_outer = (outer >= 0) & (outer < PLAN)

    @pl.when(has_outer)
    def _():
        greet((d, outer))

    ls_copy.wait()
    con_copy.wait()

    for layer in range(2):
        for k in range(8):
            spot = layer * 8 + k
            rsend[0, spot : spot + 1, :] = ls_ref[layer, 0:1, 128 * k : 128 * (k + 1)]
            rsend[1, spot : spot + 1, :] = ls_ref[layer, ROWS - 1 : ROWS, 128 * k : 128 * (k + 1)]

    pl.semaphore_wait(barrier, GROUP + RING - 2 + has_outer.astype(jnp.int32))

    def halo(source, target, number, device):
        return pltpu.make_async_remote_copy(
            src_ref=source, dst_ref=target, send_sem=hs.at[number], recv_sem=hr.at[number],
            device_id=device, device_id_type=MESH,
        )

    z_up = halo(ls_ref.at[1], zhalo.at[0], 0, (d + 1, p))
    z_down = halo(ls_ref.at[0], zhalo.at[1], 1, (d - 1, p))
    r_up = halo(rsend.at[1], rhalo.at[0], 2, (d, p + 1))
    r_down = halo(rsend.at[0], rhalo.at[1], 3, (d, p - 1))
    has = (d < DEPTH - 1, d > 0, p < PLAN - 1, p > 0)
    gets = (d > 0, d < DEPTH - 1, p > 0, p < PLAN - 1)
    lands = (zhalo.at[0], zhalo.at[1], rhalo.at[0], rhalo.at[1])
    copies = (z_up, z_down, r_up, r_down)
    for copy, there in zip(copies, has):
        pl.when(there)(copy.start)
    for land, comes in zip(lands, gets):

        @pl.when(jnp.logical_not(comes))
        def _(land=land):
            land[...] = jnp.zeros(land.shape, F32)

    for copy, comes in zip(copies, gets):
        pl.when(comes)(copy.wait_recv)
    row_id = lax.broadcasted_iota(jnp.int32, (ROWS, NX), 0)
    col_id = lax.broadcasted_iota(jnp.int32, (ROWS, NX), 1)
    field = [ls_ref[0], ls_ref[1]]
    z_flux = [flux(field[0] - zhalo[0]), flux(field[1] - field[0]), flux(zhalo[1] - field[1])]
    even, odd = [], []
    for layer in range(2):
        centre = field[layer]

        def row_of(side):
            parts = [
                jnp.broadcast_to(rhalo[side, layer * 8 + k : layer * 8 + k + 1, :], (ROWS, 128)) for k in range(8)
            ]
            return jnp.concatenate(parts, axis=1)

        bend = z_flux[layer + 1] - z_flux[layer]
        above = jnp.where(row_id == 0, row_of(0), pltpu.roll(centre, 1, 0))
        row_flux = flux(centre - above)
        last = flux(row_of(1) - centre)
        bend = bend + jnp.where(row_id == ROWS - 1, last, pltpu.roll(row_flux, ROWS - 1, 0)) - row_flux
        before = jnp.where(col_id == 0, 0.0, pltpu.roll(centre, 1, 1))
        col_flux = flux(centre - before)
        bend = bend + jnp.where(col_id == NX - 1, flux(-centre), pltpu.roll(col_flux, NX - 1, 1)) - col_flux
        density = con_ref[layer] * (0.5 * (1.0 + jnp.tanh(centre))) + bend_weight * bend
        density = jnp.where(lower, flip(density, 0, ROWS), density)
        left = flip_lanes(density[:, :HALF])
        right = density[:, HALF:]
        even.append(right + left)
        odd.append(right - left)

    block = jnp.where(lower, PLAN // 2 - 1 - p, p - PLAN // 2)
    half_lane = lax.broadcasted_iota(jnp.int32, (ROWS, 128), 1) < COEF
    wide_copy.wait()

    def send_coef(other):
        return pltpu.make_async_remote_copy(
            src_ref=csend.at[other], dst_ref=sbuf.at[block], send_sem=cs, recv_sem=cr,
            device_id=at_q(other), device_id_type=MESH,
        )

    for kind, pair in enumerate((even, odd)):
        coef = table_right(jnp.concatenate(pair, axis=0), wide[kind, 0], wide[kind, 1])
        for m in range(8):
            first = coef[:ROWS, 128 * m : 128 * (m + 1)]
            second = coef[ROWS:, 128 * m : 128 * (m + 1)]
            spot = kind * 16 + 2 * m
            csend[spot] = jnp.where(half_lane, first, pltpu.roll(second, COEF, 1))
            csend[spot + 1] = jnp.where(half_lane, pltpu.roll(first, COEF, 1), second)

        @pl.loop(0, 16)
        def _(k, kind=kind):
            other = kind * 16 + (q + k) % 16

            @pl.when(other != q)
            def _():
                send_coef(other).start()

    def respond(first, count, is_sin):
        lane = lax.broadcasted_iota(jnp.int32, (count, 128), 1)
        row = lax.broadcasted_iota(jnp.int32, (count, 128), 0) + first
        place = (q % (GROUP // 2)) * COEF + lane % COEF
        v = jnp.where((place == 0) & (q >= GROUP // 2), NX, place).astype(F32)
        scale = 2.0 * math.pi * grav_scale * thickness / (4.0 * NX * NX)
        weight = jnp.where(place == 0, scale, 2.0 * scale) * jnp.where(row == 0, 1.0, 2.0)
        layer = (2 * d + lane // COEF).astype(F32)
        rate = (top_depth + (layer + 0.5) * thickness) * (-2.0 * math.pi / (2 * NX))
        u = (jnp.where(row == 0, NX, row) if is_sin else row).astype(F32)
        return jnp.exp(jnp.sqrt(u * u + v * v) * rate) * weight

    @pl.loop(0, NX // 256)
    def _(k):
        rsp[pl.ds(pl.multiple_of(256 * k, 256), 256), :] = respond(256 * k, 256, False)

    rsp_first[...] = respond(0, 8, True)

    sbuf[block] = csend[q]
    pltpu.make_async_copy(sbuf.at[pl.ds(0, GROUP - 1)], sbuf.at[pl.ds(0, GROUP - 1)], cr).wait()

    for b in range(GROUP):
        value = sbuf[b]
        high, low = split(value)
        sst[0, ROWS * b : ROWS * (b + 1), :128] = high
        sst[0, ROWS * b : ROWS * (b + 1), 128:] = low
        sign = jnp.where((b // 2) % 2 == zh, 1.0, -1.0)
        high, low = split(value * sign)
        sst[1, ROWS * b : ROWS * (b + 1), :128] = high
        sst[1, ROWS * b : ROWS * (b + 1), 128:] = low
    tall_copy.wait()
    step = 256
    wide_half = lax.broadcasted_iota(jnp.int32, (step, 128), 1) < COEF
    for kind in range(2):

        @pl.loop(0, NX // step)
        def _(k, kind=kind):
            here = pl.ds(pl.multiple_of(k * step, step), step)
            both = matmul(tall[kind, 0, here, :], sst[kind])
            value = both[:, :128] + both[:, 128:] + matmul(tall[kind, 1, here, :], sst[kind, :, :128])
            factor = rsp[here, :]
            if kind == 1:
                fixed = jnp.concatenate([rsp_first[...], factor[8:]], axis=0)
                factor = jnp.where(k == 0, fixed, factor)
            value = value * factor
            value = value + pltpu.roll(value, COEF, 1)
            high = value.astype(BF16).astype(F32)
            pst[kind, here, :] = jnp.where(wide_half, high, value - high).astype(BF16)
            phi[kind, here, :] = jnp.where(wide_half, high, 0.0).astype(BF16)

    def send_rows(other):
        return pltpu.make_async_remote_copy(
            src_ref=xsend.at[other], dst_ref=cbuf.at[q], send_sem=xs, recv_sem=xr,
            device_id=at_q(other), device_id_type=MESH,
        )

    for part in range(2):
        cut = slice(256 * part, 256 * (part + 1))
        parity = []
        for kind in range(2):
            value = matmul(wide[kind, 0, cut, :], pst[kind]) + matmul(wide[kind, 1, cut, :], phi[kind])
            parity.append(value + pltpu.roll(value, COEF, 1))
        plus = parity[0] + parity[1]
        minus = parity[0] - parity[1]
        for g in range(4):
            up = [plus[ROWS * (4 * g + n) : ROWS * (4 * g + n + 1)] for n in range(4)]
            down = [minus[ROWS * (4 * g + n) : ROWS * (4 * g + n + 1)] for n in range(4)]
            chunk = 4 * part + g
            xsend[2 * (8 + chunk)] = jnp.where(half_lane, up[0], up[2])
            xsend[2 * (8 + chunk) + 1] = jnp.where(half_lane, up[1], up[3])
            xsend[2 * (7 - chunk)] = jnp.where(half_lane, down[3], down[1])
            xsend[2 * (7 - chunk) + 1] = jnp.where(half_lane, down[2], down[0])

        @pl.loop(0, 16)
        def _(k, part=part):
            if part == 0:
                other = 8 + (q + k) % 16
            else:
                other = (24 + (q + k) % 16) % GROUP

            @pl.when(other != q)
            def _():
                send_rows(other).start()

    cbuf[q] = xsend[q]
    pltpu.make_async_copy(cbuf.at[pl.ds(0, GROUP - 1)], cbuf.at[pl.ds(0, GROUP - 1)], xr).wait()

    parity = []
    for kind in range(2):
        tops, bottoms = [], []
        for m in range(8):
            first, second = cbuf[kind * 16 + 2 * m], cbuf[kind * 16 + 2 * m + 1]
            tops.append(jnp.where(half_lane, first, pltpu.roll(second, COEF, 1)))
            bottoms.append(jnp.where(half_lane, pltpu.roll(first, COEF, 1), second))
        value = jnp.concatenate([jnp.concatenate(tops, axis=1), jnp.concatenate(bottoms, axis=1)], axis=0)
        parity.append(table_right(value, tall[kind, 0], tall[kind, 1]))
    plus = parity[0] + parity[1]
    minus = parity[0] - parity[1]
    for other in range(RING):
        rows = slice(ROWS * (other // DEPTH), ROWS * (other // DEPTH + 1))
        col = other % DEPTH
        if col >= 4:
            gsend[other] = plus[rows, 128 * (col - 4) : 128 * (col - 3)]
        else:
            gsend[other] = minus[rows, 128 * (3 - col) : 128 * (4 - col)]

    def send_field(other):
        return pltpu.make_async_remote_copy(
            src_ref=gsend.at[other], dst_ref=gbuf.at[z], send_sem=gs, recv_sem=gr,
            device_id=at_z(other), device_id_type=MESH,
        )

    @pl.loop(0, RING - 1)
    def _(k):
        send_field((z + 8 + ((k + 1) // 2) * (1 - 2 * (k % 2)) + RING) % RING).start()

    gbuf[z] = gsend[z]
    pltpu.make_async_copy(gbuf.at[pl.ds(0, RING - 1)], gbuf.at[pl.ds(0, RING - 1)], gr).wait()
    total = gbuf[0]
    for other in range(1, RING):
        total = total + gbuf[other]
    total = jnp.where(d < DEPTH // 2, flip(total, 1, 128), total)
    out_ref[...] = jnp.where(lower, flip(total, 0, ROWS), total)

    for copy, there in zip(copies, has):
        pl.when(there)(copy.wait_send)
    pltpu.make_async_copy(csend.at[pl.ds(0, GROUP - 1)], csend.at[pl.ds(0, GROUP - 1)], cs).wait()
    pltpu.make_async_copy(xsend.at[pl.ds(0, GROUP - 1)], xsend.at[pl.ds(0, GROUP - 1)], xs).wait()
    pltpu.make_async_copy(gsend.at[pl.ds(0, RING - 1)], gsend.at[pl.ds(0, RING - 1)], gs).wait()


def solution(mesh):
    wide, tall = basis()

    def step(level_set, contrast):
        vmem = pl.BlockSpec(memory_space=pltpu.VMEM)
        anywhere = pl.BlockSpec(memory_space=pl.ANY)
        dma = pltpu.SemaphoreType.DMA
        return pl.pallas_call(
            kernel,
            out_shape=jax.ShapeDtypeStruct((ROWS, 128), F32),
            in_specs=[anywhere] * 4,
            out_specs=vmem,
            scratch_shapes=[
                pltpu.VMEM((2, ROWS, NX), F32),
                pltpu.SMEM((2,), F32),
                pltpu.VMEM((2, 2, HALF, NX), BF16),
                pltpu.VMEM((2, 2, NX, HALF), BF16),
                pltpu.VMEM((2, ROWS, NX), F32),
                pltpu.VMEM((2, 16, 128), F32),
                pltpu.VMEM((2, 16, 128), F32),
                pltpu.VMEM((GROUP, ROWS, 128), F32),
                pltpu.VMEM((GROUP, ROWS, 128), F32),
                pltpu.VMEM((2, HALF, 256), BF16),
                pltpu.VMEM((NX, 128), F32),
                pltpu.VMEM((8, 128), F32),
                pltpu.VMEM((2, NX, 128), BF16),
                pltpu.VMEM((2, NX, 128), BF16),
                pltpu.VMEM((GROUP, ROWS, 128), F32),
                pltpu.VMEM((GROUP, ROWS, 128), F32),
                pltpu.VMEM((RING, ROWS, 128), F32),
                pltpu.VMEM((RING, ROWS, 128), F32),
                dma(()), dma(()), dma(()), dma(()), dma((4,)), dma((4,)),
                dma(()), dma(()), dma(()), dma(()), dma(()), dma(()),
            ],
            compiler_params=pltpu.CompilerParams(
                collective_id=0, has_side_effects=True, vmem_limit_bytes=63 * 1024 * 1024
            ),
        )(level_set, contrast, jnp.asarray(wide), jnp.asarray(tall))

    return jax.shard_map(
        step,
        mesh=mesh,
        in_specs=(P("depth", "plan", None), P("depth")),
        out_specs=P("plan", "depth"),
        check_vma=False,
    )
```

```python
import functools
import math

import jax
import jax.numpy as jnp
import ml_dtypes
import numpy as np
from jax import lax
from jax.experimental import pallas as pl
from jax.experimental.pallas import tpu as pltpu
from jax.sharding import PartitionSpec as P

MESH = pl.DeviceIdType.MESH
F32 = jnp.float32
BF16 = jnp.bfloat16

NX = 1024
HALF = NX // 2
LAYERS = 16
DEPTH = 8
PLAN = 64
ROWS = NX // PLAN
GROUP = 32
RING = 16
COEF = 2 * NX // GROUP

bend_weight = 0.5
grav_scale = 0.05
top_depth = 0.0
thickness = 1.0


def basis():
    j = np.arange(HALF, dtype=np.float64)[:, None] + 0.5
    v = np.arange(NX, dtype=np.float64)[None, :]
    v_sin = np.where(v == 0, float(NX), v)
    both = np.stack([np.cos(np.pi * v * j / NX), np.sin(np.pi * v_sin * j / NX)])
    high = both.astype(ml_dtypes.bfloat16)
    low = (both - high.astype(np.float64)).astype(ml_dtypes.bfloat16)
    wide = np.stack([high, low], axis=1)
    return wide, np.ascontiguousarray(np.swapaxes(wide, 2, 3))


def flux(step):
    return step * lax.rsqrt(1.0 + step * step)


def flip(value, axis, size):
    index = lax.broadcasted_iota(jnp.int32, value.shape, axis)
    step = size // 2
    value = pltpu.roll(value, step, axis)
    while step > 1:
        step //= 2
        up = pltpu.roll(value, step, axis)
        down = pltpu.roll(value, size - step, axis)
        value = jnp.where((index & step) != 0, up, down)
    return value


def flip_lanes(value):
    blocks = value.shape[1] // 128
    parts = [flip(value[:, 128 * k : 128 * (k + 1)], 1, 128) for k in reversed(range(blocks))]
    return jnp.concatenate(parts, axis=1) if blocks > 1 else parts[0]


def split(value):
    high = value.astype(BF16)
    low = (value - high.astype(F32)).astype(BF16)
    return high, low


def matmul(a, b):
    return jnp.dot(a, b, preferred_element_type=F32)


def table_right(value, high_table, low_table):
    n = value.shape[0]
    high, low = split(value)
    both = matmul(jnp.concatenate([high, low], axis=0), high_table)
    return both[:n] + both[n:] + matmul(high, low_table)


def kernel(
    ls_hbm, con_hbm, wide_hbm, tall_hbm, out_ref,
    ls_ref, con_ref, wide, tall, zhalo, rsend, rhalo, csend, sbuf, sst, rsp, rsp_first, pst, phi, xsend, cbuf, gsend, gbuf,
    ls_sem, con_sem, wide_sem, tall_sem, hs, hr, cs, cr, xs, xr, gs, gr,
):
    d = lax.axis_index("depth")
    p = lax.axis_index("plan")
    core = lax.rem(p, 2)
    zh = lax.rem(lax.div(p, 2), 2)
    q = lax.div(p, 4) * 2 + core
    z = zh * DEPTH + d
    lower = p < PLAN // 2

    def at_q(other):
        return (d, lax.div(other, 2) * 4 + zh * 2 + lax.rem(other, 2))

    def at_z(other):
        return (lax.rem(other, DEPTH), p + 2 * (lax.div(other, DEPTH) - zh))

    ls_copy = pltpu.make_async_copy(ls_hbm, ls_ref, ls_sem)
    con_copy = pltpu.make_async_copy(con_hbm, con_ref, con_sem)
    ls_copy.start()
    con_copy.start()
    wide_copy = pltpu.make_async_copy(wide_hbm, wide, wide_sem)
    tall_copy = pltpu.make_async_copy(tall_hbm, tall, tall_sem)
    wide_copy.start()
    tall_copy.start()

    barrier = pltpu.get_barrier_semaphore()

    def greet(target):
        pl.semaphore_signal(barrier, inc=1, device_id=target, device_id_type=MESH)

    has = (d < DEPTH - 1, d > 0, p < PLAN - 1, p > 0)
    gets = (d > 0, d < DEPTH - 1, p > 0, p < PLAN - 1)
    pl.when(has[0])(lambda: greet((d + 1, p)))
    pl.when(has[1])(lambda: greet((d - 1, p)))
    pl.when(has[2])(lambda: greet((d, p + 1)))
    pl.when(has[3])(lambda: greet((d, p - 1)))
    outer = jnp.where(core == 0, p - 1, p + 1)
    has_outer = (outer >= 0) & (outer < PLAN)
    buddy = p + 1 - 2 * core
    for other in range(GROUP):
        target = (other // 2) * 4 + other % 2 + zh * 2
        pl.when((target != p) & (target != buddy))(lambda target=target: greet((d, target)))
    for other in range(RING):
        row = other // DEPTH
        far = (row != zh) | (other % DEPTH > d + 1) | (other % DEPTH < d - 1)
        pl.when(far)(lambda other=other, row=row: greet((other % DEPTH, p + 2 * (row - zh))))

    ls_copy.wait()
    con_copy.wait()

    for layer in range(2):
        for k in range(8):
            spot = layer * 8 + k
            rsend[0, spot : spot + 1, :] = ls_ref[layer, 0:1, 128 * k : 128 * (k + 1)]
            rsend[1, spot : spot + 1, :] = ls_ref[layer, ROWS - 1 : ROWS, 128 * k : 128 * (k + 1)]

    pl.semaphore_wait(barrier, GROUP + RING - 2 + has_outer.astype(jnp.int32))

    def halo(source, target, number, device):
        return pltpu.make_async_remote_copy(
            src_ref=source, dst_ref=target, send_sem=hs.at[number], recv_sem=hr.at[number],
            device_id=device, device_id_type=MESH,
        )

    z_up = halo(ls_ref.at[1], zhalo.at[0], 0, (d + 1, p))
    z_down = halo(ls_ref.at[0], zhalo.at[1], 1, (d - 1, p))
    r_up = halo(rsend.at[1], rhalo.at[0], 2, (d, p + 1))
    r_down = halo(rsend.at[0], rhalo.at[1], 3, (d, p - 1))
    lands = (zhalo.at[0], zhalo.at[1], rhalo.at[0], rhalo.at[1])
    copies = (z_up, z_down, r_up, r_down)
    for copy, there in zip(copies, has):
        pl.when(there)(copy.start)
    for land, comes in zip(lands, gets):

        @pl.when(jnp.logical_not(comes))
        def _(land=land):
            land[...] = jnp.zeros(land.shape, F32)

    for copy, comes in zip(copies, gets):
        pl.when(comes)(copy.wait_recv)
    row_id = lax.broadcasted_iota(jnp.int32, (ROWS, NX), 0)
    col_id = lax.broadcasted_iota(jnp.int32, (ROWS, NX), 1)
    field = [ls_ref[0], ls_ref[1]]
    z_flux = [flux(field[0] - zhalo[0]), flux(field[1] - field[0]), flux(zhalo[1] - field[1])]
    even, odd = [], []
    for layer in range(2):
        centre = field[layer]

        def row_of(side):
            parts = [
                jnp.broadcast_to(rhalo[side, layer * 8 + k : layer * 8 + k + 1, :], (ROWS, 128)) for k in range(8)
            ]
            return jnp.concatenate(parts, axis=1)

        bend = z_flux[layer + 1] - z_flux[layer]
        above = jnp.where(row_id == 0, row_of(0), pltpu.roll(centre, 1, 0))
        row_flux = flux(centre - above)
        last = flux(row_of(1) - centre)
        bend = bend + jnp.where(row_id == ROWS - 1, last, pltpu.roll(row_flux, ROWS - 1, 0)) - row_flux
        before = jnp.where(col_id == 0, 0.0, pltpu.roll(centre, 1, 1))
        col_flux = flux(centre - before)
        bend = bend + jnp.where(col_id == NX - 1, flux(-centre), pltpu.roll(col_flux, NX - 1, 1)) - col_flux
        density = con_ref[layer] * (0.5 * (1.0 + jnp.tanh(centre))) + bend_weight * bend
        density = jnp.where(lower, flip(density, 0, ROWS), density)
        left = flip_lanes(density[:, :HALF])
        right = density[:, HALF:]
        even.append(right + left)
        odd.append(right - left)

    block = jnp.where(lower, PLAN // 2 - 1 - p, p - PLAN // 2)
    half_lane = lax.broadcasted_iota(jnp.int32, (ROWS, 128), 1) < COEF
    wide_copy.wait()

    def send_coef(other):
        return pltpu.make_async_remote_copy(
            src_ref=csend.at[other], dst_ref=sbuf.at[block], send_sem=cs, recv_sem=cr,
            device_id=at_q(other), device_id_type=MESH,
        )

    for kind, pair in enumerate((even, odd)):
        coef = table_right(jnp.concatenate(pair, axis=0), wide[kind, 0], wide[kind, 1])
        for m in range(8):
            first = coef[:ROWS, 128 * m : 128 * (m + 1)]
            second = coef[ROWS:, 128 * m : 128 * (m + 1)]
            spot = kind * 16 + 2 * m
            csend[spot] = jnp.where(half_lane, first, pltpu.roll(second, COEF, 1))
            csend[spot + 1] = jnp.where(half_lane, pltpu.roll(first, COEF, 1), second)

        @pl.loop(0, 16)
        def _(k, kind=kind):
            other = kind * 16 + lax.rem(q + k, 16)

            @pl.when(other != q)
            def _():
                send_coef(other).start()

    def respond(first, count, is_sin):
        lane = lax.broadcasted_iota(jnp.int32, (count, 128), 1)
        row = lax.broadcasted_iota(jnp.int32, (count, 128), 0) + first
        place = (q % (GROUP // 2)) * COEF + lane % COEF
        v = jnp.where((place == 0) & (q >= GROUP // 2), NX, place).astype(F32)
        scale = 2.0 * math.pi * grav_scale * thickness / (4.0 * NX * NX)
        weight = jnp.where(place == 0, scale, 2.0 * scale) * jnp.where(row == 0, 1.0, 2.0)
        layer = (2 * d + lane // COEF).astype(F32)
        rate = (top_depth + (layer + 0.5) * thickness) * (-2.0 * math.pi / (2 * NX))
        u = (jnp.where(row == 0, NX, row) if is_sin else row).astype(F32)
        return jnp.exp(jnp.sqrt(u * u + v * v) * rate) * weight

    @pl.loop(0, NX // 256)
    def _(k):
        rsp[pl.ds(pl.multiple_of(256 * k, 256), 256), :] = respond(256 * k, 256, False)

    rsp_first[...] = respond(0, 8, True)

    sbuf[block] = csend[q]
    pltpu.make_async_copy(sbuf.at[pl.ds(0, GROUP - 1)], sbuf.at[pl.ds(0, GROUP - 1)], cr).wait()

    for b in range(GROUP):
        value = sbuf[b]
        high, low = split(value)
        sst[0, ROWS * b : ROWS * (b + 1), :128] = high
        sst[0, ROWS * b : ROWS * (b + 1), 128:] = low
        sign = jnp.where((b // 2) % 2 == zh, 1.0, -1.0)
        high, low = split(value * sign)
        sst[1, ROWS * b : ROWS * (b + 1), :128] = high
        sst[1, ROWS * b : ROWS * (b + 1), 128:] = low
    tall_copy.wait()
    step = 256
    wide_half = lax.broadcasted_iota(jnp.int32, (step, 128), 1) < COEF
    for kind in range(2):

        @pl.loop(0, NX // step)
        def _(k, kind=kind):
            here = pl.ds(pl.multiple_of(k * step, step), step)
            both = matmul(tall[kind, 0, here, :], sst[kind])
            value = both[:, :128] + both[:, 128:] + matmul(tall[kind, 1, here, :], sst[kind, :, :128])
            factor = rsp[here, :]
            if kind == 1:
                fixed = jnp.concatenate([rsp_first[...], factor[8:]], axis=0)
                factor = jnp.where(k == 0, fixed, factor)
            value = value * factor
            value = value + pltpu.roll(value, COEF, 1)
            high = value.astype(BF16).astype(F32)
            pst[kind, here, :] = jnp.where(wide_half, high, value - high).astype(BF16)
            phi[kind, here, :] = jnp.where(wide_half, high, 0.0).astype(BF16)

    def send_rows(other):
        return pltpu.make_async_remote_copy(
            src_ref=xsend.at[other], dst_ref=cbuf.at[q], send_sem=xs, recv_sem=xr,
            device_id=at_q(other), device_id_type=MESH,
        )

    for part in range(2):
        cut = slice(256 * part, 256 * (part + 1))
        parity = []
        for kind in range(2):
            value = matmul(wide[kind, 0, cut, :], pst[kind]) + matmul(wide[kind, 1, cut, :], phi[kind])
            parity.append(value + pltpu.roll(value, COEF, 1))
        plus = parity[0] + parity[1]
        minus = parity[0] - parity[1]
        for g in range(4):
            up = [plus[ROWS * (4 * g + n) : ROWS * (4 * g + n + 1)] for n in range(4)]
            down = [minus[ROWS * (4 * g + n) : ROWS * (4 * g + n + 1)] for n in range(4)]
            chunk = 4 * part + g
            xsend[2 * (8 + chunk)] = jnp.where(half_lane, up[0], up[2])
            xsend[2 * (8 + chunk) + 1] = jnp.where(half_lane, up[1], up[3])
            xsend[2 * (7 - chunk)] = jnp.where(half_lane, down[3], down[1])
            xsend[2 * (7 - chunk) + 1] = jnp.where(half_lane, down[2], down[0])

        @pl.loop(0, 16)
        def _(k, part=part):
            if part == 0:
                other = 8 + lax.rem(q + k, 16)
            else:
                other = lax.rem(24 + lax.rem(q + k, 16), GROUP)

            @pl.when(other != q)
            def _():
                send_rows(other).start()

    cbuf[q] = xsend[q]
    pltpu.make_async_copy(cbuf.at[pl.ds(0, GROUP - 1)], cbuf.at[pl.ds(0, GROUP - 1)], xr).wait()

    parity = []
    for kind in range(2):
        tops, bottoms = [], []
        for m in range(8):
            first, second = cbuf[kind * 16 + 2 * m], cbuf[kind * 16 + 2 * m + 1]
            tops.append(jnp.where(half_lane, first, pltpu.roll(second, COEF, 1)))
            bottoms.append(jnp.where(half_lane, pltpu.roll(first, COEF, 1), second))
        value = jnp.concatenate([jnp.concatenate(tops, axis=1), jnp.concatenate(bottoms, axis=1)], axis=0)
        parity.append(table_right(value, tall[kind, 0], tall[kind, 1]))
    plus = parity[0] + parity[1]
    minus = parity[0] - parity[1]
    for other in range(RING):
        rows = slice(ROWS * (other // DEPTH), ROWS * (other // DEPTH + 1))
        col = other % DEPTH
        if col >= 4:
            gsend[other] = plus[rows, 128 * (col - 4) : 128 * (col - 3)]
        else:
            gsend[other] = minus[rows, 128 * (3 - col) : 128 * (4 - col)]

    def send_field(other):
        return pltpu.make_async_remote_copy(
            src_ref=gsend.at[other], dst_ref=gbuf.at[z], send_sem=gs, recv_sem=gr,
            device_id=at_z(other), device_id_type=MESH,
        )

    @pl.loop(0, RING - 1)
    def _(k):
        send_field(lax.rem(z + 8 + lax.div(k + 1, 2) * (1 - 2 * lax.rem(k, 2)) + RING, RING)).start()

    gbuf[z] = gsend[z]
    pltpu.make_async_copy(gbuf.at[pl.ds(0, RING - 1)], gbuf.at[pl.ds(0, RING - 1)], gr).wait()
    total = gbuf[0]
    for other in range(1, RING):
        total = total + gbuf[other]
    total = jnp.where(d < DEPTH // 2, flip(total, 1, 128), total)
    out_ref[...] = jnp.where(lower, flip(total, 0, ROWS), total)

    for copy, there in zip(copies, has):
        pl.when(there)(copy.wait_send)
    pltpu.make_async_copy(csend.at[pl.ds(0, GROUP - 1)], csend.at[pl.ds(0, GROUP - 1)], cs).wait()
    pltpu.make_async_copy(xsend.at[pl.ds(0, GROUP - 1)], xsend.at[pl.ds(0, GROUP - 1)], xs).wait()
    pltpu.make_async_copy(gsend.at[pl.ds(0, RING - 1)], gsend.at[pl.ds(0, RING - 1)], gs).wait()


def solution(mesh):
    wide, tall = basis()

    def step(level_set, contrast):
        vmem = pl.BlockSpec(memory_space=pltpu.VMEM)
        anywhere = pl.BlockSpec(memory_space=pl.ANY)
        dma = pltpu.SemaphoreType.DMA
        return pl.pallas_call(
            kernel,
            out_shape=jax.ShapeDtypeStruct((ROWS, 128), F32),
            in_specs=[anywhere] * 4,
            out_specs=vmem,
            scratch_shapes=[
                pltpu.VMEM((2, ROWS, NX), F32),
                pltpu.SMEM((2,), F32),
                pltpu.VMEM((2, 2, HALF, NX), BF16),
                pltpu.VMEM((2, 2, NX, HALF), BF16),
                pltpu.VMEM((2, ROWS, NX), F32),
                pltpu.VMEM((2, 16, 128), F32),
                pltpu.VMEM((2, 16, 128), F32),
                pltpu.VMEM((GROUP, ROWS, 128), F32),
                pltpu.VMEM((GROUP, ROWS, 128), F32),
                pltpu.VMEM((2, HALF, 256), BF16),
                pltpu.VMEM((NX, 128), F32),
                pltpu.VMEM((8, 128), F32),
                pltpu.VMEM((2, NX, 128), BF16),
                pltpu.VMEM((2, NX, 128), BF16),
                pltpu.VMEM((GROUP, ROWS, 128), F32),
                pltpu.VMEM((GROUP, ROWS, 128), F32),
                pltpu.VMEM((RING, ROWS, 128), F32),
                pltpu.VMEM((RING, ROWS, 128), F32),
                dma(()), dma(()), dma(()), dma(()), dma((4,)), dma((4,)),
                dma(()), dma(()), dma(()), dma(()), dma(()), dma(()),
            ],
            compiler_params=pltpu.CompilerParams(
                collective_id=0, has_side_effects=True, vmem_limit_bytes=63 * 1024 * 1024
            ),
        )(level_set, contrast, jnp.asarray(wide), jnp.asarray(tall))

    return jax.shard_map(
        step,
        mesh=mesh,
        in_specs=(P("depth", "plan", None), P("depth")),
        out_specs=P("plan", "depth"),
        check_vma=False,
    )
```

```python
import functools
import math

import jax
import jax.numpy as jnp
import ml_dtypes
import numpy as np
from jax import lax
from jax.experimental import pallas as pl
from jax.experimental.pallas import tpu as pltpu
from jax.sharding import PartitionSpec as P

MESH = pl.DeviceIdType.MESH
F32 = jnp.float32
BF16 = jnp.bfloat16

NX = 1024
HALF = NX // 2
LAYERS = 16
DEPTH = 8
PLAN = 64
ROWS = NX // PLAN
GROUP = 32
RING = 16
COEF = 2 * NX // GROUP

bend_weight = 0.5
grav_scale = 0.05
top_depth = 0.0
thickness = 1.0


def basis():
    j = np.arange(HALF, dtype=np.float64)[:, None] + 0.5
    v = np.arange(NX, dtype=np.float64)[None, :]
    v_sin = np.where(v == 0, float(NX), v)
    both = np.stack([np.cos(np.pi * v * j / NX), np.sin(np.pi * v_sin * j / NX)])
    high = both.astype(ml_dtypes.bfloat16)
    low = (both - high.astype(np.float64)).astype(ml_dtypes.bfloat16)
    wide = np.stack([high, low], axis=1)
    tall = np.swapaxes(wide, 2, 3)
    order = np.arange(HALF).reshape(GROUP, 2, ROWS // 2).transpose(1, 0, 2).reshape(-1)
    return wide, np.ascontiguousarray(tall[..., order]), np.ascontiguousarray(tall)


def flux(step):
    return step * lax.rsqrt(1.0 + step * step)


def flip(value, axis, size):
    index = lax.broadcasted_iota(jnp.int32, value.shape, axis)
    step = size // 2
    value = pltpu.roll(value, step, axis)
    while step > 1:
        step //= 2
        up = pltpu.roll(value, step, axis)
        down = pltpu.roll(value, size - step, axis)
        value = jnp.where((index & step) != 0, up, down)
    return value


def flip_lanes(value):
    blocks = value.shape[1] // 128
    parts = [flip(value[:, 128 * k : 128 * (k + 1)], 1, 128) for k in reversed(range(blocks))]
    return jnp.concatenate(parts, axis=1) if blocks > 1 else parts[0]


def split(value):
    high = value.astype(BF16)
    low = (value - high.astype(F32)).astype(BF16)
    return high, low


def matmul(a, b):
    return jnp.dot(a, b, preferred_element_type=F32)


def table_right(value, high_table, low_table):
    n = value.shape[0]
    high, low = split(value)
    both = matmul(jnp.concatenate([high, low], axis=0), high_table)
    return both[:n] + both[n:] + matmul(high, low_table)


def kernel(
    ls_hbm, con_hbm, wide_hbm, mixed_hbm, tall_hbm, out_ref,
    ls_ref, con_ref, wide, mixed, tall, zhalo, rsend, rhalo, csend, sbuf, sst, acc, rsp, rsp_first, pst, phi, xsend, cbuf, gsend, gbuf,
    ls_sem, con_sem, wide_sem, mixed_sem, tall_sem, hs, hr, cs, cr, xs, xr, gs, gr,
):
    d = lax.axis_index("depth")
    p = lax.axis_index("plan")
    core = lax.rem(p, 2)
    zh = lax.rem(lax.div(p, 2), 2)
    q = lax.div(p, 4) * 2 + core
    z = zh * DEPTH + d
    lower = p < PLAN // 2

    def at_q(other):
        return (d, lax.div(other, 2) * 4 + zh * 2 + lax.rem(other, 2))

    def at_z(other):
        return (lax.rem(other, DEPTH), p + 2 * (lax.div(other, DEPTH) - zh))

    ls_copy = pltpu.make_async_copy(ls_hbm, ls_ref, ls_sem)
    con_copy = pltpu.make_async_copy(con_hbm, con_ref, con_sem)
    ls_copy.start()
    con_copy.start()
    wide_copy = pltpu.make_async_copy(wide_hbm, wide, wide_sem)
    mixed_copy = pltpu.make_async_copy(mixed_hbm, mixed, mixed_sem)
    tall_copy = pltpu.make_async_copy(tall_hbm, tall, tall_sem)
    wide_copy.start()

    barrier = pltpu.get_barrier_semaphore()

    def greet(target):
        pl.semaphore_signal(barrier, inc=1, device_id=target, device_id_type=MESH)

    has = (d < DEPTH - 1, d > 0, p < PLAN - 1, p > 0)
    gets = (d > 0, d < DEPTH - 1, p > 0, p < PLAN - 1)
    pl.when(has[0])(lambda: greet((d + 1, p)))
    pl.when(has[1])(lambda: greet((d - 1, p)))
    pl.when(has[2])(lambda: greet((d, p + 1)))
    pl.when(has[3])(lambda: greet((d, p - 1)))
    outer = jnp.where(core == 0, p - 1, p + 1)
    has_outer = (outer >= 0) & (outer < PLAN)
    buddy = p + 1 - 2 * core
    for other in range(GROUP):
        target = (other // 2) * 4 + other % 2 + zh * 2
        pl.when((target != p) & (target != buddy))(lambda target=target: greet((d, target)))
    for other in range(RING):
        row = other // DEPTH
        far = (row != zh) | (other % DEPTH > d + 1) | (other % DEPTH < d - 1)
        pl.when(far)(lambda other=other, row=row: greet((other % DEPTH, p + 2 * (row - zh))))

    ls_copy.wait()
    con_copy.wait()

    for layer in range(2):
        for k in range(8):
            spot = layer * 8 + k
            rsend[0, spot : spot + 1, :] = ls_ref[layer, 0:1, 128 * k : 128 * (k + 1)]
            rsend[1, spot : spot + 1, :] = ls_ref[layer, ROWS - 1 : ROWS, 128 * k : 128 * (k + 1)]

    pl.semaphore_wait(barrier, GROUP + RING - 2 + has_outer.astype(jnp.int32))

    def halo(source, target, number, device):
        return pltpu.make_async_remote_copy(
            src_ref=source, dst_ref=target, send_sem=hs.at[number], recv_sem=hr.at[number],
            device_id=device, device_id_type=MESH,
        )

    z_up = halo(ls_ref.at[1], zhalo.at[0], 0, (d + 1, p))
    z_down = halo(ls_ref.at[0], zhalo.at[1], 1, (d - 1, p))
    r_up = halo(rsend.at[1], rhalo.at[0], 2, (d, p + 1))
    r_down = halo(rsend.at[0], rhalo.at[1], 3, (d, p - 1))
    lands = (zhalo.at[0], zhalo.at[1], rhalo.at[0], rhalo.at[1])
    copies = (z_up, z_down, r_up, r_down)
    for copy, there in zip(copies, has):
        pl.when(there)(copy.start)
    for land, comes in zip(lands, gets):

        @pl.when(jnp.logical_not(comes))
        def _(land=land):
            land[...] = jnp.zeros(land.shape, F32)

    for copy, comes in zip(copies, gets):
        pl.when(comes)(copy.wait_recv)
    mixed_copy.start()
    tall_copy.start()
    row_id = lax.broadcasted_iota(jnp.int32, (ROWS, NX), 0)
    col_id = lax.broadcasted_iota(jnp.int32, (ROWS, NX), 1)
    field = [ls_ref[0], ls_ref[1]]
    z_flux = [flux(field[0] - zhalo[0]), flux(field[1] - field[0]), flux(zhalo[1] - field[1])]
    even, odd = [], []
    for layer in range(2):
        centre = field[layer]

        def row_of(side):
            parts = [
                jnp.broadcast_to(rhalo[side, layer * 8 + k : layer * 8 + k + 1, :], (ROWS, 128)) for k in range(8)
            ]
            return jnp.concatenate(parts, axis=1)

        bend = z_flux[layer + 1] - z_flux[layer]
        above = jnp.where(row_id == 0, row_of(0), pltpu.roll(centre, 1, 0))
        row_flux = flux(centre - above)
        last = flux(row_of(1) - centre)
        bend = bend + jnp.where(row_id == ROWS - 1, last, pltpu.roll(row_flux, ROWS - 1, 0)) - row_flux
        before = jnp.where(col_id == 0, 0.0, pltpu.roll(centre, 1, 1))
        col_flux = flux(centre - before)
        bend = bend + jnp.where(col_id == NX - 1, flux(-centre), pltpu.roll(col_flux, NX - 1, 1)) - col_flux
        density = con_ref[layer] * (0.5 * (1.0 + jnp.tanh(centre))) + bend_weight * bend
        density = jnp.where(lower, flip(density, 0, ROWS), density)
        left = flip_lanes(density[:, :HALF])
        right = density[:, HALF:]
        even.append(right + left)
        odd.append(right - left)

    block = jnp.where(lower, PLAN // 2 - 1 - p, p - PLAN // 2)
    half_lane = lax.broadcasted_iota(jnp.int32, (ROWS, 128), 1) < COEF
    wide_copy.wait()

    def send_coef(part, other):
        return pltpu.make_async_remote_copy(
            src_ref=csend.at[part, other], dst_ref=sbuf.at[part, block], send_sem=cs.at[part], recv_sem=cr.at[part],
            device_id=at_q(other), device_id_type=MESH,
        )

    def send_coefs(part, kind):
        @pl.loop(0, 16)
        def _(k):
            other = kind * 16 + lax.rem(q + k, 16)

            @pl.when(other != q)
            def _():
                send_coef(part, other).start()

    for kind, pair in enumerate((even, odd)):
        coef = table_right(jnp.concatenate(pair, axis=0), wide[kind, 0], wide[kind, 1])
        for m in range(8):
            first = coef[:ROWS, 128 * m : 128 * (m + 1)]
            second = coef[ROWS:, 128 * m : 128 * (m + 1)]
            spot = kind * 16 + 2 * m
            one = jnp.where(half_lane, first, pltpu.roll(second, COEF, 1))
            two = jnp.where(half_lane, pltpu.roll(first, COEF, 1), second)
            for part in range(2):
                csend[part, spot] = one[8 * part : 8 * part + 8]
                csend[part, spot + 1] = two[8 * part : 8 * part + 8]
        send_coefs(0, kind)
    send_coefs(1, 0)
    send_coefs(1, 1)

    def respond(first, count, is_sin):
        lane = lax.broadcasted_iota(jnp.int32, (count, 128), 1)
        row = lax.broadcasted_iota(jnp.int32, (count, 128), 0) + first
        place = (q % (GROUP // 2)) * COEF + lane % COEF
        v = jnp.where((place == 0) & (q >= GROUP // 2), NX, place).astype(F32)
        scale = 2.0 * math.pi * grav_scale * thickness / (4.0 * NX * NX)
        weight = jnp.where(place == 0, scale, 2.0 * scale) * jnp.where(row == 0, 1.0, 2.0)
        layer = (2 * d + lane // COEF).astype(F32)
        rate = (top_depth + (layer + 0.5) * thickness) * (-2.0 * math.pi / (2 * NX))
        u = (jnp.where(row == 0, NX, row) if is_sin else row).astype(F32)
        return jnp.exp(jnp.sqrt(u * u + v * v) * rate) * weight

    @pl.loop(0, NX // 256)
    def _(k):
        rsp[pl.ds(pl.multiple_of(256 * k, 256), 256), :] = respond(256 * k, 256, False)

    rsp_first[...] = respond(0, 8, True)

    step = 256
    wide_half = lax.broadcasted_iota(jnp.int32, (step, 128), 1) < COEF
    block_of = lax.div(lax.broadcasted_iota(jnp.int32, (step, 128), 0), 16)
    sign = jnp.where(lax.rem(block_of, 2) == zh, 1.0, -1.0)
    mixed_copy.wait()
    for part in range(2):
        sbuf[part, block] = csend[part, q]
        landed = sbuf.at[part, pl.ds(0, GROUP - 1)]
        pltpu.make_async_copy(landed, landed, cr.at[part]).wait()
        value = sbuf[part].reshape(step, 128)
        for kind in range(2):
            high, low = split(value * sign if kind else value)
            sst[kind, part, :, :128] = high
            sst[kind, part, :, 128:] = low
        for kind in range(2):

            @pl.loop(0, NX // step)
            def _(k, kind=kind, part=part):
                here = pl.ds(pl.multiple_of(k * step, step), step)
                cols = slice(step * part, step * (part + 1))
                both = matmul(mixed[kind, 0, here, cols], sst[kind, part])
                value = both[:, :128] + both[:, 128:] + matmul(mixed[kind, 1, here, cols], sst[kind, part, :, :128])
                if part == 0:
                    acc[kind, here, :] = value
                    return
                factor = rsp[here, :]
                if kind == 1:
                    fixed = jnp.concatenate([rsp_first[...], factor[8:]], axis=0)
                    factor = jnp.where(k == 0, fixed, factor)
                value = (value + acc[kind, here, :]) * factor
                value = value + pltpu.roll(value, COEF, 1)
                high = value.astype(BF16).astype(F32)
                pst[kind, here, :] = jnp.where(wide_half, high, value - high).astype(BF16)
                phi[kind, here, :] = jnp.where(wide_half, high, 0.0).astype(BF16)

    def send_row(part, other):
        return pltpu.make_async_remote_copy(
            src_ref=xsend.at[part, other], dst_ref=cbuf.at[part, q], send_sem=xs.at[part], recv_sem=xr.at[part],
            device_id=at_q(other), device_id_type=MESH,
        )

    def send_rows(part, chunk):
        @pl.loop(0, 16)
        def _(k):
            other = lax.rem(8 + 16 * chunk + lax.rem(q + k, 16), GROUP)

            @pl.when(other != q)
            def _():
                send_row(part, other).start()

    for chunk in range(2):
        cut = slice(256 * chunk, 256 * (chunk + 1))
        parity = []
        for kind in range(2):
            value = matmul(wide[kind, 0, cut, :], pst[kind]) + matmul(wide[kind, 1, cut, :], phi[kind])
            parity.append(value + pltpu.roll(value, COEF, 1))
        plus = parity[0] + parity[1]
        minus = parity[0] - parity[1]
        for g in range(4):
            up = [plus[ROWS * (4 * g + n) : ROWS * (4 * g + n + 1)] for n in range(4)]
            down = [minus[ROWS * (4 * g + n) : ROWS * (4 * g + n + 1)] for n in range(4)]
            place = 4 * chunk + g
            for spot, one, two in (
                (2 * (8 + place), up[0], up[2]),
                (2 * (8 + place) + 1, up[1], up[3]),
                (2 * (7 - place), down[3], down[1]),
                (2 * (7 - place) + 1, down[2], down[0]),
            ):
                value = jnp.where(half_lane, one, two)
                for part in range(2):
                    xsend[part, spot] = value[8 * part : 8 * part + 8]
        send_rows(0, chunk)
    send_rows(1, 0)
    send_rows(1, 1)

    def send_field(part, other):
        return pltpu.make_async_remote_copy(
            src_ref=gsend.at[part, other], dst_ref=gbuf.at[part, z], send_sem=gs.at[part], recv_sem=gr.at[part],
            device_id=at_z(other), device_id_type=MESH,
        )

    tall_copy.wait()
    half_lane = lax.broadcasted_iota(jnp.int32, (8, 128), 1) < COEF
    for part in range(2):
        cbuf[part, q] = xsend[part, q]
        landed = cbuf.at[part, pl.ds(0, GROUP - 1)]
        pltpu.make_async_copy(landed, landed, xr.at[part]).wait()
        parity = []
        for kind in range(2):
            tops, bottoms = [], []
            for m in range(8):
                first, second = cbuf[part, kind * 16 + 2 * m], cbuf[part, kind * 16 + 2 * m + 1]
                tops.append(jnp.where(half_lane, first, pltpu.roll(second, COEF, 1)))
                bottoms.append(jnp.where(half_lane, pltpu.roll(first, COEF, 1), second))
            value = jnp.concatenate([jnp.concatenate(tops, axis=1), jnp.concatenate(bottoms, axis=1)], axis=0)
            parity.append(table_right(value, tall[kind, 0], tall[kind, 1]))
        plus = parity[0] + parity[1]
        minus = parity[0] - parity[1]
        for other in range(RING):
            rows = slice(8 * (other // DEPTH), 8 * (other // DEPTH + 1))
            col = other % DEPTH
            if col >= 4:
                gsend[part, other] = plus[rows, 128 * (col - 4) : 128 * (col - 3)]
            else:
                gsend[part, other] = minus[rows, 128 * (3 - col) : 128 * (4 - col)]

        @pl.loop(0, RING - 1)
        def _(k, part=part):
            other = z + 8 + lax.div(k + 1, 2) * (1 - 2 * lax.rem(k, 2)) + RING
            send_field(part, lax.rem(other, RING)).start()

        gbuf[part, z] = gsend[part, z]

    halves = []
    for part in range(2):
        landed = gbuf.at[part, pl.ds(0, RING - 1)]
        pltpu.make_async_copy(landed, landed, gr.at[part]).wait()
        total = gbuf[part, 0]
        for other in range(1, RING):
            total = total + gbuf[part, other]
        halves.append(total)
    total = jnp.concatenate(halves, axis=0)
    total = jnp.where(d < DEPTH // 2, flip(total, 1, 128), total)
    out_ref[...] = jnp.where(lower, flip(total, 0, ROWS), total)

    for copy, there in zip(copies, has):
        pl.when(there)(copy.wait_send)
    for part in range(2):
        for buffer, semaphore, peers in ((csend, cs, GROUP - 1), (xsend, xs, GROUP - 1), (gsend, gs, RING - 1)):
            left = buffer.at[part, pl.ds(0, peers)]
            pltpu.make_async_copy(left, left, semaphore.at[part]).wait()


def solution(mesh):
    wide, mixed, tall = basis()

    def step(level_set, contrast):
        vmem = pl.BlockSpec(memory_space=pltpu.VMEM)
        anywhere = pl.BlockSpec(memory_space=pl.ANY)
        dma = pltpu.SemaphoreType.DMA
        return pl.pallas_call(
            kernel,
            out_shape=jax.ShapeDtypeStruct((ROWS, 128), F32),
            in_specs=[anywhere] * 5,
            out_specs=vmem,
            scratch_shapes=[
                pltpu.VMEM((2, ROWS, NX), F32),
                pltpu.SMEM((2,), F32),
                pltpu.VMEM((2, 2, HALF, NX), BF16),
                pltpu.VMEM((2, 2, NX, HALF), BF16),
                pltpu.VMEM((2, 2, NX, HALF), BF16),
                pltpu.VMEM((2, ROWS, NX), F32),
                pltpu.VMEM((2, 16, 128), F32),
                pltpu.VMEM((2, 16, 128), F32),
                pltpu.VMEM((2, GROUP, 8, 128), F32),
                pltpu.VMEM((2, GROUP, 8, 128), F32),
                pltpu.VMEM((2, 2, HALF // 2, 256), BF16),
                pltpu.VMEM((2, NX, 128), F32),
                pltpu.VMEM((NX, 128), F32),
                pltpu.VMEM((8, 128), F32),
                pltpu.VMEM((2, NX, 128), BF16),
                pltpu.VMEM((2, NX, 128), BF16),
                pltpu.VMEM((2, GROUP, 8, 128), F32),
                pltpu.VMEM((2, GROUP, 8, 128), F32),
                pltpu.VMEM((2, RING, 8, 128), F32),
                pltpu.VMEM((2, RING, 8, 128), F32),
                dma(()), dma(()), dma(()), dma(()), dma(()), dma((4,)), dma((4,)),
                dma((2,)), dma((2,)), dma((2,)), dma((2,)), dma((2,)), dma((2,)),
            ],
            compiler_params=pltpu.CompilerParams(
                collective_id=0, has_side_effects=True, vmem_limit_bytes=63 * 1024 * 1024
            ),
        )(level_set, contrast, jnp.asarray(wide), jnp.asarray(mixed), jnp.asarray(tall))

    return jax.shard_map(
        step,
        mesh=mesh,
        in_specs=(P("depth", "plan", None), P("depth")),
        out_specs=P("plan", "depth"),
        check_vma=False,
    )
```

```python
import functools
import math

import jax
import jax.numpy as jnp
import ml_dtypes
import numpy as np
from jax import lax
from jax.experimental import pallas as pl
from jax.experimental.pallas import tpu as pltpu
from jax.sharding import PartitionSpec as P

MESH = pl.DeviceIdType.MESH
F32 = jnp.float32
BF16 = jnp.bfloat16

NX = 1024
HALF = NX // 2
LAYERS = 16
DEPTH = 8
PLAN = 64
ROWS = NX // PLAN
GROUP = 32
RING = 16
COEF = 2 * NX // GROUP

bend_weight = 0.5
grav_scale = 0.05
top_depth = 0.0
thickness = 1.0


def basis():
    j = np.arange(HALF, dtype=np.float64)[:, None] + 0.5
    v = np.arange(NX, dtype=np.float64)[None, :]
    v_sin = np.where(v == 0, float(NX), v)
    both = np.stack([np.cos(np.pi * v * j / NX), np.sin(np.pi * v_sin * j / NX)])
    high = both.astype(ml_dtypes.bfloat16)
    low = (both - high.astype(np.float64)).astype(ml_dtypes.bfloat16)
    wide = np.stack([high, low], axis=1)
    return wide, np.ascontiguousarray(np.swapaxes(wide, 2, 3))


def flux(step):
    return step * lax.rsqrt(1.0 + step * step)


def flip(value, axis, size):
    index = lax.broadcasted_iota(jnp.int32, value.shape, axis)
    step = size // 2
    value = pltpu.roll(value, step, axis)
    while step > 1:
        step //= 2
        up = pltpu.roll(value, step, axis)
        down = pltpu.roll(value, size - step, axis)
        value = jnp.where((index & step) != 0, up, down)
    return value


def flip_lanes(value):
    blocks = value.shape[1] // 128
    parts = [flip(value[:, 128 * k : 128 * (k + 1)], 1, 128) for k in reversed(range(blocks))]
    return jnp.concatenate(parts, axis=1) if blocks > 1 else parts[0]


def split(value):
    high = value.astype(BF16)
    low = (value - high.astype(F32)).astype(BF16)
    return high, low


def matmul(a, b):
    return jnp.dot(a, b, preferred_element_type=F32)


def table_right(value, high_table, low_table):
    n = value.shape[0]
    high, low = split(value)
    both = matmul(jnp.concatenate([high, low], axis=0), high_table)
    return both[:n] + both[n:] + matmul(high, low_table)


def kernel(
    ls_hbm, con_hbm, wide_hbm, tall_hbm, out_ref,
    ls_ref, con_ref, wide, tall, zhalo, rsend, rhalo, csend, sbuf, sst, rsp, rsp_first, pst, phi, xsend, cbuf, gsend, gbuf,
    ls_sem, con_sem, wide_sem, tall_sem, hs, hr, cs, cr, xs, xr, gs, gr,
):
    d = lax.axis_index("depth")
    p = lax.axis_index("plan")
    core = lax.rem(p, 2)
    zh = lax.rem(lax.div(p, 2), 2)
    q = lax.div(p, 4) * 2 + core
    z = zh * DEPTH + d
    lower = p < PLAN // 2

    def at_q(other):
        return (d, lax.div(other, 2) * 4 + zh * 2 + lax.rem(other, 2))

    def at_z(other):
        return (lax.rem(other, DEPTH), p + 2 * (lax.div(other, DEPTH) - zh))

    ls_copy = pltpu.make_async_copy(ls_hbm, ls_ref, ls_sem)
    con_copy = pltpu.make_async_copy(con_hbm, con_ref, con_sem)
    ls_copy.start()
    con_copy.start()
    wide_copy = pltpu.make_async_copy(wide_hbm, wide, wide_sem)
    tall_copy = pltpu.make_async_copy(tall_hbm, tall, tall_sem)
    wide_copy.start()
    tall_copy.start()

    barrier = pltpu.get_barrier_semaphore()

    def greet(target):
        pl.semaphore_signal(barrier, inc=1, device_id=target, device_id_type=MESH)

    has = (d < DEPTH - 1, d > 0, p < PLAN - 1, p > 0)
    gets = (d > 0, d < DEPTH - 1, p > 0, p < PLAN - 1)
    pl.when(has[0])(lambda: greet((d + 1, p)))
    pl.when(has[1])(lambda: greet((d - 1, p)))
    pl.when(has[2])(lambda: greet((d, p + 1)))
    pl.when(has[3])(lambda: greet((d, p - 1)))
    outer = jnp.where(core == 0, p - 1, p + 1)
    has_outer = (outer >= 0) & (outer < PLAN)
    buddy = p + 1 - 2 * core
    for other in range(GROUP):
        target = (other // 2) * 4 + other % 2 + zh * 2
        pl.when((target != p) & (target != buddy))(lambda target=target: greet((d, target)))
    for other in range(RING):
        row = other // DEPTH
        far = (row != zh) | (other % DEPTH > d + 1) | (other % DEPTH < d - 1)
        pl.when(far)(lambda other=other, row=row: greet((other % DEPTH, p + 2 * (row - zh))))

    ls_copy.wait()
    con_copy.wait()

    for layer in range(2):
        for k in range(8):
            spot = layer * 8 + k
            rsend[0, spot : spot + 1, :] = ls_ref[layer, 0:1, 128 * k : 128 * (k + 1)]
            rsend[1, spot : spot + 1, :] = ls_ref[layer, ROWS - 1 : ROWS, 128 * k : 128 * (k + 1)]

    pl.semaphore_wait(barrier, GROUP + RING - 2 + has_outer.astype(jnp.int32))

    def halo(source, target, number, device):
        return pltpu.make_async_remote_copy(
            src_ref=source, dst_ref=target, send_sem=hs.at[number], recv_sem=hr.at[number],
            device_id=device, device_id_type=MESH,
        )

    z_up = halo(ls_ref.at[1], zhalo.at[0], 0, (d + 1, p))
    z_down = halo(ls_ref.at[0], zhalo.at[1], 1, (d - 1, p))
    r_up = halo(rsend.at[1], rhalo.at[0], 2, (d, p + 1))
    r_down = halo(rsend.at[0], rhalo.at[1], 3, (d, p - 1))
    lands = (zhalo.at[0], zhalo.at[1], rhalo.at[0], rhalo.at[1])
    copies = (z_up, z_down, r_up, r_down)
    for copy, there in zip(copies, has):
        pl.when(there)(copy.start)
    for land, comes in zip(lands, gets):

        @pl.when(jnp.logical_not(comes))
        def _(land=land):
            land[...] = jnp.zeros(land.shape, F32)

    for copy, comes in zip(copies, gets):
        pl.when(comes)(copy.wait_recv)
    row_id = lax.broadcasted_iota(jnp.int32, (ROWS, NX), 0)
    col_id = lax.broadcasted_iota(jnp.int32, (ROWS, NX), 1)
    field = [ls_ref[0], ls_ref[1]]
    z_flux = [flux(field[0] - zhalo[0]), flux(field[1] - field[0]), flux(zhalo[1] - field[1])]
    even, odd = [], []
    for layer in range(2):
        centre = field[layer]

        def row_of(side):
            parts = [
                jnp.broadcast_to(rhalo[side, layer * 8 + k : layer * 8 + k + 1, :], (ROWS, 128)) for k in range(8)
            ]
            return jnp.concatenate(parts, axis=1)

        bend = z_flux[layer + 1] - z_flux[layer]
        above = jnp.where(row_id == 0, row_of(0), pltpu.roll(centre, 1, 0))
        row_flux = flux(centre - above)
        last = flux(row_of(1) - centre)
        bend = bend + jnp.where(row_id == ROWS - 1, last, pltpu.roll(row_flux, ROWS - 1, 0)) - row_flux
        before = jnp.where(col_id == 0, 0.0, pltpu.roll(centre, 1, 1))
        col_flux = flux(centre - before)
        bend = bend + jnp.where(col_id == NX - 1, flux(-centre), pltpu.roll(col_flux, NX - 1, 1)) - col_flux
        density = con_ref[layer] * (0.5 * (1.0 + jnp.tanh(centre))) + bend_weight * bend
        density = jnp.where(lower, flip(density, 0, ROWS), density)
        left = flip_lanes(density[:, :HALF])
        right = density[:, HALF:]
        even.append(right + left)
        odd.append(right - left)

    block = jnp.where(lower, PLAN // 2 - 1 - p, p - PLAN // 2)
    half_lane = lax.broadcasted_iota(jnp.int32, (ROWS, 128), 1) < COEF
    wide_copy.wait()

    def send_coef(other):
        return pltpu.make_async_remote_copy(
            src_ref=csend.at[other], dst_ref=sbuf.at[block], send_sem=cs, recv_sem=cr,
            device_id=at_q(other), device_id_type=MESH,
        )

    for kind, pair in enumerate((even, odd)):
        coef = table_right(jnp.concatenate(pair, axis=0), wide[kind, 0], wide[kind, 1])
        for m in range(8):
            first = coef[:ROWS, 128 * m : 128 * (m + 1)]
            second = coef[ROWS:, 128 * m : 128 * (m + 1)]
            spot = kind * 16 + 2 * m
            csend[spot] = jnp.where(half_lane, first, pltpu.roll(second, COEF, 1))
            csend[spot + 1] = jnp.where(half_lane, pltpu.roll(first, COEF, 1), second)

        for k in range(16):
            other = kind * 16 + lax.rem(q + k, 16)
            if k == 0:
                pl.when(other != q)(send_coef(other).start)
            else:
                send_coef(other).start()

    def respond(first, count, is_sin):
        lane = lax.broadcasted_iota(jnp.int32, (count, 128), 1)
        row = lax.broadcasted_iota(jnp.int32, (count, 128), 0) + first
        place = (q % (GROUP // 2)) * COEF + lane % COEF
        v = jnp.where((place == 0) & (q >= GROUP // 2), NX, place).astype(F32)
        scale = 2.0 * math.pi * grav_scale * thickness / (4.0 * NX * NX)
        weight = jnp.where(place == 0, scale, 2.0 * scale) * jnp.where(row == 0, 1.0, 2.0)
        layer = (2 * d + lane // COEF).astype(F32)
        rate = (top_depth + (layer + 0.5) * thickness) * (-2.0 * math.pi / (2 * NX))
        u = (jnp.where(row == 0, NX, row) if is_sin else row).astype(F32)
        return jnp.exp(jnp.sqrt(u * u + v * v) * rate) * weight

    @pl.loop(0, NX // 256)
    def _(k):
        rsp[pl.ds(pl.multiple_of(256 * k, 256), 256), :] = respond(256 * k, 256, False)

    rsp_first[...] = respond(0, 8, True)

    sbuf[block] = csend[q]
    pltpu.make_async_copy(sbuf.at[pl.ds(0, GROUP - 1)], sbuf.at[pl.ds(0, GROUP - 1)], cr).wait()

    for b in range(GROUP):
        value = sbuf[b]
        high, low = split(value)
        sst[0, ROWS * b : ROWS * (b + 1), :128] = high
        sst[0, ROWS * b : ROWS * (b + 1), 128:] = low
        sign = jnp.where((b // 2) % 2 == zh, 1.0, -1.0)
        high, low = split(value * sign)
        sst[1, ROWS * b : ROWS * (b + 1), :128] = high
        sst[1, ROWS * b : ROWS * (b + 1), 128:] = low
    tall_copy.wait()
    step = 256
    wide_half = lax.broadcasted_iota(jnp.int32, (step, 128), 1) < COEF
    for kind in range(2):
        for k in range(NX // step):
            here = slice(k * step, (k + 1) * step)
            both = matmul(tall[kind, 0, here, :], sst[kind])
            value = both[:, :128] + both[:, 128:] + matmul(tall[kind, 1, here, :], sst[kind, :, :128])
            factor = rsp[here, :]
            if kind == 1 and k == 0:
                factor = jnp.concatenate([rsp_first[...], factor[8:]], axis=0)
            value = value * factor
            value = value + pltpu.roll(value, COEF, 1)
            high = value.astype(BF16).astype(F32)
            pst[kind, here, :] = jnp.where(wide_half, high, value - high).astype(BF16)
            phi[kind, here, :] = jnp.where(wide_half, high, 0.0).astype(BF16)

    def send_rows(other):
        return pltpu.make_async_remote_copy(
            src_ref=xsend.at[other], dst_ref=cbuf.at[q], send_sem=xs, recv_sem=xr,
            device_id=at_q(other), device_id_type=MESH,
        )

    for part in range(2):
        cut = slice(256 * part, 256 * (part + 1))
        parity = []
        for kind in range(2):
            value = matmul(wide[kind, 0, cut, :], pst[kind]) + matmul(wide[kind, 1, cut, :], phi[kind])
            parity.append(value + pltpu.roll(value, COEF, 1))
        plus = parity[0] + parity[1]
        minus = parity[0] - parity[1]
        for g in range(4):
            up = [plus[ROWS * (4 * g + n) : ROWS * (4 * g + n + 1)] for n in range(4)]
            down = [minus[ROWS * (4 * g + n) : ROWS * (4 * g + n + 1)] for n in range(4)]
            chunk = 4 * part + g
            xsend[2 * (8 + chunk)] = jnp.where(half_lane, up[0], up[2])
            xsend[2 * (8 + chunk) + 1] = jnp.where(half_lane, up[1], up[3])
            xsend[2 * (7 - chunk)] = jnp.where(half_lane, down[3], down[1])
            xsend[2 * (7 - chunk) + 1] = jnp.where(half_lane, down[2], down[0])

        for k in range(16):
            spot = lax.rem(q + k, 16)
            upper = lax.div(spot, 8)
            other = spot + 16 * (upper if part else 1 - upper)
            if k == 0:
                pl.when(other != q)(send_rows(other).start)
            else:
                send_rows(other).start()

    cbuf[q] = xsend[q]
    pltpu.make_async_copy(cbuf.at[pl.ds(0, GROUP - 1)], cbuf.at[pl.ds(0, GROUP - 1)], xr).wait()

    parity = []
    for kind in range(2):
        tops, bottoms = [], []
        for m in range(8):
            first, second = cbuf[kind * 16 + 2 * m], cbuf[kind * 16 + 2 * m + 1]
            tops.append(jnp.where(half_lane, first, pltpu.roll(second, COEF, 1)))
            bottoms.append(jnp.where(half_lane, pltpu.roll(first, COEF, 1), second))
        value = jnp.concatenate([jnp.concatenate(tops, axis=1), jnp.concatenate(bottoms, axis=1)], axis=0)
        parity.append(table_right(value, tall[kind, 0], tall[kind, 1]))
    plus = parity[0] + parity[1]
    minus = parity[0] - parity[1]
    for other in range(RING):
        rows = slice(ROWS * (other // DEPTH), ROWS * (other // DEPTH + 1))
        col = other % DEPTH
        if col >= 4:
            gsend[other] = plus[rows, 128 * (col - 4) : 128 * (col - 3)]
        else:
            gsend[other] = minus[rows, 128 * (3 - col) : 128 * (4 - col)]

    def send_field(other):
        return pltpu.make_async_remote_copy(
            src_ref=gsend.at[other], dst_ref=gbuf.at[z], send_sem=gs, recv_sem=gr,
            device_id=at_z(other), device_id_type=MESH,
        )

    for k in range(RING - 1):
        away = 8 + (k + 1) // 2 * (1 - 2 * (k % 2))
        send_field(lax.rem(z + away, RING)).start()

    gbuf[z] = gsend[z]
    pltpu.make_async_copy(gbuf.at[pl.ds(0, RING - 1)], gbuf.at[pl.ds(0, RING - 1)], gr).wait()
    total = gbuf[0]
    for other in range(1, RING):
        total = total + gbuf[other]
    total = jnp.where(d < DEPTH // 2, flip(total, 1, 128), total)
    out_ref[...] = jnp.where(lower, flip(total, 0, ROWS), total)

    for copy, there in zip(copies, has):
        pl.when(there)(copy.wait_send)
    pltpu.make_async_copy(csend.at[pl.ds(0, GROUP - 1)], csend.at[pl.ds(0, GROUP - 1)], cs).wait()
    pltpu.make_async_copy(xsend.at[pl.ds(0, GROUP - 1)], xsend.at[pl.ds(0, GROUP - 1)], xs).wait()
    pltpu.make_async_copy(gsend.at[pl.ds(0, RING - 1)], gsend.at[pl.ds(0, RING - 1)], gs).wait()


def solution(mesh):
    wide, tall = basis()

    def step(level_set, contrast):
        vmem = pl.BlockSpec(memory_space=pltpu.VMEM)
        anywhere = pl.BlockSpec(memory_space=pl.ANY)
        dma = pltpu.SemaphoreType.DMA
        return pl.pallas_call(
            kernel,
            out_shape=jax.ShapeDtypeStruct((ROWS, 128), F32),
            in_specs=[anywhere] * 4,
            out_specs=vmem,
            scratch_shapes=[
                pltpu.VMEM((2, ROWS, NX), F32),
                pltpu.SMEM((2,), F32),
                pltpu.VMEM((2, 2, HALF, NX), BF16),
                pltpu.VMEM((2, 2, NX, HALF), BF16),
                pltpu.VMEM((2, ROWS, NX), F32),
                pltpu.VMEM((2, 16, 128), F32),
                pltpu.VMEM((2, 16, 128), F32),
                pltpu.VMEM((GROUP, ROWS, 128), F32),
                pltpu.VMEM((GROUP, ROWS, 128), F32),
                pltpu.VMEM((2, HALF, 256), BF16),
                pltpu.VMEM((NX, 128), F32),
                pltpu.VMEM((8, 128), F32),
                pltpu.VMEM((2, NX, 128), BF16),
                pltpu.VMEM((2, NX, 128), BF16),
                pltpu.VMEM((GROUP, ROWS, 128), F32),
                pltpu.VMEM((GROUP, ROWS, 128), F32),
                pltpu.VMEM((RING, ROWS, 128), F32),
                pltpu.VMEM((RING, ROWS, 128), F32),
                dma(()), dma(()), dma(()), dma(()), dma((4,)), dma((4,)),
                dma(()), dma(()), dma(()), dma(()), dma(()), dma(()),
            ],
            compiler_params=pltpu.CompilerParams(
                collective_id=0, has_side_effects=True, vmem_limit_bytes=63 * 1024 * 1024
            ),
        )(level_set, contrast, jnp.asarray(wide), jnp.asarray(tall))

    return jax.shard_map(
        step,
        mesh=mesh,
        in_specs=(P("depth", "plan", None), P("depth")),
        out_specs=P("plan", "depth"),
        check_vma=False,
    )
```

```python
import functools
import math

import jax
import jax.numpy as jnp
import ml_dtypes
import numpy as np
from jax import lax
from jax.experimental import pallas as pl
from jax.experimental.pallas import tpu as pltpu
from jax.sharding import PartitionSpec as P

MESH = pl.DeviceIdType.MESH
F32 = jnp.float32
BF16 = jnp.bfloat16

NX = 1024
HALF = NX // 2
LAYERS = 16
DEPTH = 8
PLAN = 64
ROWS = NX // PLAN
GROUP = 32
RING = 16
COEF = 2 * NX // GROUP

bend_weight = 0.5
grav_scale = 0.05
top_depth = 0.0
thickness = 1.0


def basis():
    j = np.arange(HALF, dtype=np.float64)[:, None] + 0.5
    v = np.arange(NX, dtype=np.float64)[None, :]
    v_sin = np.where(v == 0, float(NX), v)
    both = np.stack([np.cos(np.pi * v * j / NX), np.sin(np.pi * v_sin * j / NX)])
    high = both.astype(ml_dtypes.bfloat16)
    low = (both - high.astype(np.float64)).astype(ml_dtypes.bfloat16)
    wide = np.stack([high, low], axis=1)
    return wide, np.ascontiguousarray(np.swapaxes(wide, 2, 3))


def flux(step):
    return step * lax.rsqrt(1.0 + step * step)


def flip(value, axis, size):
    index = lax.broadcasted_iota(jnp.int32, value.shape, axis)
    step = size // 2
    value = pltpu.roll(value, step, axis)
    while step > 1:
        step //= 2
        up = pltpu.roll(value, step, axis)
        down = pltpu.roll(value, size - step, axis)
        value = jnp.where((index & step) != 0, up, down)
    return value


def flip_lanes(value):
    blocks = value.shape[1] // 128
    parts = [flip(value[:, 128 * k : 128 * (k + 1)], 1, 128) for k in reversed(range(blocks))]
    return jnp.concatenate(parts, axis=1) if blocks > 1 else parts[0]


def split(value):
    high = value.astype(BF16)
    low = (value - high.astype(F32)).astype(BF16)
    return high, low


def matmul(a, b):
    return jnp.dot(a, b, preferred_element_type=F32)


def pair(value):
    return jnp.concatenate(split(value), axis=0)


def table_right(both, high_table, low_table):
    n = both.shape[0] // 2
    product = matmul(both, high_table)
    return product[:n] + product[n:] + matmul(both[:n], low_table)


def kernel(
    ls_hbm, con_hbm, wide_hbm, tall_hbm, out_ref,
    ls_ref, con_ref, own, part_density, wide, tall, zhalo, rsend, rhalo, csend, sbuf, sst, rsp, rsp_first, pst, phi, xsend, cbuf, gsend, gbuf,
    ls_sem, con_sem, wide_sem, tall_sem, hs, hr, cs, cr, xs, xr, gs, gr,
):
    d = lax.axis_index("depth")
    p = lax.axis_index("plan")
    core = lax.rem(p, 2)
    zh = lax.rem(lax.div(p, 2), 2)
    q = lax.div(p, 4) * 2 + core
    z = zh * DEPTH + d
    lower = p < PLAN // 2

    def at_q(other):
        return (d, lax.div(other, 2) * 4 + zh * 2 + lax.rem(other, 2))

    def at_z(other):
        return (lax.rem(other, DEPTH), p + 2 * (lax.div(other, DEPTH) - zh))

    ls_copy = pltpu.make_async_copy(ls_hbm, ls_ref, ls_sem)
    con_copy = pltpu.make_async_copy(con_hbm, con_ref, con_sem)
    ls_copy.start()
    con_copy.start()
    wide_copy = pltpu.make_async_copy(wide_hbm, wide, wide_sem)
    tall_copy = pltpu.make_async_copy(tall_hbm, tall, tall_sem)
    wide_copy.start()
    tall_copy.start()

    barrier = pltpu.get_barrier_semaphore()

    def greet(target):
        pl.semaphore_signal(barrier, inc=1, device_id=target, device_id_type=MESH)

    has = (d < DEPTH - 1, d > 0, p < PLAN - 1, p > 0)
    gets = (d > 0, d < DEPTH - 1, p > 0, p < PLAN - 1)
    xy = lax.div(p, 4)
    outer = jnp.where(core == 0, p - 1, p + 1)
    has_outer = (outer >= 0) & (outer < PLAN)
    for k in (1, RING - 1):
        greet(at_z(lax.rem(z + k, RING)))
    greet((d, p + 1 - 2 * core))
    pl.when(has_outer)(lambda: greet((d, outer)))
    for k in range(1, GROUP // 2):
        first = 4 * lax.rem(xy + k, GROUP // 2) + 2 * zh
        greet((d, first))
        greet((d, first + 1))
    for k in range(2, RING - 1):
        greet(at_z(lax.rem(z + k, RING)))

    ls_copy.wait()
    con_copy.wait()

    for layer in range(2):
        value = ls_ref[layer]
        value = jnp.where(lower, flip(value, 0, ROWS), value)
        own[layer, :, :HALF] = value[:, HALF:]
        own[layer, :, HALF:] = flip_lanes(value[:, :HALF])

    for layer in range(2):
        for k in range(8):
            spot = layer * 8 + k
            top = own[layer, 0:1, 128 * k : 128 * (k + 1)]
            bottom = own[layer, ROWS - 1 : ROWS, 128 * k : 128 * (k + 1)]
            rsend[0, spot : spot + 1, :] = jnp.where(lower, bottom, top)
            rsend[1, spot : spot + 1, :] = jnp.where(lower, top, bottom)

    pl.semaphore_wait(barrier, GROUP + RING - 2 + has_outer.astype(jnp.int32))

    def halo(source, target, number, device):
        return pltpu.make_async_remote_copy(
            src_ref=source, dst_ref=target, send_sem=hs.at[number], recv_sem=hr.at[number],
            device_id=device, device_id_type=MESH,
        )

    z_up = halo(own.at[1], zhalo.at[0], 0, (d + 1, p))
    z_down = halo(own.at[0], zhalo.at[1], 1, (d - 1, p))
    r_up = halo(rsend.at[1], rhalo.at[0], 2, (d, p + 1))
    r_down = halo(rsend.at[0], rhalo.at[1], 3, (d, p - 1))
    lands = (zhalo.at[0], zhalo.at[1], rhalo.at[0], rhalo.at[1])
    copies = (z_up, z_down, r_up, r_down)
    for copy, there in zip(copies, has):
        pl.when(there)(copy.start)
    for land, comes in zip(lands, gets):

        @pl.when(jnp.logical_not(comes))
        def _(land=land):
            land[...] = jnp.zeros(land.shape, F32)

    row_id = lax.broadcasted_iota(jnp.int32, (ROWS, NX), 0)
    lane_id = lax.broadcasted_iota(jnp.int32, (ROWS, HALF), 1)
    field = [own[0], own[1]]
    middle = flux(field[1] - field[0])
    for layer in range(2):
        centre = field[layer]
        bend = -middle if layer else middle
        inner_flux = flux(pltpu.roll(centre, 1, 0) - centre)
        bend = bend + jnp.where(row_id == 0, 0.0, inner_flux)
        bend = bend - jnp.where(row_id == ROWS - 1, 0.0, pltpu.roll(inner_flux, ROWS - 1, 0))
        sides = centre[:, :HALF], centre[:, HALF:]
        across = []
        for side in range(2):
            here = sides[side]
            inside = jnp.where(lane_id == 0, sides[1 - side], pltpu.roll(here, 1, 1))
            inner_flux = flux(inside - here)
            outside = jnp.where(lane_id == HALF - 1, flux(here), pltpu.roll(inner_flux, HALF - 1, 1))
            across.append(inner_flux - outside)
        bend = bend + jnp.concatenate(across, axis=1)
        part_density[layer] = con_ref[layer] * (0.5 * (1.0 + jnp.tanh(centre))) + bend_weight * bend

    for copy, comes in zip(copies, gets):
        pl.when(comes)(copy.wait_recv)
    even, odd = [], []
    for layer in range(2):
        centre = own[layer]
        here = slice(layer * 8, layer * 8 + 8)
        top = jnp.where(lower, rhalo[1, here, :], rhalo[0, here, :])
        bottom = jnp.where(lower, rhalo[0, here, :], rhalo[1, here, :])
        tops = [jnp.broadcast_to(top[k : k + 1], (ROWS, 128)) for k in range(8)]
        bottoms = [jnp.broadcast_to(bottom[k : k + 1], (ROWS, 128)) for k in range(8)]
        beside = jnp.where(row_id == 0, jnp.concatenate(tops, axis=1), jnp.concatenate(bottoms, axis=1))
        outer_rows = (row_id == 0) | (row_id == ROWS - 1)
        bend = flux(zhalo[layer] - centre) + jnp.where(outer_rows, flux(beside - centre), 0.0)
        density = part_density[layer] + bend_weight * bend
        even.append(density[:, :HALF] + density[:, HALF:])
        odd.append(density[:, :HALF] - density[:, HALF:])

    block = jnp.where(lower, PLAN // 2 - 1 - p, p - PLAN // 2)
    half_lane = lax.broadcasted_iota(jnp.int32, (ROWS, 128), 1) < COEF
    wide_copy.wait()

    def send_coef(other):
        return pltpu.make_async_remote_copy(
            src_ref=csend.at[other], dst_ref=sbuf.at[block], send_sem=cs, recv_sem=cr,
            device_id=at_q(other), device_id_type=MESH,
        )

    for kind, folded in enumerate((even, odd)):
        both = pair(jnp.concatenate(folded, axis=0))
        for cut in range(2):
            cols = slice(HALF * cut, HALF * (cut + 1))
            coef = table_right(both, wide[kind, 0, :, cols], wide[kind, 1, :, cols])
            start = kind * 16 + 8 * cut
            for m in range(4):
                first = coef[:ROWS, 128 * m : 128 * (m + 1)]
                second = coef[ROWS:, 128 * m : 128 * (m + 1)]
                csend[start + 2 * m] = jnp.where(half_lane, first, pltpu.roll(second, COEF, 1))
                csend[start + 2 * m + 1] = jnp.where(half_lane, pltpu.roll(first, COEF, 1), second)
            for k in range(8):
                other = start + lax.rem(q + k, 8)
                if k == 0:
                    pl.when(other != q)(send_coef(other).start)
                else:
                    send_coef(other).start()

    def respond(first, count, is_sin):
        lane = lax.broadcasted_iota(jnp.int32, (count, 128), 1)
        row = lax.broadcasted_iota(jnp.int32, (count, 128), 0) + first
        place = (q % (GROUP // 2)) * COEF + lane % COEF
        v = jnp.where((place == 0) & (q >= GROUP // 2), NX, place).astype(F32)
        scale = 2.0 * math.pi * grav_scale * thickness / (4.0 * NX * NX)
        weight = jnp.where(place == 0, scale, 2.0 * scale) * jnp.where(row == 0, 1.0, 2.0)
        layer = (2 * d + lane // COEF).astype(F32)
        rate = (top_depth + (layer + 0.5) * thickness) * (-2.0 * math.pi / (2 * NX))
        u = (jnp.where(row == 0, NX, row) if is_sin else row).astype(F32)
        return jnp.exp(jnp.sqrt(u * u + v * v) * rate) * weight

    @pl.loop(0, NX // 256)
    def _(k):
        rsp[pl.ds(pl.multiple_of(256 * k, 256), 256), :] = respond(256 * k, 256, False)

    rsp_first[...] = respond(0, 8, True)

    sbuf[block] = csend[q]
    pltpu.make_async_copy(sbuf.at[pl.ds(0, GROUP - 1)], sbuf.at[pl.ds(0, GROUP - 1)], cr).wait()

    for b in range(GROUP):
        value = sbuf[b]
        high, low = split(value)
        sst[0, ROWS * b : ROWS * (b + 1), :128] = high
        sst[0, ROWS * b : ROWS * (b + 1), 128:] = low
        sign = jnp.where((b // 2) % 2 == zh, 1.0, -1.0)
        high, low = split(value * sign)
        sst[1, ROWS * b : ROWS * (b + 1), :128] = high
        sst[1, ROWS * b : ROWS * (b + 1), 128:] = low
    tall_copy.wait()
    step = 256
    wide_half = lax.broadcasted_iota(jnp.int32, (step, 128), 1) < COEF
    for kind in range(2):
        for k in range(NX // step):
            here = slice(k * step, (k + 1) * step)
            both = matmul(tall[kind, 0, here, :], sst[kind])
            value = both[:, :128] + both[:, 128:] + matmul(tall[kind, 1, here, :], sst[kind, :, :128])
            factor = rsp[here, :]
            if kind == 1 and k == 0:
                factor = jnp.concatenate([rsp_first[...], factor[8:]], axis=0)
            value = value * factor
            value = value + pltpu.roll(value, COEF, 1)
            high = value.astype(BF16).astype(F32)
            pst[kind, here, :] = jnp.where(wide_half, high, value - high).astype(BF16)
            phi[kind, here, :] = jnp.where(wide_half, high, 0.0).astype(BF16)

    def send_rows(other):
        return pltpu.make_async_remote_copy(
            src_ref=xsend.at[other], dst_ref=cbuf.at[q], send_sem=xs, recv_sem=xr,
            device_id=at_q(other), device_id_type=MESH,
        )

    for part in range(2):
        cut = slice(256 * part, 256 * (part + 1))
        parity = []
        for kind in range(2):
            value = matmul(wide[kind, 0, cut, :], pst[kind]) + matmul(wide[kind, 1, cut, :], phi[kind])
            parity.append(value + pltpu.roll(value, COEF, 1))
        plus = parity[0] + parity[1]
        minus = parity[0] - parity[1]
        for g in range(4):
            up = [plus[ROWS * (4 * g + n) : ROWS * (4 * g + n + 1)] for n in range(4)]
            down = [minus[ROWS * (4 * g + n) : ROWS * (4 * g + n + 1)] for n in range(4)]
            chunk = 4 * part + g
            xsend[2 * (8 + chunk)] = jnp.where(half_lane, up[0], up[2])
            xsend[2 * (8 + chunk) + 1] = jnp.where(half_lane, up[1], up[3])
            xsend[2 * (7 - chunk)] = jnp.where(half_lane, down[3], down[1])
            xsend[2 * (7 - chunk) + 1] = jnp.where(half_lane, down[2], down[0])

        for k in range(16):
            spot = lax.rem(q + k, 16)
            upper = lax.div(spot, 8)
            other = spot + 16 * (upper if part else 1 - upper)
            if k == 0:
                pl.when(other != q)(send_rows(other).start)
            else:
                send_rows(other).start()

    cbuf[q] = xsend[q]
    pltpu.make_async_copy(cbuf.at[pl.ds(0, GROUP - 1)], cbuf.at[pl.ds(0, GROUP - 1)], xr).wait()

    def send_field(other):
        return pltpu.make_async_remote_copy(
            src_ref=gsend.at[other], dst_ref=gbuf.at[z], send_sem=gs, recv_sem=gr,
            device_id=at_z(other), device_id_type=MESH,
        )

    pairs = []
    for kind in range(2):
        tops, bottoms = [], []
        for m in range(8):
            first, second = cbuf[kind * 16 + 2 * m], cbuf[kind * 16 + 2 * m + 1]
            tops.append(jnp.where(half_lane, first, pltpu.roll(second, COEF, 1)))
            bottoms.append(jnp.where(half_lane, pltpu.roll(first, COEF, 1), second))
        value = jnp.concatenate([jnp.concatenate(tops, axis=1), jnp.concatenate(bottoms, axis=1)], axis=0)
        pairs.append(pair(value))
    for cut in range(2):
        cols = slice(256 * cut, 256 * (cut + 1))
        parity = [table_right(pairs[kind], tall[kind, 0, :, cols], tall[kind, 1, :, cols]) for kind in range(2)]
        plus = parity[0] + parity[1]
        minus = parity[0] - parity[1]
        for half in range(2):
            rows = slice(ROWS * half, ROWS * (half + 1))
            for n in range(2):
                lanes = slice(128 * n, 128 * (n + 1))
                gsend[DEPTH * half + 4 + 2 * cut + n] = plus[rows, lanes]
                gsend[DEPTH * half + 3 - 2 * cut - n] = minus[rows, lanes]
        for k in range(8):
            turn = lax.rem(z + k, 8)
            other = DEPTH * lax.div(turn, 4) + lax.rem(2 + 4 * cut + lax.rem(turn, 4), DEPTH)
            pl.when(other != z)(send_field(other).start)

    gbuf[z] = gsend[z]
    pltpu.make_async_copy(gbuf.at[pl.ds(0, RING - 1)], gbuf.at[pl.ds(0, RING - 1)], gr).wait()
    total = gbuf[0]
    for other in range(1, RING):
        total = total + gbuf[other]
    across = lax.broadcasted_iota(jnp.int32, (128, 128), 0) + lax.broadcasted_iota(jnp.int32, (128, 128), 1)
    reverse = jnp.where(across == 127, 1.0, 0.0).astype(BF16)
    high, rest = split(total)
    low = (total - high.astype(F32) - rest.astype(F32)).astype(BF16)
    turned = matmul(jnp.concatenate([high, rest, low], axis=0), reverse)
    turned = turned[:ROWS] + turned[ROWS : 2 * ROWS] + turned[2 * ROWS :]
    total = jnp.where(d < DEPTH // 2, turned, total)

    @pl.when(lower)
    def _():
        for row in range(ROWS):
            out_ref[ROWS - 1 - row : ROWS - row, :] = total[row : row + 1]

    @pl.when(jnp.logical_not(lower))
    def _():
        out_ref[...] = total

    for copy, there in zip(copies, has):
        pl.when(there)(copy.wait_send)
    pltpu.make_async_copy(csend.at[pl.ds(0, GROUP - 1)], csend.at[pl.ds(0, GROUP - 1)], cs).wait()
    pltpu.make_async_copy(xsend.at[pl.ds(0, GROUP - 1)], xsend.at[pl.ds(0, GROUP - 1)], xs).wait()
    pltpu.make_async_copy(gsend.at[pl.ds(0, RING - 1)], gsend.at[pl.ds(0, RING - 1)], gs).wait()


def solution(mesh):
    wide, tall = basis()

    def step(level_set, contrast):
        vmem = pl.BlockSpec(memory_space=pltpu.VMEM)
        anywhere = pl.BlockSpec(memory_space=pl.ANY)
        dma = pltpu.SemaphoreType.DMA
        return pl.pallas_call(
            kernel,
            out_shape=jax.ShapeDtypeStruct((ROWS, 128), F32),
            in_specs=[anywhere] * 4,
            out_specs=vmem,
            scratch_shapes=[
                pltpu.VMEM((2, ROWS, NX), F32),
                pltpu.SMEM((2,), F32),
                pltpu.VMEM((2, ROWS, NX), F32),
                pltpu.VMEM((2, ROWS, NX), F32),
                pltpu.VMEM((2, 2, HALF, NX), BF16),
                pltpu.VMEM((2, 2, NX, HALF), BF16),
                pltpu.VMEM((2, ROWS, NX), F32),
                pltpu.VMEM((2, 16, 128), F32),
                pltpu.VMEM((2, 16, 128), F32),
                pltpu.VMEM((GROUP, ROWS, 128), F32),
                pltpu.VMEM((GROUP, ROWS, 128), F32),
                pltpu.VMEM((2, HALF, 256), BF16),
                pltpu.VMEM((NX, 128), F32),
                pltpu.VMEM((8, 128), F32),
                pltpu.VMEM((2, NX, 128), BF16),
                pltpu.VMEM((2, NX, 128), BF16),
                pltpu.VMEM((GROUP, ROWS, 128), F32),
                pltpu.VMEM((GROUP, ROWS, 128), F32),
                pltpu.VMEM((RING, ROWS, 128), F32),
                pltpu.VMEM((RING, ROWS, 128), F32),
                dma(()), dma(()), dma(()), dma(()), dma((4,)), dma((4,)),
                dma(()), dma(()), dma(()), dma(()), dma(()), dma(()),
            ],
            compiler_params=pltpu.CompilerParams(
                collective_id=0, has_side_effects=True, vmem_limit_bytes=63 * 1024 * 1024
            ),
        )(level_set, contrast, jnp.asarray(wide), jnp.asarray(tall))

    return jax.shard_map(
        step,
        mesh=mesh,
        in_specs=(P("depth", "plan", None), P("depth")),
        out_specs=P("plan", "depth"),
        check_vma=False,
    )
```

```python
import functools
import math

import jax
import jax.numpy as jnp
import ml_dtypes
import numpy as np
from jax import lax
from jax.experimental import pallas as pl
from jax.experimental.pallas import tpu as pltpu
from jax.sharding import PartitionSpec as P

MESH = pl.DeviceIdType.MESH
F32 = jnp.float32
BF16 = jnp.bfloat16

NX = 1024
HALF = NX // 2
LAYERS = 16
DEPTH = 8
PLAN = 64
ROWS = NX // PLAN
GROUP = 32
RING = 16
COEF = 2 * NX // GROUP

bend_weight = 0.5
grav_scale = 0.05
top_depth = 0.0
thickness = 1.0


def basis():
    j = np.arange(HALF, dtype=np.float64)[:, None] + 0.5
    v = np.arange(NX, dtype=np.float64)[None, :]
    v_sin = np.where(v == 0, float(NX), v)
    both = np.stack([np.cos(np.pi * v * j / NX), np.sin(np.pi * v_sin * j / NX)])
    high = both.astype(ml_dtypes.bfloat16)
    low = (both - high.astype(np.float64)).astype(ml_dtypes.bfloat16)
    wide = np.stack([high, low], axis=1)
    return wide, np.ascontiguousarray(np.swapaxes(wide, 2, 3))


def flux(step):
    return step * lax.rsqrt(1.0 + step * step)


def flip(value, axis, size):
    index = lax.broadcasted_iota(jnp.int32, value.shape, axis)
    step = size // 2
    value = pltpu.roll(value, step, axis)
    while step > 1:
        step //= 2
        up = pltpu.roll(value, step, axis)
        down = pltpu.roll(value, size - step, axis)
        value = jnp.where((index & step) != 0, up, down)
    return value


def flip_lanes(value):
    blocks = value.shape[1] // 128
    parts = [flip(value[:, 128 * k : 128 * (k + 1)], 1, 128) for k in reversed(range(blocks))]
    return jnp.concatenate(parts, axis=1) if blocks > 1 else parts[0]


def split(value):
    high = value.astype(BF16)
    low = (value - high.astype(F32)).astype(BF16)
    return high, low


def matmul(a, b):
    return jnp.dot(a, b, preferred_element_type=F32)


def pair(value):
    return jnp.concatenate(split(value), axis=0)


def table_right(both, high_table, low_table):
    n = both.shape[0] // 2
    product = matmul(both, high_table)
    return product[:n] + product[n:] + matmul(both[:n], low_table)


def kernel(
    ls_hbm, con_hbm, wide_hbm, tall_hbm, out_ref,
    ls_ref, con_ref, own, part_density, wide, tall, zhalo, rsend, rhalo, csend, sbuf, rsp, rsp_first, pst, xsend, cbuf, gsend, gbuf,
    ls_sem, con_sem, wide_sem, tall_sem, hs, hr, cs, cr, xs, xr, gs, gr,
):
    d = lax.axis_index("depth")
    p = lax.axis_index("plan")
    core = lax.rem(p, 2)
    zh = lax.rem(lax.div(p, 2), 2)
    q = lax.div(p, 4) * 2 + core
    z = zh * DEPTH + d
    lower = p < PLAN // 2

    def at_q(other):
        return (d, lax.div(other, 2) * 4 + zh * 2 + lax.rem(other, 2))

    def at_z(other):
        return (lax.rem(other, DEPTH), p + 2 * (lax.div(other, DEPTH) - zh))

    ls_copy = pltpu.make_async_copy(ls_hbm, ls_ref, ls_sem)
    con_copy = pltpu.make_async_copy(con_hbm, con_ref, con_sem)
    ls_copy.start()
    con_copy.start()
    wide_copy = pltpu.make_async_copy(wide_hbm, wide, wide_sem)
    tall_copy = pltpu.make_async_copy(tall_hbm, tall, tall_sem)
    wide_copy.start()
    tall_copy.start()

    barrier = pltpu.get_barrier_semaphore()

    def greet(target):
        pl.semaphore_signal(barrier, inc=1, device_id=target, device_id_type=MESH)

    has = (d < DEPTH - 1, d > 0, p < PLAN - 1, p > 0)
    gets = (d > 0, d < DEPTH - 1, p > 0, p < PLAN - 1)
    xy = lax.div(p, 4)
    outer = jnp.where(core == 0, p - 1, p + 1)
    has_outer = (outer >= 0) & (outer < PLAN)
    for k in (1, RING - 1):
        greet(at_z(lax.rem(z + k, RING)))
    greet((d, p + 1 - 2 * core))
    pl.when(has_outer)(lambda: greet((d, outer)))
    for k in range(1, GROUP // 2):
        first = 4 * lax.rem(xy + k, GROUP // 2) + 2 * zh
        greet((d, first))
        greet((d, first + 1))
    for k in range(2, RING - 1):
        greet(at_z(lax.rem(z + k, RING)))

    ls_copy.wait()
    con_copy.wait()

    for layer in range(2):
        value = ls_ref[layer]
        value = jnp.where(lower, flip(value, 0, ROWS), value)
        own[layer, :, :HALF] = value[:, HALF:]
        own[layer, :, HALF:] = flip_lanes(value[:, :HALF])

    for layer in range(2):
        for k in range(8):
            spot = layer * 8 + k
            top = own[layer, 0:1, 128 * k : 128 * (k + 1)]
            bottom = own[layer, ROWS - 1 : ROWS, 128 * k : 128 * (k + 1)]
            rsend[0, spot : spot + 1, :] = jnp.where(lower, bottom, top)
            rsend[1, spot : spot + 1, :] = jnp.where(lower, top, bottom)

    pl.semaphore_wait(barrier, GROUP + RING - 2 + has_outer.astype(jnp.int32))

    def halo(source, target, number, device):
        return pltpu.make_async_remote_copy(
            src_ref=source, dst_ref=target, send_sem=hs.at[number], recv_sem=hr.at[number],
            device_id=device, device_id_type=MESH,
        )

    z_up = halo(own.at[1], zhalo.at[0], 0, (d + 1, p))
    z_down = halo(own.at[0], zhalo.at[1], 1, (d - 1, p))
    r_up = halo(rsend.at[1], rhalo.at[0], 2, (d, p + 1))
    r_down = halo(rsend.at[0], rhalo.at[1], 3, (d, p - 1))
    lands = (zhalo.at[0], zhalo.at[1], rhalo.at[0], rhalo.at[1])
    copies = (z_up, z_down, r_up, r_down)
    for copy, there in zip(copies, has):
        pl.when(there)(copy.start)
    for land, comes in zip(lands, gets):

        @pl.when(jnp.logical_not(comes))
        def _(land=land):
            land[...] = jnp.zeros(land.shape, F32)

    row_id = lax.broadcasted_iota(jnp.int32, (ROWS, NX), 0)
    lane_id = lax.broadcasted_iota(jnp.int32, (ROWS, HALF), 1)
    field = [own[0], own[1]]
    middle = flux(field[1] - field[0])
    for layer in range(2):
        centre = field[layer]
        bend = -middle if layer else middle
        inner_flux = flux(pltpu.roll(centre, 1, 0) - centre)
        bend = bend + jnp.where(row_id == 0, 0.0, inner_flux)
        bend = bend - jnp.where(row_id == ROWS - 1, 0.0, pltpu.roll(inner_flux, ROWS - 1, 0))
        sides = centre[:, :HALF], centre[:, HALF:]
        across = []
        for side in range(2):
            here = sides[side]
            inside = jnp.where(lane_id == 0, sides[1 - side], pltpu.roll(here, 1, 1))
            inner_flux = flux(inside - here)
            outside = jnp.where(lane_id == HALF - 1, flux(here), pltpu.roll(inner_flux, HALF - 1, 1))
            across.append(inner_flux - outside)
        bend = bend + jnp.concatenate(across, axis=1)
        part_density[layer] = con_ref[layer] * (0.5 * (1.0 + jnp.tanh(centre))) + bend_weight * bend

    for copy, comes in zip(copies, gets):
        pl.when(comes)(copy.wait_recv)
    even, odd = [], []
    for layer in range(2):
        centre = own[layer]
        here = slice(layer * 8, layer * 8 + 8)
        top = jnp.where(lower, rhalo[1, here, :], rhalo[0, here, :])
        bottom = jnp.where(lower, rhalo[0, here, :], rhalo[1, here, :])
        tops = [jnp.broadcast_to(top[k : k + 1], (ROWS, 128)) for k in range(8)]
        bottoms = [jnp.broadcast_to(bottom[k : k + 1], (ROWS, 128)) for k in range(8)]
        beside = jnp.where(row_id == 0, jnp.concatenate(tops, axis=1), jnp.concatenate(bottoms, axis=1))
        outer_rows = (row_id == 0) | (row_id == ROWS - 1)
        bend = flux(zhalo[layer] - centre) + jnp.where(outer_rows, flux(beside - centre), 0.0)
        density = part_density[layer] + bend_weight * bend
        even.append(density[:, :HALF] + density[:, HALF:])
        odd.append(density[:, :HALF] - density[:, HALF:])

    block = jnp.where(lower, PLAN // 2 - 1 - p, p - PLAN // 2)
    half_lane = lax.broadcasted_iota(jnp.int32, (ROWS, 128), 1) < COEF
    wide_copy.wait()

    def send_coef(other):
        return pltpu.make_async_remote_copy(
            src_ref=csend.at[other], dst_ref=sbuf.at[block], send_sem=cs, recv_sem=cr,
            device_id=at_q(other), device_id_type=MESH,
        )

    for kind, folded in enumerate((even, odd)):
        both = pair(jnp.concatenate(folded, axis=0))
        for cut in range(2):
            cols = slice(HALF * cut, HALF * (cut + 1))
            coef = table_right(both, wide[kind, 0, :, cols], wide[kind, 1, :, cols])
            start = kind * 16 + 8 * cut
            for m in range(4):
                first = coef[:ROWS, 128 * m : 128 * (m + 1)]
                second = coef[ROWS:, 128 * m : 128 * (m + 1)]
                csend[start + 2 * m] = jnp.where(half_lane, first, pltpu.roll(second, COEF, 1))
                csend[start + 2 * m + 1] = jnp.where(half_lane, pltpu.roll(first, COEF, 1), second)
            for k in range(8):
                other = start + lax.rem(q + k, 8)
                if k == 0:
                    pl.when(other != q)(send_coef(other).start)
                else:
                    send_coef(other).start()

    def respond(start, is_sin):
        row = lax.broadcasted_iota(jnp.int32, (128, 128), 0)
        col = lax.broadcasted_iota(jnp.int32, (128, 128), 1) + start
        place = lax.rem(q, GROUP // 2) * COEF + lax.rem(row, COEF)
        v = jnp.where((place == 0) & (q >= GROUP // 2), NX, place).astype(F32)
        scale = 2.0 * math.pi * grav_scale * thickness / (4.0 * NX * NX)
        weight = jnp.where(place == 0, scale, 2.0 * scale) * jnp.where(col == 0, 1.0, 2.0)
        layer = (2 * d + lax.div(row, COEF)).astype(F32)
        rate = (top_depth + (layer + 0.5) * thickness) * (-2.0 * math.pi / (2 * NX))
        u = (jnp.where(col == 0, NX, col) if is_sin else col).astype(F32)
        return jnp.exp(jnp.sqrt(u * u + v * v) * rate) * weight

    rsp_first[...] = respond(0, True)
    for k in range(NX // 128):
        rsp[:, 128 * k : 128 * (k + 1)] = respond(128 * k, False)

    sbuf[block] = csend[q]
    pltpu.make_async_copy(sbuf.at[pl.ds(0, GROUP - 1)], sbuf.at[pl.ds(0, GROUP - 1)], cr).wait()

    tall_copy.wait()
    value = sbuf[...].reshape(HALF, 128).T
    side = lax.rem(lax.div(lax.broadcasted_iota(jnp.int32, (128, HALF), 1), 2 * ROWS), 2)
    step = 256
    for kind in range(2):
        both = pair(jnp.where(side == zh, value, -value) if kind else value)
        for k in range(NX // step):
            here = slice(k * step, (k + 1) * step)
            coef = table_right(both, wide[kind, 0, :, here], wide[kind, 1, :, here])
            factor = rsp[:, here]
            if kind == 1 and k == 0:
                factor = jnp.concatenate([rsp_first[...], factor[:, 128:]], axis=1)
            coef = coef * factor
            pst[kind, :, here] = pair(coef[:COEF] + coef[COEF:])

    def send_rows(other):
        return pltpu.make_async_remote_copy(
            src_ref=xsend.at[other], dst_ref=cbuf.at[q], send_sem=xs, recv_sem=xr,
            device_id=at_q(other), device_id_type=MESH,
        )

    for part in range(2):
        cols = slice(256 * part, 256 * (part + 1))
        parity = [table_right(pst[kind], tall[kind, 0, :, cols], tall[kind, 1, :, cols]) for kind in range(2)]
        value = jnp.concatenate([parity[0] + parity[1], parity[0] - parity[1]], axis=0).T
        for g in range(4):
            plain = [value[ROWS * (4 * g + n) : ROWS * (4 * g + n + 1)] for n in range(4)]
            turned = [pltpu.roll(block_now, COEF, 1) for block_now in plain]
            chunk = 4 * part + g
            xsend[2 * (8 + chunk)] = jnp.where(half_lane, plain[0], turned[2])
            xsend[2 * (8 + chunk) + 1] = jnp.where(half_lane, plain[1], turned[3])
            xsend[2 * (7 - chunk)] = jnp.where(half_lane, turned[3], plain[1])
            xsend[2 * (7 - chunk) + 1] = jnp.where(half_lane, turned[2], plain[0])

        for k in range(16):
            spot = lax.rem(q + k, 16)
            upper = lax.div(spot, 8)
            other = spot + 16 * (upper if part else 1 - upper)
            if k == 0:
                pl.when(other != q)(send_rows(other).start)
            else:
                send_rows(other).start()

    cbuf[q] = xsend[q]
    pltpu.make_async_copy(cbuf.at[pl.ds(0, GROUP - 1)], cbuf.at[pl.ds(0, GROUP - 1)], xr).wait()

    def send_field(other):
        return pltpu.make_async_remote_copy(
            src_ref=gsend.at[other], dst_ref=gbuf.at[z], send_sem=gs, recv_sem=gr,
            device_id=at_z(other), device_id_type=MESH,
        )

    pairs = []
    for kind in range(2):
        tops, bottoms = [], []
        for m in range(8):
            first, second = cbuf[kind * 16 + 2 * m], cbuf[kind * 16 + 2 * m + 1]
            tops.append(jnp.where(half_lane, first, pltpu.roll(second, COEF, 1)))
            bottoms.append(jnp.where(half_lane, pltpu.roll(first, COEF, 1), second))
        value = jnp.concatenate([jnp.concatenate(tops, axis=1), jnp.concatenate(bottoms, axis=1)], axis=0)
        pairs.append(pair(value))
    for cut in range(2):
        cols = slice(256 * cut, 256 * (cut + 1))
        parity = [table_right(pairs[kind], tall[kind, 0, :, cols], tall[kind, 1, :, cols]) for kind in range(2)]
        plus = parity[0] + parity[1]
        minus = parity[0] - parity[1]
        for half in range(2):
            rows = slice(ROWS * half, ROWS * (half + 1))
            for n in range(2):
                lanes = slice(128 * n, 128 * (n + 1))
                gsend[DEPTH * half + 4 + 2 * cut + n] = plus[rows, lanes]
                gsend[DEPTH * half + 3 - 2 * cut - n] = minus[rows, lanes]
        for k in range(8):
            turn = lax.rem(4 * zh + lax.rem(d + 2, 4) + k, 8)
            other = DEPTH * lax.div(turn, 4) + lax.rem(2 + 4 * cut + lax.rem(turn, 4), DEPTH)
            if k == 0:
                pl.when(other != z)(send_field(other).start)
            else:
                send_field(other).start()

    gbuf[z] = gsend[z]
    pltpu.make_async_copy(gbuf.at[pl.ds(0, RING - 1)], gbuf.at[pl.ds(0, RING - 1)], gr).wait()
    total = gbuf[0]
    for other in range(1, RING):
        total = total + gbuf[other]
    across = lax.broadcasted_iota(jnp.int32, (128, 128), 0) + lax.broadcasted_iota(jnp.int32, (128, 128), 1)
    reverse = jnp.where(across == 127, 1.0, 0.0).astype(BF16)
    high, rest = split(total)
    low = (total - high.astype(F32) - rest.astype(F32)).astype(BF16)
    turned = matmul(jnp.concatenate([high, rest, low], axis=0), reverse)
    turned = turned[:ROWS] + turned[ROWS : 2 * ROWS] + turned[2 * ROWS :]
    total = jnp.where(d < DEPTH // 2, turned, total)

    @pl.when(lower)
    def _():
        for row in range(ROWS):
            out_ref[ROWS - 1 - row : ROWS - row, :] = total[row : row + 1]

    @pl.when(jnp.logical_not(lower))
    def _():
        out_ref[...] = total

    for copy, there in zip(copies, has):
        pl.when(there)(copy.wait_send)
    pltpu.make_async_copy(csend.at[pl.ds(0, GROUP - 1)], csend.at[pl.ds(0, GROUP - 1)], cs).wait()
    pltpu.make_async_copy(xsend.at[pl.ds(0, GROUP - 1)], xsend.at[pl.ds(0, GROUP - 1)], xs).wait()
    pltpu.make_async_copy(gsend.at[pl.ds(0, RING - 1)], gsend.at[pl.ds(0, RING - 1)], gs).wait()


def solution(mesh):
    wide, tall = basis()

    def step(level_set, contrast):
        vmem = pl.BlockSpec(memory_space=pltpu.VMEM)
        anywhere = pl.BlockSpec(memory_space=pl.ANY)
        dma = pltpu.SemaphoreType.DMA
        return pl.pallas_call(
            kernel,
            out_shape=jax.ShapeDtypeStruct((ROWS, 128), F32),
            in_specs=[anywhere] * 4,
            out_specs=vmem,
            scratch_shapes=[
                pltpu.VMEM((2, ROWS, NX), F32),
                pltpu.SMEM((2,), F32),
                pltpu.VMEM((2, ROWS, NX), F32),
                pltpu.VMEM((2, ROWS, NX), F32),
                pltpu.VMEM((2, 2, HALF, NX), BF16),
                pltpu.VMEM((2, 2, NX, HALF), BF16),
                pltpu.VMEM((2, ROWS, NX), F32),
                pltpu.VMEM((2, 16, 128), F32),
                pltpu.VMEM((2, 16, 128), F32),
                pltpu.VMEM((GROUP, ROWS, 128), F32),
                pltpu.VMEM((GROUP, ROWS, 128), F32),
                pltpu.VMEM((128, NX), F32),
                pltpu.VMEM((128, 128), F32),
                pltpu.VMEM((2, 128, NX), BF16),
                pltpu.VMEM((GROUP, ROWS, 128), F32),
                pltpu.VMEM((GROUP, ROWS, 128), F32),
                pltpu.VMEM((RING, ROWS, 128), F32),
                pltpu.VMEM((RING, ROWS, 128), F32),
                dma(()), dma(()), dma(()), dma(()), dma((4,)), dma((4,)),
                dma(()), dma(()), dma(()), dma(()), dma(()), dma(()),
            ],
            compiler_params=pltpu.CompilerParams(
                collective_id=0, has_side_effects=True, vmem_limit_bytes=63 * 1024 * 1024
            ),
        )(level_set, contrast, jnp.asarray(wide), jnp.asarray(tall))

    return jax.shard_map(
        step,
        mesh=mesh,
        in_specs=(P("depth", "plan", None), P("depth")),
        out_specs=P("plan", "depth"),
        check_vma=False,
    )
```

```python
import functools
import math

import jax
import jax.numpy as jnp
import ml_dtypes
import numpy as np
from jax import lax
from jax.experimental import pallas as pl
from jax.experimental.pallas import tpu as pltpu
from jax.sharding import PartitionSpec as P

MESH = pl.DeviceIdType.MESH
F32 = jnp.float32
BF16 = jnp.bfloat16

NX = 1024
HALF = NX // 2
LAYERS = 16
DEPTH = 8
PLAN = 64
ROWS = NX // PLAN
GROUP = 32
RING = 16
COEF = 2 * NX // GROUP

bend_weight = 0.5
grav_scale = 0.05
top_depth = 0.0
thickness = 1.0


def basis():
    j = np.arange(HALF, dtype=np.float64)[:, None] + 0.5
    v = np.arange(NX, dtype=np.float64)[None, :]
    table = np.cos(np.pi * v * j / NX)
    high = table.astype(ml_dtypes.bfloat16)
    low = (table - high.astype(np.float64)).astype(ml_dtypes.bfloat16)
    wide = np.stack([high, low])
    return wide, np.ascontiguousarray(np.swapaxes(wide, 1, 2))


def alternating(shape):
    return 1.0 - 2.0 * lax.rem(lax.broadcasted_iota(jnp.int32, shape, 1), 2).astype(F32)


def flux(step):
    return step * lax.rsqrt(1.0 + step * step)


def flip(value, axis, size):
    index = lax.broadcasted_iota(jnp.int32, value.shape, axis)
    step = size // 2
    value = pltpu.roll(value, step, axis)
    while step > 1:
        step //= 2
        up = pltpu.roll(value, step, axis)
        down = pltpu.roll(value, size - step, axis)
        value = jnp.where((index & step) != 0, up, down)
    return value


def flip_lanes(value):
    blocks = value.shape[1] // 128
    parts = [flip(value[:, 128 * k : 128 * (k + 1)], 1, 128) for k in reversed(range(blocks))]
    return jnp.concatenate(parts, axis=1) if blocks > 1 else parts[0]


def split(value):
    high = value.astype(BF16)
    low = (value - high.astype(F32)).astype(BF16)
    return high, low


def matmul(a, b):
    return jnp.dot(a, b, preferred_element_type=F32)


def pair(value):
    return jnp.concatenate(split(value), axis=0)


def table_right(both, high_table, low_table):
    n = both.shape[0] // 2
    product = matmul(both, high_table)
    return product[:n] + product[n:] + matmul(both[:n], low_table)


def kernel(
    ls_hbm, con_hbm, wide_hbm, tall_hbm, out_ref,
    ls_ref, con_ref, own, part_density, wide, tall, zhalo, rsend, rhalo, csend, sbuf, rsp, pst, xsend, cbuf, gsend, gbuf,
    ls_sem, con_sem, wide_sem, tall_sem, hs, hr, cs, cr, xs, xr, gs, gr,
):
    d = lax.axis_index("depth")
    p = lax.axis_index("plan")
    core = lax.rem(p, 2)
    zh = lax.rem(lax.div(p, 2), 2)
    q = lax.div(p, 4) * 2 + core
    z = zh * DEPTH + d
    lower = p < PLAN // 2

    def at_q(other):
        return (d, lax.div(other, 2) * 4 + zh * 2 + lax.rem(other, 2))

    def at_z(other):
        return (lax.rem(other, DEPTH), p + 2 * (lax.div(other, DEPTH) - zh))

    ls_copy = pltpu.make_async_copy(ls_hbm, ls_ref, ls_sem)
    con_copy = pltpu.make_async_copy(con_hbm, con_ref, con_sem)
    ls_copy.start()
    con_copy.start()
    wide_copies = [pltpu.make_async_copy(wide_hbm.at[n], wide.at[n], wide_sem.at[n]) for n in range(2)]
    tall_copies = [pltpu.make_async_copy(tall_hbm.at[n], tall.at[n], tall_sem.at[n]) for n in range(2)]
    for copy in wide_copies:
        copy.start()

    barrier = pltpu.get_barrier_semaphore()

    def greet(target):
        pl.semaphore_signal(barrier, inc=1, device_id=target, device_id_type=MESH)

    has = (d < DEPTH - 1, d > 0, p < PLAN - 1, p > 0)
    gets = (d > 0, d < DEPTH - 1, p > 0, p < PLAN - 1)
    xy = lax.div(p, 4)
    outer = jnp.where(core == 0, p - 1, p + 1)
    has_outer = (outer >= 0) & (outer < PLAN)
    for k in (1, RING - 1):
        greet(at_z(lax.rem(z + k, RING)))
    greet((d, p + 1 - 2 * core))
    pl.when(has_outer)(lambda: greet((d, outer)))
    for k in range(1, GROUP // 2):
        first = 4 * lax.rem(xy + k, GROUP // 2) + 2 * zh
        greet((d, first))
        greet((d, first + 1))
    for k in range(2, RING - 1):
        greet(at_z(lax.rem(z + k, RING)))

    ls_copy.wait()
    con_copy.wait()

    for layer in range(2):
        value = ls_ref[layer]
        value = jnp.where(lower, flip(value, 0, ROWS), value)
        own[layer, :, :HALF] = value[:, HALF:]
        own[layer, :, HALF:] = flip_lanes(value[:, :HALF])

    for layer in range(2):
        for k in range(8):
            spot = layer * 8 + k
            top = own[layer, 0:1, 128 * k : 128 * (k + 1)]
            bottom = own[layer, ROWS - 1 : ROWS, 128 * k : 128 * (k + 1)]
            rsend[0, spot : spot + 1, :] = jnp.where(lower, bottom, top)
            rsend[1, spot : spot + 1, :] = jnp.where(lower, top, bottom)

    pl.semaphore_wait(barrier, GROUP + RING - 2 + has_outer.astype(jnp.int32))

    def halo(source, target, number, device):
        return pltpu.make_async_remote_copy(
            src_ref=source, dst_ref=target, send_sem=hs.at[number], recv_sem=hr.at[number],
            device_id=device, device_id_type=MESH,
        )

    z_up = halo(own.at[1], zhalo.at[0], 0, (d + 1, p))
    z_down = halo(own.at[0], zhalo.at[1], 1, (d - 1, p))
    r_up = halo(rsend.at[1], rhalo.at[0], 2, (d, p + 1))
    r_down = halo(rsend.at[0], rhalo.at[1], 3, (d, p - 1))
    lands = (zhalo.at[0], zhalo.at[1], rhalo.at[0], rhalo.at[1])
    copies = (z_up, z_down, r_up, r_down)
    for copy, there in zip(copies, has):
        pl.when(there)(copy.start)
    for copy in tall_copies:
        copy.start()
    for land, comes in zip(lands, gets):

        @pl.when(jnp.logical_not(comes))
        def _(land=land):
            land[...] = jnp.zeros(land.shape, F32)

    row_id = lax.broadcasted_iota(jnp.int32, (ROWS, NX), 0)
    lane_id = lax.broadcasted_iota(jnp.int32, (ROWS, HALF), 1)
    field = [own[0], own[1]]
    middle = flux(field[1] - field[0])
    for layer in range(2):
        centre = field[layer]
        bend = -middle if layer else middle
        inner_flux = flux(pltpu.roll(centre, 1, 0) - centre)
        bend = bend + jnp.where(row_id == 0, 0.0, inner_flux)
        bend = bend - jnp.where(row_id == ROWS - 1, 0.0, pltpu.roll(inner_flux, ROWS - 1, 0))
        sides = centre[:, :HALF], centre[:, HALF:]
        across = []
        for side in range(2):
            here = sides[side]
            inside = jnp.where(lane_id == 0, sides[1 - side], pltpu.roll(here, 1, 1))
            inner_flux = flux(inside - here)
            outside = jnp.where(lane_id == HALF - 1, flux(here), pltpu.roll(inner_flux, HALF - 1, 1))
            across.append(inner_flux - outside)
        bend = bend + jnp.concatenate(across, axis=1)
        part_density[layer] = con_ref[layer] * (0.5 * (1.0 + jnp.tanh(centre))) + bend_weight * bend

    for copy, comes in zip(copies, gets):
        pl.when(comes)(copy.wait_recv)
    even, odd = [], []
    for layer in range(2):
        centre = own[layer]
        here = slice(layer * 8, layer * 8 + 8)
        top = jnp.where(lower, rhalo[1, here, :], rhalo[0, here, :])
        bottom = jnp.where(lower, rhalo[0, here, :], rhalo[1, here, :])
        tops = [jnp.broadcast_to(top[k : k + 1], (ROWS, 128)) for k in range(8)]
        bottoms = [jnp.broadcast_to(bottom[k : k + 1], (ROWS, 128)) for k in range(8)]
        beside = jnp.where(row_id == 0, jnp.concatenate(tops, axis=1), jnp.concatenate(bottoms, axis=1))
        outer_rows = (row_id == 0) | (row_id == ROWS - 1)
        bend = flux(zhalo[layer] - centre) + jnp.where(outer_rows, flux(beside - centre), 0.0)
        density = part_density[layer] + bend_weight * bend
        even.append(density[:, :HALF] + density[:, HALF:])
        odd.append((density[:, :HALF] - density[:, HALF:]) * alternating((ROWS, HALF)))

    block = jnp.where(lower, PLAN // 2 - 1 - p, p - PLAN // 2)
    half_lane = lax.broadcasted_iota(jnp.int32, (ROWS, 128), 1) < COEF
    for copy in wide_copies:
        copy.wait()

    def send_coef(other):
        return pltpu.make_async_remote_copy(
            src_ref=csend.at[other], dst_ref=sbuf.at[block], send_sem=cs, recv_sem=cr,
            device_id=at_q(other), device_id_type=MESH,
        )

    both = pair(jnp.concatenate(even + odd, axis=0))
    for cut in range(2):
        cols = slice(HALF * cut, HALF * (cut + 1))
        coef = table_right(both, wide[0, :, cols], wide[1, :, cols])
        for kind in range(2):
            start = kind * 16 + 8 * cut
            for m in range(4):
                first = coef[2 * ROWS * kind : 2 * ROWS * kind + ROWS, 128 * m : 128 * (m + 1)]
                second = coef[2 * ROWS * kind + ROWS : 2 * ROWS * (kind + 1), 128 * m : 128 * (m + 1)]
                csend[start + 2 * m] = jnp.where(half_lane, first, pltpu.roll(second, COEF, 1))
                csend[start + 2 * m + 1] = jnp.where(half_lane, pltpu.roll(first, COEF, 1), second)
            for k in range(8):
                other = start + lax.rem(q + k, 8)
                if k == 0:
                    pl.when(other != q)(send_coef(other).start)
                else:
                    send_coef(other).start()

    def respond(start, is_sin):
        row = lax.broadcasted_iota(jnp.int32, (128, 128), 0)
        col = lax.broadcasted_iota(jnp.int32, (128, 128), 1) + start
        place = lax.rem(q, GROUP // 2) * COEF + lax.rem(row, COEF)
        v = jnp.where(q >= GROUP // 2, NX - place, place).astype(F32)
        scale = 2.0 * math.pi * grav_scale * thickness / (4.0 * NX * NX)
        weight = jnp.where(place == 0, scale, 2.0 * scale) * jnp.where(col == 0, 1.0, 2.0)
        layer = (2 * d + lax.div(row, COEF)).astype(F32)
        rate = (top_depth + (layer + 0.5) * thickness) * (-2.0 * math.pi / (2 * NX))
        u = (NX - col if is_sin else col).astype(F32)
        return jnp.exp(jnp.sqrt(u * u + v * v) * rate) * weight

    for kind in range(2):
        for k in range(NX // 128):
            rsp[128 * kind : 128 * (kind + 1), 128 * k : 128 * (k + 1)] = respond(128 * k, kind == 1)

    sbuf[block] = csend[q]
    pltpu.make_async_copy(sbuf.at[pl.ds(0, GROUP - 1)], sbuf.at[pl.ds(0, GROUP - 1)], cr).wait()

    for copy in tall_copies:
        copy.wait()
    value = sbuf[...].reshape(HALF, 128).T
    side = lax.rem(lax.div(lax.broadcasted_iota(jnp.int32, (128, HALF), 1), 2 * ROWS), 2)
    value = jnp.concatenate([value, jnp.where(side == zh, value, -value) * alternating((128, HALF))], axis=0)
    both = pair(value)
    step = 256
    for k in range(NX // step):
        here = slice(k * step, (k + 1) * step)
        coef = table_right(both, wide[0, :, here], wide[1, :, here]) * rsp[:, here]
        cosine = coef[:COEF] + coef[COEF : 2 * COEF]
        sine = coef[2 * COEF : 3 * COEF] + coef[3 * COEF :]
        pst[:, here] = pair(jnp.concatenate([cosine, sine], axis=0))

    def send_rows(other):
        return pltpu.make_async_remote_copy(
            src_ref=xsend.at[other], dst_ref=cbuf.at[q], send_sem=xs, recv_sem=xr,
            device_id=at_q(other), device_id_type=MESH,
        )

    for part in range(2):
        cols = slice(256 * part, 256 * (part + 1))
        value = table_right(pst[...], tall[0, :, cols], tall[1, :, cols])
        evens, odds = value[:COEF], value[COEF:] * alternating((COEF, 256))
        value = jnp.concatenate([evens + odds, evens - odds], axis=0).T
        for g in range(4):
            plain = [value[ROWS * (4 * g + n) : ROWS * (4 * g + n + 1)] for n in range(4)]
            turned = [pltpu.roll(block_now, COEF, 1) for block_now in plain]
            chunk = 4 * part + g
            xsend[2 * (8 + chunk)] = jnp.where(half_lane, plain[0], turned[2])
            xsend[2 * (8 + chunk) + 1] = jnp.where(half_lane, plain[1], turned[3])
            xsend[2 * (7 - chunk)] = jnp.where(half_lane, turned[3], plain[1])
            xsend[2 * (7 - chunk) + 1] = jnp.where(half_lane, turned[2], plain[0])

        for k in range(16):
            spot = lax.rem(q + k, 16)
            upper = lax.div(spot, 8)
            other = spot + 16 * (upper if part else 1 - upper)
            if k == 0:
                pl.when(other != q)(send_rows(other).start)
            else:
                send_rows(other).start()

    cbuf[q] = xsend[q]
    pltpu.make_async_copy(cbuf.at[pl.ds(0, GROUP - 1)], cbuf.at[pl.ds(0, GROUP - 1)], xr).wait()

    def send_field(other):
        return pltpu.make_async_remote_copy(
            src_ref=gsend.at[other], dst_ref=gbuf.at[z], send_sem=gs, recv_sem=gr,
            device_id=at_z(other), device_id_type=MESH,
        )

    values = []
    for kind in range(2):
        tops, bottoms = [], []
        for m in range(8):
            first, second = cbuf[kind * 16 + 2 * m], cbuf[kind * 16 + 2 * m + 1]
            tops.append(jnp.where(half_lane, first, pltpu.roll(second, COEF, 1)))
            bottoms.append(jnp.where(half_lane, pltpu.roll(first, COEF, 1), second))
        values += [jnp.concatenate(tops, axis=1), jnp.concatenate(bottoms, axis=1)]
    both = pair(jnp.concatenate(values, axis=0))
    for cut in range(2):
        cols = slice(256 * cut, 256 * (cut + 1))
        value = table_right(both, tall[0, :, cols], tall[1, :, cols])
        evens, odds = value[: 2 * ROWS], value[2 * ROWS :] * alternating((2 * ROWS, 256))
        plus = evens + odds
        minus = evens - odds
        for half in range(2):
            rows = slice(ROWS * half, ROWS * (half + 1))
            for n in range(2):
                lanes = slice(128 * n, 128 * (n + 1))
                gsend[DEPTH * half + 4 + 2 * cut + n] = plus[rows, lanes]
                gsend[DEPTH * half + 3 - 2 * cut - n] = minus[rows, lanes]
        for k in range(8):
            turn = lax.rem(4 * zh + lax.rem(d + 2, 4) + k, 8)
            other = DEPTH * lax.div(turn, 4) + lax.rem(2 + 4 * cut + lax.rem(turn, 4), DEPTH)
            if k == 0:
                pl.when(other != z)(send_field(other).start)
            else:
                send_field(other).start()

    gbuf[z] = gsend[z]
    pltpu.make_async_copy(gbuf.at[pl.ds(0, RING - 1)], gbuf.at[pl.ds(0, RING - 1)], gr).wait()
    total = gbuf[0]
    for other in range(1, RING):
        total = total + gbuf[other]
    across = lax.broadcasted_iota(jnp.int32, (128, 128), 0) + lax.broadcasted_iota(jnp.int32, (128, 128), 1)
    reverse = jnp.where(across == 127, 1.0, 0.0).astype(BF16)
    high, rest = split(total)
    low = (total - high.astype(F32) - rest.astype(F32)).astype(BF16)
    turned = matmul(jnp.concatenate([high, rest, low], axis=0), reverse)
    turned = turned[:ROWS] + turned[ROWS : 2 * ROWS] + turned[2 * ROWS :]
    total = jnp.where(d < DEPTH // 2, turned, total)

    @pl.when(lower)
    def _():
        for row in range(ROWS):
            out_ref[ROWS - 1 - row : ROWS - row, :] = total[row : row + 1]

    @pl.when(jnp.logical_not(lower))
    def _():
        out_ref[...] = total

    for copy, there in zip(copies, has):
        pl.when(there)(copy.wait_send)
    pltpu.make_async_copy(csend.at[pl.ds(0, GROUP - 1)], csend.at[pl.ds(0, GROUP - 1)], cs).wait()
    pltpu.make_async_copy(xsend.at[pl.ds(0, GROUP - 1)], xsend.at[pl.ds(0, GROUP - 1)], xs).wait()
    pltpu.make_async_copy(gsend.at[pl.ds(0, RING - 1)], gsend.at[pl.ds(0, RING - 1)], gs).wait()


def solution(mesh):
    wide, tall = basis()

    def step(level_set, contrast):
        vmem = pl.BlockSpec(memory_space=pltpu.VMEM)
        anywhere = pl.BlockSpec(memory_space=pl.ANY)
        dma = pltpu.SemaphoreType.DMA
        return pl.pallas_call(
            kernel,
            out_shape=jax.ShapeDtypeStruct((ROWS, 128), F32),
            in_specs=[anywhere] * 4,
            out_specs=vmem,
            scratch_shapes=[
                pltpu.VMEM((2, ROWS, NX), F32),
                pltpu.SMEM((2,), F32),
                pltpu.VMEM((2, ROWS, NX), F32),
                pltpu.VMEM((2, ROWS, NX), F32),
                pltpu.VMEM((2, HALF, NX), BF16),
                pltpu.VMEM((2, NX, HALF), BF16),
                pltpu.VMEM((2, ROWS, NX), F32),
                pltpu.VMEM((2, 16, 128), F32),
                pltpu.VMEM((2, 16, 128), F32),
                pltpu.VMEM((GROUP, ROWS, 128), F32),
                pltpu.VMEM((GROUP, ROWS, 128), F32),
                pltpu.VMEM((256, NX), F32),
                pltpu.VMEM((256, NX), BF16),
                pltpu.VMEM((GROUP, ROWS, 128), F32),
                pltpu.VMEM((GROUP, ROWS, 128), F32),
                pltpu.VMEM((RING, ROWS, 128), F32),
                pltpu.VMEM((RING, ROWS, 128), F32),
                dma(()), dma(()), dma((2,)), dma((2,)), dma((4,)), dma((4,)),
                dma(()), dma(()), dma(()), dma(()), dma(()), dma(()),
            ],
            compiler_params=pltpu.CompilerParams(
                collective_id=0, has_side_effects=True, vmem_limit_bytes=63 * 1024 * 1024
            ),
        )(level_set, contrast, jnp.asarray(wide), jnp.asarray(tall))

    return jax.shard_map(
        step,
        mesh=mesh,
        in_specs=(P("depth", "plan", None), P("depth")),
        out_specs=P("plan", "depth"),
        check_vma=False,
    )
```

```python
import functools
import math

import jax
import jax.numpy as jnp
import ml_dtypes
import numpy as np
from jax import lax
from jax.experimental import pallas as pl
from jax.experimental.pallas import tpu as pltpu
from jax.sharding import PartitionSpec as P

MESH = pl.DeviceIdType.MESH
F32 = jnp.float32
BF16 = jnp.bfloat16

NX = 1024
HALF = NX // 2
LAYERS = 16
DEPTH = 8
PLAN = 64
ROWS = NX // PLAN
GROUP = 32
RING = 16
COEF = 2 * NX // GROUP

bend_weight = 0.5
grav_scale = 0.05
top_depth = 0.0
thickness = 1.0


def basis():
    j = np.arange(HALF, dtype=np.float64)[:, None] + 0.5
    v = np.arange(NX, dtype=np.float64)[None, :]
    table = np.cos(np.pi * v * j / NX)
    high = table.astype(ml_dtypes.bfloat16)
    low = (table - high.astype(np.float64)).astype(ml_dtypes.bfloat16)
    wide = np.stack([high, low])
    return wide, np.ascontiguousarray(np.swapaxes(wide, 1, 2))


def alternating(shape):
    return 1.0 - 2.0 * lax.rem(lax.broadcasted_iota(jnp.int32, shape, 1), 2).astype(F32)


def flux(step):
    return step * lax.rsqrt(1.0 + step * step)


def flip(value, axis, size):
    index = lax.broadcasted_iota(jnp.int32, value.shape, axis)
    step = size // 2
    value = pltpu.roll(value, step, axis)
    while step > 1:
        step //= 2
        up = pltpu.roll(value, step, axis)
        down = pltpu.roll(value, size - step, axis)
        value = jnp.where((index & step) != 0, up, down)
    return value


def flip_lanes(value):
    blocks = value.shape[1] // 128
    parts = [flip(value[:, 128 * k : 128 * (k + 1)], 1, 128) for k in reversed(range(blocks))]
    return jnp.concatenate(parts, axis=1) if blocks > 1 else parts[0]


def split(value):
    high = value.astype(BF16)
    low = (value - high.astype(F32)).astype(BF16)
    return high, low


def matmul(a, b):
    return jnp.dot(a, b, preferred_element_type=F32)


def pair(value):
    return jnp.concatenate(split(value), axis=0)


def table_right(both, high_table, low_table):
    n = both.shape[0] // 2
    product = matmul(both, high_table)
    return product[:n] + product[n:] + matmul(both[:n], low_table)


def kernel(
    ls_hbm, con_hbm, wide_hbm, tall_hbm, out_ref,
    ls_ref, con_ref, own, part_density, wide, tall, zhalo, rsend, rhalo, csend, sbuf, rsp, pst, xsend, cbuf, gsend, gbuf,
    ls_sem, con_sem, wide_sem, tall_sem, hs, hr, cs, cr, xs, xr, gs, gr,
):
    d = lax.axis_index("depth")
    p = lax.axis_index("plan")
    core = lax.rem(p, 2)
    zh = lax.rem(lax.div(p, 2), 2)
    q = lax.div(p, 4) * 2 + core
    z = zh * DEPTH + d
    lower = p < PLAN // 2

    def at_q(other):
        return (d, lax.div(other, 2) * 4 + zh * 2 + lax.rem(other, 2))

    def at_z(other):
        return (lax.rem(other, DEPTH), p + 2 * (lax.div(other, DEPTH) - zh))

    ls_copy = pltpu.make_async_copy(ls_hbm, ls_ref, ls_sem)
    con_copy = pltpu.make_async_copy(con_hbm, con_ref, con_sem)
    ls_copy.start()
    con_copy.start()
    wide_copies = [pltpu.make_async_copy(wide_hbm.at[n], wide.at[n], wide_sem.at[n]) for n in range(2)]
    tall_copies = [pltpu.make_async_copy(tall_hbm.at[n], tall.at[n], tall_sem.at[n]) for n in range(2)]
    for copy in wide_copies:
        copy.start()

    barrier = pltpu.get_barrier_semaphore()

    def greet(target):
        pl.semaphore_signal(barrier, inc=1, device_id=target, device_id_type=MESH)

    has = (d < DEPTH - 1, d > 0, p < PLAN - 1, p > 0)
    gets = (d > 0, d < DEPTH - 1, p > 0, p < PLAN - 1)
    xy = lax.div(p, 4)
    outer = jnp.where(core == 0, p - 1, p + 1)
    has_outer = (outer >= 0) & (outer < PLAN)
    for k in (1, RING - 1):
        greet(at_z(lax.rem(z + k, RING)))
    greet((d, p + 1 - 2 * core))
    pl.when(has_outer)(lambda: greet((d, outer)))
    for k in range(1, GROUP // 2):
        first = 4 * lax.rem(xy + k, GROUP // 2) + 2 * zh
        greet((d, first))
        greet((d, first + 1))
    for k in range(2, RING - 1):
        greet(at_z(lax.rem(z + k, RING)))

    ls_copy.wait()
    con_copy.wait()

    for layer in range(2):
        value = ls_ref[layer]
        value = jnp.where(lower, flip(value, 0, ROWS), value)
        own[layer, :, :HALF] = value[:, HALF:]
        own[layer, :, HALF:] = flip_lanes(value[:, :HALF])

    for layer in range(2):
        for k in range(8):
            spot = layer * 8 + k
            top = own[layer, 0:1, 128 * k : 128 * (k + 1)]
            bottom = own[layer, ROWS - 1 : ROWS, 128 * k : 128 * (k + 1)]
            rsend[0, spot : spot + 1, :] = jnp.where(lower, bottom, top)
            rsend[1, spot : spot + 1, :] = jnp.where(lower, top, bottom)

    pl.semaphore_wait(barrier, GROUP + RING - 2 + has_outer.astype(jnp.int32))

    def halo(source, target, number, device):
        return pltpu.make_async_remote_copy(
            src_ref=source, dst_ref=target, send_sem=hs.at[number], recv_sem=hr.at[number],
            device_id=device, device_id_type=MESH,
        )

    z_up = halo(own.at[1], zhalo.at[0], 0, (d + 1, p))
    z_down = halo(own.at[0], zhalo.at[1], 1, (d - 1, p))
    r_up = halo(rsend.at[1], rhalo.at[0], 2, (d, p + 1))
    r_down = halo(rsend.at[0], rhalo.at[1], 3, (d, p - 1))
    lands = (zhalo.at[0], zhalo.at[1], rhalo.at[0], rhalo.at[1])
    copies = (z_up, z_down, r_up, r_down)
    for copy, there in zip(copies, has):
        pl.when(there)(copy.start)
    for copy in tall_copies:
        copy.start()
    for land, comes in zip(lands, gets):

        @pl.when(jnp.logical_not(comes))
        def _(land=land):
            land[...] = jnp.zeros(land.shape, F32)

    row_id = lax.broadcasted_iota(jnp.int32, (ROWS, NX), 0)
    lane_id = lax.broadcasted_iota(jnp.int32, (ROWS, HALF), 1)
    field = [own[0], own[1]]
    middle = flux(field[1] - field[0])
    for layer in range(2):
        centre = field[layer]
        bend = -middle if layer else middle
        inner_flux = flux(pltpu.roll(centre, 1, 0) - centre)
        bend = bend + jnp.where(row_id == 0, 0.0, inner_flux)
        bend = bend - jnp.where(row_id == ROWS - 1, 0.0, pltpu.roll(inner_flux, ROWS - 1, 0))
        sides = centre[:, :HALF], centre[:, HALF:]
        across = []
        for side in range(2):
            here = sides[side]
            inside = jnp.where(lane_id == 0, sides[1 - side], pltpu.roll(here, 1, 1))
            inner_flux = flux(inside - here)
            outside = jnp.where(lane_id == HALF - 1, flux(here), pltpu.roll(inner_flux, HALF - 1, 1))
            across.append(inner_flux - outside)
        bend = bend + jnp.concatenate(across, axis=1)
        part_density[layer] = con_ref[layer] * (0.5 * (1.0 + jnp.tanh(centre))) + bend_weight * bend

    for copy, comes in zip(copies, gets):
        pl.when(comes)(copy.wait_recv)
    even, odd = [], []
    for layer in range(2):
        centre = own[layer]
        here = slice(layer * 8, layer * 8 + 8)
        top = jnp.where(lower, rhalo[1, here, :], rhalo[0, here, :])
        bottom = jnp.where(lower, rhalo[0, here, :], rhalo[1, here, :])
        tops = [jnp.broadcast_to(top[k : k + 1], (ROWS, 128)) for k in range(8)]
        bottoms = [jnp.broadcast_to(bottom[k : k + 1], (ROWS, 128)) for k in range(8)]
        beside = jnp.where(row_id == 0, jnp.concatenate(tops, axis=1), jnp.concatenate(bottoms, axis=1))
        outer_rows = (row_id == 0) | (row_id == ROWS - 1)
        bend = flux(zhalo[layer] - centre) + jnp.where(outer_rows, flux(beside - centre), 0.0)
        density = part_density[layer] + bend_weight * bend
        even.append(density[:, :HALF] + density[:, HALF:])
        odd.append((density[:, :HALF] - density[:, HALF:]) * alternating((ROWS, HALF)))

    block = jnp.where(lower, PLAN // 2 - 1 - p, p - PLAN // 2)
    half_lane = lax.broadcasted_iota(jnp.int32, (ROWS, 128), 1) < COEF
    for copy in wide_copies:
        copy.wait()

    def send_coef(other):
        return pltpu.make_async_remote_copy(
            src_ref=csend.at[other], dst_ref=sbuf.at[block], send_sem=cs, recv_sem=cr,
            device_id=at_q(other), device_id_type=MESH,
        )

    both = pair(jnp.concatenate(even + odd, axis=0))
    for cut in range(2):
        cols = slice(HALF * cut, HALF * (cut + 1))
        coef = table_right(both, wide[0, :, cols], wide[1, :, cols])
        for kind in range(2):
            start = kind * 16 + 8 * cut
            for m in range(4):
                first = coef[2 * ROWS * kind : 2 * ROWS * kind + ROWS, 128 * m : 128 * (m + 1)]
                second = coef[2 * ROWS * kind + ROWS : 2 * ROWS * (kind + 1), 128 * m : 128 * (m + 1)]
                csend[start + 2 * m] = jnp.where(half_lane, first, pltpu.roll(second, COEF, 1))
                csend[start + 2 * m + 1] = jnp.where(half_lane, pltpu.roll(first, COEF, 1), second)
            for k in range(8):
                other = start + lax.rem(q + k, 8)
                if k == 0:
                    pl.when(other != q)(send_coef(other).start)
                else:
                    send_coef(other).start()

    def respond(start, is_sin):
        row = lax.broadcasted_iota(jnp.int32, (128, 128), 0)
        col = lax.broadcasted_iota(jnp.int32, (128, 128), 1) + start
        place = lax.rem(q, GROUP // 2) * COEF + lax.rem(row, COEF)
        v = jnp.where(q >= GROUP // 2, NX - place, place).astype(F32)
        scale = 2.0 * math.pi * grav_scale * thickness / (4.0 * NX * NX)
        weight = jnp.where(place == 0, scale, 2.0 * scale) * jnp.where(col == 0, 1.0, 2.0)
        layer = (2 * d + lax.div(row, COEF)).astype(F32)
        rate = (top_depth + (layer + 0.5) * thickness) * (-2.0 * math.pi / (2 * NX))
        u = (NX - col if is_sin else col).astype(F32)
        return jnp.exp(jnp.sqrt(u * u + v * v) * rate) * weight

    for kind in range(2):
        for k in range(NX // 128):
            rsp[128 * kind : 128 * (kind + 1), 128 * k : 128 * (k + 1)] = respond(128 * k, kind == 1)

    sbuf[block] = csend[q]
    pltpu.make_async_copy(sbuf.at[pl.ds(0, GROUP - 1)], sbuf.at[pl.ds(0, GROUP - 1)], cr).wait()

    for copy in tall_copies:
        copy.wait()
    value = sbuf[...].reshape(HALF, 128).T
    side = lax.rem(lax.div(lax.broadcasted_iota(jnp.int32, (128, HALF), 1), 2 * ROWS), 2)
    value = jnp.concatenate([value, jnp.where(side == zh, value, -value) * alternating((128, HALF))], axis=0)
    both = pair(value)
    step = 256
    for k in range(NX // step):
        here = slice(k * step, (k + 1) * step)
        coef = table_right(both, wide[0, :, here], wide[1, :, here]) * rsp[:, here]
        cosine = coef[:COEF] + coef[COEF : 2 * COEF]
        sine = coef[2 * COEF : 3 * COEF] + coef[3 * COEF :]
        pst[:, here] = pair(jnp.concatenate([cosine, sine], axis=0))

    parity = lax.rem(d, 2)
    mate = d + 1 - 2 * parity

    def send_rows(member, depth, other):
        return pltpu.make_async_remote_copy(
            src_ref=xsend.at[GROUP * member + other], dst_ref=cbuf.at[GROUP * parity + q], send_sem=xs, recv_sem=xr,
            device_id=(depth, at_q(other)[1]), device_id_type=MESH,
        )

    for part in range(2):
        cols = slice(256 * part, 256 * (part + 1))
        value = table_right(pst[...], tall[0, :, cols], tall[1, :, cols])
        evens, odds = value[:COEF], value[COEF:] * alternating((COEF, 256))
        value = jnp.concatenate([evens + odds, evens - odds], axis=0).T
        for g in range(4):
            plain = [value[ROWS * (4 * g + n) : ROWS * (4 * g + n + 1)] for n in range(4)]
            turned = [pltpu.roll(block_now, COEF, 1) for block_now in plain]
            chunk = 4 * part + g
            for spot, block_now in (
                (2 * (8 + chunk), jnp.where(half_lane, plain[0], turned[2])),
                (2 * (8 + chunk) + 1, jnp.where(half_lane, plain[1], turned[3])),
                (2 * (7 - chunk), jnp.where(half_lane, turned[3], plain[1])),
                (2 * (7 - chunk) + 1, jnp.where(half_lane, turned[2], plain[0])),
            ):
                xsend[spot] = block_now[:8]
                xsend[GROUP + spot] = block_now[8:]

        for k in range(16):
            spot = lax.rem(q + k, 16)
            upper = lax.div(spot, 8)
            other = spot + 16 * (upper if part else 1 - upper)
            send_rows(1 - parity, mate, other).start()
            if k == 0:
                pl.when(other != q)(send_rows(parity, d, other).start)
            else:
                send_rows(parity, d, other).start()

    cbuf[GROUP * parity + q] = xsend[GROUP * parity + q]
    pltpu.make_async_copy(cbuf.at[pl.ds(0, 2 * GROUP - 1)], cbuf.at[pl.ds(0, 2 * GROUP - 1)], xr).wait()

    def send_field(other):
        return pltpu.make_async_remote_copy(
            src_ref=gsend.at[other], dst_ref=gbuf.at[z], send_sem=gs, recv_sem=gr,
            device_id=at_z(other), device_id_type=MESH,
        )

    values = []
    for kind in range(2):
        tops, bottoms = [], []
        for m in range(8):
            spot = kind * 16 + 2 * m
            first = cbuf[spot] + cbuf[GROUP + spot]
            second = cbuf[spot + 1] + cbuf[GROUP + spot + 1]
            tops.append(jnp.where(half_lane[:8], first, pltpu.roll(second, COEF, 1)))
            bottoms.append(jnp.where(half_lane[:8], pltpu.roll(first, COEF, 1), second))
        values += [jnp.concatenate(tops, axis=1), jnp.concatenate(bottoms, axis=1)]
    both = pair(jnp.concatenate(values, axis=0))
    for cut in range(2):
        cols = slice(256 * cut, 256 * (cut + 1))
        value = table_right(both, tall[0, :, cols], tall[1, :, cols])
        evens, odds = value[:ROWS], value[ROWS:] * alternating((ROWS, 256))
        plus = evens + odds
        minus = evens - odds
        for half in range(2):
            rows = slice(8 * half, 8 * (half + 1))
            for n in range(2):
                lanes = slice(128 * n, 128 * (n + 1))
                gsend[DEPTH * half + 4 + 2 * cut + n] = plus[rows, lanes]
                gsend[DEPTH * half + 3 - 2 * cut - n] = minus[rows, lanes]
        for k in range(8):
            turn = lax.rem(4 * zh + lax.rem(d + 2, 4) + k, 8)
            other = DEPTH * lax.div(turn, 4) + lax.rem(2 + 4 * cut + lax.rem(turn, 4), DEPTH)
            if k == 0:
                pl.when(other != z)(send_field(other).start)
            else:
                send_field(other).start()

    gbuf[z] = gsend[z]
    pltpu.make_async_copy(gbuf.at[pl.ds(0, RING - 1)], gbuf.at[pl.ds(0, RING - 1)], gr).wait()
    totals = [gbuf[0], gbuf[1]]
    for other in range(2, RING):
        totals[other % 2] = totals[other % 2] + gbuf[other]
    total = jnp.concatenate(totals, axis=0)
    across = lax.broadcasted_iota(jnp.int32, (128, 128), 0) + lax.broadcasted_iota(jnp.int32, (128, 128), 1)
    reverse = jnp.where(across == 127, 1.0, 0.0).astype(BF16)
    high, rest = split(total)
    low = (total - high.astype(F32) - rest.astype(F32)).astype(BF16)
    turned = matmul(jnp.concatenate([high, rest, low], axis=0), reverse)
    turned = turned[:ROWS] + turned[ROWS : 2 * ROWS] + turned[2 * ROWS :]
    total = jnp.where(d < DEPTH // 2, turned, total)

    @pl.when(lower)
    def _():
        for row in range(ROWS):
            out_ref[ROWS - 1 - row : ROWS - row, :] = total[row : row + 1]

    @pl.when(jnp.logical_not(lower))
    def _():
        out_ref[...] = total

    for copy, there in zip(copies, has):
        pl.when(there)(copy.wait_send)
    pltpu.make_async_copy(csend.at[pl.ds(0, GROUP - 1)], csend.at[pl.ds(0, GROUP - 1)], cs).wait()
    pltpu.make_async_copy(xsend.at[pl.ds(0, 2 * GROUP - 1)], xsend.at[pl.ds(0, 2 * GROUP - 1)], xs).wait()
    pltpu.make_async_copy(gsend.at[pl.ds(0, RING - 1)], gsend.at[pl.ds(0, RING - 1)], gs).wait()


def solution(mesh):
    wide, tall = basis()

    def step(level_set, contrast):
        vmem = pl.BlockSpec(memory_space=pltpu.VMEM)
        anywhere = pl.BlockSpec(memory_space=pl.ANY)
        dma = pltpu.SemaphoreType.DMA
        return pl.pallas_call(
            kernel,
            out_shape=jax.ShapeDtypeStruct((ROWS, 128), F32),
            in_specs=[anywhere] * 4,
            out_specs=vmem,
            scratch_shapes=[
                pltpu.VMEM((2, ROWS, NX), F32),
                pltpu.SMEM((2,), F32),
                pltpu.VMEM((2, ROWS, NX), F32),
                pltpu.VMEM((2, ROWS, NX), F32),
                pltpu.VMEM((2, HALF, NX), BF16),
                pltpu.VMEM((2, NX, HALF), BF16),
                pltpu.VMEM((2, ROWS, NX), F32),
                pltpu.VMEM((2, 16, 128), F32),
                pltpu.VMEM((2, 16, 128), F32),
                pltpu.VMEM((GROUP, ROWS, 128), F32),
                pltpu.VMEM((GROUP, ROWS, 128), F32),
                pltpu.VMEM((256, NX), F32),
                pltpu.VMEM((256, NX), BF16),
                pltpu.VMEM((2 * GROUP, 8, 128), F32),
                pltpu.VMEM((2 * GROUP, 8, 128), F32),
                pltpu.VMEM((RING, 8, 128), F32),
                pltpu.VMEM((RING, 8, 128), F32),
                dma(()), dma(()), dma((2,)), dma((2,)), dma((4,)), dma((4,)),
                dma(()), dma(()), dma(()), dma(()), dma(()), dma(()),
            ],
            compiler_params=pltpu.CompilerParams(
                collective_id=0, has_side_effects=True, vmem_limit_bytes=63 * 1024 * 1024
            ),
        )(level_set, contrast, jnp.asarray(wide), jnp.asarray(tall))

    return jax.shard_map(
        step,
        mesh=mesh,
        in_specs=(P("depth", "plan", None), P("depth")),
        out_specs=P("plan", "depth"),
        check_vma=False,
    )
```

```python
import functools
import math

import jax
import jax.numpy as jnp
import ml_dtypes
import numpy as np
from jax import lax
from jax.experimental import pallas as pl
from jax.experimental.pallas import tpu as pltpu
from jax.sharding import PartitionSpec as P

MESH = pl.DeviceIdType.MESH
F32 = jnp.float32
BF16 = jnp.bfloat16

NX = 1024
HALF = NX // 2
LAYERS = 16
DEPTH = 8
PLAN = 64
ROWS = NX // PLAN
GROUP = 32
RING = 16
COEF = 2 * NX // GROUP
SHARE = COEF // 2

bend_weight = 0.5
grav_scale = 0.05
top_depth = 0.0
thickness = 1.0


def basis():
    j = np.arange(HALF, dtype=np.float64)[:, None] + 0.5
    v = np.arange(NX, dtype=np.float64)[None, :]
    table = np.cos(np.pi * v * j / NX)
    high = table.astype(ml_dtypes.bfloat16)
    low = (table - high.astype(np.float64)).astype(ml_dtypes.bfloat16)
    wide = np.stack([high, low])
    order = np.arange(HALF).reshape(GROUP, 2, ROWS // 2).transpose(1, 0, 2).reshape(-1)
    return wide, np.ascontiguousarray(wide[:, order]), np.ascontiguousarray(np.swapaxes(wide, 1, 2))


def alternating(shape):
    return 1.0 - 2.0 * lax.rem(lax.broadcasted_iota(jnp.int32, shape, 1), 2).astype(F32)


def flux(step):
    return step * lax.rsqrt(1.0 + step * step)


def flip(value, axis, size):
    index = lax.broadcasted_iota(jnp.int32, value.shape, axis)
    step = size // 2
    value = pltpu.roll(value, step, axis)
    while step > 1:
        step //= 2
        up = pltpu.roll(value, step, axis)
        down = pltpu.roll(value, size - step, axis)
        value = jnp.where((index & step) != 0, up, down)
    return value


def flip_lanes(value):
    blocks = value.shape[1] // 128
    parts = [flip(value[:, 128 * k : 128 * (k + 1)], 1, 128) for k in reversed(range(blocks))]
    return jnp.concatenate(parts, axis=1) if blocks > 1 else parts[0]


def split(value):
    high = value.astype(BF16)
    low = (value - high.astype(F32)).astype(BF16)
    return high, low


def matmul(a, b):
    return jnp.dot(a, b, preferred_element_type=F32)


def pair(value):
    return jnp.concatenate(split(value), axis=0)


def table_right(both, high_table, low_table):
    n = both.shape[0] // 2
    product = matmul(both, high_table)
    return product[:n] + product[n:] + matmul(both[:n], low_table)


def regroup(parts):
    lane = lax.broadcasted_iota(jnp.int32, parts[0].shape, 1)
    early, even = lane < 64, lax.rem(lane, 64) < 32
    wide = [jnp.where(early, parts[g], pltpu.roll(parts[g + 2], 64, 1)) for g in range(2)]
    wide += [jnp.where(early, pltpu.roll(parts[g], 64, 1), parts[g + 2]) for g in range(2)]
    out = []
    for first, second in (wide[:2], wide[2:]):
        out.append(jnp.where(even, first, pltpu.roll(second, 32, 1)))
        out.append(jnp.where(even, pltpu.roll(first, 96, 1), second))
    return out


def kernel(
    ls_hbm, con_hbm, wide_hbm, mixed_hbm, tall_hbm, out_ref,
    ls_ref, con_ref, own, part_density, wide, mixed, tall, zhalo, rsend, rhalo, csend, sbuf, rsp, pst, xsend, cbuf, coefs, gsend, gbuf,
    ls_sem, con_sem, wide_sem, mixed_sem, tall_sem, hs, hr, cs, cr, xs, xr, gs, gr,
):
    d = lax.axis_index("depth")
    p = lax.axis_index("plan")
    core = lax.rem(p, 2)
    zh = lax.rem(lax.div(p, 2), 2)
    q = lax.div(p, 4) * 2 + core
    z = zh * DEPTH + d
    lower = p < PLAN // 2

    def at_q(other):
        return (d, lax.div(other, 2) * 4 + zh * 2 + lax.rem(other, 2))

    def at_z(other):
        return (lax.rem(other, DEPTH), p + 2 * (lax.div(other, DEPTH) - zh))

    ls_copy = pltpu.make_async_copy(ls_hbm, ls_ref, ls_sem)
    con_copy = pltpu.make_async_copy(con_hbm, con_ref, con_sem)
    ls_copy.start()
    con_copy.start()
    wide_copies = [pltpu.make_async_copy(wide_hbm.at[n], wide.at[n], wide_sem.at[n]) for n in range(2)]
    mixed_copies = [pltpu.make_async_copy(mixed_hbm.at[n], mixed.at[n], mixed_sem.at[n]) for n in range(2)]
    tall_copies = [pltpu.make_async_copy(tall_hbm.at[n], tall.at[n], tall_sem.at[n]) for n in range(2)]
    for copy in wide_copies:
        copy.start()

    barrier = pltpu.get_barrier_semaphore()

    def greet(target):
        pl.semaphore_signal(barrier, inc=1, device_id=target, device_id_type=MESH)

    has = (d < DEPTH - 1, d > 0, p < PLAN - 1, p > 0)
    gets = (d > 0, d < DEPTH - 1, p > 0, p < PLAN - 1)
    xy = lax.div(p, 4)
    outer = jnp.where(core == 0, p - 1, p + 1)
    has_outer = (outer >= 0) & (outer < PLAN)
    for k in (1, RING - 1):
        greet(at_z(lax.rem(z + k, RING)))
    greet((d, p + 1 - 2 * core))
    pl.when(has_outer)(lambda: greet((d, outer)))
    for k in range(1, GROUP // 2):
        first = 4 * lax.rem(xy + k, GROUP // 2) + 2 * zh
        greet((d, first))
        greet((d, first + 1))
    for k in range(2, RING - 1):
        greet(at_z(lax.rem(z + k, RING)))

    ls_copy.wait()
    con_copy.wait()

    for layer in range(2):
        value = ls_ref[layer]
        value = jnp.where(lower, flip(value, 0, ROWS), value)
        own[layer, :, :HALF] = value[:, HALF:]
        own[layer, :, HALF:] = flip_lanes(value[:, :HALF])

    for layer in range(2):
        for k in range(8):
            spot = layer * 8 + k
            top = own[layer, 0:1, 128 * k : 128 * (k + 1)]
            bottom = own[layer, ROWS - 1 : ROWS, 128 * k : 128 * (k + 1)]
            rsend[0, spot : spot + 1, :] = jnp.where(lower, bottom, top)
            rsend[1, spot : spot + 1, :] = jnp.where(lower, top, bottom)

    pl.semaphore_wait(barrier, GROUP + RING - 2 + has_outer.astype(jnp.int32))

    def halo(source, target, number, device):
        return pltpu.make_async_remote_copy(
            src_ref=source, dst_ref=target, send_sem=hs.at[number], recv_sem=hr.at[number],
            device_id=device, device_id_type=MESH,
        )

    z_up = halo(own.at[1], zhalo.at[0], 0, (d + 1, p))
    z_down = halo(own.at[0], zhalo.at[1], 1, (d - 1, p))
    r_up = halo(rsend.at[1], rhalo.at[0], 2, (d, p + 1))
    r_down = halo(rsend.at[0], rhalo.at[1], 3, (d, p - 1))
    lands = (zhalo.at[0], zhalo.at[1], rhalo.at[0], rhalo.at[1])
    copies = (z_up, z_down, r_up, r_down)
    for copy, there in zip(copies, has):
        pl.when(there)(copy.start)
    for copy in mixed_copies + tall_copies:
        copy.start()
    for land, comes in zip(lands, gets):

        @pl.when(jnp.logical_not(comes))
        def _(land=land):
            land[...] = jnp.zeros(land.shape, F32)

    row_id = lax.broadcasted_iota(jnp.int32, (ROWS, NX), 0)
    lane_id = lax.broadcasted_iota(jnp.int32, (ROWS, HALF), 1)
    field = [own[0], own[1]]
    middle = flux(field[1] - field[0])
    for layer in range(2):
        centre = field[layer]
        bend = -middle if layer else middle
        inner_flux = flux(pltpu.roll(centre, 1, 0) - centre)
        bend = bend + jnp.where(row_id == 0, 0.0, inner_flux)
        bend = bend - jnp.where(row_id == ROWS - 1, 0.0, pltpu.roll(inner_flux, ROWS - 1, 0))
        sides = centre[:, :HALF], centre[:, HALF:]
        across = []
        for side in range(2):
            here = sides[side]
            inside = jnp.where(lane_id == 0, sides[1 - side], pltpu.roll(here, 1, 1))
            inner_flux = flux(inside - here)
            outside = jnp.where(lane_id == HALF - 1, flux(here), pltpu.roll(inner_flux, HALF - 1, 1))
            across.append(inner_flux - outside)
        bend = bend + jnp.concatenate(across, axis=1)
        part_density[layer] = con_ref[layer] * (0.5 * (1.0 + jnp.tanh(centre))) + bend_weight * bend

    for copy, comes in zip(copies, gets):
        pl.when(comes)(copy.wait_recv)
    even, odd = [], []
    for layer in range(2):
        centre = own[layer]
        here = slice(layer * 8, layer * 8 + 8)
        top = jnp.where(lower, rhalo[1, here, :], rhalo[0, here, :])
        bottom = jnp.where(lower, rhalo[0, here, :], rhalo[1, here, :])
        tops = [jnp.broadcast_to(top[k : k + 1], (ROWS, 128)) for k in range(8)]
        bottoms = [jnp.broadcast_to(bottom[k : k + 1], (ROWS, 128)) for k in range(8)]
        beside = jnp.where(row_id == 0, jnp.concatenate(tops, axis=1), jnp.concatenate(bottoms, axis=1))
        outer_rows = (row_id == 0) | (row_id == ROWS - 1)
        bend = flux(zhalo[layer] - centre) + jnp.where(outer_rows, flux(beside - centre), 0.0)
        density = part_density[layer] + bend_weight * bend
        even.append(density[:, :HALF] + density[:, HALF:])
        odd.append((density[:, :HALF] - density[:, HALF:]) * alternating((ROWS, HALF)))

    block = jnp.where(lower, PLAN // 2 - 1 - p, p - PLAN // 2)
    parity = lax.rem(d, 2)
    mate = d + 1 - 2 * parity
    for copy in wide_copies:
        copy.wait()

    def send_coef(member, depth, other):
        return pltpu.make_async_remote_copy(
            src_ref=csend.at[2 * other + member], dst_ref=sbuf.at[GROUP * parity + block], send_sem=cs, recv_sem=cr,
            device_id=(depth, at_q(other)[1]), device_id_type=MESH,
        )

    both = pair(jnp.concatenate(even + odd, axis=0))
    for cut in range(2):
        cols = slice(HALF * cut, HALF * (cut + 1))
        coef = table_right(both, wide[0, :, cols], wide[1, :, cols])
        for kind in range(2):
            start = kind * 16 + 8 * cut
            for m in range(4):
                lanes = slice(128 * m, 128 * (m + 1))
                starts = [2 * ROWS * kind + ROWS * layer + 8 * half for half in range(2) for layer in range(2)]
                for t, value in enumerate(regroup([coef[n : n + 8, lanes] for n in starts])):
                    csend[2 * start + 4 * m + t] = value
            for k in range(8):
                other = start + lax.rem(q + k, 8)
                send_coef(1 - parity, mate, other).start()
                if k == 0:
                    pl.when(other != q)(send_coef(parity, d, other).start)
                else:
                    send_coef(parity, d, other).start()

    def respond(start, is_sin):
        row = lax.broadcasted_iota(jnp.int32, (128, 128), 0)
        col = lax.broadcasted_iota(jnp.int32, (128, 128), 1) + start
        place = lax.rem(q, GROUP // 2) * COEF + parity * SHARE + lax.rem(row, SHARE)
        v = jnp.where(q >= GROUP // 2, NX - place, place).astype(F32)
        scale = 2.0 * math.pi * grav_scale * thickness / (4.0 * NX * NX)
        weight = jnp.where(place == 0, scale, 2.0 * scale) * jnp.where(col == 0, 1.0, 2.0)
        layer = (2 * (d - parity) + lax.div(row, SHARE)).astype(F32)
        rate = (top_depth + (layer + 0.5) * thickness) * (-2.0 * math.pi / (2 * NX))
        u = (NX - col if is_sin else col).astype(F32)
        return jnp.exp(jnp.sqrt(u * u + v * v) * rate) * weight

    for kind in range(2):
        for k in range(NX // 128):
            rsp[128 * kind : 128 * (kind + 1), 128 * k : 128 * (k + 1)] = respond(128 * k, kind == 1)

    sbuf[GROUP * parity + block] = csend[2 * q + parity]
    landed = sbuf.at[pl.ds(0, 2 * GROUP - 1)]
    pltpu.make_async_copy(landed, landed, cr).wait()

    for copy in mixed_copies + tall_copies:
        copy.wait()
    layers = []
    for member in range(2):
        value = sbuf[GROUP * member : GROUP * (member + 1)].reshape(HALF // 2, 128).T
        layers.append(jnp.concatenate([value[:64], value[64:]], axis=1))
    value = jnp.concatenate(layers, axis=0)
    side = lax.rem(lax.div(lax.broadcasted_iota(jnp.int32, (128, HALF), 1), 16), 2)
    value = jnp.concatenate([value, jnp.where(side == zh, value, -value) * alternating((128, HALF))], axis=0)
    both = pair(value)
    step = 256
    for k in range(NX // step):
        here = slice(k * step, (k + 1) * step)
        coef = table_right(both, mixed[0, :, here], mixed[1, :, here]) * rsp[:, here]
        parts = [coef[SHARE * n : SHARE * (n + 1)] for n in range(8)]
        cosine = (parts[0] + parts[1]) + (parts[2] + parts[3])
        sine = (parts[4] + parts[5]) + (parts[6] + parts[7])
        pst[:, here] = pair(jnp.concatenate([cosine, sine], axis=0))

    def send_rows(member, depth, other):
        return pltpu.make_async_remote_copy(
            src_ref=xsend.at[2 * other + member], dst_ref=cbuf.at[2 * q + parity], send_sem=xs, recv_sem=xr,
            device_id=(depth, at_q(other)[1]), device_id_type=MESH,
        )

    lane = lax.broadcasted_iota(jnp.int32, (8, 128), 1)
    early, even_lane = lane < 64, lax.rem(lane, 64) < 32
    for part in range(2):
        cols = slice(256 * part, 256 * (part + 1))
        value = table_right(pst[...], tall[0, :, cols], tall[1, :, cols])
        evens, odds = value[:SHARE], value[SHARE:] * alternating((SHARE, 256))
        plus, minus = evens + odds, evens - odds
        value = jnp.concatenate([plus, minus, plus, minus], axis=0).T
        for g in range(4):
            chunk = 4 * part + g
            for member in range(2):
                ups, downs = [], []
                for n in range(4):
                    start = ROWS * (4 * g + n) + 8 * member
                    rows = value[start : start + 8]
                    later = pltpu.roll(rows, 4, 0)
                    ups.append(jnp.where(even_lane, rows, pltpu.roll(later, 32, 1)))
                    downs.append(jnp.where(even_lane, pltpu.roll(rows, 32, 1), later))
                for spot, one, two in (
                    (2 * (8 + chunk), ups[0], ups[2]),
                    (2 * (8 + chunk) + 1, ups[1], ups[3]),
                    (2 * (7 - chunk), downs[3], downs[1]),
                    (2 * (7 - chunk) + 1, downs[2], downs[0]),
                ):
                    xsend[2 * spot + member] = jnp.where(early, one, two)[:4]

        for k in range(16):
            spot = lax.rem(q + k, 16)
            upper = lax.div(spot, 8)
            other = spot + 16 * (upper if part else 1 - upper)
            send_rows(1 - parity, mate, other).start()
            if k == 0:
                pl.when(other != q)(send_rows(parity, d, other).start)
            else:
                send_rows(parity, d, other).start()

    cbuf[2 * q + parity] = xsend[2 * q + parity]
    landed = cbuf.at[pl.ds(0, 2 * GROUP - 1)]
    pltpu.make_async_copy(landed, landed, xr).wait()

    def send_field(other):
        return pltpu.make_async_remote_copy(
            src_ref=gsend.at[other], dst_ref=gbuf.at[z], send_sem=gs, recv_sem=gr,
            device_id=at_z(other), device_id_type=MESH,
        )

    for m in range(2 * NX // 128):
        parts = regroup([cbuf[4 * m + t] for t in range(4)])
        lanes = slice(128 * (m % 8), 128 * (m % 8 + 1))
        for g in range(4):
            start = ROWS * (m // 8) + 4 * g
            coefs[start : start + 4, lanes] = parts[g]
    both = pair(coefs[...])
    for cut in range(2):
        cols = slice(256 * cut, 256 * (cut + 1))
        value = table_right(both, tall[0, :, cols], tall[1, :, cols])
        evens, odds = value[:ROWS], value[ROWS:] * alternating((ROWS, 256))
        plus = evens + odds
        minus = evens - odds
        for half in range(2):
            rows = slice(8 * half, 8 * (half + 1))
            for n in range(2):
                lanes = slice(128 * n, 128 * (n + 1))
                gsend[DEPTH * half + 4 + 2 * cut + n] = plus[rows, lanes]
                gsend[DEPTH * half + 3 - 2 * cut - n] = minus[rows, lanes]
        for k in range(8):
            turn = lax.rem(4 * zh + lax.rem(d + 2, 4) + k, 8)
            other = DEPTH * lax.div(turn, 4) + lax.rem(2 + 4 * cut + lax.rem(turn, 4), DEPTH)
            if k == 0:
                pl.when(other != z)(send_field(other).start)
            else:
                send_field(other).start()

    gbuf[z] = gsend[z]
    pltpu.make_async_copy(gbuf.at[pl.ds(0, RING - 1)], gbuf.at[pl.ds(0, RING - 1)], gr).wait()
    totals = [gbuf[0], gbuf[1]]
    for other in range(2, RING):
        totals[other % 2] = totals[other % 2] + gbuf[other]
    total = jnp.concatenate(totals, axis=0)
    across = lax.broadcasted_iota(jnp.int32, (128, 128), 0) + lax.broadcasted_iota(jnp.int32, (128, 128), 1)
    reverse = jnp.where(across == 127, 1.0, 0.0).astype(BF16)
    high, rest = split(total)
    low = (total - high.astype(F32) - rest.astype(F32)).astype(BF16)
    turned = matmul(jnp.concatenate([high, rest, low], axis=0), reverse)
    turned = turned[:ROWS] + turned[ROWS : 2 * ROWS] + turned[2 * ROWS :]
    total = jnp.where(d < DEPTH // 2, turned, total)

    @pl.when(lower)
    def _():
        for row in range(ROWS):
            out_ref[ROWS - 1 - row : ROWS - row, :] = total[row : row + 1]

    @pl.when(jnp.logical_not(lower))
    def _():
        out_ref[...] = total

    for copy, there in zip(copies, has):
        pl.when(there)(copy.wait_send)
    pltpu.make_async_copy(csend.at[pl.ds(0, 2 * GROUP - 1)], csend.at[pl.ds(0, 2 * GROUP - 1)], cs).wait()
    pltpu.make_async_copy(xsend.at[pl.ds(0, 2 * GROUP - 1)], xsend.at[pl.ds(0, 2 * GROUP - 1)], xs).wait()
    pltpu.make_async_copy(gsend.at[pl.ds(0, RING - 1)], gsend.at[pl.ds(0, RING - 1)], gs).wait()


def solution(mesh):
    wide, mixed, tall = basis()

    def step(level_set, contrast):
        vmem = pl.BlockSpec(memory_space=pltpu.VMEM)
        anywhere = pl.BlockSpec(memory_space=pl.ANY)
        dma = pltpu.SemaphoreType.DMA
        return pl.pallas_call(
            kernel,
            out_shape=jax.ShapeDtypeStruct((ROWS, 128), F32),
            in_specs=[anywhere] * 5,
            out_specs=vmem,
            scratch_shapes=[
                pltpu.VMEM((2, ROWS, NX), F32),
                pltpu.SMEM((2,), F32),
                pltpu.VMEM((2, ROWS, NX), F32),
                pltpu.VMEM((2, ROWS, NX), F32),
                pltpu.VMEM((2, HALF, NX), BF16),
                pltpu.VMEM((2, HALF, NX), BF16),
                pltpu.VMEM((2, NX, HALF), BF16),
                pltpu.VMEM((2, ROWS, NX), F32),
                pltpu.VMEM((2, 16, 128), F32),
                pltpu.VMEM((2, 16, 128), F32),
                pltpu.VMEM((2 * GROUP, 8, 128), F32),
                pltpu.VMEM((2 * GROUP, 8, 128), F32),
                pltpu.VMEM((256, NX), F32),
                pltpu.VMEM((128, NX), BF16),
                pltpu.VMEM((2 * GROUP, 4, 128), F32),
                pltpu.VMEM((2 * GROUP, 4, 128), F32),
                pltpu.VMEM((2 * ROWS, NX), F32),
                pltpu.VMEM((RING, 8, 128), F32),
                pltpu.VMEM((RING, 8, 128), F32),
                dma(()), dma(()), dma((2,)), dma((2,)), dma((2,)), dma((4,)), dma((4,)),
                dma(()), dma(()), dma(()), dma(()), dma(()), dma(()),
            ],
            compiler_params=pltpu.CompilerParams(
                collective_id=0, has_side_effects=True, vmem_limit_bytes=63 * 1024 * 1024
            ),
        )(level_set, contrast, jnp.asarray(wide), jnp.asarray(mixed), jnp.asarray(tall))

    return jax.shard_map(
        step,
        mesh=mesh,
        in_specs=(P("depth", "plan", None), P("depth")),
        out_specs=P("plan", "depth"),
        check_vma=False,
    )
```

```python
import functools
import math

import jax
import jax.numpy as jnp
import ml_dtypes
import numpy as np
from jax import lax
from jax.experimental import pallas as pl
from jax.experimental.pallas import tpu as pltpu
from jax.sharding import PartitionSpec as P

MESH = pl.DeviceIdType.MESH
F32 = jnp.float32
BF16 = jnp.bfloat16

NX = 1024
HALF = NX // 2
LAYERS = 16
DEPTH = 8
PLAN = 64
ROWS = NX // PLAN
GROUP = 32
RING = 16
COEF = 2 * NX // GROUP
SHARE = COEF // 2

bend_weight = 0.5
grav_scale = 0.05
top_depth = 0.0
thickness = 1.0


def basis():
    j = np.arange(HALF, dtype=np.float64)[:, None] + 0.5
    v = np.arange(NX, dtype=np.float64)[None, :]
    table = np.cos(np.pi * v * j / NX)
    high = table.astype(ml_dtypes.bfloat16)
    low = (table - high.astype(np.float64)).astype(ml_dtypes.bfloat16)
    wide = np.stack([high, low])
    order = np.arange(HALF).reshape(GROUP, 2, ROWS // 2).transpose(1, 0, 2).reshape(-1)
    return wide, np.ascontiguousarray(wide[:, order]), np.ascontiguousarray(np.swapaxes(wide, 1, 2))


def alternating(shape):
    return 1.0 - 2.0 * lax.rem(lax.broadcasted_iota(jnp.int32, shape, 1), 2).astype(F32)


def flux(step):
    return step * lax.rsqrt(1.0 + step * step)


def flip(value, axis, size):
    index = lax.broadcasted_iota(jnp.int32, value.shape, axis)
    step = size // 2
    value = pltpu.roll(value, step, axis)
    while step > 1:
        step //= 2
        up = pltpu.roll(value, step, axis)
        down = pltpu.roll(value, size - step, axis)
        value = jnp.where((index & step) != 0, up, down)
    return value


def flip_lanes(value):
    blocks = value.shape[1] // 128
    parts = [flip(value[:, 128 * k : 128 * (k + 1)], 1, 128) for k in reversed(range(blocks))]
    return jnp.concatenate(parts, axis=1) if blocks > 1 else parts[0]


def split(value):
    high = value.astype(BF16)
    low = (value - high.astype(F32)).astype(BF16)
    return high, low


def matmul(a, b):
    return jnp.dot(a, b, preferred_element_type=F32)


def pair(value):
    return jnp.concatenate(split(value), axis=0)


def table_right(both, high_table, low_table):
    n = both.shape[0] // 2
    product = matmul(both, high_table)
    return product[:n] + product[n:] + matmul(both[:n], low_table)


def regroup(parts):
    lane = lax.broadcasted_iota(jnp.int32, parts[0].shape, 1)
    early, even = lane < 64, lax.rem(lane, 64) < 32
    wide = [jnp.where(early, parts[g], pltpu.roll(parts[g + 2], 64, 1)) for g in range(2)]
    wide += [jnp.where(early, pltpu.roll(parts[g], 64, 1), parts[g + 2]) for g in range(2)]
    out = []
    for first, second in (wide[:2], wide[2:]):
        out.append(jnp.where(even, first, pltpu.roll(second, 32, 1)))
        out.append(jnp.where(even, pltpu.roll(first, 96, 1), second))
    return out


def kernel(
    ls_hbm, con_hbm, wide_hbm, mixed_hbm, tall_hbm, out_ref,
    ls_ref, con_ref, own, part_density, wide, mixed, tall, zhalo, rsend, rhalo, csend, sbuf, rsp, acc, pst, xsend, cbuf, coefs, gsend, gbuf,
    ls_sem, con_sem, wide_sem, mixed_sem, tall_sem, hs, hr, cs, cr, xs, xr, gs, gr,
):
    d = lax.axis_index("depth")
    p = lax.axis_index("plan")
    core = lax.rem(p, 2)
    zh = lax.rem(lax.div(p, 2), 2)
    q = lax.div(p, 4) * 2 + core
    z = zh * DEPTH + d
    lower = p < PLAN // 2

    turns = [lax.rem(q + k, 8) for k in range(8)]
    places = [lax.div(turn, 2) * 4 + lax.rem(turn, 2) + 2 * zh for turn in turns]
    q_set = lax.div(q, 8)

    def at_z(other):
        return (lax.rem(other, DEPTH), p + 2 * (lax.div(other, DEPTH) - zh))

    ls_copy = pltpu.make_async_copy(ls_hbm, ls_ref, ls_sem)
    con_copy = pltpu.make_async_copy(con_hbm, con_ref, con_sem)
    ls_copy.start()
    con_copy.start()
    wide_copies = [pltpu.make_async_copy(wide_hbm.at[n], wide.at[n], wide_sem.at[n]) for n in range(2)]
    mixed_copies = [pltpu.make_async_copy(mixed_hbm.at[n], mixed.at[n], mixed_sem.at[n]) for n in range(2)]
    tall_copies = [pltpu.make_async_copy(tall_hbm.at[n], tall.at[n], tall_sem.at[n]) for n in range(2)]
    for copy in wide_copies:
        copy.start()

    barrier = pltpu.get_barrier_semaphore()

    def greet(target):
        pl.semaphore_signal(barrier, inc=1, device_id=target, device_id_type=MESH)

    has = (d < DEPTH - 1, d > 0, p < PLAN - 1, p > 0)
    gets = (d > 0, d < DEPTH - 1, p > 0, p < PLAN - 1)
    xy = lax.div(p, 4)
    outer = jnp.where(core == 0, p - 1, p + 1)
    has_outer = (outer >= 0) & (outer < PLAN)
    for k in (1, RING - 1):
        greet(at_z(lax.rem(z + k, RING)))
    greet((d, p + 1 - 2 * core))
    pl.when(has_outer)(lambda: greet((d, outer)))
    for k in range(1, GROUP // 2):
        first = 4 * lax.rem(xy + k, GROUP // 2) + 2 * zh
        greet((d, first))
        greet((d, first + 1))
    for k in range(2, RING - 1):
        greet(at_z(lax.rem(z + k, RING)))

    ls_copy.wait()
    con_copy.wait()

    for layer in range(2):
        value = ls_ref[layer]
        value = jnp.where(lower, flip(value, 0, ROWS), value)
        own[layer, :, :HALF] = value[:, HALF:]
        own[layer, :, HALF:] = flip_lanes(value[:, :HALF])

    for layer in range(2):
        for k in range(8):
            spot = layer * 8 + k
            top = own[layer, 0:1, 128 * k : 128 * (k + 1)]
            bottom = own[layer, ROWS - 1 : ROWS, 128 * k : 128 * (k + 1)]
            rsend[0, spot : spot + 1, :] = jnp.where(lower, bottom, top)
            rsend[1, spot : spot + 1, :] = jnp.where(lower, top, bottom)

    pl.semaphore_wait(barrier, GROUP + RING - 2 + has_outer.astype(jnp.int32))

    def halo(source, target, number, device):
        return pltpu.make_async_remote_copy(
            src_ref=source, dst_ref=target, send_sem=hs.at[number], recv_sem=hr.at[number],
            device_id=device, device_id_type=MESH,
        )

    z_up = halo(own.at[1], zhalo.at[0], 0, (d + 1, p))
    z_down = halo(own.at[0], zhalo.at[1], 1, (d - 1, p))
    r_up = halo(rsend.at[1], rhalo.at[0], 2, (d, p + 1))
    r_down = halo(rsend.at[0], rhalo.at[1], 3, (d, p - 1))
    lands = (zhalo.at[0], zhalo.at[1], rhalo.at[0], rhalo.at[1])
    copies = (z_up, z_down, r_up, r_down)
    for copy, there in zip(copies, has):
        pl.when(there)(copy.start)
    for copy in mixed_copies + tall_copies:
        copy.start()
    for land, comes in zip(lands, gets):

        @pl.when(jnp.logical_not(comes))
        def _(land=land):
            land[...] = jnp.zeros(land.shape, F32)

    row_id = lax.broadcasted_iota(jnp.int32, (ROWS, NX), 0)
    lane_id = lax.broadcasted_iota(jnp.int32, (ROWS, HALF), 1)
    field = [own[0], own[1]]
    middle = flux(field[1] - field[0])
    for layer in range(2):
        centre = field[layer]
        bend = -middle if layer else middle
        inner_flux = flux(pltpu.roll(centre, 1, 0) - centre)
        bend = bend + jnp.where(row_id == 0, 0.0, inner_flux)
        bend = bend - jnp.where(row_id == ROWS - 1, 0.0, pltpu.roll(inner_flux, ROWS - 1, 0))
        sides = centre[:, :HALF], centre[:, HALF:]
        across = []
        for side in range(2):
            here = sides[side]
            inside = jnp.where(lane_id == 0, sides[1 - side], pltpu.roll(here, 1, 1))
            inner_flux = flux(inside - here)
            outside = jnp.where(lane_id == HALF - 1, flux(here), pltpu.roll(inner_flux, HALF - 1, 1))
            across.append(inner_flux - outside)
        bend = bend + jnp.concatenate(across, axis=1)
        part_density[layer] = con_ref[layer] * (0.5 * (1.0 + jnp.tanh(centre))) + bend_weight * bend

    for copy, comes in zip(copies, gets):
        pl.when(comes)(copy.wait_recv)
    even, odd = [], []
    for layer in range(2):
        centre = own[layer]
        here = slice(layer * 8, layer * 8 + 8)
        top = jnp.where(lower, rhalo[1, here, :], rhalo[0, here, :])
        bottom = jnp.where(lower, rhalo[0, here, :], rhalo[1, here, :])
        tops = [jnp.broadcast_to(top[k : k + 1], (ROWS, 128)) for k in range(8)]
        bottoms = [jnp.broadcast_to(bottom[k : k + 1], (ROWS, 128)) for k in range(8)]
        beside = jnp.where(row_id == 0, jnp.concatenate(tops, axis=1), jnp.concatenate(bottoms, axis=1))
        outer_rows = (row_id == 0) | (row_id == ROWS - 1)
        bend = flux(zhalo[layer] - centre) + jnp.where(outer_rows, flux(beside - centre), 0.0)
        density = part_density[layer] + bend_weight * bend
        even.append(density[:, :HALF] + density[:, HALF:])
        odd.append((density[:, :HALF] - density[:, HALF:]) * alternating((ROWS, HALF)))

    block = jnp.where(lower, PLAN // 2 - 1 - p, p - PLAN // 2)
    parity = lax.rem(d, 2)
    mate = d + 1 - 2 * parity
    for copy in wide_copies:
        copy.wait()

    def send_coef(group, k, cross):
        member = 1 - parity if cross else parity
        return pltpu.make_async_remote_copy(
            src_ref=csend.at[2 * (8 * group + turns[k]) + member], dst_ref=sbuf.at[GROUP * cross + block],
            send_sem=cs, recv_sem=cr.at[cross],
            device_id=(mate if cross else d, 16 * group + places[k]), device_id_type=MESH,
        )

    both = pair(jnp.concatenate(even + odd, axis=0))
    for cut in range(2):
        cols = slice(HALF * cut, HALF * (cut + 1))
        coef = table_right(both, wide[0, :, cols], wide[1, :, cols])
        for kind in range(2):
            start = kind * 16 + 8 * cut
            for m in range(4):
                lanes = slice(128 * m, 128 * (m + 1))
                starts = [2 * ROWS * kind + ROWS * layer + 8 * half for half in range(2) for layer in range(2)]
                for t, value in enumerate(regroup([coef[n : n + 8, lanes] for n in starts])):
                    csend[2 * start + 4 * m + t] = value
            for k in range(1, 8):
                send_coef(start // 8, k, 0).start()
    for group in range(4):
        pl.when(group != q_set)(send_coef(group, 0, 0).start)
    for k in range(8):
        for group in range(4):
            send_coef(group, k, 1).start()

    def respond(start, cross):
        row = lax.broadcasted_iota(jnp.int32, (128, 128), 0)
        col = lax.broadcasted_iota(jnp.int32, (128, 128), 1) + start
        place = lax.rem(q, GROUP // 2) * COEF + parity * SHARE + lax.rem(row, SHARE)
        v = jnp.where(q >= GROUP // 2, NX - place, place).astype(F32)
        scale = 2.0 * math.pi * grav_scale * thickness / (4.0 * NX * NX)
        weight = jnp.where(place == 0, scale, 2.0 * scale) * jnp.where(col == 0, 1.0, 2.0)
        layer = (2 * (mate if cross else d) + lax.rem(lax.div(row, SHARE), 2)).astype(F32)
        rate = (top_depth + (layer + 0.5) * thickness) * (-2.0 * math.pi / (2 * NX))
        u = jnp.where(row >= 64, NX - col, col).astype(F32)
        return jnp.exp(jnp.sqrt(u * u + v * v) * rate) * weight

    for cross in range(2):
        for k in range(NX // 128):
            rsp[cross, :, 128 * k : 128 * (k + 1)] = respond(128 * k, cross)

    sbuf[block] = csend[2 * q + parity]
    for copy in mixed_copies + tall_copies:
        copy.wait()
    side = lax.rem(lax.div(lax.broadcasted_iota(jnp.int32, (64, HALF), 1), 16), 2)
    sign = jnp.where(side == zh, 1.0, -1.0) * alternating((64, HALF))
    step = 256
    for cross in range(2):
        landed = sbuf.at[pl.ds(GROUP * cross, GROUP - 1 + cross)]
        pltpu.make_async_copy(landed, landed, cr.at[cross]).wait()
        value = sbuf[GROUP * cross : GROUP * (cross + 1)].reshape(HALF // 2, 128).T
        value = jnp.concatenate([value[:64], value[64:]], axis=1)
        both = pair(jnp.concatenate([value, value * sign], axis=0))
        for k in range(NX // step):
            here = slice(k * step, (k + 1) * step)
            coef = table_right(both, mixed[0, :, here], mixed[1, :, here]) * rsp[cross, :, here]
            parts = [coef[SHARE * n : SHARE * (n + 1)] for n in range(4)]
            coef = jnp.concatenate([parts[0] + parts[1], parts[2] + parts[3]], axis=0)
            if cross:
                pst[:, here] = pair(coef + acc[:, here])
            else:
                acc[:, here] = coef

    def send_rows(group, k, cross):
        member = 1 - parity if cross else parity
        return pltpu.make_async_remote_copy(
            src_ref=xsend.at[2 * (8 * group + turns[k]) + member], dst_ref=cbuf.at[2 * q + parity],
            send_sem=xs, recv_sem=xr,
            device_id=(mate if cross else d, 16 * group + places[k]), device_id_type=MESH,
        )

    lane = lax.broadcasted_iota(jnp.int32, (8, 128), 1)
    early, even_lane = lane < 64, lax.rem(lane, 64) < 32
    for part in range(2):
        cols = slice(256 * part, 256 * (part + 1))
        value = table_right(pst[...], tall[0, :, cols], tall[1, :, cols])
        evens, odds = value[:SHARE], value[SHARE:] * alternating((SHARE, 256))
        plus, minus = evens + odds, evens - odds
        value = jnp.concatenate([plus, minus, plus, minus], axis=0).T
        for g in range(4):
            chunk = 4 * part + g
            for member in range(2):
                ups, downs = [], []
                for n in range(4):
                    start = ROWS * (4 * g + n) + 8 * member
                    rows = value[start : start + 8]
                    later = pltpu.roll(rows, 4, 0)
                    ups.append(jnp.where(even_lane, rows, pltpu.roll(later, 32, 1)))
                    downs.append(jnp.where(even_lane, pltpu.roll(rows, 32, 1), later))
                for spot, one, two in (
                    (2 * (8 + chunk), ups[0], ups[2]),
                    (2 * (8 + chunk) + 1, ups[1], ups[3]),
                    (2 * (7 - chunk), downs[3], downs[1]),
                    (2 * (7 - chunk) + 1, downs[2], downs[0]),
                ):
                    xsend[2 * spot + member] = jnp.where(early, one, two)[:4]

        for k in range(8):
            for group in (2 + part, 1 - part):
                send_rows(group, k, 1).start()
                if k:
                    send_rows(group, k, 0).start()
    for group in range(4):
        pl.when(group != q_set)(send_rows(group, 0, 0).start)

    cbuf[2 * q + parity] = xsend[2 * q + parity]
    landed = cbuf.at[pl.ds(0, 2 * GROUP - 1)]
    pltpu.make_async_copy(landed, landed, xr).wait()

    def send_field(far, depth):
        row = 1 - zh if far else zh
        return pltpu.make_async_remote_copy(
            src_ref=gsend.at[DEPTH * row + depth], dst_ref=gbuf.at[z], send_sem=gs, recv_sem=gr,
            device_id=(depth, p + 2 - 4 * zh if far else p), device_id_type=MESH,
        )

    steps = [lax.rem(d + 2 + k, 4) for k in range(4)]
    depths = ([2 + turn for turn in steps], [lax.rem(6 + turn, DEPTH) for turn in steps])

    for m in range(2 * NX // 128):
        parts = regroup([cbuf[4 * m + t] for t in range(4)])
        lanes = slice(128 * (m % 8), 128 * (m % 8 + 1))
        for g in range(4):
            start = ROWS * (m // 8) + 4 * g
            coefs[start : start + 4, lanes] = parts[g]
    both = pair(coefs[...])
    for cut in range(2):
        cols = slice(256 * cut, 256 * (cut + 1))
        value = table_right(both, tall[0, :, cols], tall[1, :, cols])
        evens, odds = value[:ROWS], value[ROWS:] * alternating((ROWS, 256))
        plus = evens + odds
        minus = evens - odds
        for half in range(2):
            rows = slice(8 * half, 8 * (half + 1))
            for n in range(2):
                lanes = slice(128 * n, 128 * (n + 1))
                gsend[DEPTH * half + 4 + 2 * cut + n] = plus[rows, lanes]
                gsend[DEPTH * half + 3 - 2 * cut - n] = minus[rows, lanes]
        for k in range(4):
            send_field(True, depths[cut][k]).start()
        for k in range(1, 4):
            send_field(False, depths[cut][k]).start()
    for cut in range(2):
        pl.when(depths[cut][0] != d)(send_field(False, depths[cut][0]).start)

    gbuf[z] = gsend[z]
    pltpu.make_async_copy(gbuf.at[pl.ds(0, RING - 1)], gbuf.at[pl.ds(0, RING - 1)], gr).wait()
    totals = [gbuf[0], gbuf[1]]
    for other in range(2, RING):
        totals[other % 2] = totals[other % 2] + gbuf[other]
    total = jnp.concatenate(totals, axis=0)
    across = lax.broadcasted_iota(jnp.int32, (128, 128), 0) + lax.broadcasted_iota(jnp.int32, (128, 128), 1)
    reverse = jnp.where(across == 127, 1.0, 0.0).astype(BF16)
    high, rest = split(total)
    low = (total - high.astype(F32) - rest.astype(F32)).astype(BF16)
    turned = matmul(jnp.concatenate([high, rest, low], axis=0), reverse)
    turned = turned[:ROWS] + turned[ROWS : 2 * ROWS] + turned[2 * ROWS :]
    total = jnp.where(d < DEPTH // 2, turned, total)

    @pl.when(lower)
    def _():
        for row in range(ROWS):
            out_ref[ROWS - 1 - row : ROWS - row, :] = total[row : row + 1]

    @pl.when(jnp.logical_not(lower))
    def _():
        out_ref[...] = total

    for copy, there in zip(copies, has):
        pl.when(there)(copy.wait_send)
    pltpu.make_async_copy(csend.at[pl.ds(0, 2 * GROUP - 1)], csend.at[pl.ds(0, 2 * GROUP - 1)], cs).wait()
    pltpu.make_async_copy(xsend.at[pl.ds(0, 2 * GROUP - 1)], xsend.at[pl.ds(0, 2 * GROUP - 1)], xs).wait()
    pltpu.make_async_copy(gsend.at[pl.ds(0, RING - 1)], gsend.at[pl.ds(0, RING - 1)], gs).wait()


def solution(mesh):
    wide, mixed, tall = basis()

    def step(level_set, contrast):
        vmem = pl.BlockSpec(memory_space=pltpu.VMEM)
        anywhere = pl.BlockSpec(memory_space=pl.ANY)
        dma = pltpu.SemaphoreType.DMA
        return pl.pallas_call(
            kernel,
            out_shape=jax.ShapeDtypeStruct((ROWS, 128), F32),
            in_specs=[anywhere] * 5,
            out_specs=vmem,
            scratch_shapes=[
                pltpu.VMEM((2, ROWS, NX), F32),
                pltpu.SMEM((2,), F32),
                pltpu.VMEM((2, ROWS, NX), F32),
                pltpu.VMEM((2, ROWS, NX), F32),
                pltpu.VMEM((2, HALF, NX), BF16),
                pltpu.VMEM((2, HALF, NX), BF16),
                pltpu.VMEM((2, NX, HALF), BF16),
                pltpu.VMEM((2, ROWS, NX), F32),
                pltpu.VMEM((2, 16, 128), F32),
                pltpu.VMEM((2, 16, 128), F32),
                pltpu.VMEM((2 * GROUP, 8, 128), F32),
                pltpu.VMEM((2 * GROUP, 8, 128), F32),
                pltpu.VMEM((2, 128, NX), F32),
                pltpu.VMEM((64, NX), F32),
                pltpu.VMEM((128, NX), BF16),
                pltpu.VMEM((2 * GROUP, 4, 128), F32),
                pltpu.VMEM((2 * GROUP, 4, 128), F32),
                pltpu.VMEM((2 * ROWS, NX), F32),
                pltpu.VMEM((RING, 8, 128), F32),
                pltpu.VMEM((RING, 8, 128), F32),
                dma(()), dma(()), dma((2,)), dma((2,)), dma((2,)), dma((4,)), dma((4,)),
                dma(()), dma((2,)), dma(()), dma(()), dma(()), dma(()),
            ],
            compiler_params=pltpu.CompilerParams(
                collective_id=0, has_side_effects=True, vmem_limit_bytes=63 * 1024 * 1024
            ),
        )(level_set, contrast, jnp.asarray(wide), jnp.asarray(mixed), jnp.asarray(tall))

    return jax.shard_map(
        step,
        mesh=mesh,
        in_specs=(P("depth", "plan", None), P("depth")),
        out_specs=P("plan", "depth"),
        check_vma=False,
    )
```

```python
import functools
import math

import jax
import jax.numpy as jnp
import ml_dtypes
import numpy as np
from jax import lax
from jax.experimental import pallas as pl
from jax.experimental.pallas import tpu as pltpu
from jax.sharding import PartitionSpec as P

MESH = pl.DeviceIdType.MESH
F32 = jnp.float32
BF16 = jnp.bfloat16

NX = 1024
HALF = NX // 2
LAYERS = 16
DEPTH = 8
PLAN = 64
ROWS = NX // PLAN
GROUP = 32
RING = 16
COEF = 2 * NX // GROUP
SHARE = COEF // 2

bend_weight = 0.5
grav_scale = 0.05
top_depth = 0.0
thickness = 1.0


def basis():
    j = np.arange(HALF, dtype=np.float64)[:, None] + 0.5
    v = np.arange(NX, dtype=np.float64)[None, :]
    table = np.cos(np.pi * v * j / NX)
    high = table.astype(ml_dtypes.bfloat16)
    low = (table - high.astype(np.float64)).astype(ml_dtypes.bfloat16)
    wide = np.stack([high, low])
    order = np.arange(HALF).reshape(GROUP, 2, ROWS // 2).transpose(1, 0, 2).reshape(-1)
    return wide, np.ascontiguousarray(wide[:, order]), np.ascontiguousarray(np.swapaxes(wide, 1, 2))


def alternating(shape):
    return 1.0 - 2.0 * lax.rem(lax.broadcasted_iota(jnp.int32, shape, 1), 2).astype(F32)


def flux(step):
    return step * lax.rsqrt(1.0 + step * step)


def flip(value, axis, size):
    index = lax.broadcasted_iota(jnp.int32, value.shape, axis)
    step = size // 2
    value = pltpu.roll(value, step, axis)
    while step > 1:
        step //= 2
        up = pltpu.roll(value, step, axis)
        down = pltpu.roll(value, size - step, axis)
        value = jnp.where((index & step) != 0, up, down)
    return value


def flip_lanes(value):
    blocks = value.shape[1] // 128
    parts = [flip(value[:, 128 * k : 128 * (k + 1)], 1, 128) for k in reversed(range(blocks))]
    return jnp.concatenate(parts, axis=1) if blocks > 1 else parts[0]


def split(value):
    high = value.astype(BF16)
    low = (value - high.astype(F32)).astype(BF16)
    return high, low


def matmul(a, b):
    return jnp.dot(a, b, preferred_element_type=F32)


def pair(value):
    return jnp.concatenate(split(value), axis=0)


def table_right(both, high_table, low_table):
    n = both.shape[0] // 2
    product = matmul(both, high_table)
    return product[:n] + product[n:] + matmul(both[:n], low_table)


def regroup(parts):
    lane = lax.broadcasted_iota(jnp.int32, parts[0].shape, 1)
    early, even = lane < 64, lax.rem(lane, 64) < 32
    wide = [jnp.where(early, parts[g], pltpu.roll(parts[g + 2], 64, 1)) for g in range(2)]
    wide += [jnp.where(early, pltpu.roll(parts[g], 64, 1), parts[g + 2]) for g in range(2)]
    out = []
    for first, second in (wide[:2], wide[2:]):
        out.append(jnp.where(even, first, pltpu.roll(second, 32, 1)))
        out.append(jnp.where(even, pltpu.roll(first, 96, 1), second))
    return out


def kernel(
    ls_hbm, con_hbm, wide_hbm, mixed_hbm, tall_hbm, out_ref,
    ls_ref, con_ref, own, part_density, wide, mixed, tall, zhalo, rsend, rhalo, csend, sbuf, rsp, acc, pst, xsend, cbuf, coefs, gsend, gbuf,
    ls_sem, con_sem, wide_sem, mixed_sem, tall_sem, hs, hr, cs, cr, xs, xr, gs, gr,
):
    d = lax.axis_index("depth")
    p = lax.axis_index("plan")
    core = lax.rem(p, 2)
    zh = lax.rem(lax.div(p, 2), 2)
    q = lax.div(p, 4) * 2 + core
    z = zh * DEPTH + d
    lower = p < PLAN // 2

    x, y = lax.div(p, 16), lax.rem(lax.div(p, 4), 4)
    kind_own, cut_own = lax.div(y, 2), lax.rem(x + y, 2)
    set_own = 2 * kind_own + cut_own
    coef_block = 8 * set_own + 2 * x + core
    order = (2, 6, 4, 3, 7, 5, 1, 0)
    turns = [lax.rem(2 * x + core + k, 8) for k in order]
    places = [
        [16 * lax.div(t, 2) + 4 * lax.rem(lax.div(t, 2) + cut, 2) + 2 * zh + lax.rem(t, 2) for t in turns]
        for cut in range(2)
    ]

    def at_z(other):
        return (lax.rem(other, DEPTH), p + 2 * (lax.div(other, DEPTH) - zh))

    ls_copy = pltpu.make_async_copy(ls_hbm, ls_ref, ls_sem)
    con_copy = pltpu.make_async_copy(con_hbm, con_ref, con_sem)
    ls_copy.start()
    con_copy.start()
    wide_copies = [pltpu.make_async_copy(wide_hbm.at[n], wide.at[n], wide_sem.at[n]) for n in range(2)]
    mixed_copies = [pltpu.make_async_copy(mixed_hbm.at[n], mixed.at[n], mixed_sem.at[n]) for n in range(2)]
    tall_copies = [pltpu.make_async_copy(tall_hbm.at[n], tall.at[n], tall_sem.at[n]) for n in range(2)]
    for copy in wide_copies:
        copy.start()

    barrier = pltpu.get_barrier_semaphore()

    def greet(target):
        pl.semaphore_signal(barrier, inc=1, device_id=target, device_id_type=MESH)

    has = (d < DEPTH - 1, d > 0, p < PLAN - 1, p > 0)
    gets = (d > 0, d < DEPTH - 1, p > 0, p < PLAN - 1)
    xy = lax.div(p, 4)
    outer = jnp.where(core == 0, p - 1, p + 1)
    has_outer = (outer >= 0) & (outer < PLAN)
    for k in (1, RING - 1):
        greet(at_z(lax.rem(z + k, RING)))
    greet((d, p + 1 - 2 * core))
    pl.when(has_outer)(lambda: greet((d, outer)))
    for k in range(1, GROUP // 2):
        first = 4 * lax.rem(xy + k, GROUP // 2) + 2 * zh
        greet((d, first))
        greet((d, first + 1))
    for k in range(2, RING - 1):
        greet(at_z(lax.rem(z + k, RING)))

    ls_copy.wait()
    con_copy.wait()

    for layer in range(2):
        value = ls_ref[layer]
        value = jnp.where(lower, flip(value, 0, ROWS), value)
        own[layer, :, :HALF] = value[:, HALF:]
        own[layer, :, HALF:] = flip_lanes(value[:, :HALF])

    for layer in range(2):
        for k in range(8):
            spot = layer * 8 + k
            top = own[layer, 0:1, 128 * k : 128 * (k + 1)]
            bottom = own[layer, ROWS - 1 : ROWS, 128 * k : 128 * (k + 1)]
            rsend[0, spot : spot + 1, :] = jnp.where(lower, bottom, top)
            rsend[1, spot : spot + 1, :] = jnp.where(lower, top, bottom)

    pl.semaphore_wait(barrier, GROUP + RING - 2 + has_outer.astype(jnp.int32))

    def halo(source, target, number, device):
        return pltpu.make_async_remote_copy(
            src_ref=source, dst_ref=target, send_sem=hs.at[number], recv_sem=hr.at[number],
            device_id=device, device_id_type=MESH,
        )

    z_up = halo(own.at[1], zhalo.at[0], 0, (d + 1, p))
    z_down = halo(own.at[0], zhalo.at[1], 1, (d - 1, p))
    r_up = halo(rsend.at[1], rhalo.at[0], 2, (d, p + 1))
    r_down = halo(rsend.at[0], rhalo.at[1], 3, (d, p - 1))
    lands = (zhalo.at[0], zhalo.at[1], rhalo.at[0], rhalo.at[1])
    copies = (z_up, z_down, r_up, r_down)
    for copy, there in zip(copies, has):
        pl.when(there)(copy.start)
    for copy in mixed_copies + tall_copies:
        copy.start()
    for land, comes in zip(lands, gets):

        @pl.when(jnp.logical_not(comes))
        def _(land=land):
            land[...] = jnp.zeros(land.shape, F32)

    row_id = lax.broadcasted_iota(jnp.int32, (ROWS, NX), 0)
    lane_id = lax.broadcasted_iota(jnp.int32, (ROWS, HALF), 1)
    field = [own[0], own[1]]
    middle = flux(field[1] - field[0])
    for layer in range(2):
        centre = field[layer]
        bend = -middle if layer else middle
        inner_flux = flux(pltpu.roll(centre, 1, 0) - centre)
        bend = bend + jnp.where(row_id == 0, 0.0, inner_flux)
        bend = bend - jnp.where(row_id == ROWS - 1, 0.0, pltpu.roll(inner_flux, ROWS - 1, 0))
        sides = centre[:, :HALF], centre[:, HALF:]
        across = []
        for side in range(2):
            here = sides[side]
            inside = jnp.where(lane_id == 0, sides[1 - side], pltpu.roll(here, 1, 1))
            inner_flux = flux(inside - here)
            outside = jnp.where(lane_id == HALF - 1, flux(here), pltpu.roll(inner_flux, HALF - 1, 1))
            across.append(inner_flux - outside)
        bend = bend + jnp.concatenate(across, axis=1)
        part_density[layer] = con_ref[layer] * (0.5 * (1.0 + jnp.tanh(centre))) + bend_weight * bend

    for copy, comes in zip(copies, gets):
        pl.when(comes)(copy.wait_recv)
    even, odd = [], []
    for layer in range(2):
        centre = own[layer]
        here = slice(layer * 8, layer * 8 + 8)
        top = jnp.where(lower, rhalo[1, here, :], rhalo[0, here, :])
        bottom = jnp.where(lower, rhalo[0, here, :], rhalo[1, here, :])
        tops = [jnp.broadcast_to(top[k : k + 1], (ROWS, 128)) for k in range(8)]
        bottoms = [jnp.broadcast_to(bottom[k : k + 1], (ROWS, 128)) for k in range(8)]
        beside = jnp.where(row_id == 0, jnp.concatenate(tops, axis=1), jnp.concatenate(bottoms, axis=1))
        outer_rows = (row_id == 0) | (row_id == ROWS - 1)
        bend = flux(zhalo[layer] - centre) + jnp.where(outer_rows, flux(beside - centre), 0.0)
        density = part_density[layer] + bend_weight * bend
        even.append(density[:, :HALF] + density[:, HALF:])
        odd.append((density[:, :HALF] - density[:, HALF:]) * alternating((ROWS, HALF)))

    block = jnp.where(lower, PLAN // 2 - 1 - p, p - PLAN // 2)
    parity = lax.rem(d, 2)
    mate = d + 1 - 2 * parity
    for copy in wide_copies:
        copy.wait()

    def send_coef(group, k, cross):
        member = 1 - parity if cross else parity
        return pltpu.make_async_remote_copy(
            src_ref=csend.at[2 * (8 * group + turns[k]) + member], dst_ref=sbuf.at[GROUP * cross + block],
            send_sem=cs, recv_sem=cr.at[cross],
            device_id=(mate if cross else d, 8 * (group // 2) + places[group % 2][k]), device_id_type=MESH,
        )

    both = pair(jnp.concatenate(even + odd, axis=0))
    for cut in range(2):
        cols = slice(HALF * cut, HALF * (cut + 1))
        coef = table_right(both, wide[0, :, cols], wide[1, :, cols])
        for kind in range(2):
            start = kind * 16 + 8 * cut
            for m in range(4):
                lanes = slice(128 * m, 128 * (m + 1))
                starts = [2 * ROWS * kind + ROWS * layer + 8 * half for half in range(2) for layer in range(2)]
                for t, value in enumerate(regroup([coef[n : n + 8, lanes] for n in starts])):
                    csend[2 * start + 4 * m + t] = value
        for k in range(7):
            for kind in range(2):
                send_coef(2 * kind + cut, k, 0).start()
    for group in range(4):
        pl.when(group != set_own)(send_coef(group, 7, 0).start)
    for k in range(8):
        for group in range(4):
            send_coef(group, k, 1).start()

    def respond(start, cross):
        row = lax.broadcasted_iota(jnp.int32, (128, 128), 0)
        col = lax.broadcasted_iota(jnp.int32, (128, 128), 1) + start
        place = lax.rem(coef_block, GROUP // 2) * COEF + parity * SHARE + lax.rem(row, SHARE)
        v = jnp.where(kind_own == 1, NX - place, place).astype(F32)
        scale = 2.0 * math.pi * grav_scale * thickness / (4.0 * NX * NX)
        weight = jnp.where(place == 0, scale, 2.0 * scale) * jnp.where(col == 0, 1.0, 2.0)
        layer = (2 * (mate if cross else d) + lax.rem(lax.div(row, SHARE), 2)).astype(F32)
        rate = (top_depth + (layer + 0.5) * thickness) * (-2.0 * math.pi / (2 * NX))
        u = jnp.where(row >= 64, NX - col, col).astype(F32)
        return jnp.exp(jnp.sqrt(u * u + v * v) * rate) * weight

    for cross in range(2):
        for k in range(NX // 128):
            rsp[cross, :, 128 * k : 128 * (k + 1)] = respond(128 * k, cross)

    sbuf[block] = csend[2 * coef_block + parity]
    for copy in mixed_copies + tall_copies:
        copy.wait()
    side = lax.rem(lax.div(lax.broadcasted_iota(jnp.int32, (64, HALF), 1), 16), 2)
    sign = jnp.where(side == zh, 1.0, -1.0) * alternating((64, HALF))
    step = 256
    for cross in range(2):
        landed = sbuf.at[pl.ds(GROUP * cross, GROUP - 1 + cross)]
        pltpu.make_async_copy(landed, landed, cr.at[cross]).wait()
        value = sbuf[GROUP * cross : GROUP * (cross + 1)].reshape(HALF // 2, 128).T
        value = jnp.concatenate([value[:64], value[64:]], axis=1)
        both = pair(jnp.concatenate([value, value * sign], axis=0))
        for k in range(NX // step):
            here = slice(k * step, (k + 1) * step)
            coef = table_right(both, mixed[0, :, here], mixed[1, :, here]) * rsp[cross, :, here]
            parts = [coef[SHARE * n : SHARE * (n + 1)] for n in range(4)]
            coef = jnp.concatenate([parts[0] + parts[1], parts[2] + parts[3]], axis=0)
            if cross:
                pst[:, here] = pair(coef + acc[:, here])
            else:
                acc[:, here] = coef

    low = 2 * lax.rem(y, 2) + core
    x_turns = [lax.rem(x + k, 4) for k in range(4)]
    low_turns = [lax.rem(low + k, 4) for k in range(4)]
    low_places = [4 * lax.div(t, 2) + lax.rem(t, 2) + 2 * zh for t in low_turns]

    def send_rows(part, r, k, cross):
        upper = lax.div(x_turns[r], 2)
        upper = upper if part else 1 - upper
        member = 1 - parity if cross else parity
        return pltpu.make_async_remote_copy(
            src_ref=xsend.at[2 * (8 * x_turns[r] + 4 * upper + low_turns[k]) + member],
            dst_ref=cbuf.at[2 * coef_block + parity], send_sem=xs, recv_sem=xr,
            device_id=(mate if cross else d, 16 * x_turns[r] + 8 * upper + low_places[k]), device_id_type=MESH,
        )

    lane = lax.broadcasted_iota(jnp.int32, (8, 128), 1)
    early, even_lane = lane < 64, lax.rem(lane, 64) < 32
    def columns(part):
        cols = slice(128 * part, 128 * part + 128), slice(128 * part + 256, 128 * part + 384)
        return [jnp.concatenate([tall[n, :, col] for col in cols], axis=1) for n in range(2)]

    for part in range(2):
        value = table_right(pst[...], *columns(part))
        evens, odds = value[:SHARE], value[SHARE:] * alternating((SHARE, 256))
        plus, minus = evens + odds, evens - odds
        value = jnp.concatenate([plus, minus, plus, minus], axis=0).T
        for g in range(4):
            chunk = 2 * part + 4 * (g // 2) + g % 2
            for member in range(2):
                ups, downs = [], []
                for n in range(4):
                    start = ROWS * (4 * g + n) + 8 * member
                    rows = value[start : start + 8]
                    later = pltpu.roll(rows, 4, 0)
                    ups.append(jnp.where(even_lane, rows, pltpu.roll(later, 32, 1)))
                    downs.append(jnp.where(even_lane, pltpu.roll(rows, 32, 1), later))
                for spot, one, two in (
                    (2 * (8 + chunk), ups[0], ups[2]),
                    (2 * (8 + chunk) + 1, ups[1], ups[3]),
                    (2 * (7 - chunk), downs[3], downs[1]),
                    (2 * (7 - chunk) + 1, downs[2], downs[0]),
                ):
                    xsend[2 * spot + member] = jnp.where(early, one, two)[:4]

        for r in (1, 3, 2, 0):
            for k in range(4):
                send_rows(part, r, k, 1).start()
                if r or k:
                    send_rows(part, r, k, 0).start()
    upper_own = lax.rem(lax.div(x, 2) + lax.div(y, 2), 2)
    pl.when(upper_own == 0)(send_rows(0, 0, 0, 0).start)
    pl.when(upper_own == 1)(send_rows(1, 0, 0, 0).start)

    cbuf[2 * coef_block + parity] = xsend[2 * q + parity]
    landed = cbuf.at[pl.ds(0, 2 * GROUP - 1)]
    pltpu.make_async_copy(landed, landed, xr).wait()

    def send_field(far, depth):
        row = 1 - zh if far else zh
        return pltpu.make_async_remote_copy(
            src_ref=gsend.at[DEPTH * row + depth], dst_ref=gbuf.at[z], send_sem=gs, recv_sem=gr,
            device_id=(depth, p + 2 - 4 * zh if far else p), device_id_type=MESH,
        )

    steps = [lax.rem(lax.div(d, 2) + k, 4) for k in range(4)]
    depths = ([2 * t + 1 - lax.div(t, 2) for t in steps], [2 * t + lax.div(t, 2) for t in steps])

    for m in range(2 * NX // 128):
        parts = regroup([cbuf[4 * m + t] for t in range(4)])
        lanes = slice(128 * (m % 8), 128 * (m % 8 + 1))
        for g in range(4):
            start = ROWS * (m // 8) + 4 * g
            coefs[start : start + 4, lanes] = parts[g]
    both = pair(coefs[...])
    for cut in range(2):
        value = table_right(both, *columns(cut))
        evens, odds = value[:ROWS], value[ROWS:] * alternating((ROWS, 256))
        plus = evens + odds
        minus = evens - odds
        for half in range(2):
            rows = slice(8 * half, 8 * (half + 1))
            for n in range(2):
                lanes = slice(128 * n, 128 * (n + 1))
                gsend[DEPTH * half + 4 + cut + 2 * n] = plus[rows, lanes]
                gsend[DEPTH * half + 3 - cut - 2 * n] = minus[rows, lanes]
        for k in range(4):
            send_field(True, depths[cut][k]).start()
        for k in range(1, 4):
            send_field(False, depths[cut][k]).start()
    for cut in range(2):
        pl.when(depths[cut][0] != d)(send_field(False, depths[cut][0]).start)

    gbuf[z] = gsend[z]
    pltpu.make_async_copy(gbuf.at[pl.ds(0, RING - 1)], gbuf.at[pl.ds(0, RING - 1)], gr).wait()
    totals = [gbuf[0], gbuf[1]]
    for other in range(2, RING):
        totals[other % 2] = totals[other % 2] + gbuf[other]
    total = jnp.concatenate(totals, axis=0)
    across = lax.broadcasted_iota(jnp.int32, (128, 128), 0) + lax.broadcasted_iota(jnp.int32, (128, 128), 1)
    reverse = jnp.where(across == 127, 1.0, 0.0).astype(BF16)
    high, rest = split(total)
    low = (total - high.astype(F32) - rest.astype(F32)).astype(BF16)
    turned = matmul(jnp.concatenate([high, rest, low], axis=0), reverse)
    turned = turned[:ROWS] + turned[ROWS : 2 * ROWS] + turned[2 * ROWS :]
    total = jnp.where(d < DEPTH // 2, turned, total)

    @pl.when(lower)
    def _():
        for row in range(ROWS):
            out_ref[ROWS - 1 - row : ROWS - row, :] = total[row : row + 1]

    @pl.when(jnp.logical_not(lower))
    def _():
        out_ref[...] = total

    for copy, there in zip(copies, has):
        pl.when(there)(copy.wait_send)
    pltpu.make_async_copy(csend.at[pl.ds(0, 2 * GROUP - 1)], csend.at[pl.ds(0, 2 * GROUP - 1)], cs).wait()
    pltpu.make_async_copy(xsend.at[pl.ds(0, 2 * GROUP - 1)], xsend.at[pl.ds(0, 2 * GROUP - 1)], xs).wait()
    pltpu.make_async_copy(gsend.at[pl.ds(0, RING - 1)], gsend.at[pl.ds(0, RING - 1)], gs).wait()


def solution(mesh):
    wide, mixed, tall = basis()

    def step(level_set, contrast):
        vmem = pl.BlockSpec(memory_space=pltpu.VMEM)
        anywhere = pl.BlockSpec(memory_space=pl.ANY)
        dma = pltpu.SemaphoreType.DMA
        return pl.pallas_call(
            kernel,
            out_shape=jax.ShapeDtypeStruct((ROWS, 128), F32),
            in_specs=[anywhere] * 5,
            out_specs=vmem,
            scratch_shapes=[
                pltpu.VMEM((2, ROWS, NX), F32),
                pltpu.SMEM((2,), F32),
                pltpu.VMEM((2, ROWS, NX), F32),
                pltpu.VMEM((2, ROWS, NX), F32),
                pltpu.VMEM((2, HALF, NX), BF16),
                pltpu.VMEM((2, HALF, NX), BF16),
                pltpu.VMEM((2, NX, HALF), BF16),
                pltpu.VMEM((2, ROWS, NX), F32),
                pltpu.VMEM((2, 16, 128), F32),
                pltpu.VMEM((2, 16, 128), F32),
                pltpu.VMEM((2 * GROUP, 8, 128), F32),
                pltpu.VMEM((2 * GROUP, 8, 128), F32),
                pltpu.VMEM((2, 128, NX), F32),
                pltpu.VMEM((64, NX), F32),
                pltpu.VMEM((128, NX), BF16),
                pltpu.VMEM((2 * GROUP, 4, 128), F32),
                pltpu.VMEM((2 * GROUP, 4, 128), F32),
                pltpu.VMEM((2 * ROWS, NX), F32),
                pltpu.VMEM((RING, 8, 128), F32),
                pltpu.VMEM((RING, 8, 128), F32),
                dma(()), dma(()), dma((2,)), dma((2,)), dma((2,)), dma((4,)), dma((4,)),
                dma(()), dma((2,)), dma(()), dma(()), dma(()), dma(()),
            ],
            compiler_params=pltpu.CompilerParams(
                collective_id=0, has_side_effects=True, vmem_limit_bytes=63 * 1024 * 1024
            ),
        )(level_set, contrast, jnp.asarray(wide), jnp.asarray(mixed), jnp.asarray(tall))

    return jax.shard_map(
        step,
        mesh=mesh,
        in_specs=(P("depth", "plan", None), P("depth")),
        out_specs=P("plan", "depth"),
        check_vma=False,
    )
```

```python
import functools
import math

import jax
import jax.numpy as jnp
import ml_dtypes
import numpy as np
from jax import lax
from jax.experimental import pallas as pl
from jax.experimental.pallas import tpu as pltpu
from jax.sharding import PartitionSpec as P

MESH = pl.DeviceIdType.MESH
F32 = jnp.float32
BF16 = jnp.bfloat16

NX = 1024
HALF = NX // 2
LAYERS = 16
DEPTH = 8
PLAN = 64
ROWS = NX // PLAN
GROUP = 32
RING = 16
COEF = 2 * NX // GROUP
SHARE = COEF // 2

bend_weight = 0.5
grav_scale = 0.05
top_depth = 0.0
thickness = 1.0


def basis():
    j = np.arange(HALF, dtype=np.float64)[:, None] + 0.5
    v = np.arange(NX, dtype=np.float64)[None, :]
    table = np.cos(np.pi * v * j / NX)
    high = table.astype(ml_dtypes.bfloat16)
    low = (table - high.astype(np.float64)).astype(ml_dtypes.bfloat16)
    wide = np.stack([high, low])
    order = np.arange(HALF).reshape(GROUP, 2, ROWS // 2).transpose(1, 0, 2).reshape(-1)
    return wide, np.ascontiguousarray(wide[:, order]), np.ascontiguousarray(np.swapaxes(wide, 1, 2))


def alternating(shape):
    return 1.0 - 2.0 * lax.rem(lax.broadcasted_iota(jnp.int32, shape, 1), 2).astype(F32)


def flux(step):
    return step * lax.rsqrt(1.0 + step * step)


def flip(value, axis, size):
    index = lax.broadcasted_iota(jnp.int32, value.shape, axis)
    step = size // 2
    value = pltpu.roll(value, step, axis)
    while step > 1:
        step //= 2
        up = pltpu.roll(value, step, axis)
        down = pltpu.roll(value, size - step, axis)
        value = jnp.where((index & step) != 0, up, down)
    return value


def flip_lanes(value):
    blocks = value.shape[1] // 128
    parts = [flip(value[:, 128 * k : 128 * (k + 1)], 1, 128) for k in reversed(range(blocks))]
    return jnp.concatenate(parts, axis=1) if blocks > 1 else parts[0]


def split(value):
    high = value.astype(BF16)
    low = (value - high.astype(F32)).astype(BF16)
    return high, low


def matmul(a, b):
    return jnp.dot(a, b, preferred_element_type=F32)


def pair(value):
    return jnp.concatenate(split(value), axis=0)


def table_right(both, high_table, low_table):
    n = both.shape[0] // 2
    product = matmul(both, high_table)
    return product[:n] + product[n:] + matmul(both[:n], low_table)


def regroup(parts):
    lane = lax.broadcasted_iota(jnp.int32, parts[0].shape, 1)
    early, even = lane < 64, lax.rem(lane, 64) < 32
    wide = [jnp.where(early, parts[g], pltpu.roll(parts[g + 2], 64, 1)) for g in range(2)]
    wide += [jnp.where(early, pltpu.roll(parts[g], 64, 1), parts[g + 2]) for g in range(2)]
    out = []
    for first, second in (wide[:2], wide[2:]):
        out.append(jnp.where(even, first, pltpu.roll(second, 32, 1)))
        out.append(jnp.where(even, pltpu.roll(first, 96, 1), second))
    return out


def kernel(
    ls_hbm, con_hbm, wide_hbm, mixed_hbm, tall_hbm, out_ref,
    ls_ref, con_ref, own, part_density, wide, mixed, tall, zhalo, rsend, rhalo, folded, folded_back, csend, sbuf, rsp, acc, pst, xsend, cbuf, coefs, gsend, gbuf,
    ls_sem, con_sem, wide_sem, mixed_sem, tall_sem, hs, hr, cs, cr, xs, xr, gs, gr,
):
    d = lax.axis_index("depth")
    p = lax.axis_index("plan")
    core = lax.rem(p, 2)
    zh = lax.rem(lax.div(p, 2), 2)
    q = lax.div(p, 4) * 2 + core
    z = zh * DEPTH + d
    lower = p < PLAN // 2

    x, y = lax.div(p, 16), lax.rem(lax.div(p, 4), 4)
    kind_own, cut_own = lax.div(y, 2), lax.rem(x + y, 2)
    set_own = 2 * kind_own + cut_own
    coef_block = 8 * set_own + 2 * x + core

    def turn(k):
        return lax.rem(2 * x + core + k, 8)

    def at_z(other):
        return (lax.rem(other, DEPTH), p + 2 * (lax.div(other, DEPTH) - zh))

    ls_copy = pltpu.make_async_copy(ls_hbm, ls_ref, ls_sem)
    con_copy = pltpu.make_async_copy(con_hbm, con_ref, con_sem)
    ls_copy.start()
    con_copy.start()
    wide_copies = [pltpu.make_async_copy(wide_hbm.at[n], wide.at[n], wide_sem.at[n]) for n in range(2)]
    mixed_copies = [pltpu.make_async_copy(mixed_hbm.at[n], mixed.at[n], mixed_sem.at[n]) for n in range(2)]
    tall_copies = [pltpu.make_async_copy(tall_hbm.at[n], tall.at[n], tall_sem.at[n]) for n in range(2)]
    for copy in wide_copies:
        copy.start()

    barrier = pltpu.get_barrier_semaphore()

    def greet(target):
        pl.semaphore_signal(barrier, inc=1, device_id=target, device_id_type=MESH)

    has = (d < DEPTH - 1, d > 0, p < PLAN - 1, p > 0)
    gets = (d > 0, d < DEPTH - 1, p > 0, p < PLAN - 1)
    xy = lax.div(p, 4)
    outer = jnp.where(core == 0, p - 1, p + 1)
    has_outer = (outer >= 0) & (outer < PLAN)
    for k in (1, RING - 1):
        greet(at_z(lax.rem(z + k, RING)))
    greet((d, p + 1 - 2 * core))
    pl.when(has_outer)(lambda: greet((d, outer)))

    @pl.loop(1, GROUP // 2)
    def _(k):
        first = 4 * lax.rem(xy + k, GROUP // 2) + 2 * zh
        greet((d, first))
        greet((d, first + 1))

    @pl.loop(2, RING - 1)
    def _(k):
        greet(at_z(lax.rem(z + k, RING)))


    ls_copy.wait()
    con_copy.wait()

    for layer in range(2):
        value = ls_ref[layer]
        value = jnp.where(lower, flip(value, 0, ROWS), value)
        own[layer, :, :HALF] = value[:, HALF:]
        own[layer, :, HALF:] = flip_lanes(value[:, :HALF])

    for layer in range(2):
        for k in range(8):
            spot = layer * 8 + k
            top = own[layer, 0:1, 128 * k : 128 * (k + 1)]
            bottom = own[layer, ROWS - 1 : ROWS, 128 * k : 128 * (k + 1)]
            rsend[0, spot : spot + 1, :] = jnp.where(lower, bottom, top)
            rsend[1, spot : spot + 1, :] = jnp.where(lower, top, bottom)

    pl.semaphore_wait(barrier, GROUP + RING - 2 + has_outer.astype(jnp.int32))

    def halo(source, target, number, device):
        return pltpu.make_async_remote_copy(
            src_ref=source, dst_ref=target, send_sem=hs.at[number], recv_sem=hr.at[number],
            device_id=device, device_id_type=MESH,
        )

    z_up = halo(own.at[1], zhalo.at[0], 0, (d + 1, p))
    z_down = halo(own.at[0], zhalo.at[1], 1, (d - 1, p))
    r_up = halo(rsend.at[1], rhalo.at[0], 2, (d, p + 1))
    r_down = halo(rsend.at[0], rhalo.at[1], 3, (d, p - 1))
    lands = (zhalo.at[0], zhalo.at[1], rhalo.at[0], rhalo.at[1])
    copies = (z_up, z_down, r_up, r_down)
    for copy, there in zip(copies, has):
        pl.when(there)(copy.start)
    for copy in mixed_copies + tall_copies:
        copy.start()
    for land, comes in zip(lands, gets):

        @pl.when(jnp.logical_not(comes))
        def _(land=land):
            land[...] = jnp.zeros(land.shape, F32)

    row_id = lax.broadcasted_iota(jnp.int32, (ROWS, NX), 0)
    lane_id = lax.broadcasted_iota(jnp.int32, (ROWS, HALF), 1)
    field = [own[0], own[1]]
    middle = flux(field[1] - field[0])
    for layer in range(2):
        centre = field[layer]
        bend = -middle if layer else middle
        inner_flux = flux(pltpu.roll(centre, 1, 0) - centre)
        bend = bend + jnp.where(row_id == 0, 0.0, inner_flux)
        bend = bend - jnp.where(row_id == ROWS - 1, 0.0, pltpu.roll(inner_flux, ROWS - 1, 0))
        sides = centre[:, :HALF], centre[:, HALF:]
        across = []
        for side in range(2):
            here = sides[side]
            inside = jnp.where(lane_id == 0, sides[1 - side], pltpu.roll(here, 1, 1))
            inner_flux = flux(inside - here)
            outside = jnp.where(lane_id == HALF - 1, flux(here), pltpu.roll(inner_flux, HALF - 1, 1))
            across.append(inner_flux - outside)
        bend = bend + jnp.concatenate(across, axis=1)
        part_density[layer] = con_ref[layer] * (0.5 * (1.0 + jnp.tanh(centre))) + bend_weight * bend

    for copy, comes in zip(copies, gets):
        pl.when(comes)(copy.wait_recv)
    even, odd = [], []
    for layer in range(2):
        centre = own[layer]
        here = slice(layer * 8, layer * 8 + 8)
        top = jnp.where(lower, rhalo[1, here, :], rhalo[0, here, :])
        bottom = jnp.where(lower, rhalo[0, here, :], rhalo[1, here, :])
        tops = [jnp.broadcast_to(top[k : k + 1], (ROWS, 128)) for k in range(8)]
        bottoms = [jnp.broadcast_to(bottom[k : k + 1], (ROWS, 128)) for k in range(8)]
        beside = jnp.where(row_id == 0, jnp.concatenate(tops, axis=1), jnp.concatenate(bottoms, axis=1))
        outer_rows = (row_id == 0) | (row_id == ROWS - 1)
        bend = flux(zhalo[layer] - centre) + jnp.where(outer_rows, flux(beside - centre), 0.0)
        density = part_density[layer] + bend_weight * bend
        even.append(density[:, :HALF] + density[:, HALF:])
        odd.append((density[:, :HALF] - density[:, HALF:]) * alternating((ROWS, HALF)))

    block = jnp.where(lower, PLAN // 2 - 1 - p, p - PLAN // 2)
    parity = lax.rem(d, 2)
    mate = d + 1 - 2 * parity
    for copy in wide_copies:
        copy.wait()

    def send_coef(kind, cut, k, cross):
        place = turn(k)
        x_to = lax.div(place, 2)
        target = 16 * x_to + 8 * kind + 4 * lax.rem(x_to + cut, 2) + 2 * zh + lax.rem(place, 2)
        member = 1 - parity if cross else parity
        return pltpu.make_async_remote_copy(
            src_ref=csend.at[2 * (16 * kind + 8 * cut + place) + member], dst_ref=sbuf.at[GROUP * cross + block],
            send_sem=cs, recv_sem=cr.at[cross], device_id=(mate if cross else d, target), device_id_type=MESH,
        )

    folded[...] = pair(jnp.concatenate(even + odd, axis=0))

    @pl.loop(0, 2)
    def _(cut):
        cols = pl.ds(pl.multiple_of(HALF * cut, HALF), HALF)
        coef = table_right(folded[...], wide[0, :, cols], wide[1, :, cols])
        for kind in range(2):
            for m in range(4):
                lanes = slice(128 * m, 128 * (m + 1))
                starts = [2 * ROWS * kind + ROWS * layer + 8 * half for half in range(2) for layer in range(2)]
                for t, value in enumerate(regroup([coef[n : n + 8, lanes] for n in starts])):
                    csend[16 * cut + 32 * kind + 4 * m + t] = value

        @pl.loop(1, 8)
        def _(k):
            for kind in range(2):
                send_coef(kind, cut, k, 0).start()

    for kind in range(2):
        for cut in range(2):
            pl.when(2 * kind + cut != set_own)(send_coef(kind, cut, 0, 0).start)

    @pl.loop(0, 8)
    def _(k):
        for kind in range(2):
            for cut in range(2):
                send_coef(kind, cut, k, 1).start()

    home = pltpu.make_async_copy(csend.at[2 * coef_block + parity], sbuf.at[block], cr.at[0])
    home.start()

    def respond(start, cross):
        row = lax.broadcasted_iota(jnp.int32, (128, 128), 0)
        col = lax.broadcasted_iota(jnp.int32, (128, 128), 1) + start
        place = lax.rem(coef_block, GROUP // 2) * COEF + parity * SHARE + lax.rem(row, SHARE)
        v = jnp.where(kind_own == 1, NX - place, place).astype(F32)
        scale = 2.0 * math.pi * grav_scale * thickness / (4.0 * NX * NX)
        weight = jnp.where(place == 0, scale, 2.0 * scale) * jnp.where(col == 0, 1.0, 2.0)
        layer = (2 * (mate if cross else d) + lax.rem(lax.div(row, SHARE), 2)).astype(F32)
        rate = (top_depth + (layer + 0.5) * thickness) * (-2.0 * math.pi / (2 * NX))
        u = jnp.where(row >= 64, NX - col, col).astype(F32)
        return jnp.exp(jnp.sqrt(u * u + v * v) * rate) * weight

    @pl.loop(0, NX // 128)
    def _(k):
        for cross in range(2):
            rsp[cross, :, pl.ds(pl.multiple_of(128 * k, 128), 128)] = respond(128 * k, cross)


    for copy in mixed_copies + tall_copies:
        copy.wait()
    side = lax.rem(lax.div(lax.broadcasted_iota(jnp.int32, (64, HALF), 1), 16), 2)
    sign = jnp.where(side == zh, 1.0, -1.0) * alternating((64, HALF))
    step = 256
    acc[...] = jnp.zeros(acc.shape, F32)

    @pl.loop(0, 2)
    def _(cross):
        here = pl.ds(GROUP * cross, GROUP)
        landed = sbuf.at[here]
        pltpu.make_async_copy(landed, landed, cr.at[cross]).wait()
        value = sbuf[here].reshape(HALF // 2, 128).T
        value = jnp.concatenate([value[:64], value[64:]], axis=1)
        both = pair(jnp.concatenate([value, value * sign], axis=0))
        for k in range(NX // step):
            here = slice(k * step, (k + 1) * step)
            coef = table_right(both, mixed[0, :, here], mixed[1, :, here]) * rsp[cross, :, here]
            parts = [coef[SHARE * n : SHARE * (n + 1)] for n in range(4)]
            acc[:, here] += jnp.concatenate([parts[0] + parts[1], parts[2] + parts[3]], axis=0)

    pst[...] = pair(acc[...])

    low = 2 * lax.rem(y, 2) + core

    def send_rows(part, r, k, cross):
        x_to = lax.rem(x + r, 4)
        low_to = lax.rem(low + k, 4)
        upper = lax.rem(lax.div(x_to, 2) + 1 + part, 2)
        member = 1 - parity if cross else parity
        target = 16 * x_to + 8 * upper + 4 * lax.div(low_to, 2) + lax.rem(low_to, 2) + 2 * zh
        return pltpu.make_async_remote_copy(
            src_ref=xsend.at[2 * (8 * x_to + 4 * upper + low_to) + member],
            dst_ref=cbuf.at[2 * coef_block + parity], send_sem=xs, recv_sem=xr,
            device_id=(mate if cross else d, target), device_id_type=MESH,
        )

    lane = lax.broadcasted_iota(jnp.int32, (8, 128), 1)
    early, even_lane = lane < 64, lax.rem(lane, 64) < 32

    def columns(part):
        cols = [pl.ds(pl.multiple_of(128 * part + start, 128), 128) for start in (0, 256)]
        return [jnp.concatenate([tall[n, :, col] for col in cols], axis=1) for n in range(2)]

    @pl.loop(0, 2)
    def _(part):
        value = table_right(pst[...], *columns(part))
        evens, odds = value[:SHARE], value[SHARE:] * alternating((SHARE, 256))
        plus, minus = evens + odds, evens - odds
        value = jnp.concatenate([plus, minus, plus, minus], axis=0).T
        for g in range(4):
            chunk = 2 * part + 4 * (g // 2) + g % 2
            for member in range(2):
                ups, downs = [], []
                for n in range(4):
                    start = ROWS * (4 * g + n) + 8 * member
                    rows = value[start : start + 8]
                    later = pltpu.roll(rows, 4, 0)
                    ups.append(jnp.where(even_lane, rows, pltpu.roll(later, 32, 1)))
                    downs.append(jnp.where(even_lane, pltpu.roll(rows, 32, 1), later))
                for spot, one, two in (
                    (2 * (8 + chunk), ups[0], ups[2]),
                    (2 * (8 + chunk) + 1, ups[1], ups[3]),
                    (2 * (7 - chunk), downs[3], downs[1]),
                    (2 * (7 - chunk) + 1, downs[2], downs[0]),
                ):
                    xsend[2 * spot + member] = jnp.where(early, one, two)[:4]

        send_rows(part, 0, 0, 1).start()

        @pl.loop(1, 16)
        def _(n):
            send_rows(part, lax.rem(n, 4), lax.div(n, 4), 1).start()
            send_rows(part, lax.rem(n, 4), lax.div(n, 4), 0).start()

    upper_own = lax.rem(lax.div(x, 2) + lax.div(y, 2), 2)
    pl.when(upper_own == 0)(send_rows(0, 0, 0, 0).start)
    pl.when(upper_own == 1)(send_rows(1, 0, 0, 0).start)

    cbuf[2 * coef_block + parity] = xsend[2 * q + parity]
    landed = cbuf.at[pl.ds(0, 2 * GROUP - 1)]
    pltpu.make_async_copy(landed, landed, xr).wait()

    def send_field(far, depth):
        row = 1 - zh if far else zh
        return pltpu.make_async_remote_copy(
            src_ref=gsend.at[DEPTH * row + depth], dst_ref=gbuf.at[z], send_sem=gs, recv_sem=gr,
            device_id=(depth, p + 2 - 4 * zh if far else p), device_id_type=MESH,
        )

    def depth_of(cut, k):
        t = lax.rem(lax.div(d, 2) + k, 4)
        return 2 * t + lax.rem(lax.div(t, 2) + 1 + cut, 2)

    for m in range(2 * NX // 128):
        parts = regroup([cbuf[4 * m + t] for t in range(4)])
        lanes = slice(128 * (m % 8), 128 * (m % 8 + 1))
        for g in range(4):
            start = ROWS * (m // 8) + 4 * g
            coefs[start : start + 4, lanes] = parts[g]
    folded_back[...] = pair(coefs[...])

    @pl.loop(0, 2)
    def _(cut):
        value = table_right(folded_back[...], *columns(cut))
        evens, odds = value[:ROWS], value[ROWS:] * alternating((ROWS, 256))
        plus = evens + odds
        minus = evens - odds
        for half in range(2):
            rows = slice(8 * half, 8 * (half + 1))
            for n in range(2):
                lanes = slice(128 * n, 128 * (n + 1))
                gsend[DEPTH * half + 4 + cut + 2 * n] = plus[rows, lanes]
                gsend[DEPTH * half + 3 - cut - 2 * n] = minus[rows, lanes]
        send_field(True, depth_of(cut, 0)).start()

        @pl.loop(1, 4)
        def _(k):
            send_field(True, depth_of(cut, k)).start()
            send_field(False, depth_of(cut, k)).start()

    for cut in range(2):
        pl.when(depth_of(cut, 0) != d)(send_field(False, depth_of(cut, 0)).start)

    gbuf[z] = gsend[z]
    pltpu.make_async_copy(gbuf.at[pl.ds(0, RING - 1)], gbuf.at[pl.ds(0, RING - 1)], gr).wait()
    totals = [gbuf[0], gbuf[1]]
    for other in range(2, RING):
        totals[other % 2] = totals[other % 2] + gbuf[other]
    total = jnp.concatenate(totals, axis=0)
    across = lax.broadcasted_iota(jnp.int32, (128, 128), 0) + lax.broadcasted_iota(jnp.int32, (128, 128), 1)
    reverse = jnp.where(across == 127, 1.0, 0.0).astype(BF16)
    high, rest = split(total)
    low = (total - high.astype(F32) - rest.astype(F32)).astype(BF16)
    turned = matmul(jnp.concatenate([high, rest, low], axis=0), reverse)
    turned = turned[:ROWS] + turned[ROWS : 2 * ROWS] + turned[2 * ROWS :]
    total = jnp.where(d < DEPTH // 2, turned, total)

    @pl.when(lower)
    def _():
        for row in range(ROWS):
            out_ref[ROWS - 1 - row : ROWS - row, :] = total[row : row + 1]

    @pl.when(jnp.logical_not(lower))
    def _():
        out_ref[...] = total

    for copy, there in zip(copies, has):
        pl.when(there)(copy.wait_send)
    pltpu.make_async_copy(csend.at[pl.ds(0, 2 * GROUP - 1)], csend.at[pl.ds(0, 2 * GROUP - 1)], cs).wait()
    pltpu.make_async_copy(xsend.at[pl.ds(0, 2 * GROUP - 1)], xsend.at[pl.ds(0, 2 * GROUP - 1)], xs).wait()
    pltpu.make_async_copy(gsend.at[pl.ds(0, RING - 1)], gsend.at[pl.ds(0, RING - 1)], gs).wait()


def solution(mesh):
    wide, mixed, tall = basis()

    def step(level_set, contrast):
        vmem = pl.BlockSpec(memory_space=pltpu.VMEM)
        anywhere = pl.BlockSpec(memory_space=pl.ANY)
        dma = pltpu.SemaphoreType.DMA
        return pl.pallas_call(
            kernel,
            out_shape=jax.ShapeDtypeStruct((ROWS, 128), F32),
            in_specs=[anywhere] * 5,
            out_specs=vmem,
            scratch_shapes=[
                pltpu.VMEM((2, ROWS, NX), F32),
                pltpu.SMEM((2,), F32),
                pltpu.VMEM((2, ROWS, NX), F32),
                pltpu.VMEM((2, ROWS, NX), F32),
                pltpu.VMEM((2, HALF, NX), BF16),
                pltpu.VMEM((2, HALF, NX), BF16),
                pltpu.VMEM((2, NX, HALF), BF16),
                pltpu.VMEM((2, ROWS, NX), F32),
                pltpu.VMEM((2, 16, 128), F32),
                pltpu.VMEM((2, 16, 128), F32),
                pltpu.VMEM((128, HALF), BF16),
                pltpu.VMEM((64, NX), BF16),
                pltpu.VMEM((2 * GROUP, 8, 128), F32),
                pltpu.VMEM((2 * GROUP, 8, 128), F32),
                pltpu.VMEM((2, 128, NX), F32),
                pltpu.VMEM((64, NX), F32),
                pltpu.VMEM((128, NX), BF16),
                pltpu.VMEM((2 * GROUP, 4, 128), F32),
                pltpu.VMEM((2 * GROUP, 4, 128), F32),
                pltpu.VMEM((2 * ROWS, NX), F32),
                pltpu.VMEM((RING, 8, 128), F32),
                pltpu.VMEM((RING, 8, 128), F32),
                dma(()), dma(()), dma((2,)), dma((2,)), dma((2,)), dma((4,)), dma((4,)),
                dma(()), dma((2,)), dma(()), dma(()), dma(()), dma(()),
            ],
            compiler_params=pltpu.CompilerParams(
                collective_id=0, has_side_effects=True, vmem_limit_bytes=63 * 1024 * 1024
            ),
        )(level_set, contrast, jnp.asarray(wide), jnp.asarray(mixed), jnp.asarray(tall))

    return jax.shard_map(
        step,
        mesh=mesh,
        in_specs=(P("depth", "plan", None), P("depth")),
        out_specs=P("plan", "depth"),
        check_vma=False,
    )
```

```python
import functools
import math

import jax
import jax.numpy as jnp
import ml_dtypes
import numpy as np
from jax import lax
from jax.experimental import pallas as pl
from jax.experimental.pallas import tpu as pltpu
from jax.sharding import PartitionSpec as P

MESH = pl.DeviceIdType.MESH
F32 = jnp.float32
BF16 = jnp.bfloat16

NX = 1024
HALF = NX // 2
LAYERS = 16
DEPTH = 8
PLAN = 64
ROWS = NX // PLAN
GROUP = 32
RING = 16
COEF = 2 * NX // GROUP
SHARE = COEF // 2

bend_weight = 0.5
grav_scale = 0.05
top_depth = 0.0
thickness = 1.0


def basis():
    j = np.arange(HALF, dtype=np.float64)[:, None] + 0.5
    v = np.arange(NX, dtype=np.float64)[None, :]
    table = np.cos(np.pi * v * j / NX)
    high = table.astype(ml_dtypes.bfloat16)
    low = (table - high.astype(np.float64)).astype(ml_dtypes.bfloat16)
    wide = np.stack([high, low])
    order = np.arange(HALF).reshape(GROUP, 2, ROWS // 2).transpose(1, 0, 2).reshape(-1)
    return wide, np.ascontiguousarray(wide[:, order]), np.ascontiguousarray(np.swapaxes(wide, 1, 2))


def alternating(shape):
    return 1.0 - 2.0 * lax.rem(lax.broadcasted_iota(jnp.int32, shape, 1), 2).astype(F32)


def flux(step):
    return step * lax.rsqrt(1.0 + step * step)


def flip(value, axis, size):
    index = lax.broadcasted_iota(jnp.int32, value.shape, axis)
    step = size // 2
    value = pltpu.roll(value, step, axis)
    while step > 1:
        step //= 2
        up = pltpu.roll(value, step, axis)
        down = pltpu.roll(value, size - step, axis)
        value = jnp.where((index & step) != 0, up, down)
    return value


def flip_lanes(value):
    blocks = value.shape[1] // 128
    parts = [flip(value[:, 128 * k : 128 * (k + 1)], 1, 128) for k in reversed(range(blocks))]
    return jnp.concatenate(parts, axis=1) if blocks > 1 else parts[0]


def split(value):
    high = value.astype(BF16)
    low = (value - high.astype(F32)).astype(BF16)
    return high, low


def matmul(a, b):
    return jnp.dot(a, b, preferred_element_type=F32)


def pair(value):
    return jnp.concatenate(split(value), axis=0)


def table_right(both, high_table, low_table):
    n = both.shape[0] // 2
    product = matmul(both, high_table)
    return product[:n] + product[n:] + matmul(both[:n], low_table)


def regroup(parts):
    lane = lax.broadcasted_iota(jnp.int32, parts[0].shape, 1)
    early, even = lane < 64, lax.rem(lane, 64) < 32
    wide = [jnp.where(early, parts[g], pltpu.roll(parts[g + 2], 64, 1)) for g in range(2)]
    wide += [jnp.where(early, pltpu.roll(parts[g], 64, 1), parts[g + 2]) for g in range(2)]
    out = []
    for first, second in (wide[:2], wide[2:]):
        out.append(jnp.where(even, first, pltpu.roll(second, 32, 1)))
        out.append(jnp.where(even, pltpu.roll(first, 96, 1), second))
    return out


def kernel(
    ls_hbm, con_hbm, wide_hbm, mixed_hbm, tall_hbm, out_ref,
    ls_ref, con_ref, own, part_density, wide, mixed, tall, zhalo, rsend, rhalo, csend, sbuf, rsp, acc, pst, xsend, cbuf, coefs, gsend, gbuf,
    ls_sem, con_sem, wide_sem, mixed_sem, tall_sem, hs, hr, cs, cr, xs, xr, gs, gr, news,
):
    d = lax.axis_index("depth")
    p = lax.axis_index("plan")
    core = lax.rem(p, 2)
    zh = lax.rem(lax.div(p, 2), 2)
    q = lax.div(p, 4) * 2 + core
    z = zh * DEPTH + d
    lower = p < PLAN // 2

    x, y = lax.div(p, 16), lax.rem(lax.div(p, 4), 4)
    kind_own, cut_own = lax.div(y, 2), lax.rem(x + y, 2)
    set_own = 2 * kind_own + cut_own
    coef_block = 8 * set_own + 2 * x + core
    order = (2, 6, 4, 3, 7, 5, 1, 0)
    turns = [lax.rem(2 * x + core + k, 8) for k in order]
    places = [
        [16 * lax.div(t, 2) + 4 * lax.rem(lax.div(t, 2) + cut, 2) + 2 * zh + lax.rem(t, 2) for t in turns]
        for cut in range(2)
    ]

    def at_z(other):
        return (lax.rem(other, DEPTH), p + 2 * (lax.div(other, DEPTH) - zh))

    ls_copy = pltpu.make_async_copy(ls_hbm, ls_ref, ls_sem)
    con_copy = pltpu.make_async_copy(con_hbm, con_ref, con_sem)
    ls_copy.start()
    con_copy.start()
    wide_copies = [pltpu.make_async_copy(wide_hbm.at[n], wide.at[n], wide_sem.at[n]) for n in range(2)]
    mixed_copies = [pltpu.make_async_copy(mixed_hbm.at[n], mixed.at[n], mixed_sem.at[n]) for n in range(2)]
    tall_copies = [pltpu.make_async_copy(tall_hbm.at[n], tall.at[n], tall_sem.at[n]) for n in range(2)]
    for copy in wide_copies:
        copy.start()

    barrier = pltpu.get_barrier_semaphore()

    def greet(target):
        pl.semaphore_signal(barrier, inc=1, device_id=target, device_id_type=MESH)

    has = (d < DEPTH - 1, d > 0, p < PLAN - 1, p > 0)
    gets = (d > 0, d < DEPTH - 1, p > 0, p < PLAN - 1)
    outer = jnp.where(core == 0, p - 1, p + 1)
    has_outer = (outer >= 0) & (outer < PLAN)
    x_line = [(d, p + 16 * (lax.rem(x + k, 4) - x)) for k in (1, 3, 2)]
    y_line = [(d, p + 4 * (lax.rem(y + k, 4) - y)) for k in (1, 3, 2)]
    buddy = (d, p + 1 - 2 * core)

    def z_pair(k):
        return [at_z(lax.rem(z + away, RING)) for away in (k, RING - k)]

    for target in z_pair(1) + [buddy]:
        greet(target)
    pl.when(has_outer)(lambda: greet((d, outer)))
    for target in x_line + y_line:
        greet(target)

    def tell(number, targets):
        for target in targets:
            pl.semaphore_signal(news.at[number], inc=1, device_id=target, device_id_type=MESH)

    def hear(number, count):
        pl.semaphore_wait(news.at[number], count)

    ls_copy.wait()
    con_copy.wait()

    for layer in range(2):
        value = ls_ref[layer]
        value = jnp.where(lower, flip(value, 0, ROWS), value)
        own[layer, :, :HALF] = value[:, HALF:]
        own[layer, :, HALF:] = flip_lanes(value[:, :HALF])

    for layer in range(2):
        for k in range(8):
            spot = layer * 8 + k
            top = own[layer, 0:1, 128 * k : 128 * (k + 1)]
            bottom = own[layer, ROWS - 1 : ROWS, 128 * k : 128 * (k + 1)]
            rsend[0, spot : spot + 1, :] = jnp.where(lower, bottom, top)
            rsend[1, spot : spot + 1, :] = jnp.where(lower, top, bottom)

    pl.semaphore_wait(barrier, 9 + has_outer.astype(jnp.int32))

    def halo(source, target, number, device):
        return pltpu.make_async_remote_copy(
            src_ref=source, dst_ref=target, send_sem=hs.at[number], recv_sem=hr.at[number],
            device_id=device, device_id_type=MESH,
        )

    z_up = halo(own.at[1], zhalo.at[0], 0, (d + 1, p))
    z_down = halo(own.at[0], zhalo.at[1], 1, (d - 1, p))
    r_up = halo(rsend.at[1], rhalo.at[0], 2, (d, p + 1))
    r_down = halo(rsend.at[0], rhalo.at[1], 3, (d, p - 1))
    lands = (zhalo.at[0], zhalo.at[1], rhalo.at[0], rhalo.at[1])
    copies = (z_up, z_down, r_up, r_down)
    for copy, there in zip(copies, has):
        pl.when(there)(copy.start)
    tell(0, y_line)
    tell(1, z_pair(1))
    for copy in mixed_copies + tall_copies:
        copy.start()
    for land, comes in zip(lands, gets):

        @pl.when(jnp.logical_not(comes))
        def _(land=land):
            land[...] = jnp.zeros(land.shape, F32)

    row_id = lax.broadcasted_iota(jnp.int32, (ROWS, NX), 0)
    lane_id = lax.broadcasted_iota(jnp.int32, (ROWS, HALF), 1)
    field = [own[0], own[1]]
    middle = flux(field[1] - field[0])
    for layer in range(2):
        centre = field[layer]
        bend = -middle if layer else middle
        inner_flux = flux(pltpu.roll(centre, 1, 0) - centre)
        bend = bend + jnp.where(row_id == 0, 0.0, inner_flux)
        bend = bend - jnp.where(row_id == ROWS - 1, 0.0, pltpu.roll(inner_flux, ROWS - 1, 0))
        sides = centre[:, :HALF], centre[:, HALF:]
        across = []
        for side in range(2):
            here = sides[side]
            inside = jnp.where(lane_id == 0, sides[1 - side], pltpu.roll(here, 1, 1))
            inner_flux = flux(inside - here)
            outside = jnp.where(lane_id == HALF - 1, flux(here), pltpu.roll(inner_flux, HALF - 1, 1))
            across.append(inner_flux - outside)
        bend = bend + jnp.concatenate(across, axis=1)
        part_density[layer] = con_ref[layer] * (0.5 * (1.0 + jnp.tanh(centre))) + bend_weight * bend

    hear(0, 3)
    tell(2, [buddy])

    for copy, comes in zip(copies, gets):
        pl.when(comes)(copy.wait_recv)
    even, odd = [], []
    for layer in range(2):
        centre = own[layer]
        here = slice(layer * 8, layer * 8 + 8)
        top = jnp.where(lower, rhalo[1, here, :], rhalo[0, here, :])
        bottom = jnp.where(lower, rhalo[0, here, :], rhalo[1, here, :])
        tops = [jnp.broadcast_to(top[k : k + 1], (ROWS, 128)) for k in range(8)]
        bottoms = [jnp.broadcast_to(bottom[k : k + 1], (ROWS, 128)) for k in range(8)]
        beside = jnp.where(row_id == 0, jnp.concatenate(tops, axis=1), jnp.concatenate(bottoms, axis=1))
        outer_rows = (row_id == 0) | (row_id == ROWS - 1)
        bend = flux(zhalo[layer] - centre) + jnp.where(outer_rows, flux(beside - centre), 0.0)
        density = part_density[layer] + bend_weight * bend
        even.append(density[:, :HALF] + density[:, HALF:])
        odd.append((density[:, :HALF] - density[:, HALF:]) * alternating((ROWS, HALF)))

    block = jnp.where(lower, PLAN // 2 - 1 - p, p - PLAN // 2)
    parity = lax.rem(d, 2)
    mate = d + 1 - 2 * parity
    hear(2, 1)
    hear(1, 2)
    tell(3, [(mate, p)])
    for copy in wide_copies:
        copy.wait()

    def send_coef(group, k, cross):
        member = 1 - parity if cross else parity
        return pltpu.make_async_remote_copy(
            src_ref=csend.at[2 * (8 * group + turns[k]) + member], dst_ref=sbuf.at[GROUP * cross + block],
            send_sem=cs, recv_sem=cr.at[cross],
            device_id=(mate if cross else d, 8 * (group // 2) + places[group % 2][k]), device_id_type=MESH,
        )

    both = pair(jnp.concatenate(even + odd, axis=0))
    for cut in range(2):
        cols = slice(HALF * cut, HALF * (cut + 1))
        coef = table_right(both, wide[0, :, cols], wide[1, :, cols])
        for kind in range(2):
            start = kind * 16 + 8 * cut
            for m in range(4):
                lanes = slice(128 * m, 128 * (m + 1))
                starts = [2 * ROWS * kind + ROWS * layer + 8 * half for half in range(2) for layer in range(2)]
                for t, value in enumerate(regroup([coef[n : n + 8, lanes] for n in starts])):
                    csend[2 * start + 4 * m + t] = value
        for k in range(7):
            for kind in range(2):
                send_coef(2 * kind + cut, k, 0).start()
    for group in range(4):
        pl.when(group != set_own)(send_coef(group, 7, 0).start)
    hear(3, 1)
    tell(4, z_pair(2))
    for k in range(8):
        for group in range(4):
            send_coef(group, k, 1).start()

    def respond(start, cross):
        row = lax.broadcasted_iota(jnp.int32, (128, 128), 0)
        col = lax.broadcasted_iota(jnp.int32, (128, 128), 1) + start
        place = lax.rem(coef_block, GROUP // 2) * COEF + parity * SHARE + lax.rem(row, SHARE)
        v = jnp.where(kind_own == 1, NX - place, place).astype(F32)
        scale = 2.0 * math.pi * grav_scale * thickness / (4.0 * NX * NX)
        weight = jnp.where(place == 0, scale, 2.0 * scale) * jnp.where(col == 0, 1.0, 2.0)
        layer = (2 * (mate if cross else d) + lax.rem(lax.div(row, SHARE), 2)).astype(F32)
        rate = (top_depth + (layer + 0.5) * thickness) * (-2.0 * math.pi / (2 * NX))
        u = jnp.where(row >= 64, NX - col, col).astype(F32)
        return jnp.exp(jnp.sqrt(u * u + v * v) * rate) * weight

    for cross in range(2):
        for k in range(NX // 128):
            rsp[cross, :, 128 * k : 128 * (k + 1)] = respond(128 * k, cross)

    hear(4, 2)
    tell(5, z_pair(4))
    sbuf[block] = csend[2 * coef_block + parity]
    for copy in mixed_copies + tall_copies:
        copy.wait()
    side = lax.rem(lax.div(lax.broadcasted_iota(jnp.int32, (64, HALF), 1), 16), 2)
    sign = jnp.where(side == zh, 1.0, -1.0) * alternating((64, HALF))
    step = 256
    for cross in range(2):
        landed = sbuf.at[pl.ds(GROUP * cross, GROUP - 1 + cross)]
        pltpu.make_async_copy(landed, landed, cr.at[cross]).wait()
        value = sbuf[GROUP * cross : GROUP * (cross + 1)].reshape(HALF // 2, 128).T
        value = jnp.concatenate([value[:64], value[64:]], axis=1)
        both = pair(jnp.concatenate([value, value * sign], axis=0))
        for k in range(NX // step):
            here = slice(k * step, (k + 1) * step)
            coef = table_right(both, mixed[0, :, here], mixed[1, :, here]) * rsp[cross, :, here]
            parts = [coef[SHARE * n : SHARE * (n + 1)] for n in range(4)]
            coef = jnp.concatenate([parts[0] + parts[1], parts[2] + parts[3]], axis=0)
            if cross:
                pst[:, here] = pair(coef + acc[:, here])
            else:
                acc[:, here] = coef

    low = 2 * lax.rem(y, 2) + core
    x_turns = [lax.rem(x + k, 4) for k in range(4)]
    low_turns = [lax.rem(low + k, 4) for k in range(4)]
    low_places = [4 * lax.div(t, 2) + lax.rem(t, 2) + 2 * zh for t in low_turns]

    def send_rows(part, r, k, cross):
        upper = lax.div(x_turns[r], 2)
        upper = upper if part else 1 - upper
        member = 1 - parity if cross else parity
        return pltpu.make_async_remote_copy(
            src_ref=xsend.at[2 * (8 * x_turns[r] + 4 * upper + low_turns[k]) + member],
            dst_ref=cbuf.at[2 * coef_block + parity], send_sem=xs, recv_sem=xr,
            device_id=(mate if cross else d, 16 * x_turns[r] + 8 * upper + low_places[k]), device_id_type=MESH,
        )

    lane = lax.broadcasted_iota(jnp.int32, (8, 128), 1)
    early, even_lane = lane < 64, lax.rem(lane, 64) < 32
    def columns(part):
        cols = slice(128 * part, 128 * part + 128), slice(128 * part + 256, 128 * part + 384)
        return [jnp.concatenate([tall[n, :, col] for col in cols], axis=1) for n in range(2)]

    for part in range(2):
        value = table_right(pst[...], *columns(part))
        evens, odds = value[:SHARE], value[SHARE:] * alternating((SHARE, 256))
        plus, minus = evens + odds, evens - odds
        value = jnp.concatenate([plus, minus, plus, minus], axis=0).T
        for g in range(4):
            chunk = 2 * part + 4 * (g // 2) + g % 2
            for member in range(2):
                ups, downs = [], []
                for n in range(4):
                    start = ROWS * (4 * g + n) + 8 * member
                    rows = value[start : start + 8]
                    later = pltpu.roll(rows, 4, 0)
                    ups.append(jnp.where(even_lane, rows, pltpu.roll(later, 32, 1)))
                    downs.append(jnp.where(even_lane, pltpu.roll(rows, 32, 1), later))
                for spot, one, two in (
                    (2 * (8 + chunk), ups[0], ups[2]),
                    (2 * (8 + chunk) + 1, ups[1], ups[3]),
                    (2 * (7 - chunk), downs[3], downs[1]),
                    (2 * (7 - chunk) + 1, downs[2], downs[0]),
                ):
                    xsend[2 * spot + member] = jnp.where(early, one, two)[:4]

        for r in (1, 3, 2, 0):
            for k in range(4):
                send_rows(part, r, k, 1).start()
                if r or k:
                    send_rows(part, r, k, 0).start()
    upper_own = lax.rem(lax.div(x, 2) + lax.div(y, 2), 2)
    pl.when(upper_own == 0)(send_rows(0, 0, 0, 0).start)
    pl.when(upper_own == 1)(send_rows(1, 0, 0, 0).start)

    hear(5, 2)
    cbuf[2 * coef_block + parity] = xsend[2 * q + parity]
    landed = cbuf.at[pl.ds(0, 2 * GROUP - 1)]
    pltpu.make_async_copy(landed, landed, xr).wait()

    def send_field(far, depth):
        row = 1 - zh if far else zh
        return pltpu.make_async_remote_copy(
            src_ref=gsend.at[DEPTH * row + depth], dst_ref=gbuf.at[z], send_sem=gs, recv_sem=gr,
            device_id=(depth, p + 2 - 4 * zh if far else p), device_id_type=MESH,
        )

    steps = [lax.rem(lax.div(d, 2) + k, 4) for k in range(4)]
    depths = ([2 * t + 1 - lax.div(t, 2) for t in steps], [2 * t + lax.div(t, 2) for t in steps])

    for m in range(2 * NX // 128):
        parts = regroup([cbuf[4 * m + t] for t in range(4)])
        lanes = slice(128 * (m % 8), 128 * (m % 8 + 1))
        for g in range(4):
            start = ROWS * (m // 8) + 4 * g
            coefs[start : start + 4, lanes] = parts[g]
    both = pair(coefs[...])
    for cut in range(2):
        value = table_right(both, *columns(cut))
        evens, odds = value[:ROWS], value[ROWS:] * alternating((ROWS, 256))
        plus = evens + odds
        minus = evens - odds
        for half in range(2):
            rows = slice(8 * half, 8 * (half + 1))
            for n in range(2):
                lanes = slice(128 * n, 128 * (n + 1))
                gsend[DEPTH * half + 4 + cut + 2 * n] = plus[rows, lanes]
                gsend[DEPTH * half + 3 - cut - 2 * n] = minus[rows, lanes]
        for k in range(4):
            send_field(True, depths[cut][k]).start()
        for k in range(1, 4):
            send_field(False, depths[cut][k]).start()
    for cut in range(2):
        pl.when(depths[cut][0] != d)(send_field(False, depths[cut][0]).start)

    gbuf[z] = gsend[z]
    pltpu.make_async_copy(gbuf.at[pl.ds(0, RING - 1)], gbuf.at[pl.ds(0, RING - 1)], gr).wait()
    totals = [gbuf[0], gbuf[1]]
    for other in range(2, RING):
        totals[other % 2] = totals[other % 2] + gbuf[other]
    total = jnp.concatenate(totals, axis=0)
    across = lax.broadcasted_iota(jnp.int32, (128, 128), 0) + lax.broadcasted_iota(jnp.int32, (128, 128), 1)
    reverse = jnp.where(across == 127, 1.0, 0.0).astype(BF16)
    high, rest = split(total)
    low = (total - high.astype(F32) - rest.astype(F32)).astype(BF16)
    turned = matmul(jnp.concatenate([high, rest, low], axis=0), reverse)
    turned = turned[:ROWS] + turned[ROWS : 2 * ROWS] + turned[2 * ROWS :]
    total = jnp.where(d < DEPTH // 2, turned, total)

    @pl.when(lower)
    def _():
        for row in range(ROWS):
            out_ref[ROWS - 1 - row : ROWS - row, :] = total[row : row + 1]

    @pl.when(jnp.logical_not(lower))
    def _():
        out_ref[...] = total

    for copy, there in zip(copies, has):
        pl.when(there)(copy.wait_send)
    pltpu.make_async_copy(csend.at[pl.ds(0, 2 * GROUP - 1)], csend.at[pl.ds(0, 2 * GROUP - 1)], cs).wait()
    pltpu.make_async_copy(xsend.at[pl.ds(0, 2 * GROUP - 1)], xsend.at[pl.ds(0, 2 * GROUP - 1)], xs).wait()
    pltpu.make_async_copy(gsend.at[pl.ds(0, RING - 1)], gsend.at[pl.ds(0, RING - 1)], gs).wait()


def solution(mesh):
    wide, mixed, tall = basis()

    def step(level_set, contrast):
        vmem = pl.BlockSpec(memory_space=pltpu.VMEM)
        anywhere = pl.BlockSpec(memory_space=pl.ANY)
        dma = pltpu.SemaphoreType.DMA
        return pl.pallas_call(
            kernel,
            out_shape=jax.ShapeDtypeStruct((ROWS, 128), F32),
            in_specs=[anywhere] * 5,
            out_specs=vmem,
            scratch_shapes=[
                pltpu.VMEM((2, ROWS, NX), F32),
                pltpu.SMEM((2,), F32),
                pltpu.VMEM((2, ROWS, NX), F32),
                pltpu.VMEM((2, ROWS, NX), F32),
                pltpu.VMEM((2, HALF, NX), BF16),
                pltpu.VMEM((2, HALF, NX), BF16),
                pltpu.VMEM((2, NX, HALF), BF16),
                pltpu.VMEM((2, ROWS, NX), F32),
                pltpu.VMEM((2, 16, 128), F32),
                pltpu.VMEM((2, 16, 128), F32),
                pltpu.VMEM((2 * GROUP, 8, 128), F32),
                pltpu.VMEM((2 * GROUP, 8, 128), F32),
                pltpu.VMEM((2, 128, NX), F32),
                pltpu.VMEM((64, NX), F32),
                pltpu.VMEM((128, NX), BF16),
                pltpu.VMEM((2 * GROUP, 4, 128), F32),
                pltpu.VMEM((2 * GROUP, 4, 128), F32),
                pltpu.VMEM((2 * ROWS, NX), F32),
                pltpu.VMEM((RING, 8, 128), F32),
                pltpu.VMEM((RING, 8, 128), F32),
                dma(()), dma(()), dma((2,)), dma((2,)), dma((2,)), dma((4,)), dma((4,)),
                dma(()), dma((2,)), dma(()), dma(()), dma(()), dma(()), pltpu.SemaphoreType.REGULAR((6,)),
            ],
            compiler_params=pltpu.CompilerParams(
                collective_id=0, has_side_effects=True, vmem_limit_bytes=63 * 1024 * 1024
            ),
        )(level_set, contrast, jnp.asarray(wide), jnp.asarray(mixed), jnp.asarray(tall))

    return jax.shard_map(
        step,
        mesh=mesh,
        in_specs=(P("depth", "plan", None), P("depth")),
        out_specs=P("plan", "depth"),
        check_vma=False,
    )
```

```python
import functools
import math

import jax
import jax.numpy as jnp
import ml_dtypes
import numpy as np
from jax import lax
from jax.experimental import pallas as pl
from jax.experimental.pallas import tpu as pltpu
from jax.sharding import PartitionSpec as P

MESH = pl.DeviceIdType.MESH
F32 = jnp.float32
BF16 = jnp.bfloat16

NX = 1024
HALF = NX // 2
LAYERS = 16
DEPTH = 8
PLAN = 64
ROWS = NX // PLAN
GROUP = 32
RING = 16
COEF = 2 * NX // GROUP
SHARE = COEF // 2

bend_weight = 0.5
grav_scale = 0.05
top_depth = 0.0
thickness = 1.0


def basis():
    j = np.arange(HALF, dtype=np.float64)[:, None] + 0.5
    v = np.arange(NX, dtype=np.float64)[None, :]
    table = np.cos(np.pi * v * j / NX)
    high = table.astype(ml_dtypes.bfloat16)
    low = (table - high.astype(np.float64)).astype(ml_dtypes.bfloat16)
    wide = np.stack([high, low])
    order = np.arange(HALF).reshape(GROUP, 2, ROWS // 2).transpose(1, 0, 2).reshape(-1)
    return wide, np.ascontiguousarray(wide[:, order]), np.ascontiguousarray(np.swapaxes(wide, 1, 2))


def alternating(shape):
    return 1.0 - 2.0 * lax.rem(lax.broadcasted_iota(jnp.int32, shape, 1), 2).astype(F32)


def flux(step):
    return step * lax.rsqrt(1.0 + step * step)


def flip(value, axis, size):
    index = lax.broadcasted_iota(jnp.int32, value.shape, axis)
    step = size // 2
    value = pltpu.roll(value, step, axis)
    while step > 1:
        step //= 2
        up = pltpu.roll(value, step, axis)
        down = pltpu.roll(value, size - step, axis)
        value = jnp.where((index & step) != 0, up, down)
    return value


def flip_lanes(value):
    blocks = value.shape[1] // 128
    parts = [flip(value[:, 128 * k : 128 * (k + 1)], 1, 128) for k in reversed(range(blocks))]
    return jnp.concatenate(parts, axis=1) if blocks > 1 else parts[0]


def split(value):
    high = value.astype(BF16)
    low = (value - high.astype(F32)).astype(BF16)
    return high, low


def matmul(a, b):
    return jnp.dot(a, b, preferred_element_type=F32)


def pair(value):
    return jnp.concatenate(split(value), axis=0)


def table_right(both, high_table, low_table):
    n = both.shape[0] // 2
    product = matmul(both, high_table)
    return product[:n] + product[n:] + matmul(both[:n], low_table)


def regroup(parts):
    lane = lax.broadcasted_iota(jnp.int32, parts[0].shape, 1)
    early, even = lane < 64, lax.rem(lane, 64) < 32
    wide = [jnp.where(early, parts[g], pltpu.roll(parts[g + 2], 64, 1)) for g in range(2)]
    wide += [jnp.where(early, pltpu.roll(parts[g], 64, 1), parts[g + 2]) for g in range(2)]
    out = []
    for first, second in (wide[:2], wide[2:]):
        out.append(jnp.where(even, first, pltpu.roll(second, 32, 1)))
        out.append(jnp.where(even, pltpu.roll(first, 96, 1), second))
    return out


def kernel(
    ls_hbm, con_hbm, wide_hbm, mixed_hbm, tall_hbm, out_ref,
    ls_ref, con_ref, own, part_density, wide, mixed, tall, zhalo, rsend, rhalo, csend, sbuf, rsp, acc, pst, xsend, cbuf, coefs, gsend, gbuf,
    ls_sem, con_sem, wide_sem, mixed_sem, tall_sem, hs, hr, cs, cr, xs, xr, gs, gr, news,
):
    d = lax.axis_index("depth")
    p = lax.axis_index("plan")
    core = lax.rem(p, 2)
    zh = lax.rem(lax.div(p, 2), 2)
    q = lax.div(p, 4) * 2 + core
    z = zh * DEPTH + d
    lower = p < PLAN // 2

    x, y = lax.div(p, 16), lax.rem(lax.div(p, 4), 4)
    kind_own, cut_own = lax.div(y, 2), lax.rem(x + y, 2)
    set_own = 2 * kind_own + cut_own
    coef_block = 8 * set_own + 2 * x + core
    parity = lax.rem(d, 2)
    mate = d + 1 - 2 * parity
    order = (2, 6, 4, 3, 7, 5, 1, 0)
    turns = [lax.rem(2 * x + core + k, 8) for k in order]
    places = [
        [16 * lax.div(t, 2) + 4 * lax.rem(lax.div(t, 2) + cut, 2) + 2 * zh + lax.rem(t, 2) for t in turns]
        for cut in range(2)
    ]

    def at_z(other):
        return (lax.rem(other, DEPTH), p + 2 * (lax.div(other, DEPTH) - zh))

    ls_copy = pltpu.make_async_copy(ls_hbm, ls_ref, ls_sem)
    con_copy = pltpu.make_async_copy(con_hbm, con_ref, con_sem)
    ls_copy.start()
    con_copy.start()
    wide_copies = [pltpu.make_async_copy(wide_hbm.at[n], wide.at[n], wide_sem.at[n]) for n in range(2)]
    mixed_copies = [pltpu.make_async_copy(mixed_hbm.at[n], mixed.at[n], mixed_sem.at[n]) for n in range(2)]
    tall_copies = [pltpu.make_async_copy(tall_hbm.at[n], tall.at[n], tall_sem.at[n]) for n in range(2)]
    for copy in wide_copies:
        copy.start()

    barrier = pltpu.get_barrier_semaphore()

    def greet(target):
        pl.semaphore_signal(barrier, inc=1, device_id=target, device_id_type=MESH)

    has = (d < DEPTH - 1, d > 0, p < PLAN - 1, p > 0)
    gets = (d > 0, d < DEPTH - 1, p > 0, p < PLAN - 1)
    outer = jnp.where(core == 0, p - 1, p + 1)
    has_outer = (outer >= 0) & (outer < PLAN)
    x_line = [(d, p + 16 * (lax.rem(x + k, 4) - x)) for k in (1, 3, 2)]
    y_line = [(d, p + 4 * (lax.rem(y + k, 4) - y)) for k in (1, 3, 2)]
    buddy = (d, p + 1 - 2 * core)

    def z_pair(k):
        return [at_z(lax.rem(z + away, RING)) for away in (k, RING - k)]

    for target in z_pair(1) + [buddy]:
        greet(target)
    pl.when(has_outer)(lambda: greet((d, outer)))
    for target in x_line + y_line:
        greet(target)

    def tell(number, targets):
        for target in targets:
            pl.semaphore_signal(news.at[number], inc=1, device_id=target, device_id_type=MESH)

    def hear(number, count):
        pl.semaphore_wait(news.at[number], count)

    ls_copy.wait()
    con_copy.wait()

    for layer in range(2):
        value = ls_ref[layer]
        value = jnp.where(lower, flip(value, 0, ROWS), value)
        own[layer, :, :HALF] = value[:, HALF:]
        own[layer, :, HALF:] = flip_lanes(value[:, :HALF])

    for layer in range(2):
        for k in range(8):
            spot = layer * 8 + k
            top = own[layer, 0:1, 128 * k : 128 * (k + 1)]
            bottom = own[layer, ROWS - 1 : ROWS, 128 * k : 128 * (k + 1)]
            rsend[0, spot : spot + 1, :] = jnp.where(lower, bottom, top)
            rsend[1, spot : spot + 1, :] = jnp.where(lower, top, bottom)

    pl.semaphore_wait(barrier, 9 + has_outer.astype(jnp.int32))

    def halo(source, target, number, device):
        return pltpu.make_async_remote_copy(
            src_ref=source, dst_ref=target, send_sem=hs.at[number], recv_sem=hr.at[number],
            device_id=device, device_id_type=MESH,
        )

    z_up = halo(own.at[1], zhalo.at[0], 0, (d + 1, p))
    z_down = halo(own.at[0], zhalo.at[1], 1, (d - 1, p))
    r_up = halo(rsend.at[1], rhalo.at[0], 2, (d, p + 1))
    r_down = halo(rsend.at[0], rhalo.at[1], 3, (d, p - 1))
    lands = (zhalo.at[0], zhalo.at[1], rhalo.at[0], rhalo.at[1])
    copies = (z_up, z_down, r_up, r_down)
    for copy, there in zip(copies, has):
        pl.when(there)(copy.start)
    tell(0, y_line)
    tell(1, z_pair(1))
    for copy in mixed_copies + tall_copies:
        copy.start()
    for land, comes in zip(lands, gets):

        @pl.when(jnp.logical_not(comes))
        def _(land=land):
            land[...] = jnp.zeros(land.shape, F32)

    row_id = lax.broadcasted_iota(jnp.int32, (ROWS, NX), 0)
    lane_id = lax.broadcasted_iota(jnp.int32, (ROWS, HALF), 1)
    field = [own[0], own[1]]
    middle = flux(field[1] - field[0])
    for layer in range(2):
        centre = field[layer]
        bend = -middle if layer else middle
        inner_flux = flux(pltpu.roll(centre, 1, 0) - centre)
        bend = bend + jnp.where(row_id == 0, 0.0, inner_flux)
        bend = bend - jnp.where(row_id == ROWS - 1, 0.0, pltpu.roll(inner_flux, ROWS - 1, 0))
        sides = centre[:, :HALF], centre[:, HALF:]
        across = []
        for side in range(2):
            here = sides[side]
            inside = jnp.where(lane_id == 0, sides[1 - side], pltpu.roll(here, 1, 1))
            inner_flux = flux(inside - here)
            outside = jnp.where(lane_id == HALF - 1, flux(here), pltpu.roll(inner_flux, HALF - 1, 1))
            across.append(inner_flux - outside)
        bend = bend + jnp.concatenate(across, axis=1)
        part_density[layer] = con_ref[layer] * (0.5 * (1.0 + jnp.tanh(centre))) + bend_weight * bend

    hear(0, 3)
    tell(2, [buddy])

    def respond(start, cross):
        row = lax.broadcasted_iota(jnp.int32, (128, 128), 0)
        col = lax.broadcasted_iota(jnp.int32, (128, 128), 1) + start
        place = lax.rem(coef_block, GROUP // 2) * COEF + parity * SHARE + lax.rem(row, SHARE)
        v = jnp.where(kind_own == 1, NX - place, place).astype(F32)
        scale = 2.0 * math.pi * grav_scale * thickness / (4.0 * NX * NX)
        weight = jnp.where(place == 0, scale, 2.0 * scale) * jnp.where(col == 0, 1.0, 2.0)
        layer = (2 * (mate if cross else d) + lax.rem(lax.div(row, SHARE), 2)).astype(F32)
        rate = (top_depth + (layer + 0.5) * thickness) * (-2.0 * math.pi / (2 * NX))
        u = jnp.where(row >= 64, NX - col, col).astype(F32)
        return jnp.exp(jnp.sqrt(u * u + v * v) * rate) * weight

    for cross in range(2):
        for k in range(NX // 128):
            rsp[cross, :, 128 * k : 128 * (k + 1)] = respond(128 * k, cross)

    for copy, comes in zip(copies, gets):
        pl.when(comes)(copy.wait_recv)
    even, odd = [], []
    for layer in range(2):
        centre = own[layer]
        here = slice(layer * 8, layer * 8 + 8)
        top = jnp.where(lower, rhalo[1, here, :], rhalo[0, here, :])
        bottom = jnp.where(lower, rhalo[0, here, :], rhalo[1, here, :])
        tops = [jnp.broadcast_to(top[k : k + 1], (ROWS, 128)) for k in range(8)]
        bottoms = [jnp.broadcast_to(bottom[k : k + 1], (ROWS, 128)) for k in range(8)]
        beside = jnp.where(row_id == 0, jnp.concatenate(tops, axis=1), jnp.concatenate(bottoms, axis=1))
        outer_rows = (row_id == 0) | (row_id == ROWS - 1)
        bend = flux(zhalo[layer] - centre) + jnp.where(outer_rows, flux(beside - centre), 0.0)
        density = part_density[layer] + bend_weight * bend
        even.append(density[:, :HALF] + density[:, HALF:])
        odd.append((density[:, :HALF] - density[:, HALF:]) * alternating((ROWS, HALF)))

    block = jnp.where(lower, PLAN // 2 - 1 - p, p - PLAN // 2)
    hear(2, 1)
    hear(1, 2)
    tell(3, [(mate, p)])
    for copy in wide_copies:
        copy.wait()

    def send_coef(group, k, cross):
        member = 1 - parity if cross else parity
        return pltpu.make_async_remote_copy(
            src_ref=csend.at[2 * (8 * group + turns[k]) + member], dst_ref=sbuf.at[GROUP * cross + block],
            send_sem=cs, recv_sem=cr.at[cross],
            device_id=(mate if cross else d, 8 * (group // 2) + places[group % 2][k]), device_id_type=MESH,
        )

    both = pair(jnp.concatenate(even + odd, axis=0))
    for cut in range(2):
        cols = slice(HALF * cut, HALF * (cut + 1))
        coef = table_right(both, wide[0, :, cols], wide[1, :, cols])
        for kind in range(2):
            start = kind * 16 + 8 * cut
            for m in range(4):
                lanes = slice(128 * m, 128 * (m + 1))
                starts = [2 * ROWS * kind + ROWS * layer + 8 * half for half in range(2) for layer in range(2)]
                for t, value in enumerate(regroup([coef[n : n + 8, lanes] for n in starts])):
                    csend[2 * start + 4 * m + t] = value
        for k in range(7):
            for kind in range(2):
                send_coef(2 * kind + cut, k, 0).start()
    for group in range(4):
        pl.when(group != set_own)(send_coef(group, 7, 0).start)
    hear(3, 1)
    tell(4, z_pair(2))
    for k in range(8):
        for group in range(4):
            send_coef(group, k, 1).start()

    hear(4, 2)
    tell(5, z_pair(4))
    sbuf[block] = csend[2 * coef_block + parity]
    for copy in mixed_copies + tall_copies:
        copy.wait()
    side = lax.rem(lax.div(lax.broadcasted_iota(jnp.int32, (64, HALF), 1), 16), 2)
    sign = jnp.where(side == zh, 1.0, -1.0) * alternating((64, HALF))
    step = 256
    for cross in range(2):
        landed = sbuf.at[pl.ds(GROUP * cross, GROUP - 1 + cross)]
        pltpu.make_async_copy(landed, landed, cr.at[cross]).wait()
        value = sbuf[GROUP * cross : GROUP * (cross + 1)].reshape(HALF // 2, 128).T
        value = jnp.concatenate([value[:64], value[64:]], axis=1)
        both = pair(jnp.concatenate([value, value * sign], axis=0))
        for k in range(NX // step):
            here = slice(k * step, (k + 1) * step)
            coef = table_right(both, mixed[0, :, here], mixed[1, :, here]) * rsp[cross, :, here]
            parts = [coef[SHARE * n : SHARE * (n + 1)] for n in range(4)]
            coef = jnp.concatenate([parts[0] + parts[1], parts[2] + parts[3]], axis=0)
            if cross:
                pst[:, here] = pair(coef + acc[:, here])
            else:
                acc[:, here] = coef

    low = 2 * lax.rem(y, 2) + core
    x_turns = [lax.rem(x + k, 4) for k in range(4)]
    low_turns = [lax.rem(low + k, 4) for k in range(4)]
    low_places = [4 * lax.div(t, 2) + lax.rem(t, 2) + 2 * zh for t in low_turns]

    def send_rows(part, r, k, cross):
        upper = lax.div(x_turns[r], 2)
        upper = upper if part else 1 - upper
        member = 1 - parity if cross else parity
        return pltpu.make_async_remote_copy(
            src_ref=xsend.at[2 * (8 * x_turns[r] + 4 * upper + low_turns[k]) + member],
            dst_ref=cbuf.at[2 * coef_block + parity], send_sem=xs, recv_sem=xr,
            device_id=(mate if cross else d, 16 * x_turns[r] + 8 * upper + low_places[k]), device_id_type=MESH,
        )

    lane = lax.broadcasted_iota(jnp.int32, (8, 128), 1)
    early, even_lane = lane < 64, lax.rem(lane, 64) < 32
    def columns(part):
        cols = slice(128 * part, 128 * part + 128), slice(128 * part + 256, 128 * part + 384)
        return [jnp.concatenate([tall[n, :, col] for col in cols], axis=1) for n in range(2)]

    for part in range(2):
        value = table_right(pst[...], *columns(part))
        evens, odds = value[:SHARE], value[SHARE:] * alternating((SHARE, 256))
        plus, minus = evens + odds, evens - odds
        value = jnp.concatenate([plus, minus, plus, minus], axis=0).T
        for g in range(4):
            chunk = 2 * part + 4 * (g // 2) + g % 2
            for member in range(2):
                ups, downs = [], []
                for n in range(4):
                    start = ROWS * (4 * g + n) + 8 * member
                    rows = value[start : start + 8]
                    later = pltpu.roll(rows, 4, 0)
                    ups.append(jnp.where(even_lane, rows, pltpu.roll(later, 32, 1)))
                    downs.append(jnp.where(even_lane, pltpu.roll(rows, 32, 1), later))
                for spot, one, two in (
                    (2 * (8 + chunk), ups[0], ups[2]),
                    (2 * (8 + chunk) + 1, ups[1], ups[3]),
                    (2 * (7 - chunk), downs[3], downs[1]),
                    (2 * (7 - chunk) + 1, downs[2], downs[0]),
                ):
                    xsend[2 * spot + member] = jnp.where(early, one, two)[:4]

        for r in (1, 3, 2, 0):
            for k in range(4):
                send_rows(part, r, k, 1).start()
                if r or k:
                    send_rows(part, r, k, 0).start()
    upper_own = lax.rem(lax.div(x, 2) + lax.div(y, 2), 2)
    pl.when(upper_own == 0)(send_rows(0, 0, 0, 0).start)
    pl.when(upper_own == 1)(send_rows(1, 0, 0, 0).start)

    hear(5, 2)
    cbuf[2 * coef_block + parity] = xsend[2 * q + parity]
    landed = cbuf.at[pl.ds(0, 2 * GROUP - 1)]
    pltpu.make_async_copy(landed, landed, xr).wait()

    def send_field(far, depth):
        row = 1 - zh if far else zh
        return pltpu.make_async_remote_copy(
            src_ref=gsend.at[DEPTH * row + depth], dst_ref=gbuf.at[z], send_sem=gs, recv_sem=gr,
            device_id=(depth, p + 2 - 4 * zh if far else p), device_id_type=MESH,
        )

    steps = [lax.rem(lax.div(d, 2) + k, 4) for k in range(4)]
    depths = ([2 * t + 1 - lax.div(t, 2) for t in steps], [2 * t + lax.div(t, 2) for t in steps])

    for m in range(2 * NX // 128):
        parts = regroup([cbuf[4 * m + t] for t in range(4)])
        lanes = slice(128 * (m % 8), 128 * (m % 8 + 1))
        for g in range(4):
            start = ROWS * (m // 8) + 4 * g
            coefs[start : start + 4, lanes] = parts[g]
    both = pair(coefs[...])
    for cut in range(2):
        value = table_right(both, *columns(cut))
        evens, odds = value[:ROWS], value[ROWS:] * alternating((ROWS, 256))
        plus = evens + odds
        minus = evens - odds
        for half in range(2):
            rows = slice(8 * half, 8 * (half + 1))
            for n in range(2):
                lanes = slice(128 * n, 128 * (n + 1))
                gsend[DEPTH * half + 4 + cut + 2 * n] = plus[rows, lanes]
                gsend[DEPTH * half + 3 - cut - 2 * n] = minus[rows, lanes]
        for k in range(4):
            send_field(True, depths[cut][k]).start()
        for k in range(1, 4):
            send_field(False, depths[cut][k]).start()
    for cut in range(2):
        pl.when(depths[cut][0] != d)(send_field(False, depths[cut][0]).start)

    gbuf[z] = gsend[z]
    pltpu.make_async_copy(gbuf.at[pl.ds(0, RING - 1)], gbuf.at[pl.ds(0, RING - 1)], gr).wait()
    totals = [gbuf[0], gbuf[1]]
    for other in range(2, RING):
        totals[other % 2] = totals[other % 2] + gbuf[other]
    total = jnp.concatenate(totals, axis=0)
    across = lax.broadcasted_iota(jnp.int32, (128, 128), 0) + lax.broadcasted_iota(jnp.int32, (128, 128), 1)
    reverse = jnp.where(across == 127, 1.0, 0.0).astype(BF16)
    high, rest = split(total)
    low = (total - high.astype(F32) - rest.astype(F32)).astype(BF16)
    turned = matmul(jnp.concatenate([high, rest, low], axis=0), reverse)
    turned = turned[:ROWS] + turned[ROWS : 2 * ROWS] + turned[2 * ROWS :]
    total = jnp.where(d < DEPTH // 2, turned, total)

    @pl.when(lower)
    def _():
        for row in range(ROWS):
            out_ref[ROWS - 1 - row : ROWS - row, :] = total[row : row + 1]

    @pl.when(jnp.logical_not(lower))
    def _():
        out_ref[...] = total

    for copy, there in zip(copies, has):
        pl.when(there)(copy.wait_send)
    pltpu.make_async_copy(csend.at[pl.ds(0, 2 * GROUP - 1)], csend.at[pl.ds(0, 2 * GROUP - 1)], cs).wait()
    pltpu.make_async_copy(xsend.at[pl.ds(0, 2 * GROUP - 1)], xsend.at[pl.ds(0, 2 * GROUP - 1)], xs).wait()
    pltpu.make_async_copy(gsend.at[pl.ds(0, RING - 1)], gsend.at[pl.ds(0, RING - 1)], gs).wait()


def solution(mesh):
    wide, mixed, tall = basis()

    def step(level_set, contrast):
        vmem = pl.BlockSpec(memory_space=pltpu.VMEM)
        anywhere = pl.BlockSpec(memory_space=pl.ANY)
        dma = pltpu.SemaphoreType.DMA
        return pl.pallas_call(
            kernel,
            out_shape=jax.ShapeDtypeStruct((ROWS, 128), F32),
            in_specs=[anywhere] * 5,
            out_specs=vmem,
            scratch_shapes=[
                pltpu.VMEM((2, ROWS, NX), F32),
                pltpu.SMEM((2,), F32),
                pltpu.VMEM((2, ROWS, NX), F32),
                pltpu.VMEM((2, ROWS, NX), F32),
                pltpu.VMEM((2, HALF, NX), BF16),
                pltpu.VMEM((2, HALF, NX), BF16),
                pltpu.VMEM((2, NX, HALF), BF16),
                pltpu.VMEM((2, ROWS, NX), F32),
                pltpu.VMEM((2, 16, 128), F32),
                pltpu.VMEM((2, 16, 128), F32),
                pltpu.VMEM((2 * GROUP, 8, 128), F32),
                pltpu.VMEM((2 * GROUP, 8, 128), F32),
                pltpu.VMEM((2, 128, NX), F32),
                pltpu.VMEM((64, NX), F32),
                pltpu.VMEM((128, NX), BF16),
                pltpu.VMEM((2 * GROUP, 4, 128), F32),
                pltpu.VMEM((2 * GROUP, 4, 128), F32),
                pltpu.VMEM((2 * ROWS, NX), F32),
                pltpu.VMEM((RING, 8, 128), F32),
                pltpu.VMEM((RING, 8, 128), F32),
                dma(()), dma(()), dma((2,)), dma((2,)), dma((2,)), dma((4,)), dma((4,)),
                dma(()), dma((2,)), dma(()), dma(()), dma(()), dma(()), pltpu.SemaphoreType.REGULAR((6,)),
            ],
            compiler_params=pltpu.CompilerParams(
                collective_id=0, has_side_effects=True, vmem_limit_bytes=55176 * 1024
            ),
        )(level_set, contrast, jnp.asarray(wide), jnp.asarray(mixed), jnp.asarray(tall))

    return jax.shard_map(
        step,
        mesh=mesh,
        in_specs=(P("depth", "plan", None), P("depth")),
        out_specs=P("plan", "depth"),
        check_vma=False,
    )
```

```python
import functools
import math

import jax
import jax.numpy as jnp
import ml_dtypes
import numpy as np
from jax import lax
from jax.experimental import pallas as pl
from jax.experimental.pallas import tpu as pltpu
from jax.sharding import PartitionSpec as P

MESH = pl.DeviceIdType.MESH
F32 = jnp.float32
BF16 = jnp.bfloat16

NX = 1024
HALF = NX // 2
LAYERS = 16
DEPTH = 8
PLAN = 64
ROWS = NX // PLAN
GROUP = 32
RING = 16
COEF = 2 * NX // GROUP
SHARE = COEF // 2

bend_weight = 0.5
grav_scale = 0.05
top_depth = 0.0
thickness = 1.0


def basis():
    j = np.arange(HALF, dtype=np.float64)[:, None] + 0.5
    v = np.arange(NX, dtype=np.float64)[None, :]
    table = np.cos(np.pi * v * j / NX)
    high = table.astype(ml_dtypes.bfloat16)
    low = (table - high.astype(np.float64)).astype(ml_dtypes.bfloat16)
    wide = np.stack([high, low])
    order = np.arange(HALF).reshape(GROUP, 2, ROWS // 2).transpose(1, 0, 2).reshape(-1)
    return wide, np.ascontiguousarray(wide[:, order]), np.ascontiguousarray(np.swapaxes(wide, 1, 2))


def alternating(shape):
    return 1.0 - 2.0 * lax.rem(lax.broadcasted_iota(jnp.int32, shape, 1), 2).astype(F32)


def flux(step):
    return step * lax.rsqrt(1.0 + step * step)


def flip(value, axis, size):
    index = lax.broadcasted_iota(jnp.int32, value.shape, axis)
    step = size // 2
    value = pltpu.roll(value, step, axis)
    while step > 1:
        step //= 2
        up = pltpu.roll(value, step, axis)
        down = pltpu.roll(value, size - step, axis)
        value = jnp.where((index & step) != 0, up, down)
    return value


def flip_lanes(value):
    blocks = value.shape[1] // 128
    parts = [flip(value[:, 128 * k : 128 * (k + 1)], 1, 128) for k in reversed(range(blocks))]
    return jnp.concatenate(parts, axis=1) if blocks > 1 else parts[0]


def split(value):
    high = value.astype(BF16)
    low = (value - high.astype(F32)).astype(BF16)
    return high, low


def matmul(a, b):
    return jnp.dot(a, b, preferred_element_type=F32)


def pair(value):
    return jnp.concatenate(split(value), axis=0)


def table_right(both, high_table, low_table):
    n = both.shape[0] // 2
    product = matmul(both, high_table)
    return product[:n] + product[n:] + matmul(both[:n], low_table)


def regroup(parts):
    lane = lax.broadcasted_iota(jnp.int32, parts[0].shape, 1)
    early, even = lane < 64, lax.rem(lane, 64) < 32
    wide = [jnp.where(early, parts[g], pltpu.roll(parts[g + 2], 64, 1)) for g in range(2)]
    wide += [jnp.where(early, pltpu.roll(parts[g], 64, 1), parts[g + 2]) for g in range(2)]
    out = []
    for first, second in (wide[:2], wide[2:]):
        out.append(jnp.where(even, first, pltpu.roll(second, 32, 1)))
        out.append(jnp.where(even, pltpu.roll(first, 96, 1), second))
    return out


def kernel(
    ls_hbm, con_hbm, wide_hbm, mixed_hbm, tall_hbm, out_ref,
    ls_ref, con_ref, part_density, wide, mixed, tall, zhalo, rsend, rhalo, csend, sbuf, rsp, acc, pst, xsend, cbuf, coefs, gsend, gbuf,
    ls_sem, con_sem, wide_sem, mixed_sem, tall_sem, hs, hr, cs, cr, xs, xr, gs, gr, news,
):
    d = lax.axis_index("depth")
    p = lax.axis_index("plan")
    core = lax.rem(p, 2)
    zh = lax.rem(lax.div(p, 2), 2)
    q = lax.div(p, 4) * 2 + core
    z = zh * DEPTH + d
    lower = p < PLAN // 2

    x, y = lax.div(p, 16), lax.rem(lax.div(p, 4), 4)
    kind_own, cut_own = lax.div(y, 2), lax.rem(x + y, 2)
    set_own = 2 * kind_own + cut_own
    coef_block = 8 * set_own + 2 * x + core
    parity = lax.rem(d, 2)
    mate = d + 1 - 2 * parity
    order = (2, 6, 4, 3, 7, 5, 1, 0)
    turns = [lax.rem(2 * x + core + k, 8) for k in order]
    places = [
        [16 * lax.div(t, 2) + 4 * lax.rem(lax.div(t, 2) + cut, 2) + 2 * zh + lax.rem(t, 2) for t in turns]
        for cut in range(2)
    ]

    def at_z(other):
        return (lax.rem(other, DEPTH), p + 2 * (lax.div(other, DEPTH) - zh))

    ls_copy = pltpu.make_async_copy(ls_hbm, ls_ref, ls_sem)
    con_copy = pltpu.make_async_copy(con_hbm, con_ref, con_sem)
    ls_copy.start()
    con_copy.start()
    wide_copies = [pltpu.make_async_copy(wide_hbm.at[n], wide.at[n], wide_sem.at[n]) for n in range(2)]
    mixed_copies = [pltpu.make_async_copy(mixed_hbm.at[n], mixed.at[n], mixed_sem.at[n]) for n in range(2)]
    tall_copies = [pltpu.make_async_copy(tall_hbm.at[n], tall.at[n], tall_sem.at[n]) for n in range(2)]
    for copy in wide_copies:
        copy.start()

    barrier = pltpu.get_barrier_semaphore()

    def greet(target):
        pl.semaphore_signal(barrier, inc=1, device_id=target, device_id_type=MESH)

    has = (d < DEPTH - 1, d > 0, p < PLAN - 1, p > 0)
    gets = (d > 0, d < DEPTH - 1, p > 0, p < PLAN - 1)
    outer = jnp.where(core == 0, p - 1, p + 1)
    has_outer = (outer >= 0) & (outer < PLAN)
    x_line = [(d, p + 16 * (lax.rem(x + k, 4) - x)) for k in (1, 3, 2)]
    y_line = [(d, p + 4 * (lax.rem(y + k, 4) - y)) for k in (1, 3, 2)]
    buddy = (d, p + 1 - 2 * core)

    def z_pair(k):
        return [at_z(lax.rem(z + away, RING)) for away in (k, RING - k)]

    for target in z_pair(1) + [buddy]:
        greet(target)
    pl.when(has_outer)(lambda: greet((d, outer)))
    for target in x_line + y_line:
        greet(target)

    def tell(number, targets):
        for target in targets:
            pl.semaphore_signal(news.at[number], inc=1, device_id=target, device_id_type=MESH)

    def hear(number, count):
        pl.semaphore_wait(news.at[number], count)

    pl.semaphore_wait(barrier, 9 + has_outer.astype(jnp.int32))

    def halo(source, target, number, device):
        return pltpu.make_async_remote_copy(
            src_ref=source, dst_ref=target, send_sem=hs.at[number], recv_sem=hr.at[number],
            device_id=device, device_id_type=MESH,
        )

    z_up = halo(ls_hbm.at[1], zhalo.at[0], 0, (d + 1, p))
    z_down = halo(ls_hbm.at[0], zhalo.at[1], 1, (d - 1, p))
    r_up = halo(rsend.at[1], rhalo.at[0], 2, (d, p + 1))
    r_down = halo(rsend.at[0], rhalo.at[1], 3, (d, p - 1))
    lands = (zhalo.at[0], zhalo.at[1], rhalo.at[0], rhalo.at[1])
    copies = (z_up, z_down, r_up, r_down)
    for copy, there in zip(copies[:2], has[:2]):
        pl.when(there)(copy.start)
    tell(0, y_line)
    tell(1, z_pair(1))
    ls_copy.wait()
    for layer in range(2):
        for k in range(8):
            spot = layer * 8 + k
            lanes = slice(128 * k, 128 * (k + 1))
            rsend[0, spot : spot + 1, :] = ls_ref[layer, 0:1, lanes]
            rsend[1, spot : spot + 1, :] = ls_ref[layer, ROWS - 1 : ROWS, lanes]
    for copy, there in zip(copies[2:], has[2:]):
        pl.when(there)(copy.start)
    for copy in mixed_copies + tall_copies:
        copy.start()
    con_copy.wait()
    for land, comes in zip(lands, gets):

        @pl.when(jnp.logical_not(comes))
        def _(land=land):
            land[...] = jnp.zeros(land.shape, F32)

    row_id = lax.broadcasted_iota(jnp.int32, (ROWS, NX), 0)
    col_id = lax.broadcasted_iota(jnp.int32, (ROWS, NX), 1)
    field = [ls_ref[0], ls_ref[1]]
    middle = flux(field[1] - field[0])
    for layer in range(2):
        centre = field[layer]
        bend = -middle if layer else middle
        row_flux = flux(pltpu.roll(centre, 1, 0) - centre)
        bend = bend + jnp.where(row_id == 0, 0.0, row_flux)
        bend = bend - jnp.where(row_id == ROWS - 1, 0.0, pltpu.roll(row_flux, ROWS - 1, 0))
        col_flux = flux(jnp.where(col_id == 0, 0.0, pltpu.roll(centre, 1, 1)) - centre)
        bend = bend + col_flux - jnp.where(col_id == NX - 1, flux(centre), pltpu.roll(col_flux, NX - 1, 1))
        part_density[layer] = con_ref[layer] * (0.5 * (1.0 + jnp.tanh(centre))) + bend_weight * bend

    hear(0, 3)
    tell(2, [buddy])

    def respond(start, cross):
        row = lax.broadcasted_iota(jnp.int32, (128, 128), 0)
        col = lax.broadcasted_iota(jnp.int32, (128, 128), 1) + start
        place = lax.rem(coef_block, GROUP // 2) * COEF + parity * SHARE + lax.rem(row, SHARE)
        v = jnp.where(kind_own == 1, NX - place, place).astype(F32)
        scale = 2.0 * math.pi * grav_scale * thickness / (4.0 * NX * NX)
        weight = jnp.where(place == 0, scale, 2.0 * scale) * jnp.where(col == 0, 1.0, 2.0)
        layer = (2 * (mate if cross else d) + lax.rem(lax.div(row, SHARE), 2)).astype(F32)
        rate = (top_depth + (layer + 0.5) * thickness) * (-2.0 * math.pi / (2 * NX))
        u = jnp.where(row >= 64, NX - col, col).astype(F32)
        return jnp.exp(jnp.sqrt(u * u + v * v) * rate) * weight

    for cross in range(2):
        for k in range(NX // 128):
            rsp[cross, :, 128 * k : 128 * (k + 1)] = respond(128 * k, cross)

    for copy, comes in zip(copies, gets):
        pl.when(comes)(copy.wait_recv)
    even, odd = [], []
    for layer in range(2):
        centre = ls_ref[layer]
        here = slice(layer * 8, layer * 8 + 8)
        top, bottom = rhalo[0, here, :], rhalo[1, here, :]
        tops = [jnp.broadcast_to(top[k : k + 1], (ROWS, 128)) for k in range(8)]
        bottoms = [jnp.broadcast_to(bottom[k : k + 1], (ROWS, 128)) for k in range(8)]
        beside = jnp.where(row_id == 0, jnp.concatenate(tops, axis=1), jnp.concatenate(bottoms, axis=1))
        outer_rows = (row_id == 0) | (row_id == ROWS - 1)
        bend = flux(zhalo[layer] - centre) + jnp.where(outer_rows, flux(beside - centre), 0.0)
        density = part_density[layer] + bend_weight * bend
        density = jnp.where(lower, flip(density, 0, ROWS), density)
        left, right = flip_lanes(density[:, :HALF]), density[:, HALF:]
        even.append(right + left)
        odd.append((right - left) * alternating((ROWS, HALF)))

    block = jnp.where(lower, PLAN // 2 - 1 - p, p - PLAN // 2)
    hear(2, 1)
    hear(1, 2)
    tell(3, [(mate, p)])
    for copy in wide_copies:
        copy.wait()

    def send_coef(group, k, cross):
        member = 1 - parity if cross else parity
        return pltpu.make_async_remote_copy(
            src_ref=csend.at[2 * (8 * group + turns[k]) + member], dst_ref=sbuf.at[GROUP * cross + block],
            send_sem=cs, recv_sem=cr.at[cross],
            device_id=(mate if cross else d, 8 * (group // 2) + places[group % 2][k]), device_id_type=MESH,
        )

    both = pair(jnp.concatenate(even + odd, axis=0))
    for cut in range(2):
        cols = slice(HALF * cut, HALF * (cut + 1))
        coef = table_right(both, wide[0, :, cols], wide[1, :, cols])
        for kind in range(2):
            start = kind * 16 + 8 * cut
            for m in range(4):
                lanes = slice(128 * m, 128 * (m + 1))
                starts = [2 * ROWS * kind + ROWS * layer + 8 * half for half in range(2) for layer in range(2)]
                for t, value in enumerate(regroup([coef[n : n + 8, lanes] for n in starts])):
                    csend[2 * start + 4 * m + t] = value
        for k in range(7):
            for kind in range(2):
                send_coef(2 * kind + cut, k, 0).start()
    for group in range(4):
        pl.when(group != set_own)(send_coef(group, 7, 0).start)
    hear(3, 1)
    tell(4, z_pair(2))
    for k in range(8):
        for group in range(4):
            send_coef(group, k, 1).start()

    hear(4, 2)
    tell(5, z_pair(4))
    sbuf[block] = csend[2 * coef_block + parity]
    for copy in mixed_copies + tall_copies:
        copy.wait()
    side = lax.rem(lax.div(lax.broadcasted_iota(jnp.int32, (64, HALF), 1), 16), 2)
    sign = jnp.where(side == zh, 1.0, -1.0) * alternating((64, HALF))
    step = 256
    for cross in range(2):
        landed = sbuf.at[pl.ds(GROUP * cross, GROUP - 1 + cross)]
        pltpu.make_async_copy(landed, landed, cr.at[cross]).wait()
        value = sbuf[GROUP * cross : GROUP * (cross + 1)].reshape(HALF // 2, 128).T
        value = jnp.concatenate([value[:64], value[64:]], axis=1)
        both = pair(jnp.concatenate([value, value * sign], axis=0))
        for k in range(NX // step):
            here = slice(k * step, (k + 1) * step)
            coef = table_right(both, mixed[0, :, here], mixed[1, :, here]) * rsp[cross, :, here]
            parts = [coef[SHARE * n : SHARE * (n + 1)] for n in range(4)]
            coef = jnp.concatenate([parts[0] + parts[1], parts[2] + parts[3]], axis=0)
            if cross:
                pst[:, here] = pair(coef + acc[:, here])
            else:
                acc[:, here] = coef

    low = 2 * lax.rem(y, 2) + core
    x_turns = [lax.rem(x + k, 4) for k in range(4)]
    low_turns = [lax.rem(low + k, 4) for k in range(4)]
    low_places = [4 * lax.div(t, 2) + lax.rem(t, 2) + 2 * zh for t in low_turns]

    def send_rows(part, r, k, cross):
        upper = lax.div(x_turns[r], 2)
        upper = upper if part else 1 - upper
        member = 1 - parity if cross else parity
        return pltpu.make_async_remote_copy(
            src_ref=xsend.at[2 * (8 * x_turns[r] + 4 * upper + low_turns[k]) + member],
            dst_ref=cbuf.at[2 * coef_block + parity], send_sem=xs, recv_sem=xr,
            device_id=(mate if cross else d, 16 * x_turns[r] + 8 * upper + low_places[k]), device_id_type=MESH,
        )

    lane = lax.broadcasted_iota(jnp.int32, (8, 128), 1)
    early, even_lane = lane < 64, lax.rem(lane, 64) < 32
    def columns(part):
        cols = slice(128 * part, 128 * part + 128), slice(128 * part + 256, 128 * part + 384)
        return [jnp.concatenate([tall[n, :, col] for col in cols], axis=1) for n in range(2)]

    for part in range(2):
        value = table_right(pst[...], *columns(part))
        evens, odds = value[:SHARE], value[SHARE:] * alternating((SHARE, 256))
        plus, minus = evens + odds, evens - odds
        value = jnp.concatenate([plus, minus, plus, minus], axis=0).T
        for g in range(4):
            chunk = 2 * part + 4 * (g // 2) + g % 2
            for member in range(2):
                ups, downs = [], []
                for n in range(4):
                    start = ROWS * (4 * g + n) + 8 * member
                    rows = value[start : start + 8]
                    later = pltpu.roll(rows, 4, 0)
                    ups.append(jnp.where(even_lane, rows, pltpu.roll(later, 32, 1)))
                    downs.append(jnp.where(even_lane, pltpu.roll(rows, 32, 1), later))
                for spot, one, two in (
                    (2 * (8 + chunk), ups[0], ups[2]),
                    (2 * (8 + chunk) + 1, ups[1], ups[3]),
                    (2 * (7 - chunk), downs[3], downs[1]),
                    (2 * (7 - chunk) + 1, downs[2], downs[0]),
                ):
                    xsend[2 * spot + member] = jnp.where(early, one, two)[:4]

        for r in (1, 3, 2, 0):
            for k in range(4):
                send_rows(part, r, k, 1).start()
                if r or k:
                    send_rows(part, r, k, 0).start()
    upper_own = lax.rem(lax.div(x, 2) + lax.div(y, 2), 2)
    pl.when(upper_own == 0)(send_rows(0, 0, 0, 0).start)
    pl.when(upper_own == 1)(send_rows(1, 0, 0, 0).start)

    hear(5, 2)
    cbuf[2 * coef_block + parity] = xsend[2 * q + parity]
    landed = cbuf.at[pl.ds(0, 2 * GROUP - 1)]
    pltpu.make_async_copy(landed, landed, xr).wait()

    def send_field(far, depth):
        row = 1 - zh if far else zh
        return pltpu.make_async_remote_copy(
            src_ref=gsend.at[DEPTH * row + depth], dst_ref=gbuf.at[z], send_sem=gs, recv_sem=gr,
            device_id=(depth, p + 2 - 4 * zh if far else p), device_id_type=MESH,
        )

    steps = [lax.rem(lax.div(d, 2) + k, 4) for k in range(4)]
    depths = ([2 * t + 1 - lax.div(t, 2) for t in steps], [2 * t + lax.div(t, 2) for t in steps])

    for m in range(2 * NX // 128):
        parts = regroup([cbuf[4 * m + t] for t in range(4)])
        lanes = slice(128 * (m % 8), 128 * (m % 8 + 1))
        for g in range(4):
            start = ROWS * (m // 8) + 4 * g
            coefs[start : start + 4, lanes] = parts[g]
    both = pair(coefs[...])
    for cut in range(2):
        value = table_right(both, *columns(cut))
        evens, odds = value[:ROWS], value[ROWS:] * alternating((ROWS, 256))
        plus = evens + odds
        minus = evens - odds
        for half in range(2):
            rows = slice(8 * half, 8 * (half + 1))
            for n in range(2):
                lanes = slice(128 * n, 128 * (n + 1))
                gsend[DEPTH * half + 4 + cut + 2 * n] = plus[rows, lanes]
                gsend[DEPTH * half + 3 - cut - 2 * n] = minus[rows, lanes]
        for k in range(4):
            send_field(True, depths[cut][k]).start()
        for k in range(1, 4):
            send_field(False, depths[cut][k]).start()
    for cut in range(2):
        pl.when(depths[cut][0] != d)(send_field(False, depths[cut][0]).start)

    gbuf[z] = gsend[z]
    pltpu.make_async_copy(gbuf.at[pl.ds(0, RING - 1)], gbuf.at[pl.ds(0, RING - 1)], gr).wait()
    totals = [gbuf[0], gbuf[1]]
    for other in range(2, RING):
        totals[other % 2] = totals[other % 2] + gbuf[other]
    total = jnp.concatenate(totals, axis=0)
    across = lax.broadcasted_iota(jnp.int32, (128, 128), 0) + lax.broadcasted_iota(jnp.int32, (128, 128), 1)
    reverse = jnp.where(across == 127, 1.0, 0.0).astype(BF16)
    high, rest = split(total)
    low = (total - high.astype(F32) - rest.astype(F32)).astype(BF16)
    turned = matmul(jnp.concatenate([high, rest, low], axis=0), reverse)
    turned = turned[:ROWS] + turned[ROWS : 2 * ROWS] + turned[2 * ROWS :]
    total = jnp.where(d < DEPTH // 2, turned, total)

    @pl.when(lower)
    def _():
        for row in range(ROWS):
            out_ref[ROWS - 1 - row : ROWS - row, :] = total[row : row + 1]

    @pl.when(jnp.logical_not(lower))
    def _():
        out_ref[...] = total

    for copy, there in zip(copies, has):
        pl.when(there)(copy.wait_send)
    pltpu.make_async_copy(csend.at[pl.ds(0, 2 * GROUP - 1)], csend.at[pl.ds(0, 2 * GROUP - 1)], cs).wait()
    pltpu.make_async_copy(xsend.at[pl.ds(0, 2 * GROUP - 1)], xsend.at[pl.ds(0, 2 * GROUP - 1)], xs).wait()
    pltpu.make_async_copy(gsend.at[pl.ds(0, RING - 1)], gsend.at[pl.ds(0, RING - 1)], gs).wait()


def solution(mesh):
    wide, mixed, tall = basis()

    def step(level_set, contrast):
        vmem = pl.BlockSpec(memory_space=pltpu.VMEM)
        anywhere = pl.BlockSpec(memory_space=pl.ANY)
        dma = pltpu.SemaphoreType.DMA
        return pl.pallas_call(
            kernel,
            out_shape=jax.ShapeDtypeStruct((ROWS, 128), F32),
            in_specs=[anywhere] * 5,
            out_specs=vmem,
            scratch_shapes=[
                pltpu.VMEM((2, ROWS, NX), F32),
                pltpu.SMEM((2,), F32),
                pltpu.VMEM((2, ROWS, NX), F32),
                pltpu.VMEM((2, HALF, NX), BF16),
                pltpu.VMEM((2, HALF, NX), BF16),
                pltpu.VMEM((2, NX, HALF), BF16),
                pltpu.VMEM((2, ROWS, NX), F32),
                pltpu.VMEM((2, 16, 128), F32),
                pltpu.VMEM((2, 16, 128), F32),
                pltpu.VMEM((2 * GROUP, 8, 128), F32),
                pltpu.VMEM((2 * GROUP, 8, 128), F32),
                pltpu.VMEM((2, 128, NX), F32),
                pltpu.VMEM((64, NX), F32),
                pltpu.VMEM((128, NX), BF16),
                pltpu.VMEM((2 * GROUP, 4, 128), F32),
                pltpu.VMEM((2 * GROUP, 4, 128), F32),
                pltpu.VMEM((2 * ROWS, NX), F32),
                pltpu.VMEM((RING, 8, 128), F32),
                pltpu.VMEM((RING, 8, 128), F32),
                dma(()), dma(()), dma((2,)), dma((2,)), dma((2,)), dma((4,)), dma((4,)),
                dma(()), dma((2,)), dma(()), dma(()), dma(()), dma(()), pltpu.SemaphoreType.REGULAR((6,)),
            ],
            compiler_params=pltpu.CompilerParams(
                collective_id=0, has_side_effects=True, vmem_limit_bytes=55176 * 1024
            ),
        )(level_set, contrast, jnp.asarray(wide), jnp.asarray(mixed), jnp.asarray(tall))

    return jax.shard_map(
        step,
        mesh=mesh,
        in_specs=(P("depth", "plan", None), P("depth")),
        out_specs=P("plan", "depth"),
        check_vma=False,
    )
```

```python
import functools
import math

import jax
import jax.numpy as jnp
import ml_dtypes
import numpy as np
from jax import lax
from jax.experimental import pallas as pl
from jax.experimental.pallas import tpu as pltpu
from jax.sharding import PartitionSpec as P

MESH = pl.DeviceIdType.MESH
F32 = jnp.float32
BF16 = jnp.bfloat16

NX = 1024
HALF = NX // 2
LAYERS = 16
DEPTH = 8
PLAN = 64
ROWS = NX // PLAN
GROUP = 32
RING = 16
COEF = 2 * NX // GROUP
SHARE = COEF // 2

bend_weight = 0.5
grav_scale = 0.05
top_depth = 0.0
thickness = 1.0


def basis():
    j = np.arange(HALF, dtype=np.float64)[:, None] + 0.5
    v = np.arange(NX, dtype=np.float64)[None, :]
    table = np.cos(np.pi * v * j / NX)
    high = table.astype(ml_dtypes.bfloat16)
    low = (table - high.astype(np.float64)).astype(ml_dtypes.bfloat16)
    wide = np.stack([high, low])
    order = np.arange(HALF).reshape(GROUP, 2, ROWS // 2).transpose(1, 0, 2).reshape(-1)
    return wide, np.ascontiguousarray(wide[:, order]), np.ascontiguousarray(np.swapaxes(wide, 1, 2))


def alternating(shape):
    return 1.0 - 2.0 * lax.rem(lax.broadcasted_iota(jnp.int32, shape, 1), 2).astype(F32)


def flux(step):
    return step * lax.rsqrt(1.0 + step * step)


def flip(value, axis, size):
    index = lax.broadcasted_iota(jnp.int32, value.shape, axis)
    step = size // 2
    value = pltpu.roll(value, step, axis)
    while step > 1:
        step //= 2
        up = pltpu.roll(value, step, axis)
        down = pltpu.roll(value, size - step, axis)
        value = jnp.where((index & step) != 0, up, down)
    return value


def flip_lanes(value):
    blocks = value.shape[1] // 128
    parts = [flip(value[:, 128 * k : 128 * (k + 1)], 1, 128) for k in reversed(range(blocks))]
    return jnp.concatenate(parts, axis=1) if blocks > 1 else parts[0]


def split(value):
    high = value.astype(BF16)
    low = (value - high.astype(F32)).astype(BF16)
    return high, low


def matmul(a, b):
    return jnp.dot(a, b, preferred_element_type=F32)


def pair(value):
    return jnp.concatenate(split(value), axis=0)


def table_right(both, high_table, low_table):
    n = both.shape[0] // 2
    product = matmul(both, high_table)
    return product[:n] + product[n:] + matmul(both[:n], low_table)


def regroup(parts):
    lane = lax.broadcasted_iota(jnp.int32, parts[0].shape, 1)
    early, even = lane < 64, lax.rem(lane, 64) < 32
    wide = [jnp.where(early, parts[g], pltpu.roll(parts[g + 2], 64, 1)) for g in range(2)]
    wide += [jnp.where(early, pltpu.roll(parts[g], 64, 1), parts[g + 2]) for g in range(2)]
    out = []
    for first, second in (wide[:2], wide[2:]):
        out.append(jnp.where(even, first, pltpu.roll(second, 32, 1)))
        out.append(jnp.where(even, pltpu.roll(first, 96, 1), second))
    return out


def kernel(
    ls_hbm, con_hbm, wide_hbm, mixed_hbm, tall_hbm, out_ref,
    ls_ref, con_ref, own, part_density, wide, mixed, tall, zhalo, rsend, rhalo, csend, sbuf, rsp, acc, pst, xsend, cbuf, coefs, gsend, gbuf,
    ls_sem, con_sem, wide_sem, mixed_sem, tall_sem, hs, hr, cs, cr, xs, xr, gs, gr, news,
):
    d = lax.axis_index("depth")
    p = lax.axis_index("plan")
    core = lax.rem(p, 2)
    zh = lax.rem(lax.div(p, 2), 2)
    q = lax.div(p, 4) * 2 + core
    z = zh * DEPTH + d
    lower = p < PLAN // 2

    x, y = lax.div(p, 16), lax.rem(lax.div(p, 4), 4)
    kind_own, cut_own = lax.div(y, 2), lax.rem(x + y, 2)
    set_own = 2 * kind_own + cut_own
    coef_block = 8 * set_own + 2 * x + core
    parity = lax.rem(d, 2)
    mate = d + 1 - 2 * parity
    order = (2, 6, 4, 3, 7, 5, 1, 0)
    turns = [lax.rem(2 * x + core + k, 8) for k in order]
    places = [
        [16 * lax.div(t, 2) + 4 * lax.rem(lax.div(t, 2) + cut, 2) + 2 * zh + lax.rem(t, 2) for t in turns]
        for cut in range(2)
    ]

    def at_z(other):
        return (lax.rem(other, DEPTH), p + 2 * (lax.div(other, DEPTH) - zh))

    barrier = pltpu.get_barrier_semaphore()

    def greet(target):
        pl.semaphore_signal(barrier, inc=1, device_id=target, device_id_type=MESH)

    has = (d < DEPTH - 1, d > 0, p < PLAN - 1, p > 0)
    gets = (d > 0, d < DEPTH - 1, p > 0, p < PLAN - 1)
    outer = jnp.where(core == 0, p - 1, p + 1)
    has_outer = (outer >= 0) & (outer < PLAN)
    x_line = [(d, p + 16 * (lax.rem(x + k, 4) - x)) for k in (1, 3, 2)]
    y_line = [(d, p + 4 * (lax.rem(y + k, 4) - y)) for k in (1, 3, 2)]
    buddy = (d, p + 1 - 2 * core)

    def z_pair(k):
        return [at_z(lax.rem(z + away, RING)) for away in (k, RING - k)]

    pl.when(has_outer)(lambda: greet((d, outer)))
    ls_copy = pltpu.make_async_copy(ls_hbm, ls_ref, ls_sem)
    con_copy = pltpu.make_async_copy(con_hbm, con_ref, con_sem)
    ls_copy.start()
    con_copy.start()
    wide_copies = [pltpu.make_async_copy(wide_hbm.at[n], wide.at[n], wide_sem.at[n]) for n in range(2)]
    mixed_copies = [pltpu.make_async_copy(mixed_hbm.at[n], mixed.at[n], mixed_sem.at[n]) for n in range(2)]
    tall_copies = [pltpu.make_async_copy(tall_hbm.at[n], tall.at[n], tall_sem.at[n]) for n in range(2)]
    for copy in wide_copies:
        copy.start()
    for target in z_pair(1) + [buddy] + x_line + y_line:
        greet(target)

    def tell(number, targets):
        for target in targets:
            pl.semaphore_signal(news.at[number], inc=1, device_id=target, device_id_type=MESH)

    def hear(number, count):
        pl.semaphore_wait(news.at[number], count)

    pl.semaphore_wait(barrier, 9 + has_outer.astype(jnp.int32))

    def halo(source, target, number, device):
        return pltpu.make_async_remote_copy(
            src_ref=source, dst_ref=target, send_sem=hs.at[number], recv_sem=hr.at[number],
            device_id=device, device_id_type=MESH,
        )

    z_up = halo(ls_hbm.at[1], zhalo.at[0], 0, (d + 1, p))
    z_down = halo(ls_hbm.at[0], zhalo.at[1], 1, (d - 1, p))
    r_up = halo(rsend.at[1], rhalo.at[0], 2, (d, p + 1))
    r_down = halo(rsend.at[0], rhalo.at[1], 3, (d, p - 1))
    lands = (zhalo.at[0], zhalo.at[1], rhalo.at[0], rhalo.at[1])
    copies = (z_up, z_down, r_up, r_down)
    for copy, there in zip(copies[:2], has[:2]):
        pl.when(there)(copy.start)
    ls_copy.wait()

    for layer in range(2):
        for k in range(8):
            spot = layer * 8 + k
            block = 4 + k if k < 4 else 7 - k
            lanes = slice(128 * block, 128 * (block + 1))
            rsend[0, spot : spot + 1, :] = ls_ref[layer, 0:1, lanes]
            rsend[1, spot : spot + 1, :] = ls_ref[layer, ROWS - 1 : ROWS, lanes]
    turned = lax.rem(lax.broadcasted_iota(jnp.int32, (16, 128), 0), 8) >= 4
    for side in range(2):
        rsend[side] = jnp.where(turned, flip(rsend[side], 1, 128), rsend[side])

    for copy, there in zip(copies[2:], has[2:]):
        pl.when(there)(copy.start)
    tell(0, y_line)
    tell(1, z_pair(1))
    for copy in mixed_copies + tall_copies:
        copy.start()

    def fold(value):
        value = jnp.where(lower, flip(value, 0, ROWS), value)
        return jnp.concatenate([value[:, HALF:], flip_lanes(value[:, :HALF])], axis=1)

    for layer in range(2):
        own[layer] = fold(ls_ref[layer])
    con_copy.wait()

    for land, comes in zip(lands, gets):

        @pl.when(jnp.logical_not(comes))
        def _(land=land):
            land[...] = jnp.zeros(land.shape, F32)

    row_id = lax.broadcasted_iota(jnp.int32, (ROWS, NX), 0)
    lane_id = lax.broadcasted_iota(jnp.int32, (ROWS, HALF), 1)
    field = [own[0], own[1]]
    middle = flux(field[1] - field[0])
    for layer in range(2):
        centre = field[layer]
        bend = -middle if layer else middle
        inner_flux = flux(pltpu.roll(centre, 1, 0) - centre)
        bend = bend + jnp.where(row_id == 0, 0.0, inner_flux)
        bend = bend - jnp.where(row_id == ROWS - 1, 0.0, pltpu.roll(inner_flux, ROWS - 1, 0))
        sides = centre[:, :HALF], centre[:, HALF:]
        across = []
        for side in range(2):
            here = sides[side]
            inside = jnp.where(lane_id == 0, sides[1 - side], pltpu.roll(here, 1, 1))
            inner_flux = flux(inside - here)
            outside = jnp.where(lane_id == HALF - 1, flux(here), pltpu.roll(inner_flux, HALF - 1, 1))
            across.append(inner_flux - outside)
        bend = bend + jnp.concatenate(across, axis=1)
        part_density[layer] = con_ref[layer] * (0.5 * (1.0 + jnp.tanh(centre))) + bend_weight * bend

    hear(0, 3)
    tell(2, [buddy])

    for layer in range(2):
        pl.when(gets[layer])(copies[layer].wait_recv)
        part_density[layer] += bend_weight * flux(fold(zhalo[layer]) - own[layer])
    for number in (2, 3):
        pl.when(gets[number])(copies[number].wait_recv)
    even, odd = [], []
    for layer in range(2):
        centre = own[layer]
        here = slice(layer * 8, layer * 8 + 8)
        top = jnp.where(lower, rhalo[1, here, :], rhalo[0, here, :])
        bottom = jnp.where(lower, rhalo[0, here, :], rhalo[1, here, :])
        tops = [jnp.broadcast_to(top[k : k + 1], (ROWS, 128)) for k in range(8)]
        bottoms = [jnp.broadcast_to(bottom[k : k + 1], (ROWS, 128)) for k in range(8)]
        beside = jnp.where(row_id == 0, jnp.concatenate(tops, axis=1), jnp.concatenate(bottoms, axis=1))
        outer_rows = (row_id == 0) | (row_id == ROWS - 1)
        density = part_density[layer] + jnp.where(outer_rows, bend_weight * flux(beside - centre), 0.0)
        even.append(density[:, :HALF] + density[:, HALF:])
        odd.append((density[:, :HALF] - density[:, HALF:]) * alternating((ROWS, HALF)))

    block = jnp.where(lower, PLAN // 2 - 1 - p, p - PLAN // 2)
    hear(2, 1)
    hear(1, 2)
    tell(3, [(mate, p)])
    for copy in wide_copies:
        copy.wait()

    def send_coef(group, k, cross):
        member = 1 - parity if cross else parity
        return pltpu.make_async_remote_copy(
            src_ref=csend.at[2 * (8 * group + turns[k]) + member], dst_ref=sbuf.at[GROUP * cross + block],
            send_sem=cs, recv_sem=cr.at[cross],
            device_id=(mate if cross else d, 8 * (group // 2) + places[group % 2][k]), device_id_type=MESH,
        )

    both = pair(jnp.concatenate(even + odd, axis=0))
    for cut in range(2):
        cols = slice(HALF * cut, HALF * (cut + 1))
        coef = table_right(both, wide[0, :, cols], wide[1, :, cols])
        for kind in range(2):
            start = kind * 16 + 8 * cut
            for m in range(4):
                lanes = slice(128 * m, 128 * (m + 1))
                starts = [2 * ROWS * kind + ROWS * layer + 8 * half for half in range(2) for layer in range(2)]
                for t, value in enumerate(regroup([coef[n : n + 8, lanes] for n in starts])):
                    csend[2 * start + 4 * m + t] = value
        for k in range(7):
            for kind in range(2):
                send_coef(2 * kind + cut, k, 0).start()
    for group in range(4):
        pl.when(group != set_own)(send_coef(group, 7, 0).start)
    hear(3, 1)
    tell(4, z_pair(2))
    for k in range(8):
        for group in range(4):
            send_coef(group, k, 1).start()

    def respond(start, cross):
        row = lax.broadcasted_iota(jnp.int32, (128, 128), 0)
        col = lax.broadcasted_iota(jnp.int32, (128, 128), 1) + start
        place = lax.rem(coef_block, GROUP // 2) * COEF + parity * SHARE + lax.rem(row, SHARE)
        v = jnp.where(kind_own == 1, NX - place, place).astype(F32)
        scale = 2.0 * math.pi * grav_scale * thickness / (4.0 * NX * NX)
        weight = jnp.where(place == 0, scale, 2.0 * scale) * jnp.where(col == 0, 1.0, 2.0)
        layer = (2 * (mate if cross else d) + lax.rem(lax.div(row, SHARE), 2)).astype(F32)
        rate = (top_depth + (layer + 0.5) * thickness) * (-2.0 * math.pi / (2 * NX))
        u = jnp.where(row >= 64, NX - col, col).astype(F32)
        return jnp.exp(jnp.sqrt(u * u + v * v) * rate) * weight

    for cross in range(2):
        for k in range(NX // 128):
            rsp[cross, :, 128 * k : 128 * (k + 1)] = respond(128 * k, cross)

    hear(4, 2)
    tell(5, z_pair(4))
    sbuf[block] = csend[2 * coef_block + parity]
    for copy in mixed_copies + tall_copies:
        copy.wait()
    side = lax.rem(lax.div(lax.broadcasted_iota(jnp.int32, (64, HALF), 1), 16), 2)
    sign = jnp.where(side == zh, 1.0, -1.0) * alternating((64, HALF))
    step = 256
    for cross in range(2):
        landed = sbuf.at[pl.ds(GROUP * cross, GROUP - 1 + cross)]
        pltpu.make_async_copy(landed, landed, cr.at[cross]).wait()
        value = sbuf[GROUP * cross : GROUP * (cross + 1)].reshape(HALF // 2, 128).T
        value = jnp.concatenate([value[:64], value[64:]], axis=1)
        both = pair(jnp.concatenate([value, value * sign], axis=0))
        for k in range(NX // step):
            here = slice(k * step, (k + 1) * step)
            coef = table_right(both, mixed[0, :, here], mixed[1, :, here]) * rsp[cross, :, here]
            parts = [coef[SHARE * n : SHARE * (n + 1)] for n in range(4)]
            coef = jnp.concatenate([parts[0] + parts[1], parts[2] + parts[3]], axis=0)
            if cross:
                pst[:, here] = pair(coef + acc[:, here])
            else:
                acc[:, here] = coef

    low = 2 * lax.rem(y, 2) + core
    x_turns = [lax.rem(x + k, 4) for k in range(4)]
    low_turns = [lax.rem(low + k, 4) for k in range(4)]
    low_places = [4 * lax.div(t, 2) + lax.rem(t, 2) + 2 * zh for t in low_turns]

    def send_rows(part, r, k, cross):
        upper = lax.div(x_turns[r], 2)
        upper = upper if part else 1 - upper
        member = 1 - parity if cross else parity
        return pltpu.make_async_remote_copy(
            src_ref=xsend.at[2 * (8 * x_turns[r] + 4 * upper + low_turns[k]) + member],
            dst_ref=cbuf.at[2 * coef_block + parity], send_sem=xs, recv_sem=xr,
            device_id=(mate if cross else d, 16 * x_turns[r] + 8 * upper + low_places[k]), device_id_type=MESH,
        )

    lane = lax.broadcasted_iota(jnp.int32, (8, 128), 1)
    early, even_lane = lane < 64, lax.rem(lane, 64) < 32
    def columns(part):
        cols = slice(128 * part, 128 * part + 128), slice(128 * part + 256, 128 * part + 384)
        return [jnp.concatenate([tall[n, :, col] for col in cols], axis=1) for n in range(2)]

    for part in range(2):
        value = table_right(pst[...], *columns(part))
        evens, odds = value[:SHARE], value[SHARE:] * alternating((SHARE, 256))
        plus, minus = evens + odds, evens - odds
        value = jnp.concatenate([plus, minus, plus, minus], axis=0).T
        for g in range(4):
            chunk = 2 * part + 4 * (g // 2) + g % 2
            for member in range(2):
                ups, downs = [], []
                for n in range(4):
                    start = ROWS * (4 * g + n) + 8 * member
                    rows = value[start : start + 8]
                    later = pltpu.roll(rows, 4, 0)
                    ups.append(jnp.where(even_lane, rows, pltpu.roll(later, 32, 1)))
                    downs.append(jnp.where(even_lane, pltpu.roll(rows, 32, 1), later))
                for spot, one, two in (
                    (2 * (8 + chunk), ups[0], ups[2]),
                    (2 * (8 + chunk) + 1, ups[1], ups[3]),
                    (2 * (7 - chunk), downs[3], downs[1]),
                    (2 * (7 - chunk) + 1, downs[2], downs[0]),
                ):
                    xsend[2 * spot + member] = jnp.where(early, one, two)[:4]

        for r in (1, 3, 2, 0):
            for k in range(4):
                send_rows(part, r, k, 1).start()
                if r or k:
                    send_rows(part, r, k, 0).start()
    upper_own = lax.rem(lax.div(x, 2) + lax.div(y, 2), 2)
    pl.when(upper_own == 0)(send_rows(0, 0, 0, 0).start)
    pl.when(upper_own == 1)(send_rows(1, 0, 0, 0).start)

    hear(5, 2)
    cbuf[2 * coef_block + parity] = xsend[2 * q + parity]
    landed = cbuf.at[pl.ds(0, 2 * GROUP - 1)]
    pltpu.make_async_copy(landed, landed, xr).wait()

    def send_field(far, depth):
        row = 1 - zh if far else zh
        return pltpu.make_async_remote_copy(
            src_ref=gsend.at[DEPTH * row + depth], dst_ref=gbuf.at[z], send_sem=gs, recv_sem=gr,
            device_id=(depth, p + 2 - 4 * zh if far else p), device_id_type=MESH,
        )

    steps = [lax.rem(lax.div(d, 2) + k, 4) for k in range(4)]
    depths = ([2 * t + 1 - lax.div(t, 2) for t in steps], [2 * t + lax.div(t, 2) for t in steps])

    for m in range(2 * NX // 128):
        parts = regroup([cbuf[4 * m + t] for t in range(4)])
        lanes = slice(128 * (m % 8), 128 * (m % 8 + 1))
        for g in range(4):
            start = ROWS * (m // 8) + 4 * g
            coefs[start : start + 4, lanes] = parts[g]
    both = pair(coefs[...])
    for cut in range(2):
        value = table_right(both, *columns(cut))
        evens, odds = value[:ROWS], value[ROWS:] * alternating((ROWS, 256))
        plus = evens + odds
        minus = evens - odds
        for half in range(2):
            rows = slice(8 * half, 8 * (half + 1))
            for n in range(2):
                lanes = slice(128 * n, 128 * (n + 1))
                gsend[DEPTH * half + 4 + cut + 2 * n] = plus[rows, lanes]
                gsend[DEPTH * half + 3 - cut - 2 * n] = minus[rows, lanes]
        for k in range(4):
            send_field(True, depths[cut][k]).start()
        for k in range(1, 4):
            send_field(False, depths[cut][k]).start()
    for cut in range(2):
        pl.when(depths[cut][0] != d)(send_field(False, depths[cut][0]).start)

    gbuf[z] = gsend[z]
    pltpu.make_async_copy(gbuf.at[pl.ds(0, RING - 1)], gbuf.at[pl.ds(0, RING - 1)], gr).wait()
    totals = [gbuf[0], gbuf[1]]
    for other in range(2, RING):
        totals[other % 2] = totals[other % 2] + gbuf[other]
    total = jnp.concatenate(totals, axis=0)
    across = lax.broadcasted_iota(jnp.int32, (128, 128), 0) + lax.broadcasted_iota(jnp.int32, (128, 128), 1)
    reverse = jnp.where(across == 127, 1.0, 0.0).astype(BF16)
    high, rest = split(total)
    low = (total - high.astype(F32) - rest.astype(F32)).astype(BF16)
    turned = matmul(jnp.concatenate([high, rest, low], axis=0), reverse)
    turned = turned[:ROWS] + turned[ROWS : 2 * ROWS] + turned[2 * ROWS :]
    total = jnp.where(d < DEPTH // 2, turned, total)

    @pl.when(lower)
    def _():
        for row in range(ROWS):
            out_ref[ROWS - 1 - row : ROWS - row, :] = total[row : row + 1]

    @pl.when(jnp.logical_not(lower))
    def _():
        out_ref[...] = total

    for copy, there in zip(copies, has):
        pl.when(there)(copy.wait_send)
    pltpu.make_async_copy(csend.at[pl.ds(0, 2 * GROUP - 1)], csend.at[pl.ds(0, 2 * GROUP - 1)], cs).wait()
    pltpu.make_async_copy(xsend.at[pl.ds(0, 2 * GROUP - 1)], xsend.at[pl.ds(0, 2 * GROUP - 1)], xs).wait()
    pltpu.make_async_copy(gsend.at[pl.ds(0, RING - 1)], gsend.at[pl.ds(0, RING - 1)], gs).wait()


def solution(mesh):
    wide, mixed, tall = basis()

    def step(level_set, contrast):
        vmem = pl.BlockSpec(memory_space=pltpu.VMEM)
        anywhere = pl.BlockSpec(memory_space=pl.ANY)
        dma = pltpu.SemaphoreType.DMA
        return pl.pallas_call(
            kernel,
            out_shape=jax.ShapeDtypeStruct((ROWS, 128), F32),
            in_specs=[anywhere] * 5,
            out_specs=vmem,
            scratch_shapes=[
                pltpu.VMEM((2, ROWS, NX), F32),
                pltpu.SMEM((2,), F32),
                pltpu.VMEM((2, ROWS, NX), F32),
                pltpu.VMEM((2, ROWS, NX), F32),
                pltpu.VMEM((2, HALF, NX), BF16),
                pltpu.VMEM((2, HALF, NX), BF16),
                pltpu.VMEM((2, NX, HALF), BF16),
                pltpu.VMEM((2, ROWS, NX), F32),
                pltpu.VMEM((2, 16, 128), F32),
                pltpu.VMEM((2, 16, 128), F32),
                pltpu.VMEM((2 * GROUP, 8, 128), F32),
                pltpu.VMEM((2 * GROUP, 8, 128), F32),
                pltpu.VMEM((2, 128, NX), F32),
                pltpu.VMEM((64, NX), F32),
                pltpu.VMEM((128, NX), BF16),
                pltpu.VMEM((2 * GROUP, 4, 128), F32),
                pltpu.VMEM((2 * GROUP, 4, 128), F32),
                pltpu.VMEM((2 * ROWS, NX), F32),
                pltpu.VMEM((RING, 8, 128), F32),
                pltpu.VMEM((RING, 8, 128), F32),
                dma(()), dma(()), dma((2,)), dma((2,)), dma((2,)), dma((4,)), dma((4,)),
                dma(()), dma((2,)), dma(()), dma(()), dma(()), dma(()), pltpu.SemaphoreType.REGULAR((6,)),
            ],
            compiler_params=pltpu.CompilerParams(
                collective_id=0, has_side_effects=True, vmem_limit_bytes=55176 * 1024
            ),
        )(level_set, contrast, jnp.asarray(wide), jnp.asarray(mixed), jnp.asarray(tall))

    return jax.shard_map(
        step,
        mesh=mesh,
        in_specs=(P("depth", "plan", None), P("depth")),
        out_specs=P("plan", "depth"),
        check_vma=False,
    )
```

```python
import functools
import math

import jax
import jax.numpy as jnp
import ml_dtypes
import numpy as np
from jax import lax
from jax.experimental import pallas as pl
from jax.experimental.pallas import tpu as pltpu
from jax.sharding import PartitionSpec as P

MESH = pl.DeviceIdType.MESH
F32 = jnp.float32
BF16 = jnp.bfloat16

NX = 1024
HALF = NX // 2
LAYERS = 16
DEPTH = 8
PLAN = 64
ROWS = NX // PLAN
GROUP = 32
RING = 16
COEF = 2 * NX // GROUP
SHARE = COEF // 2

bend_weight = 0.5
grav_scale = 0.05
top_depth = 0.0
thickness = 1.0


def basis():
    j = np.arange(HALF, dtype=np.float64)[:, None] + 0.5
    v = np.arange(NX, dtype=np.float64)[None, :]
    table = np.cos(np.pi * v * j / NX)
    high = table.astype(ml_dtypes.bfloat16)
    low = (table - high.astype(np.float64)).astype(ml_dtypes.bfloat16)
    wide = np.stack([high, low])
    order = np.arange(HALF).reshape(GROUP, 2, ROWS // 2).transpose(1, 0, 2).reshape(-1)
    return wide, np.ascontiguousarray(wide[:, order]), np.ascontiguousarray(np.swapaxes(wide, 1, 2))


def alternating(shape):
    return 1.0 - 2.0 * lax.rem(lax.broadcasted_iota(jnp.int32, shape, 1), 2).astype(F32)


def flux(step):
    return step * lax.rsqrt(1.0 + step * step)


def flip(value, axis, size):
    index = lax.broadcasted_iota(jnp.int32, value.shape, axis)
    step = size // 2
    value = pltpu.roll(value, step, axis)
    while step > 1:
        step //= 2
        up = pltpu.roll(value, step, axis)
        down = pltpu.roll(value, size - step, axis)
        value = jnp.where((index & step) != 0, up, down)
    return value


def flip_lanes(value):
    blocks = value.shape[1] // 128
    parts = [flip(value[:, 128 * k : 128 * (k + 1)], 1, 128) for k in reversed(range(blocks))]
    return jnp.concatenate(parts, axis=1) if blocks > 1 else parts[0]


def split(value):
    high = value.astype(BF16)
    low = (value - high.astype(F32)).astype(BF16)
    return high, low


def matmul(a, b):
    return jnp.dot(a, b, preferred_element_type=F32)


def pair(value):
    return jnp.concatenate(split(value), axis=0)


def table_right(both, high_table, low_table):
    n = both.shape[0] // 2
    product = matmul(both, high_table)
    return product[:n] + product[n:] + matmul(both[:n], low_table)


def regroup(parts):
    lane = lax.broadcasted_iota(jnp.int32, parts[0].shape, 1)
    early, even = lane < 64, lax.rem(lane, 64) < 32
    wide = [jnp.where(early, parts[g], pltpu.roll(parts[g + 2], 64, 1)) for g in range(2)]
    wide += [jnp.where(early, pltpu.roll(parts[g], 64, 1), parts[g + 2]) for g in range(2)]
    out = []
    for first, second in (wide[:2], wide[2:]):
        out.append(jnp.where(even, first, pltpu.roll(second, 32, 1)))
        out.append(jnp.where(even, pltpu.roll(first, 96, 1), second))
    return out


def kernel(
    ls_hbm, con_hbm, wide_hbm, mixed_hbm, tall_hbm, out_ref,
    ls_ref, con_ref, own, part_density, wide, mixed, tall, zhalo, rsend, rhalo, csend, sbuf, rsp, acc, pst, xsend, cbuf, coefs, gsend, gbuf,
    ls_sem, con_sem, wide_sem, mixed_sem, tall_sem, hs, hr, cs, cr, xs, xr, gs, gr, news,
):
    d = lax.axis_index("depth")
    p = lax.axis_index("plan")
    core = lax.rem(p, 2)
    zh = lax.rem(lax.div(p, 2), 2)
    q = lax.div(p, 4) * 2 + core
    z = zh * DEPTH + d
    lower = p < PLAN // 2

    x, y = lax.div(p, 16), lax.rem(lax.div(p, 4), 4)
    kind_own, cut_own = lax.div(y, 2), lax.rem(x + y, 2)
    set_own = 2 * kind_own + cut_own
    coef_block = 8 * set_own + 2 * x + core
    parity = lax.rem(d, 2)
    mate = d + 1 - 2 * parity
    order = (2, 6, 4, 3, 7, 5, 1, 0)
    turns = [lax.rem(2 * x + core + k, 8) for k in order]
    places = [
        [16 * lax.div(t, 2) + 4 * lax.rem(lax.div(t, 2) + cut, 2) + 2 * zh + lax.rem(t, 2) for t in turns]
        for cut in range(2)
    ]

    def at_z(other):
        return (lax.rem(other, DEPTH), p + 2 * (lax.div(other, DEPTH) - zh))

    ls_copy = pltpu.make_async_copy(ls_hbm, ls_ref, ls_sem)
    con_copy = pltpu.make_async_copy(con_hbm, con_ref, con_sem)
    ls_copy.start()
    con_copy.start()
    wide_copies = [pltpu.make_async_copy(wide_hbm.at[n], wide.at[n], wide_sem.at[n]) for n in range(2)]
    mixed_copies = [pltpu.make_async_copy(mixed_hbm.at[n], mixed.at[n], mixed_sem.at[n]) for n in range(2)]
    tall_copies = [pltpu.make_async_copy(tall_hbm.at[n], tall.at[n], tall_sem.at[n]) for n in range(2)]
    for copy in wide_copies:
        copy.start()

    barrier = pltpu.get_barrier_semaphore()

    def greet(target):
        pl.semaphore_signal(barrier, inc=1, device_id=target, device_id_type=MESH)

    has = (d < DEPTH - 1, d > 0, p < PLAN - 1, p > 0)
    gets = (d > 0, d < DEPTH - 1, p > 0, p < PLAN - 1)
    outer = jnp.where(core == 0, p - 1, p + 1)
    has_outer = (outer >= 0) & (outer < PLAN)
    x_line = [(d, p + 16 * (lax.rem(x + k, 4) - x)) for k in (1, 3, 2)]
    y_line = [(d, p + 4 * (lax.rem(y + k, 4) - y)) for k in (1, 3, 2)]
    buddy = (d, p + 1 - 2 * core)

    def z_pair(k):
        return [at_z(lax.rem(z + away, RING)) for away in (k, RING - k)]

    for target in z_pair(1) + [buddy]:
        greet(target)
    pl.when(has_outer)(lambda: greet((d, outer)))
    for target in x_line + y_line:
        greet(target)

    def tell(number, targets):
        for target in targets:
            pl.semaphore_signal(news.at[number], inc=1, device_id=target, device_id_type=MESH)

    def hear(number, count):
        pl.semaphore_wait(news.at[number], count)

    ls_copy.wait()
    con_copy.wait()

    for layer in range(2):
        value = ls_ref[layer]
        value = jnp.where(lower, flip(value, 0, ROWS), value)
        own[layer, :, :HALF] = value[:, HALF:]
        own[layer, :, HALF:] = flip_lanes(value[:, :HALF])

    for layer in range(2):
        for k in range(8):
            spot = layer * 8 + k
            top = own[layer, 0:1, 128 * k : 128 * (k + 1)]
            bottom = own[layer, ROWS - 1 : ROWS, 128 * k : 128 * (k + 1)]
            rsend[0, spot : spot + 1, :] = jnp.where(lower, bottom, top)
            rsend[1, spot : spot + 1, :] = jnp.where(lower, top, bottom)

    pl.semaphore_wait(barrier, 9 + has_outer.astype(jnp.int32))

    def halo(source, target, number, device):
        return pltpu.make_async_remote_copy(
            src_ref=source, dst_ref=target, send_sem=hs.at[number], recv_sem=hr.at[number],
            device_id=device, device_id_type=MESH,
        )

    z_up = halo(own.at[1], zhalo.at[0], 0, (d + 1, p))
    z_down = halo(own.at[0], zhalo.at[1], 1, (d - 1, p))
    r_up = halo(rsend.at[1], rhalo.at[0], 2, (d, p + 1))
    r_down = halo(rsend.at[0], rhalo.at[1], 3, (d, p - 1))
    lands = (zhalo.at[0], zhalo.at[1], rhalo.at[0], rhalo.at[1])
    copies = (z_up, z_down, r_up, r_down)
    for copy, there in zip(copies, has):
        pl.when(there)(copy.start)
    tell(0, y_line)
    tell(1, z_pair(1))
    for copy in mixed_copies + tall_copies:
        copy.start()
    for land, comes in zip(lands, gets):

        @pl.when(jnp.logical_not(comes))
        def _(land=land):
            land[...] = jnp.zeros(land.shape, F32)

    row_id = lax.broadcasted_iota(jnp.int32, (ROWS, NX), 0)
    lane_id = lax.broadcasted_iota(jnp.int32, (ROWS, HALF), 1)
    field = [own[0], own[1]]
    middle = flux(field[1] - field[0])
    for layer in range(2):
        centre = field[layer]
        bend = -middle if layer else middle
        inner_flux = flux(pltpu.roll(centre, 1, 0) - centre)
        bend = bend + jnp.where(row_id == 0, 0.0, inner_flux)
        bend = bend - jnp.where(row_id == ROWS - 1, 0.0, pltpu.roll(inner_flux, ROWS - 1, 0))
        sides = centre[:, :HALF], centre[:, HALF:]
        across = []
        for side in range(2):
            here = sides[side]
            inside = jnp.where(lane_id == 0, sides[1 - side], pltpu.roll(here, 1, 1))
            inner_flux = flux(inside - here)
            outside = jnp.where(lane_id == HALF - 1, flux(here), pltpu.roll(inner_flux, HALF - 1, 1))
            across.append(inner_flux - outside)
        bend = bend + jnp.concatenate(across, axis=1)
        part_density[layer] = con_ref[layer] * (0.5 * (1.0 + jnp.tanh(centre))) + bend_weight * bend

    hear(0, 3)
    tell(2, [buddy])

    def respond(start):
        row = lax.broadcasted_iota(jnp.int32, (64, 128), 0)
        col = lax.broadcasted_iota(jnp.int32, (64, 128), 1) + start
        place = lax.rem(coef_block, GROUP // 2) * COEF + parity * SHARE + lax.rem(row, SHARE)
        v = jnp.where(kind_own == 1, NX - place, place).astype(F32)
        u = jnp.where(row >= SHARE, NX - col, col).astype(F32)
        scale = 2.0 * math.pi * grav_scale * thickness / (4.0 * NX * NX)
        weight = jnp.where(place == 0, scale, 2.0 * scale) * jnp.where(col == 0, 1.0, 2.0)
        kappa = jnp.sqrt(u * u + v * v) * (2.0 * math.pi / (2 * NX))
        next_layer = jnp.exp(-thickness * kappa)
        for cross, depth in enumerate((d, mate)):
            top = top_depth + (2.0 * depth.astype(F32) + 0.5) * thickness
            first = jnp.exp(-top * kappa) * weight
            second = first * next_layer
            for n, value in enumerate((first[:SHARE], second[:SHARE], first[SHARE:], second[SHARE:])):
                rsp[cross, SHARE * n : SHARE * (n + 1), start : start + 128] = value

    for k in range(NX // 128):
        respond(128 * k)

    for layer in range(2):
        pl.when(gets[layer])(copies[layer].wait_recv)
    for layer in range(2):
        part_density[layer] += bend_weight * flux(zhalo[layer] - own[layer])
    for number in (2, 3):
        pl.when(gets[number])(copies[number].wait_recv)
    even, odd = [], []
    for layer in range(2):
        centre = own[layer]
        here = slice(layer * 8, layer * 8 + 8)
        top = jnp.where(lower, rhalo[1, here, :], rhalo[0, here, :])
        bottom = jnp.where(lower, rhalo[0, here, :], rhalo[1, here, :])
        tops = [jnp.broadcast_to(top[k : k + 1], (ROWS, 128)) for k in range(8)]
        bottoms = [jnp.broadcast_to(bottom[k : k + 1], (ROWS, 128)) for k in range(8)]
        beside = jnp.where(row_id == 0, jnp.concatenate(tops, axis=1), jnp.concatenate(bottoms, axis=1))
        outer_rows = (row_id == 0) | (row_id == ROWS - 1)
        density = part_density[layer] + jnp.where(outer_rows, bend_weight * flux(beside - centre), 0.0)
        even.append(density[:, :HALF] + density[:, HALF:])
        odd.append((density[:, :HALF] - density[:, HALF:]) * alternating((ROWS, HALF)))

    block = jnp.where(lower, PLAN // 2 - 1 - p, p - PLAN // 2)
    hear(2, 1)
    hear(1, 2)
    tell(3, [(mate, p)])
    for copy in wide_copies:
        copy.wait()

    def send_coef(group, k, cross):
        member = 1 - parity if cross else parity
        return pltpu.make_async_remote_copy(
            src_ref=csend.at[2 * (8 * group + turns[k]) + member], dst_ref=sbuf.at[GROUP * cross + block],
            send_sem=cs, recv_sem=cr.at[cross],
            device_id=(mate if cross else d, 8 * (group // 2) + places[group % 2][k]), device_id_type=MESH,
        )

    both = pair(jnp.concatenate(even + odd, axis=0))
    for cut in range(2):
        cols = slice(HALF * cut, HALF * (cut + 1))
        coef = table_right(both, wide[0, :, cols], wide[1, :, cols])
        for kind in range(2):
            start = kind * 16 + 8 * cut
            for m in range(4):
                lanes = slice(128 * m, 128 * (m + 1))
                starts = [2 * ROWS * kind + ROWS * layer + 8 * half for half in range(2) for layer in range(2)]
                for t, value in enumerate(regroup([coef[n : n + 8, lanes] for n in starts])):
                    csend[2 * start + 4 * m + t] = value
        for k in range(7):
            for kind in range(2):
                send_coef(2 * kind + cut, k, 0).start()
    for group in range(4):
        pl.when(group != set_own)(send_coef(group, 7, 0).start)
    hear(3, 1)
    tell(4, z_pair(2))
    for k in range(8):
        for group in range(4):
            send_coef(group, k, 1).start()

    hear(4, 2)
    tell(5, z_pair(4))
    sbuf[block] = csend[2 * coef_block + parity]
    for copy in mixed_copies + tall_copies:
        copy.wait()
    side = lax.rem(lax.div(lax.broadcasted_iota(jnp.int32, (64, HALF), 1), 16), 2)
    sign = jnp.where(side == zh, 1.0, -1.0) * alternating((64, HALF))
    step = 256
    for cross in range(2):
        landed = sbuf.at[pl.ds(GROUP * cross, GROUP - 1 + cross)]
        pltpu.make_async_copy(landed, landed, cr.at[cross]).wait()
        value = sbuf[GROUP * cross : GROUP * (cross + 1)].reshape(HALF // 2, 128).T
        value = jnp.concatenate([value[:64], value[64:]], axis=1)
        both = pair(jnp.concatenate([value, value * sign], axis=0))
        for k in range(NX // step):
            here = slice(k * step, (k + 1) * step)
            coef = table_right(both, mixed[0, :, here], mixed[1, :, here]) * rsp[cross, :, here]
            parts = [coef[SHARE * n : SHARE * (n + 1)] for n in range(4)]
            coef = jnp.concatenate([parts[0] + parts[1], parts[2] + parts[3]], axis=0)
            if cross:
                pst[:, here] = pair(coef + acc[:, here])
            else:
                acc[:, here] = coef

    low = 2 * lax.rem(y, 2) + core
    x_turns = [lax.rem(x + k, 4) for k in range(4)]
    low_turns = [lax.rem(low + k, 4) for k in range(4)]
    low_places = [4 * lax.div(t, 2) + lax.rem(t, 2) + 2 * zh for t in low_turns]

    def send_rows(part, r, k, cross):
        upper = lax.div(x_turns[r], 2)
        upper = upper if part else 1 - upper
        member = 1 - parity if cross else parity
        return pltpu.make_async_remote_copy(
            src_ref=xsend.at[2 * (8 * x_turns[r] + 4 * upper + low_turns[k]) + member],
            dst_ref=cbuf.at[2 * coef_block + parity], send_sem=xs, recv_sem=xr,
            device_id=(mate if cross else d, 16 * x_turns[r] + 8 * upper + low_places[k]), device_id_type=MESH,
        )

    lane = lax.broadcasted_iota(jnp.int32, (8, 128), 1)
    early, even_lane = lane < 64, lax.rem(lane, 64) < 32
    def columns(part):
        cols = slice(128 * part, 128 * part + 128), slice(128 * part + 256, 128 * part + 384)
        return [jnp.concatenate([tall[n, :, col] for col in cols], axis=1) for n in range(2)]

    for part in range(2):
        value = table_right(pst[...], *columns(part))
        evens, odds = value[:SHARE], value[SHARE:] * alternating((SHARE, 256))
        plus, minus = evens + odds, evens - odds
        value = jnp.concatenate([plus, minus, plus, minus], axis=0).T
        for g in range(4):
            chunk = 2 * part + 4 * (g // 2) + g % 2
            for member in range(2):
                ups, downs = [], []
                for n in range(4):
                    start = ROWS * (4 * g + n) + 8 * member
                    rows = value[start : start + 8]
                    later = pltpu.roll(rows, 4, 0)
                    ups.append(jnp.where(even_lane, rows, pltpu.roll(later, 32, 1)))
                    downs.append(jnp.where(even_lane, pltpu.roll(rows, 32, 1), later))
                for spot, one, two in (
                    (2 * (8 + chunk), ups[0], ups[2]),
                    (2 * (8 + chunk) + 1, ups[1], ups[3]),
                    (2 * (7 - chunk), downs[3], downs[1]),
                    (2 * (7 - chunk) + 1, downs[2], downs[0]),
                ):
                    xsend[2 * spot + member] = jnp.where(early, one, two)[:4]

        for r in (1, 3, 2, 0):
            for k in range(4):
                send_rows(part, r, k, 1).start()
                if r or k:
                    send_rows(part, r, k, 0).start()
    upper_own = lax.rem(lax.div(x, 2) + lax.div(y, 2), 2)
    pl.when(upper_own == 0)(send_rows(0, 0, 0, 0).start)
    pl.when(upper_own == 1)(send_rows(1, 0, 0, 0).start)

    hear(5, 2)
    cbuf[2 * coef_block + parity] = xsend[2 * q + parity]
    landed = cbuf.at[pl.ds(0, 2 * GROUP - 1)]
    pltpu.make_async_copy(landed, landed, xr).wait()

    def send_field(far, depth):
        row = 1 - zh if far else zh
        return pltpu.make_async_remote_copy(
            src_ref=gsend.at[DEPTH * row + depth], dst_ref=gbuf.at[z], send_sem=gs, recv_sem=gr,
            device_id=(depth, p + 2 - 4 * zh if far else p), device_id_type=MESH,
        )

    steps = [lax.rem(lax.div(d, 2) + k, 4) for k in range(4)]
    depths = ([2 * t + 1 - lax.div(t, 2) for t in steps], [2 * t + lax.div(t, 2) for t in steps])

    for m in range(2 * NX // 128):
        parts = regroup([cbuf[4 * m + t] for t in range(4)])
        lanes = slice(128 * (m % 8), 128 * (m % 8 + 1))
        for g in range(4):
            start = ROWS * (m // 8) + 4 * g
            coefs[start : start + 4, lanes] = parts[g]
    both = pair(coefs[...])
    for cut in range(2):
        value = table_right(both, *columns(cut))
        evens, odds = value[:ROWS], value[ROWS:] * alternating((ROWS, 256))
        plus = evens + odds
        minus = evens - odds
        for half in range(2):
            rows = slice(8 * half, 8 * (half + 1))
            for n in range(2):
                lanes = slice(128 * n, 128 * (n + 1))
                gsend[DEPTH * half + 4 + cut + 2 * n] = plus[rows, lanes]
                gsend[DEPTH * half + 3 - cut - 2 * n] = minus[rows, lanes]
        for k in range(4):
            send_field(True, depths[cut][k]).start()
        for k in range(1, 4):
            send_field(False, depths[cut][k]).start()
    for cut in range(2):
        pl.when(depths[cut][0] != d)(send_field(False, depths[cut][0]).start)

    gbuf[z] = gsend[z]
    pltpu.make_async_copy(gbuf.at[pl.ds(0, RING - 1)], gbuf.at[pl.ds(0, RING - 1)], gr).wait()
    totals = [gbuf[0], gbuf[1]]
    for other in range(2, RING):
        totals[other % 2] = totals[other % 2] + gbuf[other]
    total = jnp.concatenate(totals, axis=0)
    across = lax.broadcasted_iota(jnp.int32, (128, 128), 0) + lax.broadcasted_iota(jnp.int32, (128, 128), 1)
    reverse = jnp.where(across == 127, 1.0, 0.0).astype(BF16)
    high, rest = split(total)
    low = (total - high.astype(F32) - rest.astype(F32)).astype(BF16)
    turned = matmul(jnp.concatenate([high, rest, low], axis=0), reverse)
    turned = turned[:ROWS] + turned[ROWS : 2 * ROWS] + turned[2 * ROWS :]
    total = jnp.where(d < DEPTH // 2, turned, total)

    @pl.when(lower)
    def _():
        for row in range(ROWS):
            out_ref[ROWS - 1 - row : ROWS - row, :] = total[row : row + 1]

    @pl.when(jnp.logical_not(lower))
    def _():
        out_ref[...] = total

    for copy, there in zip(copies, has):
        pl.when(there)(copy.wait_send)
    pltpu.make_async_copy(csend.at[pl.ds(0, 2 * GROUP - 1)], csend.at[pl.ds(0, 2 * GROUP - 1)], cs).wait()
    pltpu.make_async_copy(xsend.at[pl.ds(0, 2 * GROUP - 1)], xsend.at[pl.ds(0, 2 * GROUP - 1)], xs).wait()
    pltpu.make_async_copy(gsend.at[pl.ds(0, RING - 1)], gsend.at[pl.ds(0, RING - 1)], gs).wait()


def solution(mesh):
    wide, mixed, tall = basis()

    def step(level_set, contrast):
        vmem = pl.BlockSpec(memory_space=pltpu.VMEM)
        anywhere = pl.BlockSpec(memory_space=pl.ANY)
        dma = pltpu.SemaphoreType.DMA
        return pl.pallas_call(
            kernel,
            out_shape=jax.ShapeDtypeStruct((ROWS, 128), F32),
            in_specs=[anywhere] * 5,
            out_specs=vmem,
            scratch_shapes=[
                pltpu.VMEM((2, ROWS, NX), F32),
                pltpu.SMEM((2,), F32),
                pltpu.VMEM((2, ROWS, NX), F32),
                pltpu.VMEM((2, ROWS, NX), F32),
                pltpu.VMEM((2, HALF, NX), BF16),
                pltpu.VMEM((2, HALF, NX), BF16),
                pltpu.VMEM((2, NX, HALF), BF16),
                pltpu.VMEM((2, ROWS, NX), F32),
                pltpu.VMEM((2, 16, 128), F32),
                pltpu.VMEM((2, 16, 128), F32),
                pltpu.VMEM((2 * GROUP, 8, 128), F32),
                pltpu.VMEM((2 * GROUP, 8, 128), F32),
                pltpu.VMEM((2, 128, NX), F32),
                pltpu.VMEM((64, NX), F32),
                pltpu.VMEM((128, NX), BF16),
                pltpu.VMEM((2 * GROUP, 4, 128), F32),
                pltpu.VMEM((2 * GROUP, 4, 128), F32),
                pltpu.VMEM((2 * ROWS, NX), F32),
                pltpu.VMEM((RING, 8, 128), F32),
                pltpu.VMEM((RING, 8, 128), F32),
                dma(()), dma(()), dma((2,)), dma((2,)), dma((2,)), dma((4,)), dma((4,)),
                dma(()), dma((2,)), dma(()), dma(()), dma(()), dma(()), pltpu.SemaphoreType.REGULAR((6,)),
            ],
            compiler_params=pltpu.CompilerParams(
                collective_id=0, has_side_effects=True, vmem_limit_bytes=55176 * 1024
            ),
        )(level_set, contrast, jnp.asarray(wide), jnp.asarray(mixed), jnp.asarray(tall))

    return jax.shard_map(
        step,
        mesh=mesh,
        in_specs=(P("depth", "plan", None), P("depth")),
        out_specs=P("plan", "depth"),
        check_vma=False,
    )
```

```python
import functools
import math

import jax
import jax.numpy as jnp
import ml_dtypes
import numpy as np
from jax import lax
from jax.experimental import pallas as pl
from jax.experimental.pallas import tpu as pltpu
from jax.sharding import PartitionSpec as P

MESH = pl.DeviceIdType.MESH
F32 = jnp.float32
BF16 = jnp.bfloat16

NX = 1024
HALF = NX // 2
LAYERS = 16
DEPTH = 8
PLAN = 64
ROWS = NX // PLAN
GROUP = 32
RING = 16
COEF = 2 * NX // GROUP
SHARE = COEF // 2

bend_weight = 0.5
grav_scale = 0.05
top_depth = 0.0
thickness = 1.0


def basis():
    j = np.arange(HALF, dtype=np.float64)[:, None] + 0.5
    v = np.arange(NX, dtype=np.float64)[None, :]
    table = np.cos(np.pi * v * j / NX)
    high = table.astype(ml_dtypes.bfloat16)
    low = (table - high.astype(np.float64)).astype(ml_dtypes.bfloat16)
    wide = np.stack([high, low])
    order = np.arange(HALF).reshape(GROUP, 2, ROWS // 2).transpose(1, 0, 2).reshape(-1)
    return wide, np.ascontiguousarray(wide[:, order]), np.ascontiguousarray(np.swapaxes(wide, 1, 2))


def alternating(shape):
    return 1.0 - 2.0 * lax.rem(lax.broadcasted_iota(jnp.int32, shape, 1), 2).astype(F32)


def flux(step):
    return step * lax.rsqrt(1.0 + step * step)


def flip(value, axis, size):
    index = lax.broadcasted_iota(jnp.int32, value.shape, axis)
    step = size // 2
    value = pltpu.roll(value, step, axis)
    while step > 1:
        step //= 2
        up = pltpu.roll(value, step, axis)
        down = pltpu.roll(value, size - step, axis)
        value = jnp.where((index & step) != 0, up, down)
    return value


def flip_lanes(value):
    blocks = value.shape[1] // 128
    parts = [flip(value[:, 128 * k : 128 * (k + 1)], 1, 128) for k in reversed(range(blocks))]
    return jnp.concatenate(parts, axis=1) if blocks > 1 else parts[0]


def split(value):
    high = value.astype(BF16)
    low = (value - high.astype(F32)).astype(BF16)
    return high, low


def matmul(a, b):
    return jnp.dot(a, b, preferred_element_type=F32)


def pair(value):
    return jnp.concatenate(split(value), axis=0)


def table_right(both, high_table, low_table):
    n = both.shape[0] // 2
    product = matmul(both, high_table)
    return product[:n] + product[n:] + matmul(both[:n], low_table)


def regroup(parts):
    lane = lax.broadcasted_iota(jnp.int32, parts[0].shape, 1)
    early, even = lane < 64, lax.rem(lane, 64) < 32
    wide = [jnp.where(early, parts[g], pltpu.roll(parts[g + 2], 64, 1)) for g in range(2)]
    wide += [jnp.where(early, pltpu.roll(parts[g], 64, 1), parts[g + 2]) for g in range(2)]
    out = []
    for first, second in (wide[:2], wide[2:]):
        out.append(jnp.where(even, first, pltpu.roll(second, 32, 1)))
        out.append(jnp.where(even, pltpu.roll(first, 96, 1), second))
    return out


def kernel(
    ls_hbm, con_hbm, wide_hbm, mixed_hbm, tall_hbm, out_ref,
    ls_ref, con_ref, own, part_density, wide, mixed, tall, zhalo, rsend, rhalo, csend, sbuf, rsp, acc, pst, xsend, cbuf, coefs, gsend, gbuf,
    ls_sem, con_sem, wide_sem, mixed_sem, tall_sem, hs, hr, cs, cr, xs, xr, gs, gr, news,
):
    d = lax.axis_index("depth")
    p = lax.axis_index("plan")
    core = lax.rem(p, 2)
    zh = lax.rem(lax.div(p, 2), 2)
    q = lax.div(p, 4) * 2 + core
    z = zh * DEPTH + d
    lower = p < PLAN // 2

    x, y = lax.div(p, 16), lax.rem(lax.div(p, 4), 4)
    kind_own, cut_own = lax.div(y, 2), lax.rem(x + y, 2)
    set_own = 2 * kind_own + cut_own
    coef_block = 8 * set_own + 2 * x + core
    parity = lax.rem(d, 2)
    mate = d + 1 - 2 * parity
    order = (2, 6, 4, 3, 7, 5, 1, 0)
    turns = [lax.rem(2 * x + core + k, 8) for k in order]
    places = [
        [16 * lax.div(t, 2) + 4 * lax.rem(lax.div(t, 2) + cut, 2) + 2 * zh + lax.rem(t, 2) for t in turns]
        for cut in range(2)
    ]

    def at_z(other):
        return (lax.rem(other, DEPTH), p + 2 * (lax.div(other, DEPTH) - zh))

    ls_copy = pltpu.make_async_copy(ls_hbm, ls_ref, ls_sem)
    con_copy = pltpu.make_async_copy(con_hbm, con_ref, con_sem)
    ls_copy.start()
    con_copy.start()
    wide_copies = [pltpu.make_async_copy(wide_hbm.at[n], wide.at[n], wide_sem.at[n]) for n in range(2)]
    mixed_copies = [pltpu.make_async_copy(mixed_hbm.at[n], mixed.at[n], mixed_sem.at[n]) for n in range(2)]
    tall_copies = [pltpu.make_async_copy(tall_hbm.at[n], tall.at[n], tall_sem.at[n]) for n in range(2)]
    for copy in wide_copies:
        copy.start()

    barrier = pltpu.get_barrier_semaphore()

    def greet(target):
        pl.semaphore_signal(barrier, inc=1, device_id=target, device_id_type=MESH)

    has = (d < DEPTH - 1, d > 0, p < PLAN - 1, p > 0)
    gets = (d > 0, d < DEPTH - 1, p > 0, p < PLAN - 1)
    outer = jnp.where(core == 0, p - 1, p + 1)
    has_outer = (outer >= 0) & (outer < PLAN)
    x_line = [(d, p + 16 * (lax.rem(x + k, 4) - x)) for k in (1, 3, 2)]
    y_line = [(d, p + 4 * (lax.rem(y + k, 4) - y)) for k in (1, 3, 2)]
    buddy = (d, p + 1 - 2 * core)

    def z_pair(k):
        return [at_z(lax.rem(z + away, RING)) for away in (k, RING - k)]

    for target in z_pair(1) + [buddy]:
        greet(target)
    pl.when(has_outer)(lambda: greet((d, outer)))
    for target in x_line + y_line:
        greet(target)

    def tell(number, targets):
        for target in targets:
            pl.semaphore_signal(news.at[number], inc=1, device_id=target, device_id_type=MESH)

    def hear(number, count):
        pl.semaphore_wait(news.at[number], count)

    ls_copy.wait()
    con_copy.wait()

    for layer in range(2):
        value = ls_ref[layer]
        value = jnp.where(lower, flip(value, 0, ROWS), value)
        own[layer, :, :HALF] = value[:, HALF:]
        own[layer, :, HALF:] = flip_lanes(value[:, :HALF])

    for layer in range(2):
        for k in range(8):
            spot = layer * 8 + k
            top = own[layer, 0:1, 128 * k : 128 * (k + 1)]
            bottom = own[layer, ROWS - 1 : ROWS, 128 * k : 128 * (k + 1)]
            rsend[0, spot : spot + 1, :] = jnp.where(lower, bottom, top)
            rsend[1, spot : spot + 1, :] = jnp.where(lower, top, bottom)

    pl.semaphore_wait(barrier, 9 + has_outer.astype(jnp.int32))

    def halo(source, target, number, device):
        return pltpu.make_async_remote_copy(
            src_ref=source, dst_ref=target, send_sem=hs.at[number], recv_sem=hr.at[number],
            device_id=device, device_id_type=MESH,
        )

    z_up = halo(own.at[1], zhalo.at[0], 0, (d + 1, p))
    z_down = halo(own.at[0], zhalo.at[1], 1, (d - 1, p))
    r_up = halo(rsend.at[1], rhalo.at[0], 2, (d, p + 1))
    r_down = halo(rsend.at[0], rhalo.at[1], 3, (d, p - 1))
    lands = (zhalo.at[0], zhalo.at[1], rhalo.at[0], rhalo.at[1])
    copies = (z_up, z_down, r_up, r_down)
    for copy, there in zip(copies, has):
        pl.when(there)(copy.start)
    tell(0, y_line)
    tell(1, z_pair(1))
    for copy in mixed_copies + tall_copies:
        copy.start()
    for land, comes in zip(lands, gets):

        @pl.when(jnp.logical_not(comes))
        def _(land=land):
            land[...] = jnp.zeros(land.shape, F32)

    row_id = lax.broadcasted_iota(jnp.int32, (ROWS, NX), 0)
    lane_id = lax.broadcasted_iota(jnp.int32, (ROWS, HALF), 1)
    field = [own[0], own[1]]
    middle = flux(field[1] - field[0])
    for layer in range(2):
        centre = field[layer]
        bend = -middle if layer else middle
        inner_flux = flux(pltpu.roll(centre, 1, 0) - centre)
        bend = bend + jnp.where(row_id == 0, 0.0, inner_flux)
        bend = bend - jnp.where(row_id == ROWS - 1, 0.0, pltpu.roll(inner_flux, ROWS - 1, 0))
        sides = centre[:, :HALF], centre[:, HALF:]
        across = []
        for side in range(2):
            here = sides[side]
            inside = jnp.where(lane_id == 0, sides[1 - side], pltpu.roll(here, 1, 1))
            inner_flux = flux(inside - here)
            outside = jnp.where(lane_id == HALF - 1, flux(here), pltpu.roll(inner_flux, HALF - 1, 1))
            across.append(inner_flux - outside)
        bend = bend + jnp.concatenate(across, axis=1)
        part_density[layer] = con_ref[layer] * (0.5 * (1.0 + jnp.tanh(centre))) + bend_weight * bend

    hear(0, 3)
    tell(2, [buddy])

    def respond(start):
        row = lax.broadcasted_iota(jnp.int32, (64, 128), 0)
        col = lax.broadcasted_iota(jnp.int32, (64, 128), 1) + start
        place = lax.rem(coef_block, GROUP // 2) * COEF + parity * SHARE + lax.rem(row, SHARE)
        v = jnp.where(kind_own == 1, NX - place, place).astype(F32)
        u = jnp.where(row >= SHARE, NX - col, col).astype(F32)
        scale = 2.0 * math.pi * grav_scale * thickness / (4.0 * NX * NX)
        weight = jnp.where(place == 0, scale, 2.0 * scale) * jnp.where(col == 0, 1.0, 2.0)
        kappa = jnp.sqrt(u * u + v * v) * (2.0 * math.pi / (2 * NX))
        next_layer = jnp.exp(-thickness * kappa)
        for cross, depth in enumerate((d, mate)):
            top = top_depth + (2.0 * depth.astype(F32) + 0.5) * thickness
            first = jnp.exp(-top * kappa) * weight
            second = first * next_layer
            for n, value in enumerate((first[:SHARE], second[:SHARE], first[SHARE:], second[SHARE:])):
                rsp[cross, SHARE * n : SHARE * (n + 1), start : start + 128] = value

    for k in range(NX // 128):
        respond(128 * k)

    hear(2, 1)
    hear(1, 2)
    tell(3, [(mate, p)])
    for layer in range(2):
        pl.when(gets[layer])(copies[layer].wait_recv)
    for layer in range(2):
        part_density[layer] += bend_weight * flux(zhalo[layer] - own[layer])
    for number in (2, 3):
        pl.when(gets[number])(copies[number].wait_recv)
    even, odd = [], []
    for layer in range(2):
        centre = own[layer]
        here = slice(layer * 8, layer * 8 + 8)
        top = jnp.where(lower, rhalo[1, here, :], rhalo[0, here, :])
        bottom = jnp.where(lower, rhalo[0, here, :], rhalo[1, here, :])
        tops = [jnp.broadcast_to(top[k : k + 1], (ROWS, 128)) for k in range(8)]
        bottoms = [jnp.broadcast_to(bottom[k : k + 1], (ROWS, 128)) for k in range(8)]
        beside = jnp.where(row_id == 0, jnp.concatenate(tops, axis=1), jnp.concatenate(bottoms, axis=1))
        outer_rows = (row_id == 0) | (row_id == ROWS - 1)
        density = part_density[layer] + jnp.where(outer_rows, bend_weight * flux(beside - centre), 0.0)
        even.append(density[:, :HALF] + density[:, HALF:])
        odd.append((density[:, :HALF] - density[:, HALF:]) * alternating((ROWS, HALF)))

    block = jnp.where(lower, PLAN // 2 - 1 - p, p - PLAN // 2)
    hear(3, 1)
    tell(4, z_pair(2))
    for copy in wide_copies:
        copy.wait()

    def send_coef(group, k, cross):
        member = 1 - parity if cross else parity
        return pltpu.make_async_remote_copy(
            src_ref=csend.at[2 * (8 * group + turns[k]) + member], dst_ref=sbuf.at[GROUP * cross + block],
            send_sem=cs, recv_sem=cr.at[cross],
            device_id=(mate if cross else d, 8 * (group // 2) + places[group % 2][k]), device_id_type=MESH,
        )

    both = pair(jnp.concatenate(even + odd, axis=0))
    for cut in range(2):
        cols = slice(HALF * cut, HALF * (cut + 1))
        coef = table_right(both, wide[0, :, cols], wide[1, :, cols])
        for kind in range(2):
            start = kind * 16 + 8 * cut
            for m in range(4):
                lanes = slice(128 * m, 128 * (m + 1))
                starts = [2 * ROWS * kind + ROWS * layer + 8 * half for half in range(2) for layer in range(2)]
                for t, value in enumerate(regroup([coef[n : n + 8, lanes] for n in starts])):
                    csend[2 * start + 4 * m + t] = value
        for k in range(7):
            for kind in range(2):
                send_coef(2 * kind + cut, k, 0).start()
    for group in range(4):
        pl.when(group != set_own)(send_coef(group, 7, 0).start)
    for k in range(8):
        for group in range(4):
            send_coef(group, k, 1).start()

    hear(4, 2)
    tell(5, z_pair(4))
    sbuf[block] = csend[2 * coef_block + parity]
    for copy in mixed_copies + tall_copies:
        copy.wait()
    side = lax.rem(lax.div(lax.broadcasted_iota(jnp.int32, (64, HALF), 1), 16), 2)
    sign = jnp.where(side == zh, 1.0, -1.0) * alternating((64, HALF))
    step = 256
    for cross in range(2):
        landed = sbuf.at[pl.ds(GROUP * cross, GROUP - 1 + cross)]
        pltpu.make_async_copy(landed, landed, cr.at[cross]).wait()
        value = sbuf[GROUP * cross : GROUP * (cross + 1)].reshape(HALF // 2, 128).T
        value = jnp.concatenate([value[:64], value[64:]], axis=1)
        both = pair(jnp.concatenate([value, value * sign], axis=0))
        for k in range(NX // step):
            here = slice(k * step, (k + 1) * step)
            coef = table_right(both, mixed[0, :, here], mixed[1, :, here]) * rsp[cross, :, here]
            parts = [coef[SHARE * n : SHARE * (n + 1)] for n in range(4)]
            coef = jnp.concatenate([parts[0] + parts[1], parts[2] + parts[3]], axis=0)
            if cross:
                pst[:, here] = pair(coef + acc[:, here])
            else:
                acc[:, here] = coef

    low = 2 * lax.rem(y, 2) + core
    x_turns = [lax.rem(x + k, 4) for k in range(4)]
    low_turns = [lax.rem(low + k, 4) for k in range(4)]
    low_places = [4 * lax.div(t, 2) + lax.rem(t, 2) + 2 * zh for t in low_turns]

    def send_rows(part, r, k, cross):
        upper = lax.div(x_turns[r], 2)
        upper = upper if part else 1 - upper
        member = 1 - parity if cross else parity
        return pltpu.make_async_remote_copy(
            src_ref=xsend.at[2 * (8 * x_turns[r] + 4 * upper + low_turns[k]) + member],
            dst_ref=cbuf.at[2 * coef_block + parity], send_sem=xs, recv_sem=xr,
            device_id=(mate if cross else d, 16 * x_turns[r] + 8 * upper + low_places[k]), device_id_type=MESH,
        )

    lane = lax.broadcasted_iota(jnp.int32, (8, 128), 1)
    early, even_lane = lane < 64, lax.rem(lane, 64) < 32
    def columns(part):
        cols = slice(128 * part, 128 * part + 128), slice(128 * part + 256, 128 * part + 384)
        return [jnp.concatenate([tall[n, :, col] for col in cols], axis=1) for n in range(2)]

    for part in range(2):
        value = table_right(pst[...], *columns(part))
        evens, odds = value[:SHARE], value[SHARE:] * alternating((SHARE, 256))
        plus, minus = evens + odds, evens - odds
        value = jnp.concatenate([plus, minus, plus, minus], axis=0).T
        for g in range(4):
            chunk = 2 * part + 4 * (g // 2) + g % 2
            for member in range(2):
                ups, downs = [], []
                for n in range(4):
                    start = ROWS * (4 * g + n) + 8 * member
                    rows = value[start : start + 8]
                    later = pltpu.roll(rows, 4, 0)
                    ups.append(jnp.where(even_lane, rows, pltpu.roll(later, 32, 1)))
                    downs.append(jnp.where(even_lane, pltpu.roll(rows, 32, 1), later))
                for spot, one, two in (
                    (2 * (8 + chunk), ups[0], ups[2]),
                    (2 * (8 + chunk) + 1, ups[1], ups[3]),
                    (2 * (7 - chunk), downs[3], downs[1]),
                    (2 * (7 - chunk) + 1, downs[2], downs[0]),
                ):
                    xsend[2 * spot + member] = jnp.where(early, one, two)[:4]

        for r in (1, 3, 2, 0):
            for k in range(4):
                send_rows(part, r, k, 1).start()
                if r or k:
                    send_rows(part, r, k, 0).start()
    upper_own = lax.rem(lax.div(x, 2) + lax.div(y, 2), 2)
    pl.when(upper_own == 0)(send_rows(0, 0, 0, 0).start)
    pl.when(upper_own == 1)(send_rows(1, 0, 0, 0).start)

    hear(5, 2)
    cbuf[2 * coef_block + parity] = xsend[2 * q + parity]
    landed = cbuf.at[pl.ds(0, 2 * GROUP - 1)]
    pltpu.make_async_copy(landed, landed, xr).wait()

    def send_field(far, depth):
        row = 1 - zh if far else zh
        return pltpu.make_async_remote_copy(
            src_ref=gsend.at[DEPTH * row + depth], dst_ref=gbuf.at[z], send_sem=gs, recv_sem=gr,
            device_id=(depth, p + 2 - 4 * zh if far else p), device_id_type=MESH,
        )

    steps = [lax.rem(lax.div(d, 2) + k, 4) for k in range(4)]
    depths = ([2 * t + 1 - lax.div(t, 2) for t in steps], [2 * t + lax.div(t, 2) for t in steps])

    for m in range(2 * NX // 128):
        parts = regroup([cbuf[4 * m + t] for t in range(4)])
        lanes = slice(128 * (m % 8), 128 * (m % 8 + 1))
        for g in range(4):
            start = ROWS * (m // 8) + 4 * g
            coefs[start : start + 4, lanes] = parts[g]
    both = pair(coefs[...])
    for cut in range(2):
        value = table_right(both, *columns(cut))
        evens, odds = value[:ROWS], value[ROWS:] * alternating((ROWS, 256))
        plus = evens + odds
        minus = evens - odds
        for half in range(2):
            rows = slice(8 * half, 8 * (half + 1))
            for n in range(2):
                lanes = slice(128 * n, 128 * (n + 1))
                gsend[DEPTH * half + 4 + cut + 2 * n] = plus[rows, lanes]
                gsend[DEPTH * half + 3 - cut - 2 * n] = minus[rows, lanes]
        for k in range(4):
            send_field(True, depths[cut][k]).start()
        for k in range(1, 4):
            send_field(False, depths[cut][k]).start()
    for cut in range(2):
        pl.when(depths[cut][0] != d)(send_field(False, depths[cut][0]).start)

    gbuf[z] = gsend[z]
    pltpu.make_async_copy(gbuf.at[pl.ds(0, RING - 1)], gbuf.at[pl.ds(0, RING - 1)], gr).wait()
    totals = [gbuf[0], gbuf[1]]
    for other in range(2, RING):
        totals[other % 2] = totals[other % 2] + gbuf[other]
    total = jnp.concatenate(totals, axis=0)
    across = lax.broadcasted_iota(jnp.int32, (128, 128), 0) + lax.broadcasted_iota(jnp.int32, (128, 128), 1)
    reverse = jnp.where(across == 127, 1.0, 0.0).astype(BF16)
    high, rest = split(total)
    low = (total - high.astype(F32) - rest.astype(F32)).astype(BF16)
    turned = matmul(jnp.concatenate([high, rest, low], axis=0), reverse)
    turned = turned[:ROWS] + turned[ROWS : 2 * ROWS] + turned[2 * ROWS :]
    total = jnp.where(d < DEPTH // 2, turned, total)

    @pl.when(lower)
    def _():
        for row in range(ROWS):
            out_ref[ROWS - 1 - row : ROWS - row, :] = total[row : row + 1]

    @pl.when(jnp.logical_not(lower))
    def _():
        out_ref[...] = total

    for copy, there in zip(copies, has):
        pl.when(there)(copy.wait_send)
    pltpu.make_async_copy(csend.at[pl.ds(0, 2 * GROUP - 1)], csend.at[pl.ds(0, 2 * GROUP - 1)], cs).wait()
    pltpu.make_async_copy(xsend.at[pl.ds(0, 2 * GROUP - 1)], xsend.at[pl.ds(0, 2 * GROUP - 1)], xs).wait()
    pltpu.make_async_copy(gsend.at[pl.ds(0, RING - 1)], gsend.at[pl.ds(0, RING - 1)], gs).wait()


def solution(mesh):
    wide, mixed, tall = basis()

    def step(level_set, contrast):
        vmem = pl.BlockSpec(memory_space=pltpu.VMEM)
        anywhere = pl.BlockSpec(memory_space=pl.ANY)
        dma = pltpu.SemaphoreType.DMA
        return pl.pallas_call(
            kernel,
            out_shape=jax.ShapeDtypeStruct((ROWS, 128), F32),
            in_specs=[anywhere] * 5,
            out_specs=vmem,
            scratch_shapes=[
                pltpu.VMEM((2, ROWS, NX), F32),
                pltpu.SMEM((2,), F32),
                pltpu.VMEM((2, ROWS, NX), F32),
                pltpu.VMEM((2, ROWS, NX), F32),
                pltpu.VMEM((2, HALF, NX), BF16),
                pltpu.VMEM((2, HALF, NX), BF16),
                pltpu.VMEM((2, NX, HALF), BF16),
                pltpu.VMEM((2, ROWS, NX), F32),
                pltpu.VMEM((2, 16, 128), F32),
                pltpu.VMEM((2, 16, 128), F32),
                pltpu.VMEM((2 * GROUP, 8, 128), F32),
                pltpu.VMEM((2 * GROUP, 8, 128), F32),
                pltpu.VMEM((2, 128, NX), F32),
                pltpu.VMEM((64, NX), F32),
                pltpu.VMEM((128, NX), BF16),
                pltpu.VMEM((2 * GROUP, 4, 128), F32),
                pltpu.VMEM((2 * GROUP, 4, 128), F32),
                pltpu.VMEM((2 * ROWS, NX), F32),
                pltpu.VMEM((RING, 8, 128), F32),
                pltpu.VMEM((RING, 8, 128), F32),
                dma(()), dma(()), dma((2,)), dma((2,)), dma((2,)), dma((4,)), dma((4,)),
                dma(()), dma((2,)), dma(()), dma(()), dma(()), dma(()), pltpu.SemaphoreType.REGULAR((6,)),
            ],
            compiler_params=pltpu.CompilerParams(
                collective_id=0, has_side_effects=True, vmem_limit_bytes=55176 * 1024
            ),
        )(level_set, contrast, jnp.asarray(wide), jnp.asarray(mixed), jnp.asarray(tall))

    return jax.shard_map(
        step,
        mesh=mesh,
        in_specs=(P("depth", "plan", None), P("depth")),
        out_specs=P("plan", "depth"),
        check_vma=False,
    )
```

```python
import functools
import math

import jax
import jax.numpy as jnp
import ml_dtypes
import numpy as np
from jax import lax
from jax.experimental import pallas as pl
from jax.experimental.pallas import tpu as pltpu
from jax.sharding import PartitionSpec as P

MESH = pl.DeviceIdType.MESH
F32 = jnp.float32
BF16 = jnp.bfloat16

NX = 1024
HALF = NX // 2
LAYERS = 16
DEPTH = 8
PLAN = 64
ROWS = NX // PLAN
GROUP = 32
RING = 16
COEF = 2 * NX // GROUP
SHARE = COEF // 2

bend_weight = 0.5
grav_scale = 0.05
top_depth = 0.0
thickness = 1.0


def basis():
    j = np.arange(HALF, dtype=np.float64)[:, None] + 0.5
    v = np.arange(NX, dtype=np.float64)[None, :]
    table = np.cos(np.pi * v * j / NX)
    high = table.astype(ml_dtypes.bfloat16)
    low = (table - high.astype(np.float64)).astype(ml_dtypes.bfloat16)
    wide = np.stack([high, low])
    order = np.arange(HALF).reshape(GROUP, 2, ROWS // 2).transpose(1, 0, 2).reshape(-1)
    return wide, np.ascontiguousarray(wide[:, order]), np.ascontiguousarray(np.swapaxes(wide, 1, 2))


def alternating(shape):
    return 1.0 - 2.0 * lax.rem(lax.broadcasted_iota(jnp.int32, shape, 1), 2).astype(F32)


def flux(step):
    return step * lax.rsqrt(1.0 + step * step)


def flip(value, axis, size):
    index = lax.broadcasted_iota(jnp.int32, value.shape, axis)
    step = size // 2
    value = pltpu.roll(value, step, axis)
    while step > 1:
        step //= 2
        up = pltpu.roll(value, step, axis)
        down = pltpu.roll(value, size - step, axis)
        value = jnp.where((index & step) != 0, up, down)
    return value


def flip_lanes(value):
    blocks = value.shape[1] // 128
    parts = [flip(value[:, 128 * k : 128 * (k + 1)], 1, 128) for k in reversed(range(blocks))]
    return jnp.concatenate(parts, axis=1) if blocks > 1 else parts[0]


def split(value):
    high = value.astype(BF16)
    low = (value - high.astype(F32)).astype(BF16)
    return high, low


def matmul(a, b):
    return jnp.dot(a, b, preferred_element_type=F32)


def pair(value):
    return jnp.concatenate(split(value), axis=0)


def table_right(both, high_table, low_table):
    n = both.shape[0] // 2
    product = matmul(both, high_table)
    return product[:n] + product[n:] + matmul(both[:n], low_table)


def regroup(parts):
    lane = lax.broadcasted_iota(jnp.int32, parts[0].shape, 1)
    early, even = lane < 64, lax.rem(lane, 64) < 32
    wide = [jnp.where(early, parts[g], pltpu.roll(parts[g + 2], 64, 1)) for g in range(2)]
    wide += [jnp.where(early, pltpu.roll(parts[g], 64, 1), parts[g + 2]) for g in range(2)]
    out = []
    for first, second in (wide[:2], wide[2:]):
        out.append(jnp.where(even, first, pltpu.roll(second, 32, 1)))
        out.append(jnp.where(even, pltpu.roll(first, 96, 1), second))
    return out


def kernel(
    ls_hbm, con_hbm, wide_hbm, mixed_hbm, tall_hbm, out_ref,
    ls_ref, con_ref, own, part_density, wide, mixed, tall, zhalo, rsend, rhalo, csend, sbuf, rsp, pst, xsend, cbuf, coefs, gsend, gbuf,
    ls_sem, con_sem, wide_sem, mixed_sem, tall_sem, hs, hr, cs, cr, xs, xr, gs, gr, news,
):
    d = lax.axis_index("depth")
    p = lax.axis_index("plan")
    core = lax.rem(p, 2)
    zh = lax.rem(lax.div(p, 2), 2)
    q = lax.div(p, 4) * 2 + core
    z = zh * DEPTH + d
    lower = p < PLAN // 2

    x, y = lax.div(p, 16), lax.rem(lax.div(p, 4), 4)
    kind_own, cut_own = lax.div(y, 2), lax.rem(x + y, 2)
    set_own = 2 * kind_own + cut_own
    coef_block = 8 * set_own + 2 * x + core
    parity = lax.rem(d, 2)
    mate = d + 1 - 2 * parity
    order = (2, 6, 4, 3, 7, 5, 1, 0)
    turns = [lax.rem(2 * x + core + k, 8) for k in order]
    places = [
        [16 * lax.div(t, 2) + 4 * lax.rem(lax.div(t, 2) + cut, 2) + 2 * zh + lax.rem(t, 2) for t in turns]
        for cut in range(2)
    ]

    def at_z(other):
        return (lax.rem(other, DEPTH), p + 2 * (lax.div(other, DEPTH) - zh))

    ls_copy = pltpu.make_async_copy(ls_hbm, ls_ref, ls_sem)
    con_copy = pltpu.make_async_copy(con_hbm, con_ref, con_sem)
    ls_copy.start()
    con_copy.start()
    wide_copies = [pltpu.make_async_copy(wide_hbm.at[n], wide.at[n], wide_sem.at[n]) for n in range(2)]
    mixed_copies = [pltpu.make_async_copy(mixed_hbm.at[n], mixed.at[n], mixed_sem.at[n]) for n in range(2)]
    tall_copies = [pltpu.make_async_copy(tall_hbm.at[n], tall.at[n], tall_sem.at[n]) for n in range(2)]
    for copy in wide_copies:
        copy.start()

    barrier = pltpu.get_barrier_semaphore()

    def greet(target):
        pl.semaphore_signal(barrier, inc=1, device_id=target, device_id_type=MESH)

    has = (d < DEPTH - 1, d > 0, p < PLAN - 1, p > 0)
    gets = (d > 0, d < DEPTH - 1, p > 0, p < PLAN - 1)
    outer = jnp.where(core == 0, p - 1, p + 1)
    has_outer = (outer >= 0) & (outer < PLAN)
    x_line = [(d, p + 16 * (lax.rem(x + k, 4) - x)) for k in (1, 3, 2)]
    y_line = [(d, p + 4 * (lax.rem(y + k, 4) - y)) for k in (1, 3, 2)]
    buddy = (d, p + 1 - 2 * core)

    def z_pair(k):
        return [at_z(lax.rem(z + away, RING)) for away in (k, RING - k)]

    for target in z_pair(1) + [buddy]:
        greet(target)
    pl.when(has_outer)(lambda: greet((d, outer)))
    for target in x_line + y_line:
        greet(target)

    def tell(number, targets):
        for target in targets:
            pl.semaphore_signal(news.at[number], inc=1, device_id=target, device_id_type=MESH)

    def hear(number, count):
        pl.semaphore_wait(news.at[number], count)

    ls_copy.wait()
    con_copy.wait()

    for layer in range(2):
        value = ls_ref[layer]
        value = jnp.where(lower, flip(value, 0, ROWS), value)
        own[layer, :, :HALF] = value[:, HALF:]
        own[layer, :, HALF:] = flip_lanes(value[:, :HALF])

    for layer in range(2):
        for k in range(8):
            spot = layer * 8 + k
            top = own[layer, 0:1, 128 * k : 128 * (k + 1)]
            bottom = own[layer, ROWS - 1 : ROWS, 128 * k : 128 * (k + 1)]
            rsend[0, spot : spot + 1, :] = jnp.where(lower, bottom, top)
            rsend[1, spot : spot + 1, :] = jnp.where(lower, top, bottom)

    pl.semaphore_wait(barrier, 9 + has_outer.astype(jnp.int32))

    def halo(source, target, number, device):
        return pltpu.make_async_remote_copy(
            src_ref=source, dst_ref=target, send_sem=hs.at[number], recv_sem=hr.at[number],
            device_id=device, device_id_type=MESH,
        )

    z_up = halo(own.at[1], zhalo.at[0], 0, (d + 1, p))
    z_down = halo(own.at[0], zhalo.at[1], 1, (d - 1, p))
    r_up = halo(rsend.at[1], rhalo.at[0], 2, (d, p + 1))
    r_down = halo(rsend.at[0], rhalo.at[1], 3, (d, p - 1))
    lands = (zhalo.at[0], zhalo.at[1], rhalo.at[0], rhalo.at[1])
    copies = (z_up, z_down, r_up, r_down)
    for copy, there in zip(copies, has):
        pl.when(there)(copy.start)
    tell(0, y_line)
    tell(1, z_pair(1))
    for copy in mixed_copies + tall_copies:
        copy.start()
    for land, comes in zip(lands, gets):

        @pl.when(jnp.logical_not(comes))
        def _(land=land):
            land[...] = jnp.zeros(land.shape, F32)

    row_id = lax.broadcasted_iota(jnp.int32, (ROWS, NX), 0)
    lane_id = lax.broadcasted_iota(jnp.int32, (ROWS, HALF), 1)
    field = [own[0], own[1]]
    middle = flux(field[1] - field[0])
    for layer in range(2):
        centre = field[layer]
        bend = -middle if layer else middle
        inner_flux = flux(pltpu.roll(centre, 1, 0) - centre)
        bend = bend + jnp.where(row_id == 0, 0.0, inner_flux)
        bend = bend - jnp.where(row_id == ROWS - 1, 0.0, pltpu.roll(inner_flux, ROWS - 1, 0))
        sides = centre[:, :HALF], centre[:, HALF:]
        across = []
        for side in range(2):
            here = sides[side]
            inside = jnp.where(lane_id == 0, sides[1 - side], pltpu.roll(here, 1, 1))
            inner_flux = flux(inside - here)
            outside = jnp.where(lane_id == HALF - 1, flux(here), pltpu.roll(inner_flux, HALF - 1, 1))
            across.append(inner_flux - outside)
        bend = bend + jnp.concatenate(across, axis=1)
        part_density[layer] = con_ref[layer] * (0.5 * (1.0 + jnp.tanh(centre))) + bend_weight * bend

    hear(0, 3)
    tell(2, [buddy])

    def respond(start):
        row = lax.broadcasted_iota(jnp.int32, (64, 128), 0)
        col = lax.broadcasted_iota(jnp.int32, (64, 128), 1) + start
        place = lax.rem(coef_block, GROUP // 2) * COEF + parity * SHARE + lax.rem(row, SHARE)
        v = jnp.where(kind_own == 1, NX - place, place).astype(F32)
        u = jnp.where(row >= SHARE, NX - col, col).astype(F32)
        scale = 2.0 * math.pi * grav_scale * thickness / (4.0 * NX * NX)
        weight = jnp.where(place == 0, scale, 2.0 * scale) * jnp.where(col == 0, 1.0, 2.0)
        kappa = jnp.sqrt(u * u + v * v) * (2.0 * math.pi / (2 * NX))
        next_layer = jnp.exp(-thickness * kappa)
        for cross, depth in enumerate((d, mate)):
            top = top_depth + (2.0 * depth.astype(F32) + 0.5) * thickness
            first = jnp.exp(-top * kappa) * weight
            second = first * next_layer
            for n, value in enumerate((first[:SHARE], second[:SHARE], first[SHARE:], second[SHARE:])):
                rsp[cross, SHARE * n : SHARE * (n + 1), start : start + 128] = value

    for k in range(NX // 128):
        respond(128 * k)

    for layer in range(2):
        pl.when(gets[layer])(copies[layer].wait_recv)
    for layer in range(2):
        part_density[layer] += bend_weight * flux(zhalo[layer] - own[layer])
    for number in (2, 3):
        pl.when(gets[number])(copies[number].wait_recv)
    even, odd = [], []
    for layer in range(2):
        centre = own[layer]
        here = slice(layer * 8, layer * 8 + 8)
        top = jnp.where(lower, rhalo[1, here, :], rhalo[0, here, :])
        bottom = jnp.where(lower, rhalo[0, here, :], rhalo[1, here, :])
        tops = [jnp.broadcast_to(top[k : k + 1], (ROWS, 128)) for k in range(8)]
        bottoms = [jnp.broadcast_to(bottom[k : k + 1], (ROWS, 128)) for k in range(8)]
        beside = jnp.where(row_id == 0, jnp.concatenate(tops, axis=1), jnp.concatenate(bottoms, axis=1))
        outer_rows = (row_id == 0) | (row_id == ROWS - 1)
        density = part_density[layer] + jnp.where(outer_rows, bend_weight * flux(beside - centre), 0.0)
        even.append(density[:, :HALF] + density[:, HALF:])
        odd.append((density[:, :HALF] - density[:, HALF:]) * alternating((ROWS, HALF)))

    block = jnp.where(lower, PLAN // 2 - 1 - p, p - PLAN // 2)
    hear(2, 1)
    hear(1, 2)
    tell(3, [(mate, p)])
    for copy in wide_copies:
        copy.wait()

    def send_coef(group, k, cross):
        member = 1 - parity if cross else parity
        return pltpu.make_async_remote_copy(
            src_ref=csend.at[2 * (8 * group + turns[k]) + member], dst_ref=sbuf.at[GROUP * cross + block],
            send_sem=cs, recv_sem=cr.at[cross],
            device_id=(mate if cross else d, 8 * (group // 2) + places[group % 2][k]), device_id_type=MESH,
        )

    both = pair(jnp.concatenate(even + odd, axis=0))
    for cut in range(2):
        cols = slice(HALF * cut, HALF * (cut + 1))
        coef = table_right(both, wide[0, :, cols], wide[1, :, cols])
        for kind in range(2):
            start = kind * 16 + 8 * cut
            for m in range(4):
                lanes = slice(128 * m, 128 * (m + 1))
                starts = [2 * ROWS * kind + ROWS * layer + 8 * half for half in range(2) for layer in range(2)]
                for t, value in enumerate(regroup([coef[n : n + 8, lanes] for n in starts])):
                    csend[2 * start + 4 * m + t] = value
        for k in range(7):
            for kind in range(2):
                send_coef(2 * kind + cut, k, 0).start()
    for group in range(4):
        pl.when(group != set_own)(send_coef(group, 7, 0).start)
    hear(3, 1)
    tell(4, z_pair(2))
    for k in range(8):
        for group in range(4):
            send_coef(group, k, 1).start()

    hear(4, 2)
    tell(5, z_pair(4))
    sbuf[block] = csend[2 * coef_block + parity]
    for copy in mixed_copies + tall_copies:
        copy.wait()
    side = lax.rem(lax.div(lax.broadcasted_iota(jnp.int32, (64, HALF), 1), 16), 2)
    sign = jnp.where(side == zh, 1.0, -1.0) * alternating((64, HALF))
    step = 256
    values = []
    for cross in range(2):
        landed = sbuf.at[pl.ds(GROUP * cross, GROUP - 1 + cross)]
        pltpu.make_async_copy(landed, landed, cr.at[cross]).wait()
        value = sbuf[GROUP * cross : GROUP * (cross + 1)].reshape(HALF // 2, 128).T
        value = jnp.concatenate([value[:64], value[64:]], axis=1)
        values += [value, value * sign]
    both = pair(jnp.concatenate(values, axis=0))
    for k in range(NX // step):
        here = slice(k * step, (k + 1) * step)
        coef = table_right(both, mixed[0, :, here], mixed[1, :, here])
        coef = coef * jnp.concatenate([rsp[0, :, here], rsp[1, :, here]], axis=0)
        parts = [coef[SHARE * n : SHARE * (n + 1)] for n in range(8)]
        cosine = (parts[0] + parts[1]) + (parts[4] + parts[5])
        sine = (parts[2] + parts[3]) + (parts[6] + parts[7])
        pst[:, here] = pair(jnp.concatenate([cosine, sine], axis=0))

    low = 2 * lax.rem(y, 2) + core
    x_turns = [lax.rem(x + k, 4) for k in range(4)]
    low_turns = [lax.rem(low + k, 4) for k in range(4)]
    low_places = [4 * lax.div(t, 2) + lax.rem(t, 2) + 2 * zh for t in low_turns]

    def send_rows(part, r, k, cross):
        upper = lax.div(x_turns[r], 2)
        upper = upper if part else 1 - upper
        member = 1 - parity if cross else parity
        return pltpu.make_async_remote_copy(
            src_ref=xsend.at[2 * (8 * x_turns[r] + 4 * upper + low_turns[k]) + member],
            dst_ref=cbuf.at[2 * coef_block + parity], send_sem=xs, recv_sem=xr,
            device_id=(mate if cross else d, 16 * x_turns[r] + 8 * upper + low_places[k]), device_id_type=MESH,
        )

    lane = lax.broadcasted_iota(jnp.int32, (8, 128), 1)
    early, even_lane = lane < 64, lax.rem(lane, 64) < 32
    def columns(part):
        cols = slice(128 * part, 128 * part + 128), slice(128 * part + 256, 128 * part + 384)
        return [jnp.concatenate([tall[n, :, col] for col in cols], axis=1) for n in range(2)]

    for part in range(2):
        value = table_right(pst[...], *columns(part))
        evens, odds = value[:SHARE], value[SHARE:] * alternating((SHARE, 256))
        plus, minus = evens + odds, evens - odds
        value = jnp.concatenate([plus, minus, plus, minus], axis=0).T
        for g in range(4):
            chunk = 2 * part + 4 * (g // 2) + g % 2
            for member in range(2):
                ups, downs = [], []
                for n in range(4):
                    start = ROWS * (4 * g + n) + 8 * member
                    rows = value[start : start + 8]
                    later = pltpu.roll(rows, 4, 0)
                    ups.append(jnp.where(even_lane, rows, pltpu.roll(later, 32, 1)))
                    downs.append(jnp.where(even_lane, pltpu.roll(rows, 32, 1), later))
                for spot, one, two in (
                    (2 * (8 + chunk), ups[0], ups[2]),
                    (2 * (8 + chunk) + 1, ups[1], ups[3]),
                    (2 * (7 - chunk), downs[3], downs[1]),
                    (2 * (7 - chunk) + 1, downs[2], downs[0]),
                ):
                    xsend[2 * spot + member] = jnp.where(early, one, two)[:4]

        for r in (1, 3, 2, 0):
            for k in range(4):
                send_rows(part, r, k, 1).start()
                if r or k:
                    send_rows(part, r, k, 0).start()
    upper_own = lax.rem(lax.div(x, 2) + lax.div(y, 2), 2)
    pl.when(upper_own == 0)(send_rows(0, 0, 0, 0).start)
    pl.when(upper_own == 1)(send_rows(1, 0, 0, 0).start)

    hear(5, 2)
    cbuf[2 * coef_block + parity] = xsend[2 * q + parity]
    landed = cbuf.at[pl.ds(0, 2 * GROUP - 1)]
    pltpu.make_async_copy(landed, landed, xr).wait()

    def send_field(far, depth):
        row = 1 - zh if far else zh
        return pltpu.make_async_remote_copy(
            src_ref=gsend.at[DEPTH * row + depth], dst_ref=gbuf.at[z], send_sem=gs, recv_sem=gr,
            device_id=(depth, p + 2 - 4 * zh if far else p), device_id_type=MESH,
        )

    steps = [lax.rem(lax.div(d, 2) + k, 4) for k in range(4)]
    depths = ([2 * t + 1 - lax.div(t, 2) for t in steps], [2 * t + lax.div(t, 2) for t in steps])

    for m in range(2 * NX // 128):
        parts = regroup([cbuf[4 * m + t] for t in range(4)])
        lanes = slice(128 * (m % 8), 128 * (m % 8 + 1))
        for g in range(4):
            start = ROWS * (m // 8) + 4 * g
            coefs[start : start + 4, lanes] = parts[g]
    both = pair(coefs[...])
    for cut in range(2):
        value = table_right(both, *columns(cut))
        evens, odds = value[:ROWS], value[ROWS:] * alternating((ROWS, 256))
        plus = evens + odds
        minus = evens - odds
        for half in range(2):
            rows = slice(8 * half, 8 * (half + 1))
            for n in range(2):
                lanes = slice(128 * n, 128 * (n + 1))
                gsend[DEPTH * half + 4 + cut + 2 * n] = plus[rows, lanes]
                gsend[DEPTH * half + 3 - cut - 2 * n] = minus[rows, lanes]
        for k in range(4):
            send_field(True, depths[cut][k]).start()
        for k in range(1, 4):
            send_field(False, depths[cut][k]).start()
    for cut in range(2):
        pl.when(depths[cut][0] != d)(send_field(False, depths[cut][0]).start)

    gbuf[z] = gsend[z]
    pltpu.make_async_copy(gbuf.at[pl.ds(0, RING - 1)], gbuf.at[pl.ds(0, RING - 1)], gr).wait()
    totals = [gbuf[0], gbuf[1]]
    for other in range(2, RING):
        totals[other % 2] = totals[other % 2] + gbuf[other]
    total = jnp.concatenate(totals, axis=0)
    across = lax.broadcasted_iota(jnp.int32, (128, 128), 0) + lax.broadcasted_iota(jnp.int32, (128, 128), 1)
    reverse = jnp.where(across == 127, 1.0, 0.0).astype(BF16)
    high, rest = split(total)
    low = (total - high.astype(F32) - rest.astype(F32)).astype(BF16)
    turned = matmul(jnp.concatenate([high, rest, low], axis=0), reverse)
    turned = turned[:ROWS] + turned[ROWS : 2 * ROWS] + turned[2 * ROWS :]
    total = jnp.where(d < DEPTH // 2, turned, total)

    @pl.when(lower)
    def _():
        for row in range(ROWS):
            out_ref[ROWS - 1 - row : ROWS - row, :] = total[row : row + 1]

    @pl.when(jnp.logical_not(lower))
    def _():
        out_ref[...] = total

    for copy, there in zip(copies, has):
        pl.when(there)(copy.wait_send)
    pltpu.make_async_copy(csend.at[pl.ds(0, 2 * GROUP - 1)], csend.at[pl.ds(0, 2 * GROUP - 1)], cs).wait()
    pltpu.make_async_copy(xsend.at[pl.ds(0, 2 * GROUP - 1)], xsend.at[pl.ds(0, 2 * GROUP - 1)], xs).wait()
    pltpu.make_async_copy(gsend.at[pl.ds(0, RING - 1)], gsend.at[pl.ds(0, RING - 1)], gs).wait()


def solution(mesh):
    wide, mixed, tall = basis()

    def step(level_set, contrast):
        vmem = pl.BlockSpec(memory_space=pltpu.VMEM)
        anywhere = pl.BlockSpec(memory_space=pl.ANY)
        dma = pltpu.SemaphoreType.DMA
        return pl.pallas_call(
            kernel,
            out_shape=jax.ShapeDtypeStruct((ROWS, 128), F32),
            in_specs=[anywhere] * 5,
            out_specs=vmem,
            scratch_shapes=[
                pltpu.VMEM((2, ROWS, NX), F32),
                pltpu.SMEM((2,), F32),
                pltpu.VMEM((2, ROWS, NX), F32),
                pltpu.VMEM((2, ROWS, NX), F32),
                pltpu.VMEM((2, HALF, NX), BF16),
                pltpu.VMEM((2, HALF, NX), BF16),
                pltpu.VMEM((2, NX, HALF), BF16),
                pltpu.VMEM((2, ROWS, NX), F32),
                pltpu.VMEM((2, 16, 128), F32),
                pltpu.VMEM((2, 16, 128), F32),
                pltpu.VMEM((2 * GROUP, 8, 128), F32),
                pltpu.VMEM((2 * GROUP, 8, 128), F32),
                pltpu.VMEM((2, 128, NX), F32),
                pltpu.VMEM((128, NX), BF16),
                pltpu.VMEM((2 * GROUP, 4, 128), F32),
                pltpu.VMEM((2 * GROUP, 4, 128), F32),
                pltpu.VMEM((2 * ROWS, NX), F32),
                pltpu.VMEM((RING, 8, 128), F32),
                pltpu.VMEM((RING, 8, 128), F32),
                dma(()), dma(()), dma((2,)), dma((2,)), dma((2,)), dma((4,)), dma((4,)),
                dma(()), dma((2,)), dma(()), dma(()), dma(()), dma(()), pltpu.SemaphoreType.REGULAR((6,)),
            ],
            compiler_params=pltpu.CompilerParams(
                collective_id=0, has_side_effects=True, vmem_limit_bytes=55176 * 1024
            ),
        )(level_set, contrast, jnp.asarray(wide), jnp.asarray(mixed), jnp.asarray(tall))

    return jax.shard_map(
        step,
        mesh=mesh,
        in_specs=(P("depth", "plan", None), P("depth")),
        out_specs=P("plan", "depth"),
        check_vma=False,
    )
```

```python
import functools
import math

import jax
import jax.numpy as jnp
import ml_dtypes
import numpy as np
from jax import lax
from jax.experimental import pallas as pl
from jax.experimental.pallas import tpu as pltpu
from jax.sharding import PartitionSpec as P

MESH = pl.DeviceIdType.MESH
F32 = jnp.float32
BF16 = jnp.bfloat16

NX = 1024
HALF = NX // 2
LAYERS = 16
DEPTH = 8
PLAN = 64
ROWS = NX // PLAN
GROUP = 32
RING = 16
COEF = 2 * NX // GROUP
SHARE = COEF // 2

bend_weight = 0.5
grav_scale = 0.05
top_depth = 0.0
thickness = 1.0


def basis():
    j = np.arange(HALF, dtype=np.float64)[:, None] + 0.5
    v = np.arange(NX, dtype=np.float64)[None, :]
    table = np.cos(np.pi * v * j / NX)
    high = table.astype(ml_dtypes.bfloat16)
    low = (table - high.astype(np.float64)).astype(ml_dtypes.bfloat16)
    wide = np.stack([high, low])
    order = np.arange(HALF).reshape(GROUP, 2, ROWS // 2).transpose(1, 0, 2).reshape(-1)
    return wide, np.ascontiguousarray(wide[:, order]), np.ascontiguousarray(np.swapaxes(wide, 1, 2))


def alternating(shape):
    return 1.0 - 2.0 * lax.rem(lax.broadcasted_iota(jnp.int32, shape, 1), 2).astype(F32)


def flux(step):
    return step * lax.rsqrt(1.0 + step * step)


def flip(value, axis, size):
    index = lax.broadcasted_iota(jnp.int32, value.shape, axis)
    step = size // 2
    value = pltpu.roll(value, step, axis)
    while step > 1:
        step //= 2
        up = pltpu.roll(value, step, axis)
        down = pltpu.roll(value, size - step, axis)
        value = jnp.where((index & step) != 0, up, down)
    return value


def flip_lanes(value):
    blocks = value.shape[1] // 128
    parts = [flip(value[:, 128 * k : 128 * (k + 1)], 1, 128) for k in reversed(range(blocks))]
    return jnp.concatenate(parts, axis=1) if blocks > 1 else parts[0]


def split(value):
    high = value.astype(BF16)
    low = (value - high.astype(F32)).astype(BF16)
    return high, low


def matmul(a, b):
    return jnp.dot(a, b, preferred_element_type=F32)


def pair(value):
    return jnp.concatenate(split(value), axis=0)


def table_right(both, high_table, low_table):
    n = both.shape[0] // 2
    product = matmul(both, high_table)
    return product[:n] + product[n:] + matmul(both[:n], low_table)


def regroup(parts):
    lane = lax.broadcasted_iota(jnp.int32, parts[0].shape, 1)
    early, even = lane < 64, lax.rem(lane, 64) < 32
    wide = [jnp.where(early, parts[g], pltpu.roll(parts[g + 2], 64, 1)) for g in range(2)]
    wide += [jnp.where(early, pltpu.roll(parts[g], 64, 1), parts[g + 2]) for g in range(2)]
    out = []
    for first, second in (wide[:2], wide[2:]):
        out.append(jnp.where(even, first, pltpu.roll(second, 32, 1)))
        out.append(jnp.where(even, pltpu.roll(first, 96, 1), second))
    return out


def kernel(
    ls_hbm, con_hbm, wide_hbm, mixed_hbm, tall_hbm, out_ref,
    ls_ref, con_ref, own, part_density, wide, mixed, tall, zhalo, rsend, rhalo, csend, sbuf, rsp, acc, pst, xsend, cbuf, coefs, gsend, gbuf,
    ls_sem, con_sem, wide_sem, mixed_sem, tall_sem, hs, hr, cs, cr, xs, xr, gs, gr, news,
):
    d = lax.axis_index("depth")
    p = lax.axis_index("plan")
    core = lax.rem(p, 2)
    zh = lax.rem(lax.div(p, 2), 2)
    q = lax.div(p, 4) * 2 + core
    z = zh * DEPTH + d
    lower = p < PLAN // 2

    x, y = lax.div(p, 16), lax.rem(lax.div(p, 4), 4)
    kind_own, cut_own = lax.div(y, 2), lax.rem(x + y, 2)
    set_own = 2 * kind_own + cut_own
    coef_block = 8 * set_own + 2 * x + core
    parity = lax.rem(d, 2)
    mate = d + 1 - 2 * parity
    order = (2, 6, 4, 3, 7, 5, 1, 0)
    turns = [lax.rem(2 * x + core + k, 8) for k in order]
    places = [
        [16 * lax.div(t, 2) + 4 * lax.rem(lax.div(t, 2) + cut, 2) + 2 * zh + lax.rem(t, 2) for t in turns]
        for cut in range(2)
    ]

    def at_z(other):
        return (lax.rem(other, DEPTH), p + 2 * (lax.div(other, DEPTH) - zh))

    ls_copy = pltpu.make_async_copy(ls_hbm, ls_ref, ls_sem)
    con_copy = pltpu.make_async_copy(con_hbm, con_ref, con_sem)
    ls_copy.start()
    con_copy.start()
    wide_copies = [pltpu.make_async_copy(wide_hbm.at[n], wide.at[n], wide_sem.at[n]) for n in range(2)]
    mixed_copies = [pltpu.make_async_copy(mixed_hbm.at[n], mixed.at[n], mixed_sem.at[n]) for n in range(2)]
    tall_copies = [pltpu.make_async_copy(tall_hbm.at[n], tall.at[n], tall_sem.at[n]) for n in range(2)]
    for copy in wide_copies:
        copy.start()

    barrier = pltpu.get_barrier_semaphore()

    def greet(target):
        pl.semaphore_signal(barrier, inc=1, device_id=target, device_id_type=MESH)

    has = (d < DEPTH - 1, d > 0, p < PLAN - 1, p > 0)
    gets = (d > 0, d < DEPTH - 1, p > 0, p < PLAN - 1)
    outer = jnp.where(core == 0, p - 1, p + 1)
    has_outer = (outer >= 0) & (outer < PLAN)
    x_line = [(d, p + 16 * (lax.rem(x + k, 4) - x)) for k in (1, 3, 2)]
    y_line = [(d, p + 4 * (lax.rem(y + k, 4) - y)) for k in (1, 3, 2)]
    buddy = (d, p + 1 - 2 * core)

    def z_pair(k):
        return [at_z(lax.rem(z + away, RING)) for away in (k, RING - k)]

    for target in z_pair(1) + [buddy]:
        greet(target)
    pl.when(has_outer)(lambda: greet((d, outer)))
    for target in x_line + y_line:
        greet(target)

    def tell(number, targets):
        for target in targets:
            pl.semaphore_signal(news.at[number], inc=1, device_id=target, device_id_type=MESH)

    def hear(number, count):
        pl.semaphore_wait(news.at[number], count)

    ls_copy.wait()
    con_copy.wait()

    for layer in range(2):
        value = ls_ref[layer]
        value = jnp.where(lower, flip(value, 0, ROWS), value)
        own[layer, :, :HALF] = value[:, HALF:]
        own[layer, :, HALF:] = flip_lanes(value[:, :HALF])

    for layer in range(2):
        for k in range(8):
            spot = layer * 8 + k
            top = own[layer, 0:1, 128 * k : 128 * (k + 1)]
            bottom = own[layer, ROWS - 1 : ROWS, 128 * k : 128 * (k + 1)]
            rsend[0, spot : spot + 1, :] = jnp.where(lower, bottom, top)
            rsend[1, spot : spot + 1, :] = jnp.where(lower, top, bottom)

    pl.semaphore_wait(barrier, 9 + has_outer.astype(jnp.int32))

    def halo(source, target, number, device):
        return pltpu.make_async_remote_copy(
            src_ref=source, dst_ref=target, send_sem=hs.at[number], recv_sem=hr.at[number],
            device_id=device, device_id_type=MESH,
        )

    z_up = halo(own.at[1], zhalo.at[0], 0, (d + 1, p))
    z_down = halo(own.at[0], zhalo.at[1], 1, (d - 1, p))
    r_up = halo(rsend.at[1], rhalo.at[0], 2, (d, p + 1))
    r_down = halo(rsend.at[0], rhalo.at[1], 3, (d, p - 1))
    lands = (zhalo.at[0], zhalo.at[1], rhalo.at[0], rhalo.at[1])
    copies = (z_up, z_down, r_up, r_down)
    for copy, there in zip(copies, has):
        pl.when(there)(copy.start)
    tell(0, y_line)
    tell(1, z_pair(1))
    for copy in mixed_copies + tall_copies:
        copy.start()
    for land, comes in zip(lands, gets):

        @pl.when(jnp.logical_not(comes))
        def _(land=land):
            land[...] = jnp.zeros(land.shape, F32)

    row_id = lax.broadcasted_iota(jnp.int32, (ROWS, NX), 0)
    lane_id = lax.broadcasted_iota(jnp.int32, (ROWS, HALF), 1)
    field = [own[0], own[1]]
    middle = flux(field[1] - field[0])
    for layer in range(2):
        centre = field[layer]
        bend = -middle if layer else middle
        inner_flux = flux(pltpu.roll(centre, 1, 0) - centre)
        bend = bend + jnp.where(row_id == 0, 0.0, inner_flux)
        bend = bend - jnp.where(row_id == ROWS - 1, 0.0, pltpu.roll(inner_flux, ROWS - 1, 0))
        sides = centre[:, :HALF], centre[:, HALF:]
        across = []
        for side in range(2):
            here = sides[side]
            inside = jnp.where(lane_id == 0, sides[1 - side], pltpu.roll(here, 1, 1))
            inner_flux = flux(inside - here)
            outside = jnp.where(lane_id == HALF - 1, flux(here), pltpu.roll(inner_flux, HALF - 1, 1))
            across.append(inner_flux - outside)
        bend = bend + jnp.concatenate(across, axis=1)
        part_density[layer] = con_ref[layer] * (0.5 * (1.0 + jnp.tanh(centre))) + bend_weight * bend

    hear(0, 3)
    tell(2, [buddy])

    def respond(start):
        row = lax.broadcasted_iota(jnp.int32, (64, 128), 0)
        col = lax.broadcasted_iota(jnp.int32, (64, 128), 1) + start
        place = lax.rem(coef_block, GROUP // 2) * COEF + parity * SHARE + lax.rem(row, SHARE)
        v = jnp.where(kind_own == 1, NX - place, place).astype(F32)
        u = jnp.where(row >= SHARE, NX - col, col).astype(F32)
        scale = 2.0 * math.pi * grav_scale * thickness / (4.0 * NX * NX)
        weight = jnp.where(place == 0, scale, 2.0 * scale) * jnp.where(col == 0, 1.0, 2.0)
        kappa = jnp.sqrt(u * u + v * v) * (2.0 * math.pi / (2 * NX))
        next_layer = jnp.exp(-thickness * kappa)
        for cross, depth in enumerate((d, mate)):
            top = top_depth + (2.0 * depth.astype(F32) + 0.5) * thickness
            first = jnp.exp(-top * kappa) * weight
            second = first * next_layer
            for n, value in enumerate((first[:SHARE], second[:SHARE], first[SHARE:], second[SHARE:])):
                rsp[cross, SHARE * n : SHARE * (n + 1), start : start + 128] = value

    for k in range(NX // 128):
        respond(128 * k)

    hear(2, 1)
    hear(1, 2)
    tell(3, [(mate, p)])
    for layer in range(2):
        pl.when(gets[layer])(copies[layer].wait_recv)
    for layer in range(2):
        part_density[layer] += bend_weight * flux(zhalo[layer] - own[layer])
    for number in (2, 3):
        pl.when(gets[number])(copies[number].wait_recv)
    even, odd = [], []
    for layer in range(2):
        centre = own[layer]
        here = slice(layer * 8, layer * 8 + 8)
        top = jnp.where(lower, rhalo[1, here, :], rhalo[0, here, :])
        bottom = jnp.where(lower, rhalo[0, here, :], rhalo[1, here, :])
        tops = [jnp.broadcast_to(top[k : k + 1], (ROWS, 128)) for k in range(8)]
        bottoms = [jnp.broadcast_to(bottom[k : k + 1], (ROWS, 128)) for k in range(8)]
        beside = jnp.where(row_id == 0, jnp.concatenate(tops, axis=1), jnp.concatenate(bottoms, axis=1))
        outer_rows = (row_id == 0) | (row_id == ROWS - 1)
        density = part_density[layer] + jnp.where(outer_rows, bend_weight * flux(beside - centre), 0.0)
        even.append(density[:, :HALF] + density[:, HALF:])
        odd.append((density[:, :HALF] - density[:, HALF:]) * alternating((ROWS, HALF)))

    block = jnp.where(lower, PLAN // 2 - 1 - p, p - PLAN // 2)
    hear(3, 1)
    tell(4, z_pair(2))
    for copy in wide_copies:
        copy.wait()

    def send_coef(group, k, cross):
        member = 1 - parity if cross else parity
        return pltpu.make_async_remote_copy(
            src_ref=csend.at[2 * (8 * group + turns[k]) + member], dst_ref=sbuf.at[GROUP * cross + block],
            send_sem=cs, recv_sem=cr.at[cross],
            device_id=(mate if cross else d, 8 * (group // 2) + places[group % 2][k]), device_id_type=MESH,
        )

    both = pair(jnp.concatenate(even + odd, axis=0))
    for cut in range(2):
        cols = slice(HALF * cut, HALF * (cut + 1))
        coef = table_right(both, wide[0, :, cols], wide[1, :, cols])
        for kind in range(2):
            start = kind * 16 + 8 * cut
            for m in range(4):
                lanes = slice(128 * m, 128 * (m + 1))
                starts = [2 * ROWS * kind + ROWS * layer + 8 * half for half in range(2) for layer in range(2)]
                for t, value in enumerate(regroup([coef[n : n + 8, lanes] for n in starts])):
                    csend[2 * start + 4 * m + t] = value
        for k in range(7):
            for kind in range(2):
                send_coef(2 * kind + cut, k, 0).start()
        for k in range(8):
            for kind in range(2):
                send_coef(2 * kind + cut, k, 1).start()
    for group in range(4):
        pl.when(group != set_own)(send_coef(group, 7, 0).start)

    hear(4, 2)
    tell(5, z_pair(4))
    sbuf[block] = csend[2 * coef_block + parity]
    for copy in mixed_copies + tall_copies:
        copy.wait()
    side = lax.rem(lax.div(lax.broadcasted_iota(jnp.int32, (64, HALF), 1), 16), 2)
    sign = jnp.where(side == zh, 1.0, -1.0) * alternating((64, HALF))
    step = 256
    for cross in range(2):
        landed = sbuf.at[pl.ds(GROUP * cross, GROUP - 1 + cross)]
        pltpu.make_async_copy(landed, landed, cr.at[cross]).wait()
        value = sbuf[GROUP * cross : GROUP * (cross + 1)].reshape(HALF // 2, 128).T
        value = jnp.concatenate([value[:64], value[64:]], axis=1)
        both = pair(jnp.concatenate([value, value * sign], axis=0))
        for k in range(NX // step):
            here = slice(k * step, (k + 1) * step)
            coef = table_right(both, mixed[0, :, here], mixed[1, :, here]) * rsp[cross, :, here]
            parts = [coef[SHARE * n : SHARE * (n + 1)] for n in range(4)]
            coef = jnp.concatenate([parts[0] + parts[1], parts[2] + parts[3]], axis=0)
            if cross:
                pst[:, here] = pair(coef + acc[:, here])
            else:
                acc[:, here] = coef

    low = 2 * lax.rem(y, 2) + core
    x_turns = [lax.rem(x + k, 4) for k in range(4)]
    low_turns = [lax.rem(low + k, 4) for k in range(4)]
    low_places = [4 * lax.div(t, 2) + lax.rem(t, 2) + 2 * zh for t in low_turns]

    def send_rows(part, r, k, cross):
        upper = lax.div(x_turns[r], 2)
        upper = upper if part else 1 - upper
        member = 1 - parity if cross else parity
        return pltpu.make_async_remote_copy(
            src_ref=xsend.at[2 * (8 * x_turns[r] + 4 * upper + low_turns[k]) + member],
            dst_ref=cbuf.at[2 * coef_block + parity], send_sem=xs, recv_sem=xr,
            device_id=(mate if cross else d, 16 * x_turns[r] + 8 * upper + low_places[k]), device_id_type=MESH,
        )

    lane = lax.broadcasted_iota(jnp.int32, (8, 128), 1)
    early, even_lane = lane < 64, lax.rem(lane, 64) < 32
    def columns(part):
        cols = slice(128 * part, 128 * part + 128), slice(128 * part + 256, 128 * part + 384)
        return [jnp.concatenate([tall[n, :, col] for col in cols], axis=1) for n in range(2)]

    for part in range(2):
        value = table_right(pst[...], *columns(part))
        evens, odds = value[:SHARE], value[SHARE:] * alternating((SHARE, 256))
        plus, minus = evens + odds, evens - odds
        value = jnp.concatenate([plus, minus, plus, minus], axis=0).T
        for g in range(4):
            chunk = 2 * part + 4 * (g // 2) + g % 2
            for member in range(2):
                ups, downs = [], []
                for n in range(4):
                    start = ROWS * (4 * g + n) + 8 * member
                    rows = value[start : start + 8]
                    later = pltpu.roll(rows, 4, 0)
                    ups.append(jnp.where(even_lane, rows, pltpu.roll(later, 32, 1)))
                    downs.append(jnp.where(even_lane, pltpu.roll(rows, 32, 1), later))
                for spot, one, two in (
                    (2 * (8 + chunk), ups[0], ups[2]),
                    (2 * (8 + chunk) + 1, ups[1], ups[3]),
                    (2 * (7 - chunk), downs[3], downs[1]),
                    (2 * (7 - chunk) + 1, downs[2], downs[0]),
                ):
                    xsend[2 * spot + member] = jnp.where(early, one, two)[:4]

        for r in (1, 3, 2, 0):
            for k in range(4):
                send_rows(part, r, k, 1).start()
                if r or k:
                    send_rows(part, r, k, 0).start()
    upper_own = lax.rem(lax.div(x, 2) + lax.div(y, 2), 2)
    pl.when(upper_own == 0)(send_rows(0, 0, 0, 0).start)
    pl.when(upper_own == 1)(send_rows(1, 0, 0, 0).start)

    hear(5, 2)
    cbuf[2 * coef_block + parity] = xsend[2 * q + parity]
    landed = cbuf.at[pl.ds(0, 2 * GROUP - 1)]
    pltpu.make_async_copy(landed, landed, xr).wait()

    def send_field(far, depth):
        row = 1 - zh if far else zh
        return pltpu.make_async_remote_copy(
            src_ref=gsend.at[DEPTH * row + depth], dst_ref=gbuf.at[z], send_sem=gs, recv_sem=gr,
            device_id=(depth, p + 2 - 4 * zh if far else p), device_id_type=MESH,
        )

    steps = [lax.rem(lax.div(d, 2) + k, 4) for k in range(4)]
    depths = ([2 * t + 1 - lax.div(t, 2) for t in steps], [2 * t + lax.div(t, 2) for t in steps])

    for m in range(2 * NX // 128):
        parts = regroup([cbuf[4 * m + t] for t in range(4)])
        lanes = slice(128 * (m % 8), 128 * (m % 8 + 1))
        for g in range(4):
            start = ROWS * (m // 8) + 4 * g
            coefs[start : start + 4, lanes] = parts[g]
    both = pair(coefs[...])
    for cut in range(2):
        value = table_right(both, *columns(cut))
        evens, odds = value[:ROWS], value[ROWS:] * alternating((ROWS, 256))
        plus = evens + odds
        minus = evens - odds
        for half in range(2):
            rows = slice(8 * half, 8 * (half + 1))
            for n in range(2):
                lanes = slice(128 * n, 128 * (n + 1))
                gsend[DEPTH * half + 4 + cut + 2 * n] = plus[rows, lanes]
                gsend[DEPTH * half + 3 - cut - 2 * n] = minus[rows, lanes]
        for k in range(4):
            send_field(True, depths[cut][k]).start()
        for k in range(1, 4):
            send_field(False, depths[cut][k]).start()
    for cut in range(2):
        pl.when(depths[cut][0] != d)(send_field(False, depths[cut][0]).start)

    gbuf[z] = gsend[z]
    pltpu.make_async_copy(gbuf.at[pl.ds(0, RING - 1)], gbuf.at[pl.ds(0, RING - 1)], gr).wait()
    totals = [gbuf[0], gbuf[1]]
    for other in range(2, RING):
        totals[other % 2] = totals[other % 2] + gbuf[other]
    total = jnp.concatenate(totals, axis=0)
    across = lax.broadcasted_iota(jnp.int32, (128, 128), 0) + lax.broadcasted_iota(jnp.int32, (128, 128), 1)
    reverse = jnp.where(across == 127, 1.0, 0.0).astype(BF16)
    high, rest = split(total)
    low = (total - high.astype(F32) - rest.astype(F32)).astype(BF16)
    turned = matmul(jnp.concatenate([high, rest, low], axis=0), reverse)
    turned = turned[:ROWS] + turned[ROWS : 2 * ROWS] + turned[2 * ROWS :]
    total = jnp.where(d < DEPTH // 2, turned, total)

    @pl.when(lower)
    def _():
        for row in range(ROWS):
            out_ref[ROWS - 1 - row : ROWS - row, :] = total[row : row + 1]

    @pl.when(jnp.logical_not(lower))
    def _():
        out_ref[...] = total

    for copy, there in zip(copies, has):
        pl.when(there)(copy.wait_send)
    pltpu.make_async_copy(csend.at[pl.ds(0, 2 * GROUP - 1)], csend.at[pl.ds(0, 2 * GROUP - 1)], cs).wait()
    pltpu.make_async_copy(xsend.at[pl.ds(0, 2 * GROUP - 1)], xsend.at[pl.ds(0, 2 * GROUP - 1)], xs).wait()
    pltpu.make_async_copy(gsend.at[pl.ds(0, RING - 1)], gsend.at[pl.ds(0, RING - 1)], gs).wait()


def solution(mesh):
    wide, mixed, tall = basis()

    def step(level_set, contrast):
        vmem = pl.BlockSpec(memory_space=pltpu.VMEM)
        anywhere = pl.BlockSpec(memory_space=pl.ANY)
        dma = pltpu.SemaphoreType.DMA
        return pl.pallas_call(
            kernel,
            out_shape=jax.ShapeDtypeStruct((ROWS, 128), F32),
            in_specs=[anywhere] * 5,
            out_specs=vmem,
            scratch_shapes=[
                pltpu.VMEM((2, ROWS, NX), F32),
                pltpu.SMEM((2,), F32),
                pltpu.VMEM((2, ROWS, NX), F32),
                pltpu.VMEM((2, ROWS, NX), F32),
                pltpu.VMEM((2, HALF, NX), BF16),
                pltpu.VMEM((2, HALF, NX), BF16),
                pltpu.VMEM((2, NX, HALF), BF16),
                pltpu.VMEM((2, ROWS, NX), F32),
                pltpu.VMEM((2, 16, 128), F32),
                pltpu.VMEM((2, 16, 128), F32),
                pltpu.VMEM((2 * GROUP, 8, 128), F32),
                pltpu.VMEM((2 * GROUP, 8, 128), F32),
                pltpu.VMEM((2, 128, NX), F32),
                pltpu.VMEM((64, NX), F32),
                pltpu.VMEM((128, NX), BF16),
                pltpu.VMEM((2 * GROUP, 4, 128), F32),
                pltpu.VMEM((2 * GROUP, 4, 128), F32),
                pltpu.VMEM((2 * ROWS, NX), F32),
                pltpu.VMEM((RING, 8, 128), F32),
                pltpu.VMEM((RING, 8, 128), F32),
                dma(()), dma(()), dma((2,)), dma((2,)), dma((2,)), dma((4,)), dma((4,)),
                dma(()), dma((2,)), dma(()), dma(()), dma(()), dma(()), pltpu.SemaphoreType.REGULAR((6,)),
            ],
            compiler_params=pltpu.CompilerParams(
                collective_id=0, has_side_effects=True, vmem_limit_bytes=55176 * 1024
            ),
        )(level_set, contrast, jnp.asarray(wide), jnp.asarray(mixed), jnp.asarray(tall))

    return jax.shard_map(
        step,
        mesh=mesh,
        in_specs=(P("depth", "plan", None), P("depth")),
        out_specs=P("plan", "depth"),
        check_vma=False,
    )
```
